128 devices in a mesh: fsdp: 8 (over x, z_hi), ctx: 4 (over z_lo, core), tp: 4 (over y).
Axes of the slice: x: 4, y: 4, z: 4 (z_hi: 2, z_lo: 2; z = z_hi * 2 + z_lo), core: 2. Of those that a mesh axis runs over, the one named last changes fastest.
Arguments:
- hidden_in: bfloat16 [8192, 1536], P(('fsdp', 'ctx')), may hold values from -6 to 6
- cotangent: bfloat16 [8192, 1536], P(('fsdp', 'ctx')), may hold values from -6 to 6
- seq_lengths: int32 [32], replicated, may hold values from 1 to 1021, as said below
- deal_order: int32 [8192], replicated, may hold values from 0 to 8191, as said below
- mixer_gain: bfloat16 [1536], P(('fsdp', 'ctx')), may hold values from 0.5 to 1.5
- mixer_project: bfloat16 [1536, 3, 1536], P(('fsdp', 'ctx'), None, 'tp'), may hold values from -0.15625 to 0.15625
- mixer_kernel: bfloat16 [3, 1536], replicated, may hold values from -2.390625 to 2.390625
- mixer_output: bfloat16 [1536, 1536], P('tp', ('fsdp', 'ctx')), may hold values from -0.15625 to 0.15625
- first_gain: bfloat16 [1536], P(('fsdp', 'ctx')), may hold values from 0.5 to 1.5
- first_gateup: bfloat16 [1536, 2, 6912], P(('fsdp', 'ctx'), None, 'tp'), may hold values from -0.15625 to 0.15625
- first_down: bfloat16 [6912, 1536], P('tp', ('fsdp', 'ctx')), may hold values from -0.078125 to 0.078125
- attend_gain: bfloat16 [1536], P(('fsdp', 'ctx')), may hold values from 0.5 to 1.5
- attend_project: bfloat16 [1536, 2560], P(('fsdp', 'ctx'), 'tp'), may hold values from -0.15625 to 0.15625
- query_gain: bfloat16 [64], replicated, may hold values from 0.5 to 1.5
- key_gain: bfloat16 [64], replicated, may hold values from 0.5 to 1.5
- attend_output: bfloat16 [1536, 1536], P('tp', ('fsdp', 'ctx')), may hold values from -0.875 to 0.875
- second_gain: bfloat16 [1536], P(('fsdp', 'ctx')), may hold values from 0.5 to 1.5
- second_gateup: bfloat16 [1536, 2, 6912], P(('fsdp', 'ctx'), None, 'tp'), may hold values from -0.15625 to 0.15625
- second_down: bfloat16 [6912, 1536], P('tp', ('fsdp', 'ctx')), may hold values from -0.078125 to 0.078125
Outputs:
- layer_out: bfloat16 [8192, 1536], P(('fsdp', 'ctx'))
- input_gradient: bfloat16 [8192, 1536], P(('fsdp', 'ctx'))
- mixer_gain_gradient: float32 [1536], P(('fsdp', 'ctx'))
- mixer_project_gradient: float32 [1536, 3, 1536], P(('fsdp', 'ctx'), None, 'tp')
- mixer_kernel_gradient: float32 [3, 1536], replicated
- mixer_output_gradient: float32 [1536, 1536], P('tp', ('fsdp', 'ctx'))
- first_gain_gradient: float32 [1536], P(('fsdp', 'ctx'))
- first_gateup_gradient: float32 [1536, 2, 6912], P(('fsdp', 'ctx'), None, 'tp')
- first_down_gradient: float32 [6912, 1536], P('tp', ('fsdp', 'ctx'))
- attend_gain_gradient: float32 [1536], P(('fsdp', 'ctx'))
- attend_project_gradient: float32 [1536, 2560], P(('fsdp', 'ctx'), 'tp')
- query_gain_gradient: float32 [64], replicated
- key_gain_gradient: float32 [64], replicated
- attend_output_gradient: float32 [1536, 1536], P('tp', ('fsdp', 'ctx'))
- second_gain_gradient: float32 [1536], P(('fsdp', 'ctx'))
- second_gateup_gradient: float32 [1536, 2, 6912], P(('fsdp', 'ctx'), None, 'tp')
- second_down_gradient: float32 [6912, 1536], P('tp', ('fsdp', 'ctx'))
The draws below stay inside these ranges and needn't reach their ends.
Inputs may be any that keep to these rules, and one draw needn't show every extreme that they name: `seq_lengths`: sequences 4 * g to 4 * g + 3 fill dealt rows g * 1024 to (g + 1) * 1024 - 1 exactly; in each such group one sequence covers all but at most 128 of its rows. deal_order is a permutation. Dealt rows come in aligned blocks of 8; each block holds 8 consecutive arrival tokens in order, starting at a multiple of 8; the 256 dealt rows of each device take exactly one block from the 256 arrival rows of every device.
All inputs are finite; a program needn't handle non-finite values.
Results may differ from the reference program's by a relative error of at most 0.02.
The reference program's roundings to bfloat16 on the way count: a program that leaves them out, or rounds other values in their place, can miss the bound.
Values may be sent and summed in bfloat16 or wider, within the bound.
No kernel may reach another device: no remote copies, remote signals or barrier semaphores. Data moves between devices by JAX's collectives and lax.ppermute only.
A program may use at most 256 MiB of HBM per device.

```python
import jax
import jax.numpy as jnp
from jax import lax

D = 1536
FF = 6912
H = 24
KVH = 8
HD = 64
KERNEL = 3
TOK_DEV = 256
SEQ_G = 4
SHARDS = 32
PIECE = 8
GROUP = 1024
TOKENS = 8192
N_FSDP = 8
N_CTX = 4


def draw_seq_lengths(key, part):
    key = jax.random.fold_in(key, 7)
    subkeys = jax.random.split(key, 3)
    spare_rows = jax.random.randint(subkeys[0], (N_FSDP,), SEQ_G - 1, TOK_DEV // 2 + 1)
    spare_rows = spare_rows.at[0].set(SEQ_G - 1)
    random_bits = jax.random.randint(subkeys[1], (N_FSDP, SEQ_G), 0, 1 << 20)
    remaining = spare_rows
    shorts = []
    for j in range(SEQ_G - 2):
        parts_left = SEQ_G - 1 - j
        short_size = 1 + random_bits[:, j] % (remaining - parts_left + 1)
        shorts.append(short_size)
        remaining = remaining - short_size
    shorts.append(remaining)
    shorts = jnp.stack(shorts, axis=1)
    longest = TOK_DEV * N_CTX - spare_rows
    long_slot = jax.random.randint(subkeys[2], (N_FSDP, 1), 0, SEQ_G)
    slot_index = jnp.arange(SEQ_G)[None, :]
    short_pick = jnp.clip(slot_index - (slot_index > long_slot).astype(jnp.int32), 0, SEQ_G - 2)
    picked = jnp.take_along_axis(shorts, jnp.broadcast_to(short_pick, (N_FSDP, SEQ_G)), axis=1)
    result = jnp.where(slot_index == long_slot, longest[:, None], picked)
    return result.reshape(-1).astype(jnp.int32)


def draw_deal_order(key, part):
    key = jax.random.fold_in(key, 5)
    subkeys = jax.random.split(key, 2)
    source_order = jax.vmap(lambda subkey: jax.random.permutation(subkey, SHARDS))(jax.random.split(subkeys[0], SHARDS))
    piece_order = jax.vmap(lambda subkey: jax.random.permutation(subkey, SHARDS))(jax.random.split(subkeys[1], SHARDS))
    dealt_rows = jnp.arange(TOKENS)
    d = dealt_rows // TOK_DEV
    q = dealt_rows % TOK_DEV // PIECE
    i = dealt_rows % PIECE
    s = source_order[d, q]
    l = piece_order[s, d]
    return (s * TOK_DEV + l * PIECE + i).astype(jnp.int32)


def block_levels(own_key, extent, shards, smallest, largest):
    def one(position, shards_of):
        steps = jax.random.uniform(jax.random.fold_in(jax.random.fold_in(own_key, 6), position), (shards_of,), jnp.float32, smallest / len(shards), largest / len(shards))
        return jnp.repeat(jnp.exp(steps), extent[position] // shards_of).reshape((-1,) + (1,) * (len(extent) - position - 1))

    gain = one(*shards[0])
    for cut in shards[1:]:
        gain = gain * one(*cut)
    return gain


def normal_values(key, extent, spread, reach, pieces=(), kind=jnp.bfloat16):
    gain = block_levels(key, extent, pieces, -0.22, 0.18) if pieces else 1.0
    entries = jax.random.normal(key, extent, jnp.float32) * spread * gain
    return jnp.minimum(jnp.maximum(entries, -reach), reach).astype(kind)


def setup_inputs(seed: int = 0) -> dict:
    streams_of = jax.random.split(jax.random.key(seed), 20)
    hidden_in = normal_values(streams_of[0], (TOKENS, D), 1.0, 6.0, ((0, 32),))
    cotangent = normal_values(streams_of[1], (TOKENS, D), 1.0, 6.0, ((0, 32),))
    seq_lengths = draw_seq_lengths(jax.random.fold_in(streams_of[19], 71), 0)
    deal_order = draw_deal_order(jax.random.fold_in(streams_of[19], 71), 0)
    mixer_gain = jnp.clip(1.0 + 0.1 * jax.random.normal(streams_of[4], (D,), jnp.float32), 0.5, 1.5).astype(jnp.bfloat16)
    mixer_project = normal_values(streams_of[5], (D, 3, D), D ** -0.5, 0.15625, ((0, 32), (2, 4)))
    mixer_kernel = normal_values(streams_of[6], (KERNEL, D), 0.6, 2.390625)
    mixer_output = normal_values(streams_of[7], (D, D), D ** -0.5, 0.15625, ((0, 4), (1, 32)))
    first_gain = jnp.clip(1.0 + 0.1 * jax.random.normal(streams_of[8], (D,), jnp.float32), 0.5, 1.5).astype(jnp.bfloat16)
    first_gateup = normal_values(streams_of[9], (D, 2, FF), D ** -0.5, 0.15625, ((0, 32), (2, 4)))
    first_down = normal_values(streams_of[10], (FF, D), FF ** -0.5, 0.078125, ((0, 4), (1, 32)))
    attend_gain = jnp.clip(1.0 + 0.1 * jax.random.normal(streams_of[11], (D,), jnp.float32), 0.5, 1.5).astype(jnp.bfloat16)
    attend_project = normal_values(streams_of[12], (D, KVH * (H // KVH + 2) * HD), D ** -0.5, 0.15625, ((0, 32), (1, 4)))
    query_gain = jnp.clip(1.0 + 0.1 * jax.random.normal(streams_of[13], (HD,), jnp.float32), 0.5, 1.5).astype(jnp.bfloat16)
    key_gain = jnp.clip(1.0 + 0.1 * jax.random.normal(streams_of[14], (HD,), jnp.float32), 0.5, 1.5).astype(jnp.bfloat16)
    attend_output = normal_values(streams_of[15], (H * HD, D), (H * HD // 32) ** -0.5, 0.875, ((0, 4), (1, 32)))
    second_gain = jnp.clip(1.0 + 0.1 * jax.random.normal(streams_of[16], (D,), jnp.float32), 0.5, 1.5).astype(jnp.bfloat16)
    second_gateup = normal_values(streams_of[17], (D, 2, FF), D ** -0.5, 0.15625, ((0, 32), (2, 4)))
    second_down = normal_values(streams_of[18], (FF, D), FF ** -0.5, 0.078125, ((0, 4), (1, 32)))
    return {"hidden_in": hidden_in, "cotangent": cotangent, "seq_lengths": seq_lengths, "deal_order": deal_order, "mixer_gain": mixer_gain, "mixer_project": mixer_project, "mixer_kernel": mixer_kernel, "mixer_output": mixer_output, "first_gain": first_gain, "first_gateup": first_gateup, "first_down": first_down, "attend_gain": attend_gain, "attend_project": attend_project, "query_gain": query_gain, "key_gain": key_gain, "attend_output": attend_output, "second_gain": second_gain, "second_gateup": second_gateup, "second_down": second_down}


EPSILON = 1e-05
ROPE_BASE = 1000000.0
NEGATIVE = -1e+30
HIGH = lax.Precision.HIGHEST

@jax.custom_vjp
def low(v):
    return lax.optimization_barrier(v.astype(jnp.bfloat16)).astype(jnp.float32)

@jax.custom_vjp
def low_back(v):
    return v

def low_keep(v):
    return (low(v), None)

def low_pass(kept, grad):
    return (grad,)

def back_keep(v):
    return (v, None)

def back_low(kept, grad):
    return (low(grad),)
low.defvjp(low_keep, low_pass)
low_back.defvjp(back_keep, back_low)

def normalize(values, scales):
    return values * lax.rsqrt(lax.optimization_barrier(jnp.mean(values * values, axis=-1, keepdims=True)) + EPSILON) * scales

def rotate(values, places):
    half_dim = values.shape[-1] // 2
    frequency = ROPE_BASE ** (-(jnp.arange(half_dim).astype(jnp.float32) * 2.0 / values.shape[-1]))
    angles = places.astype(jnp.float32)[:, None] * frequency[None, :]
    shape_out = (values.shape[0],) + (1,) * (values.ndim - 2) + (half_dim,)
    cosine = jnp.cos(angles).reshape(shape_out)
    sine_part = jnp.sin(angles).reshape(shape_out)
    first_half = values[..., :half_dim]
    second_half = values[..., half_dim:]
    return jnp.concatenate([first_half * cosine - second_half * sine_part, second_half * cosine + first_half * sine_part], axis=-1)

def locate(lengths, positions):
    seq_ends = jnp.cumsum(lengths)
    segment = lax.optimization_barrier(jnp.sum((positions[:, None] >= seq_ends[None, :]).astype(jnp.int32), axis=1))
    starts = seq_ends - lengths
    first_row = lax.optimization_barrier(jnp.sum(jnp.where(segment[:, None] == jnp.arange(lengths.shape[0]).astype(jnp.int32)[None, :], starts[None, :], 0), axis=1))
    return (segment, positions - first_row)

def shortconv(extended, kernel_in, segment):
    kernel_taps = kernel_in.shape[0]
    out_rows = extended.shape[0] - kernel_taps + 1
    result = kernel_in[0] * extended[kernel_taps - 1:]
    for t in range(1, kernel_taps):
        earlier = extended[kernel_taps - 1 - t:kernel_taps - 1 - t + out_rows]
        same_seq = (segment[kernel_taps - 1 - t:kernel_taps - 1 - t + out_rows] == segment[kernel_taps - 1:]).astype(jnp.float32)[:, None]
        result = result + kernel_in[t] * earlier * same_seq
    return result

def feed_forward(stream, scales, gate_weight, down_proj):
    normed = low(normalize(stream, scales))
    gate_up = low_back(jnp.einsum('td,dwf->twf', normed, gate_weight, precision=HIGH))
    active = low(jax.nn.silu(gate_up[:, 0]) * gate_up[:, 1])
    return stream + low_back(jnp.dot(active, down_proj, precision=HIGH))

def attend_group(group_block):
    query, key_rows, value_rows, segment, places = group_block
    scores = low_back(jnp.einsum('tkgd,nkd->kgtn', query, key_rows, precision=HIGH) * HD ** (-0.5))
    allowed = (segment[:, None] == segment[None, :]) & (places[None, :] <= places[:, None])
    softmax_rows = jax.nn.softmax(jnp.where(allowed, scores, NEGATIVE), axis=-1)
    attended = jnp.einsum('kgtn,nkd->tkgd', low(softmax_rows), value_rows, precision=HIGH)
    return low(low_back(attended)).reshape(query.shape[0], -1)

def forward(stream, segment, places, weights):
    mixer_gain, mixer_project, mixer_kernel, mixer_output, first_gain, first_gateup, first_down, attend_gain, attend_project, query_gain, key_gain, attend_output, second_gain, second_gateup, second_down = weights
    normed = low(normalize(stream, mixer_gain))
    projected = low_back(jnp.einsum('td,dwc->twc', normed, mixer_project, precision=HIGH))
    product = low(projected[:, 0] * projected[:, 2])
    kernel_taps = mixer_kernel.shape[0]
    extended = jnp.concatenate([jnp.zeros((kernel_taps - 1, product.shape[1]), product.dtype), product])
    segment_ext = jnp.concatenate([jnp.full((kernel_taps - 1,), -1, jnp.int32), segment])
    conv_out = shortconv(extended, mixer_kernel, segment_ext)
    gated_rows = low(projected[:, 1] * conv_out)
    stream = stream + low_back(jnp.dot(gated_rows, mixer_output, precision=HIGH))
    stream = feed_forward(stream, first_gain, first_gateup, first_down)
    normed = low(normalize(stream, attend_gain))
    groups = H // KVH
    projected = low_back(jnp.dot(normed, attend_project, precision=HIGH)).reshape(TOKENS, KVH, groups + 2, HD)
    query = low(rotate(normalize(projected[:, :, :groups], query_gain), places))
    key_rows = low(rotate(normalize(projected[:, :, groups], key_gain), places))
    value_rows = low(projected[:, :, groups + 1])
    blocks = (query.reshape(N_FSDP, GROUP, KVH, groups, HD), key_rows.reshape(N_FSDP, GROUP, KVH, HD), value_rows.reshape(N_FSDP, GROUP, KVH, HD), segment.reshape(N_FSDP, GROUP), places.reshape(N_FSDP, GROUP))
    attended = lax.map(jax.checkpoint(attend_group), blocks).reshape(TOKENS, H * HD)
    stream = stream + low_back(jnp.dot(attended, attend_output, precision=HIGH))
    return feed_forward(stream, second_gain, second_gateup, second_down)

def reference(hidden_in, cotangent, seq_lengths, deal_order, mixer_gain, mixer_project, mixer_kernel, mixer_output, first_gain, first_gateup, first_down, attend_gain, attend_project, query_gain, key_gain, attend_output, second_gain, second_gateup, second_down):
    positions = jnp.arange(TOKENS).astype(jnp.int32)
    segment, places = locate(seq_lengths, positions)
    dealt = hidden_in[deal_order].astype(jnp.float32)
    upstream = cotangent[deal_order].astype(jnp.float32)
    weights = tuple((member.astype(jnp.float32) for member in (mixer_gain, mixer_project, mixer_kernel, mixer_output, first_gain, first_gateup, first_down, attend_gain, attend_project, query_gain, key_gain, attend_output, second_gain, second_gateup, second_down)))

    def wrapped(stream, *params):
        return forward(stream, segment, places, params)
    output, pullback = jax.vjp(wrapped, dealt, *weights)
    gradients = pullback(upstream)
    layer_out = jnp.zeros(output.shape, output.dtype).at[deal_order].set(output).astype(jnp.bfloat16)
    input_gradient = jnp.zeros(output.shape, output.dtype).at[deal_order].set(gradients[0]).astype(jnp.bfloat16)
    return (layer_out, input_gradient, gradients[1], gradients[2], gradients[3], gradients[4], gradients[5], gradients[6], gradients[7], gradients[8], gradients[9], gradients[10], gradients[11], gradients[12], gradients[13], gradients[14], gradients[15])
```

```python
import jax
import jax.numpy as jnp
from jax import lax
from jax.sharding import PartitionSpec as P

H = 24
KVH = 8
HD = 64

EPSILON = 1e-05
ROPE_BASE = 1000000.0
NEGATIVE = -1e30

TOKEN_AXES = ("fsdp", "ctx")
RING = 4
CORES = 2
F32 = jnp.float32
BF16 = jnp.bfloat16


def norm_rows(values, scales):
    return values * lax.rsqrt(jnp.mean(values * values, axis=-1, keepdims=True) + EPSILON) * scales


def rotate(values, cosine, sine):
    half_dim = values.shape[-1] // 2
    shape_out = (values.shape[0],) + (1,) * (values.ndim - 2) + (half_dim,)
    cosine = cosine.reshape(shape_out)
    sine = sine.reshape(shape_out)
    first_half = values[..., :half_dim]
    second_half = values[..., half_dim:]
    return jnp.concatenate(
        [
            first_half * cosine - second_half * sine,
            second_half * cosine + first_half * sine,
        ],
        axis=-1,
    )


def locate(lengths, positions):
    seq_ends = jnp.cumsum(lengths)
    segment = jnp.sum((positions[:, None] >= seq_ends[None, :]).astype(jnp.int32), axis=1)
    starts = seq_ends - lengths
    first_row = jnp.sum(
        jnp.where(segment[:, None] == jnp.arange(lengths.shape[0])[None, :], starts[None, :], 0),
        axis=1,
    )
    return (segment, positions - first_row)


def shortconv(extended, kernel_in, segment):
    kernel_taps = kernel_in.shape[0]
    out_rows = extended.shape[0] - kernel_taps + 1
    result = kernel_in[0] * extended[kernel_taps - 1 :]
    for t in range(1, kernel_taps):
        earlier = extended[kernel_taps - 1 - t : kernel_taps - 1 - t + out_rows]
        same_seq = (
            segment[kernel_taps - 1 - t : kernel_taps - 1 - t + out_rows]
            == segment[kernel_taps - 1 :]
        ).astype(F32)[:, None]
        result = result + kernel_in[t] * earlier * same_seq
    return result


def from_behind(block, axis, distance):
    devices = range(lax.axis_size(axis))
    route = [(i - distance, i) for i in devices if i - distance in devices]
    return lax.ppermute(block, axis, route)


def shift_chip(block, along_x, distance):
    route = []
    for x in range(RING):
        for z in range(RING):
            for core in range(CORES):
                to_x = (x + distance) % RING if along_x else x
                to_z = z if along_x else (z + distance) % RING
                route.append(
                    ((x * RING + z) * CORES + core, (to_x * RING + to_z) * CORES + core)
                )
    return lax.ppermute(block, TOKEN_AXES, route)


def swap_ctx(block, mask):
    return lax.ppermute(block, "ctx", [(i, i ^ mask) for i in range(lax.axis_size("ctx"))])


def shift_tp(block, distance):
    members = lax.axis_size("tp")
    return lax.ppermute(block, "tp", [(i, (i + distance) % members) for i in range(members)])


def tp_gather(shard):
    members = lax.axis_size("tp")
    return jnp.concatenate([shard] + [shift_tp(shard, k) for k in range(1, members)], axis=0)


def tp_reduce(partial):
    members = lax.axis_size("tp")
    rows = partial.shape[0] // members
    total = partial[:rows].astype(F32)
    for k in range(1, members):
        total = total + shift_tp(partial[k * rows : (k + 1) * rows], -k).astype(F32)
    return total


def reorder(rows):
    members = lax.axis_size("tp")
    own = lax.axis_index("tp")
    chunk = rows.shape[0] // members
    return jnp.concatenate(
        [
            lax.dynamic_slice_in_dim(rows, (own - k) % members * chunk, chunk, 0)
            for k in range(members)
        ],
        axis=0,
    )


def times(left, right):
    return lax.dot_general(left, right, (((1,), (0,)), ((), ())), preferred_element_type=F32)


def times_t(left, right):
    return lax.dot_general(left, right, (((1,), (1,)), ((), ())), preferred_element_type=F32)


def pair(rows):
    return jnp.concatenate([rows, swap_ctx(rows, 1)], axis=0)


def block_order(x_first):
    device = lax.axis_index(TOKEN_AXES)
    core = device % CORES
    z = device // CORES % RING
    x = device // (CORES * RING)
    outer, inner = jnp.meshgrid(jnp.arange(RING), jnp.arange(RING), indexing="ij")
    step_x, step_z = (outer, inner) if x_first else (inner, outer)
    return ((((x + step_x) % RING) * RING + (z + step_z) % RING) * CORES + core).reshape(-1)


def left_blocks(paired, x_first):
    tokens, width = paired.shape
    shards = lax.axis_size(TOKEN_AXES)
    columns = paired.T.reshape(shards, width // shards, tokens)
    picked = jnp.take(columns, block_order(x_first), axis=0, mode="clip")
    return picked.reshape(RING, -1, tokens)


def reduce_gradient(left, right, x_first):
    parts = [times(left[k], right).astype(BF16) for k in range(RING)]
    rows = parts[0].shape[0] // RING
    got = [parts[0]] + [shift_chip(parts[k], x_first, k) for k in range(1, RING)]
    sums = [
        sum(part[m * rows : (m + 1) * rows].astype(F32) for part in got) for m in range(RING)
    ]
    total = sums[0]
    for m in range(1, RING):
        total = total + shift_chip(sums[m].astype(BF16), not x_first, m).astype(F32)
    return total


def ffn_forward(stream, gain, gateup, down_t):
    hidden = down_t.shape[1]
    normed = tp_gather(norm_rows(stream, gain).astype(BF16))
    gate = times(normed, gateup[:, :hidden])
    up = times(normed, gateup[:, hidden:])
    active = (jax.nn.silu(gate) * up).astype(BF16)
    result = stream + tp_reduce(times_t(active, down_t).astype(BF16))
    return result, (normed, gate, up, active)


def ffn_backward(stream, kept, gain, gateup, down_t, upward, back, down_x_first):
    normed, gate, up, active = kept
    d_active = times(back, down_t)
    unused, pullback = jax.vjp(lambda a, b: jax.nn.silu(a) * b, gate, up)
    d_gate, d_up = pullback(d_active)
    d_gate = d_gate.astype(BF16)
    d_up = d_up.astype(BF16)
    d_both = jnp.concatenate([d_gate, d_up], axis=1)
    d_normed = tp_reduce(times_t(d_both, gateup).astype(BF16))
    unused, pullback = jax.vjp(norm_rows, stream, gain)
    d_stream, d_gain = pullback(d_normed)
    normed_pair = pair(normed)
    back_pair = pair(back)
    gate_grad = reduce_gradient(left_blocks(normed_pair, True), pair(d_gate), True)
    up_grad = reduce_gradient(left_blocks(normed_pair, False), pair(d_up), False)
    down_grad = reduce_gradient(
        left_blocks(back_pair, down_x_first), pair(active), down_x_first
    )
    return upward + d_stream, d_gain, gate_grad, up_grad, down_grad


def body(
    hidden_in,
    cotangent,
    seq_lengths,
    deal_order,
    mixer_gain,
    mixer_project,
    mixer_kernel,
    mixer_output,
    first_gain,
    first_gateup,
    first_down,
    attend_gain,
    attend_project,
    query_gain,
    key_gain,
    attend_output,
    second_gain,
    second_gateup,
    second_down,
):
    shards = lax.axis_size(TOKEN_AXES)
    contexts = lax.axis_size("ctx")
    members = lax.axis_size("tp")
    row_count, width = hidden_in.shape
    piece_rows = row_count // shards
    chunk = row_count // members
    device = lax.axis_index(TOKEN_AXES)
    own = lax.axis_index("tp")
    depth = mixer_gain.shape[0]
    channels = mixer_output.shape[0]
    hidden = first_down.shape[0]
    heads_width = attend_output.shape[0]

    first_pack = jnp.concatenate(
        [
            mixer_project.reshape(depth, -1),
            mixer_output.T,
            first_gateup.reshape(depth, -1),
            first_down.T,
        ],
        axis=1,
    )
    second_pack = jnp.concatenate(
        [
            attend_project,
            attend_output.T,
            second_gateup.reshape(depth, -1),
            second_down.T,
        ],
        axis=1,
    )
    first_all = lax.all_gather(first_pack, TOKEN_AXES, axis=0, tiled=True)
    second_all = lax.all_gather(second_pack, TOKEN_AXES, axis=0, tiled=True)
    cut = 3 * channels
    project_a = first_all[:, :cut]
    output_a_t = first_all[:, cut : cut + channels]
    cut = cut + channels
    gateup_f = first_all[:, cut : cut + 2 * hidden]
    down_f_t = first_all[:, cut + 2 * hidden :]
    cut = attend_project.shape[1]
    project_b = second_all[:, :cut]
    output_b_t = second_all[:, cut : cut + heads_width]
    cut = cut + heads_width
    gateup_s = second_all[:, cut : cut + 2 * hidden]
    down_s_t = second_all[:, cut + 2 * hidden :]

    piece_table = deal_order.reshape(shards, shards, piece_rows)[:, :, 0]
    anchor = piece_table // row_count
    anchor_piece = piece_table % row_count // piece_rows
    send_piece = jnp.sum(jnp.where(anchor == device, anchor_piece, 0), axis=1)
    my_anchor = lax.dynamic_index_in_dim(anchor, device, 0, keepdims=False)
    gains_row = jnp.concatenate(
        [mixer_gain, first_gain, attend_gain, second_gain, jnp.zeros((width - 4 * depth,), BF16)]
    )
    outgoing = jnp.concatenate(
        [
            hidden_in.reshape(shards, piece_rows, width)[send_piece],
            cotangent.reshape(shards, piece_rows, width)[send_piece],
            jnp.broadcast_to(gains_row, (shards, 8, width)),
        ],
        axis=1,
    )
    arrived = lax.all_to_all(outgoing, TOKEN_AXES, split_axis=0, concat_axis=0, tiled=True)
    tokens = arrived[:, :piece_rows][my_anchor].reshape(row_count, width)
    back_s = arrived[:, piece_rows : 2 * piece_rows][my_anchor].reshape(row_count, width)
    gains = (
        arrived[:, 2 * piece_rows, : 4 * depth]
        .reshape(shards, 4, depth)
        .transpose(1, 0, 2)
        .reshape(4, width)
        .astype(F32)
    )
    gain_a, gain_f, gain_b, gain_s = gains[0], gains[1], gains[2], gains[3]
    stream0 = lax.dynamic_slice_in_dim(tokens, own * chunk, chunk, 0).astype(F32)
    upstream = lax.dynamic_slice_in_dim(back_s, own * chunk, chunk, 0).astype(F32)
    back_s = reorder(back_s)

    kernel_taps = mixer_kernel.shape[0]
    halo = kernel_taps - 1
    local_rows = device * row_count + jnp.arange(row_count)
    halo_segment, unused = locate(
        seq_lengths, local_rows[0] - halo + jnp.arange(row_count + halo)
    )
    offsets = reorder(jnp.arange(row_count))
    segment, places = locate(seq_lengths, device * row_count + offsets)
    ctx = lax.axis_index("ctx")
    group_rows = jnp.concatenate(
        [
            (lax.axis_index("fsdp") * contexts + (ctx ^ mask)) * row_count + offsets
            for mask in range(contexts)
        ]
    )
    key_segment, key_places = locate(seq_lengths, group_rows)
    allowed = (segment[:, None] == key_segment[None, :]) & (key_places[None, :] <= places[:, None])
    half_dim = HD // 2
    frequency = ROPE_BASE ** (-(jnp.arange(half_dim).astype(F32) * 2.0 / HD))
    angles = places.astype(F32)[:, None] * frequency[None, :]
    cosine = jnp.cos(angles)
    sine = jnp.sin(angles)

    kernel_local = lax.dynamic_slice_in_dim(mixer_kernel, own * channels, channels, 1).astype(F32)
    mixer_in = norm_rows(tokens.astype(F32), gain_a).astype(BF16)
    halo_pad = 16
    halo_in = from_behind(mixer_in[row_count - halo_pad :], "ctx", 1)
    proj_a = times(jnp.concatenate([halo_in, mixer_in]), project_a)
    proj_b_part = proj_a[:, :channels]
    proj_c_part = proj_a[halo_pad:, channels : 2 * channels]
    proj_x_part = proj_a[:, 2 * channels :]
    extended = (proj_b_part * proj_x_part)[halo_pad - halo :].astype(BF16).astype(F32)
    conv_out = shortconv(extended, kernel_local, halo_segment)
    gated_rows = reorder((proj_c_part * conv_out).astype(BF16))
    stream1 = stream0 + tp_reduce(times_t(gated_rows, output_a_t).astype(BF16))
    stream2, kept_first = ffn_forward(stream1, gain_f, gateup_f, down_f_t)

    groups = H // KVH
    score_scale = HD ** (-0.5)
    qgain_f = query_gain.astype(F32)
    kgain_f = key_gain.astype(F32)

    def qk_maps(query_in, key_in, gain_q, gain_k):
        return (
            rotate(norm_rows(query_in, gain_q), cosine, sine),
            rotate(norm_rows(key_in, gain_k), cosine, sine),
        )

    attend_in = tp_gather(norm_rows(stream2, gain_b).astype(BF16))
    proj_b = times(attend_in, project_b).reshape(row_count, -1, groups + 2, HD)
    kv_heads = proj_b.shape[1]
    query_raw = proj_b[:, :, :groups]
    key_raw = proj_b[:, :, groups]
    query_f, key_f = qk_maps(query_raw, key_raw, qgain_f, kgain_f)
    query_b = query_f.astype(BF16)
    key_value = jnp.concatenate(
        [
            key_f.astype(BF16).reshape(row_count, -1),
            proj_b[:, :, groups + 1].astype(BF16).reshape(row_count, -1),
        ],
        axis=1,
    )
    key_value_all = jnp.concatenate(
        [key_value] + [swap_ctx(key_value, mask) for mask in range(1, contexts)], axis=0
    )
    key_all = key_value_all[:, : kv_heads * HD].reshape(-1, kv_heads, HD)
    value_all = key_value_all[:, kv_heads * HD :].reshape(-1, kv_heads, HD)
    scores = (
        jnp.einsum("tkgd,nkd->kgtn", query_b, key_all, preferred_element_type=F32) * score_scale
    )
    masked = jnp.where(allowed, scores, NEGATIVE)
    row_top = jnp.max(masked, axis=-1, keepdims=True)
    exponent = jnp.exp(masked - row_top)
    row_total = jnp.sum(exponent, axis=-1, keepdims=True)
    softmax_rows = exponent / row_total
    log_total = row_top + jnp.log(row_total)
    attended = (
        jnp.einsum(
            "kgtn,nkd->tkgd", softmax_rows.astype(BF16), value_all, preferred_element_type=F32
        )
        .astype(BF16)
        .reshape(row_count, -1)
    )
    stream3 = stream2 + tp_reduce(times_t(attended, output_b_t).astype(BF16))
    stream4, kept_second = ffn_forward(stream3, gain_s, gateup_s, down_s_t)

    d_stream3, gain_s_grad, gate_s_grad, up_s_grad, down_s_grad = ffn_backward(
        stream3, kept_second, gain_s, gateup_s, down_s_t, upstream, back_s, True
    )
    back_b = tp_gather(d_stream3.astype(BF16))
    d_attended_b = times(back_b, output_b_t).astype(BF16).reshape(row_count, -1, groups, HD)
    scores_again = (
        jnp.einsum("tkgd,nkd->kgtn", query_b, key_all, preferred_element_type=F32) * score_scale
    )
    probs_again = jnp.where(allowed, jnp.exp(scores_again - log_total), 0.0)
    d_probs = jnp.einsum("tkgd,nkd->kgtn", d_attended_b, value_all, preferred_element_type=F32)
    d_values = jnp.einsum(
        "kgtn,tkgd->nkd", probs_again.astype(BF16), d_attended_b, preferred_element_type=F32
    )
    inner_sum = jnp.sum(probs_again * d_probs, axis=-1, keepdims=True)
    d_scores = (probs_again * (d_probs - inner_sum)).astype(BF16)
    d_query = (
        jnp.einsum("kgtn,nkd->tkgd", d_scores, key_all, preferred_element_type=F32) * score_scale
    )
    d_keys = (
        jnp.einsum("kgtn,tkgd->nkd", d_scores, query_b, preferred_element_type=F32) * score_scale
    )
    d_key_value = jnp.concatenate(
        [d_keys.reshape(-1, kv_heads * HD), d_values.reshape(-1, kv_heads * HD)], axis=1
    )
    d_local = d_key_value[:row_count]
    for mask in range(1, contexts):
        part = d_key_value[mask * row_count : (mask + 1) * row_count].astype(BF16)
        d_local = d_local + swap_ctx(part, mask).astype(F32)
    d_key_local = d_local[:, : kv_heads * HD].reshape(row_count, kv_heads, HD)
    d_value_local = d_local[:, kv_heads * HD :].reshape(row_count, kv_heads, HD)
    unused, pullback = jax.vjp(qk_maps, query_raw, key_raw, qgain_f, kgain_f)
    d_query_raw, d_key_raw, qgain_grad, kgain_grad = pullback((d_query, d_key_local))
    d_proj_b = (
        jnp.concatenate([d_query_raw, d_key_raw[:, :, None], d_value_local[:, :, None]], axis=2)
        .astype(BF16)
        .reshape(row_count, -1)
    )
    d_attend_in = tp_reduce(times_t(d_proj_b, project_b).astype(BF16))
    unused, pullback = jax.vjp(norm_rows, stream2, gain_b)
    d_norm_b, gain_b_grad = pullback(d_attend_in)
    d_stream2 = d_stream3 + d_norm_b
    project_b_grad = reduce_gradient(left_blocks(pair(attend_in), False), pair(d_proj_b), False)
    output_b_grad = reduce_gradient(left_blocks(pair(back_b), False), pair(attended), False)

    back_f = tp_gather(d_stream2.astype(BF16))
    d_stream1, gain_f_grad, gate_f_grad, up_f_grad, down_f_grad = ffn_backward(
        stream1, kept_first, gain_f, gateup_f, down_f_t, d_stream2, back_f, False
    )
    back_a = tp_gather(d_stream1.astype(BF16))
    d_gated = reorder(times(back_a, output_a_t))
    d_cgate = d_gated * conv_out
    d_conv = d_gated * proj_c_part
    unused, pullback = jax.vjp(
        lambda ext_rows, kernel_in: shortconv(ext_rows, kernel_in, halo_segment),
        extended,
        kernel_local,
    )
    d_extended, kernel_grad = pullback(d_conv)
    returned = from_behind(d_extended[:halo], "ctx", -1)
    d_product = d_extended[halo:] + jnp.concatenate(
        [jnp.zeros((row_count - halo, channels), F32), returned]
    )
    d_proj_a = jnp.concatenate(
        [
            d_product * proj_x_part[halo_pad:],
            d_cgate,
            d_product * proj_b_part[halo_pad:],
        ],
        axis=1,
    ).astype(BF16)
    d_mixer_in = tp_reduce(times_t(reorder(d_proj_a), project_a).astype(BF16))
    unused, pullback = jax.vjp(norm_rows, stream0, gain_a)
    d_norm_a, gain_a_grad = pullback(d_mixer_in)
    d_stream0 = d_stream1 + d_norm_a
    project_a_grad = reduce_gradient(left_blocks(pair(mixer_in), True), pair(d_proj_a), True)
    output_a_grad = reduce_gradient(left_blocks(pair(back_a), False), pair(gated_rows), False)

    slot_for_anchor = jnp.sum(
        jnp.where(
            my_anchor[None, :] == jnp.arange(shards)[:, None], jnp.arange(shards)[None, :], 0
        ),
        axis=1,
    )
    dest_for_piece = jnp.sum(
        jnp.where(
            send_piece[None, :] == jnp.arange(shards)[:, None], jnp.arange(shards)[None, :], 0
        ),
        axis=1,
    )
    pieces = shards // members
    slot_place = (own - slot_for_anchor // pieces) % members * pieces + slot_for_anchor % pieces
    out_rows = tp_gather(stream4.astype(BF16)).reshape(shards, piece_rows, width)[slot_place]
    out_home = lax.all_to_all(out_rows, TOKEN_AXES, split_axis=0, concat_axis=0, tiled=True)
    layer_out = out_home[dest_for_piece].reshape(row_count, width)

    def row_of(values):
        flat = values.reshape(-1)
        return jnp.concatenate([flat, jnp.zeros((width - flat.shape[0],), F32)])

    small = jnp.stack(
        [
            gain_a_grad,
            gain_f_grad,
            gain_b_grad,
            gain_s_grad,
            row_of(jnp.concatenate([qgain_grad, kgain_grad])),
            row_of(kernel_grad),
        ]
        + [jnp.zeros((width,), F32)] * 10
    )
    last = tp_gather(jnp.concatenate([d_stream0.astype(BF16), small.astype(BF16)]))
    last = last.reshape(members, chunk + 16, width)
    grad_rows = last[:, :chunk].reshape(shards, piece_rows, width)[slot_place]
    smalls = last[:, chunk:].astype(F32)
    summed = jnp.sum(smalls[:, :5], axis=0)
    gain_sums = summed[:4].reshape(4, shards, depth).transpose(1, 0, 2).reshape(shards, 4 * depth)
    head_sums = summed[4, : 2 * HD]
    kernel_rows = reorder(smalls[:, 5, : kernel_taps * channels])
    kernel_rows = kernel_rows.reshape(members, kernel_taps, channels).transpose(1, 0, 2)
    shared = jnp.concatenate([kernel_rows.reshape(-1), head_sums])
    fill = 4 * width - 4 * depth - shared.shape[0]
    small_rows = jnp.concatenate(
        [
            gain_sums,
            jnp.broadcast_to(shared, (shards, shared.shape[0])),
            jnp.zeros((shards, fill), F32),
        ],
        axis=1,
    ).astype(BF16)
    home = lax.all_to_all(
        jnp.concatenate([grad_rows, small_rows.reshape(shards, 4, width)], axis=1),
        TOKEN_AXES,
        split_axis=0,
        concat_axis=0,
        tiled=True,
    )
    input_gradient = home[:, :piece_rows][dest_for_piece].reshape(row_count, width)
    totals = jnp.sum(home[:, piece_rows:].astype(F32), axis=0).reshape(-1)
    gain_totals = totals[: 4 * depth].reshape(4, depth)
    kernel_end = 4 * depth + kernel_taps * width
    kernel_total = totals[4 * depth : kernel_end].reshape(kernel_taps, width)
    qgain_total = totals[kernel_end : kernel_end + HD]
    kgain_total = totals[kernel_end + HD : kernel_end + 2 * HD]

    return (
        layer_out,
        input_gradient,
        gain_totals[0],
        project_a_grad.reshape(depth, 3, channels),
        kernel_total,
        output_a_grad.T,
        gain_totals[1],
        jnp.stack([gate_f_grad, up_f_grad], axis=1),
        down_f_grad.T,
        gain_totals[2],
        project_b_grad,
        qgain_total,
        kgain_total,
        output_b_grad.T,
        gain_totals[3],
        jnp.stack([gate_s_grad, up_s_grad], axis=1),
        down_s_grad.T,
    )


def solution(mesh):
    tokens = P(TOKEN_AXES, None)
    rows = P(TOKEN_AXES)
    three = P(TOKEN_AXES, None, "tp")
    two = P(TOKEN_AXES, "tp")
    turned = P("tp", TOKEN_AXES)
    return jax.shard_map(
        body,
        mesh=mesh,
        in_specs=(
            tokens, tokens, P(), P(),
            rows, three, P(), turned,
            rows, three, turned,
            rows, two, P(), P(), turned,
            rows, three, turned,
        ),
        out_specs=(
            tokens, tokens,
            rows, three, P(), turned,
            rows, three, turned,
            rows, two, P(), P(), turned,
            rows, three, turned,
        ),
        check_vma=False,
    )
```

```python
import functools

import jax
import jax.numpy as jnp
from jax import lax
from jax.experimental import pallas as pl
from jax.experimental.pallas import tpu as pltpu
from jax.sharding import Mesh, PartitionSpec as P

H = 24
KVH = 8
HD = 64

EPSILON = 1e-05
ROPE_BASE = 1000000.0
NEGATIVE = -1e30

CHIP_AXES = ("x", "z_hi", "z_lo")
TOKEN_AXES = CHIP_AXES + ("core",)
GROUP_AXES = ("x", "z_hi")
CTX_AXES = ("z_lo", "core")
TILE = 256
VMEM_LIMIT = 48 * 1024 * 1024
F32 = jnp.float32
BF16 = jnp.bfloat16


def norm_rows(values, scales):
    return values * lax.rsqrt(jnp.mean(values * values, axis=-1, keepdims=True) + EPSILON) * scales


def rotate(values, cosine, sine):
    half_dim = values.shape[-1] // 2
    shape_out = (values.shape[0],) + (1,) * (values.ndim - 2) + (half_dim,)
    cosine = cosine.reshape(shape_out)
    sine = sine.reshape(shape_out)
    first_half = values[..., :half_dim]
    second_half = values[..., half_dim:]
    return jnp.concatenate(
        [
            first_half * cosine - second_half * sine,
            second_half * cosine + first_half * sine,
        ],
        axis=-1,
    )


def locate(lengths, positions):
    seq_ends = jnp.cumsum(lengths)
    segment = jnp.sum((positions[:, None] >= seq_ends[None, :]).astype(jnp.int32), axis=1)
    starts = seq_ends - lengths
    first_row = jnp.sum(
        jnp.where(segment[:, None] == jnp.arange(lengths.shape[0])[None, :], starts[None, :], 0),
        axis=1,
    )
    return (segment, positions - first_row)


def shortconv(extended, kernel_in, segment):
    kernel_taps = kernel_in.shape[0]
    out_rows = extended.shape[0] - kernel_taps + 1
    result = kernel_in[0] * extended[kernel_taps - 1 :]
    for t in range(1, kernel_taps):
        earlier = extended[kernel_taps - 1 - t : kernel_taps - 1 - t + out_rows]
        same_seq = (
            segment[kernel_taps - 1 - t : kernel_taps - 1 - t + out_rows]
            == segment[kernel_taps - 1 :]
        ).astype(F32)[:, None]
        result = result + kernel_in[t] * earlier * same_seq
    return result


def from_behind(block, distance):
    devices = range(lax.axis_size(CTX_AXES))
    route = [(i - distance, i) for i in devices if i - distance in devices]
    return lax.ppermute(block, CTX_AXES, route)


def swap_ctx(block, mask):
    return lax.ppermute(block, CTX_AXES, [(i, i ^ mask) for i in range(lax.axis_size(CTX_AXES))])


def swap_core(block):
    return lax.ppermute(block, "core", [(0, 1), (1, 0)])


def shift_tp(block, distance):
    members = lax.axis_size("tp")
    return lax.ppermute(block, "tp", [(i, (i + distance) % members) for i in range(members)])


def tp_gather(shard):
    return [shard] + [shift_tp(shard, k) for k in range(1, lax.axis_size("tp"))]


def tp_chunks(partial):
    rows = partial.shape[0] // lax.axis_size("tp")
    return [
        partial[k * rows : (k + 1) * rows].astype(F32 if k == 0 else BF16)
        for k in range(lax.axis_size("tp"))
    ]


def tp_reduce(chunks):
    total = chunks[0]
    for k in range(1, len(chunks)):
        total = total + shift_tp(chunks[k], -k).astype(F32)
    return total


def reorder(rows):
    members = lax.axis_size("tp")
    own = lax.axis_index("tp")
    chunk = rows.shape[0] // members
    return jnp.concatenate(
        [
            lax.dynamic_slice_in_dim(rows, (own - k) % members * chunk, chunk, 0)
            for k in range(members)
        ],
        axis=0,
    )


def times(left, right):
    return lax.dot_general(left, right, (((1,), (0,)), ((), ())), preferred_element_type=F32)


def times_t(left, right):
    return lax.dot_general(left, right, (((1,), (1,)), ((), ())), preferred_element_type=F32)


def assemble(chunk_refs, target):
    rows = chunk_refs[0].shape[0]
    for k, ref in enumerate(chunk_refs):
        target[k * rows : (k + 1) * rows, :] = ref[...]


def spread(total, chunk_refs):
    rows = chunk_refs[0].shape[0]
    for k, ref in enumerate(chunk_refs):
        ref[...] = total[k * rows : (k + 1) * rows, :].astype(ref.dtype)


def whole(shape):
    return pl.BlockSpec(shape, lambda *_: (0,) * len(shape))


def weight_specs(depth, steps):
    return [
        pl.BlockSpec((depth, 2 * TILE), lambda j: (0, j)),
        pl.BlockSpec((depth, TILE), lambda j: (0, 2 * steps + j)),
    ]


def chunk_shapes(count, rows, width):
    return [jax.ShapeDtypeStruct((rows, width), F32 if k == 0 else BF16) for k in range(count)]


def ffn_forward_kernel(count, *refs):
    x_refs, (gu_ref, dn_ref), outs = refs[:count], refs[count : count + 2], refs[count + 2 : -2]
    x_all, total = refs[-2:]
    step = pl.program_id(0)

    @pl.when(step == 0)
    def _():
        assemble(x_refs, x_all)
        total[...] = jnp.zeros_like(total)

    both = times(x_all[...], gu_ref[...])
    gate, up = both[:, :TILE], both[:, TILE:]
    active = (gate * jax.nn.sigmoid(gate) * up).astype(BF16)
    total[...] += times_t(active, dn_ref[...])

    @pl.when(step == pl.num_programs(0) - 1)
    def _():
        spread(total[...], outs)


def ffn_forward(chunks, pack, steps):
    count, (rows, width) = len(chunks), chunks[0].shape
    tokens = count * rows
    return pl.pallas_call(
        functools.partial(ffn_forward_kernel, count),
        grid=(steps,),
        in_specs=[whole((rows, width))] * count + weight_specs(width, steps),
        out_specs=[whole((rows, width))] * count,
        out_shape=chunk_shapes(count, rows, width),
        scratch_shapes=[pltpu.VMEM((tokens, width), BF16), pltpu.VMEM((tokens, width), F32)],
        compiler_params=pltpu.CompilerParams(vmem_limit_bytes=VMEM_LIMIT),
        cost_estimate=pl.CostEstimate(
            flops=2 * tokens * width * 3 * TILE * steps,
            bytes_accessed=2 * width * 3 * TILE * steps,
            transcendentals=tokens * TILE * steps,
        ),
        name="ffn_forward",
    )(*chunks, pack, pack)


def ffn_backward_kernel(count, forward, core_ref, *refs):
    x_refs, b_refs = refs[:count], refs[count : 2 * count]
    gu_ref, dn_ref = refs[2 * count : 2 * count + 2]
    place = 2 * count + 2
    back_outs = refs[place : place + count]
    place += count
    if forward:
        outs = refs[place : place + count]
        place += count
    keep_ref, side_ref = refs[place : place + 2]
    scratch = refs[place + 2 :]
    x_all, b_all, d_total = scratch[:3]
    step = pl.program_id(0)
    width = x_all.shape[1]

    @pl.when(step == 0)
    def _():
        assemble(x_refs, x_all)
        assemble(b_refs, b_all)
        side_ref[:, :width] = x_all[...]
        side_ref[:, width : 2 * width] = b_all[...]
        d_total[...] = jnp.zeros_like(d_total)
        if forward:
            scratch[3][...] = jnp.zeros_like(scratch[3])

    both = times(x_all[...], gu_ref[...])
    gate, up = both[:, :TILE], both[:, TILE:]
    d_active = times(b_all[...], dn_ref[...])
    sigmoid = jax.nn.sigmoid(gate)
    silu = gate * sigmoid
    active = (silu * up).astype(BF16)
    if forward:
        scratch[3][...] += times_t(active, dn_ref[...])
    d_gate = (d_active * up * (sigmoid * (1.0 + gate * (1.0 - sigmoid)))).astype(BF16)
    d_up = (d_active * silu).astype(BF16)
    d_total[...] += times_t(jnp.concatenate([d_gate, d_up], axis=1), gu_ref[...])
    first = core_ref[0] == 0
    half = TILE // 2
    low, high = active[:, :half], active[:, half:]
    start = pl.multiple_of(2 * width + step * (TILE + half), half)

    @pl.when(first)
    def _():
        keep_ref[:, :TILE] = d_gate
        keep_ref[:, TILE:] = low
        side_ref[:, pl.ds(start, TILE)] = d_up
        side_ref[:, pl.ds(start + TILE, half)] = high

    @pl.when(jnp.logical_not(first))
    def _():
        keep_ref[:, :TILE] = d_up
        keep_ref[:, TILE:] = high
        side_ref[:, pl.ds(start, TILE)] = d_gate
        side_ref[:, pl.ds(start + TILE, half)] = low

    @pl.when(step == pl.num_programs(0) - 1)
    def _():
        spread(d_total[...], back_outs)
        if forward:
            spread(scratch[3][...], outs)


def ffn_backward(core, chunks, back_chunks, pack, steps, forward):
    count, (rows, width) = len(chunks), chunks[0].shape
    tokens = count * rows
    block = TILE + TILE // 2
    ways = 2 if forward else 1
    side_width = 2 * width + steps * block
    results = pl.pallas_call(
        functools.partial(ffn_backward_kernel, count, forward),
        grid=(steps,),
        in_specs=[pl.BlockSpec(memory_space=pltpu.SMEM)]
        + [whole((rows, width))] * (2 * count)
        + weight_specs(width, steps),
        out_specs=[whole((rows, width))] * (ways * count)
        + [pl.BlockSpec((tokens, block), lambda j: (0, j)), whole((tokens, side_width))],
        out_shape=chunk_shapes(count, rows, width) * ways
        + [
            jax.ShapeDtypeStruct((tokens, steps * block), BF16),
            jax.ShapeDtypeStruct((tokens, side_width), BF16),
        ],
        scratch_shapes=[pltpu.VMEM((tokens, width), BF16)] * 2
        + [pltpu.VMEM((tokens, width), F32)] * ways,
        compiler_params=pltpu.CompilerParams(vmem_limit_bytes=VMEM_LIMIT),
        cost_estimate=pl.CostEstimate(
            flops=2 * tokens * width * (4 + ways) * TILE * steps,
            bytes_accessed=2 * width * 3 * TILE * steps + 4 * tokens * side_width,
            transcendentals=tokens * TILE * steps,
        ),
        name="ffn_both" if forward else "ffn_backward",
    )(core, *chunks, *back_chunks, pack, pack)
    return results[:count], results[count : ways * count], results[-2], results[-1]


def gradient_kernel(cut, whole_steps, *refs):
    one_own, one_other, two_own, two_other, own_ref, other_ref = refs[:6]
    out_ref, one_t, two_t = refs[-3:]
    tokens = one_own.shape[0]
    step = pl.program_id(0)

    @pl.when(step == 0)
    def _():
        one_t[:, :tokens] = one_own[...].T
        one_t[:, tokens:] = one_other[...].T
        two_t[:, :tokens] = two_own[...].T
        two_t[:, tokens:] = two_other[...].T

    right = jnp.concatenate([own_ref[...], other_ref[...]], axis=0)
    if whole_steps:

        @pl.when(step < whole_steps)
        def _():
            out_ref[...] = times(one_t[...], right).astype(BF16)

        @pl.when(step >= whole_steps)
        def _():
            out_ref[...] = times(two_t[...], right).astype(BF16)

    else:
        out_ref[:, :cut] = times(one_t[...], right[:, :cut]).astype(BF16)
        out_ref[:, cut:] = times(two_t[...], right[:, cut:]).astype(BF16)


def gradient(lefts, own, other, other_start, block, steps, cut, whole_steps, width, out_width, out_start, target):
    tokens = own.shape[0]

    def left_spec(index):
        return pl.BlockSpec((tokens, width), lambda j: (0, index))

    in_specs = [left_spec(index) for unused, index in lefts] + [
        pl.BlockSpec((tokens, block), lambda j: (0, j)),
        pl.BlockSpec((tokens, block), lambda j: (0, other_start + j)),
    ]
    operands = [array for array, unused in lefts] + [own, other]
    aliases = {}
    if target is not None:
        in_specs.append(pl.BlockSpec(memory_space=pl.ANY))
        operands.append(target)
        aliases = {len(operands) - 1: 0}
    return pl.pallas_call(
        functools.partial(gradient_kernel, cut, whole_steps),
        grid=(steps,),
        in_specs=in_specs,
        out_specs=pl.BlockSpec((width, block), lambda j: (0, out_start + j)),
        out_shape=jax.ShapeDtypeStruct((width, out_width), BF16),
        scratch_shapes=[pltpu.VMEM((width, 2 * tokens), BF16)] * 2,
        input_output_aliases=aliases,
        compiler_params=pltpu.CompilerParams(vmem_limit_bytes=VMEM_LIMIT),
        cost_estimate=pl.CostEstimate(
            flops=4 * tokens * width * block * steps,
            bytes_accessed=2 * width * block * steps,
            transcendentals=0,
        ),
        name="weight_gradient",
    )(*operands)


def reduce_gradient(partial):
    core = lax.axis_index("core")
    summed = lax.psum_scatter(partial, CHIP_AXES, scatter_dimension=0, tiled=True)
    rows = summed.shape[0] // 2
    mine = lax.dynamic_slice_in_dim(summed, core * rows, rows, 0)
    other = swap_core(lax.dynamic_slice_in_dim(summed, (1 - core) * rows, rows, 0))
    first = core == 0
    return jnp.where(first, mine, other).astype(F32), jnp.where(first, other, mine).astype(F32)


def ffn_gradients(low, high, steps, hidden):
    depth = low.shape[0]
    low = low.reshape(depth, steps, -1)
    high = high.reshape(depth, steps, -1)
    gate = low[:, :, :TILE].reshape(depth, -1)[:, :hidden]
    up = high[:, :, :TILE].reshape(depth, -1)[:, :hidden]
    down = jnp.concatenate([low[:, :, TILE:], high[:, :, TILE:]], axis=2)
    return jnp.stack([gate, up], axis=1), down.reshape(depth, -1)[:, :hidden].T


def halves(proj, out):
    first = lax.axis_index("core") == 0
    half = (proj.shape[1] + out.shape[1]) // 2
    late = jnp.concatenate([proj[:, half:], out], axis=1)
    early = proj[:, :half]
    return jnp.where(first, early, late), jnp.where(first, late, early)


def body(
    hidden_in,
    cotangent,
    seq_lengths,
    deal_order,
    mixer_gain,
    mixer_project,
    mixer_kernel,
    mixer_output,
    first_gain,
    first_gateup,
    first_down,
    attend_gain,
    attend_project,
    query_gain,
    key_gain,
    attend_output,
    second_gain,
    second_gateup,
    second_down,
):
    shards = lax.axis_size(TOKEN_AXES)
    contexts = lax.axis_size(CTX_AXES)
    members = lax.axis_size("tp")
    row_count, width = hidden_in.shape
    piece_rows = row_count // shards
    part_rows = piece_rows // members
    chunk = row_count // members
    device = lax.axis_index(TOKEN_AXES)
    own = lax.axis_index("tp")
    core = lax.axis_index("core")
    core_ref = core.reshape(1).astype(jnp.int32)
    depth = mixer_gain.shape[0]
    channels = mixer_output.shape[0]
    hidden = first_down.shape[0]
    heads_width = attend_output.shape[0]
    steps = -(-hidden // TILE)
    padded = steps * TILE
    ffn_width = 3 * padded
    block = TILE + TILE // 2

    def pack_ffn(gateup, down):
        wide = jnp.pad(gateup, ((0, 0), (0, 0), (0, padded - hidden)))
        wide = wide.reshape(depth, 2, steps, TILE).transpose(0, 2, 1, 3).reshape(depth, -1)
        return [wide, jnp.pad(down.T, ((0, 0), (0, padded - hidden)))]

    first_pack = jnp.concatenate(
        pack_ffn(first_gateup, first_down) + [mixer_project.reshape(depth, -1), mixer_output.T],
        axis=1,
    )
    second_pack = jnp.concatenate(
        pack_ffn(second_gateup, second_down) + [attend_project, attend_output.T], axis=1
    )
    first_all = lax.all_gather(first_pack, TOKEN_AXES, axis=0, tiled=True)
    second_all = lax.all_gather(second_pack, TOKEN_AXES, axis=0, tiled=True)
    project_a = first_all[:, ffn_width : ffn_width + 3 * channels]
    output_a_t = first_all[:, ffn_width + 3 * channels :]
    project_b = second_all[:, ffn_width : ffn_width + attend_project.shape[1]]
    output_b_t = second_all[:, ffn_width + attend_project.shape[1] :]

    piece_table = deal_order.reshape(shards, shards, piece_rows)[:, :, 0]
    anchor = piece_table // row_count
    anchor_piece = piece_table % row_count // piece_rows
    send_piece = jnp.sum(jnp.where(anchor == device, anchor_piece, 0), axis=1)
    my_anchor = lax.dynamic_index_in_dim(anchor, device, 0, keepdims=False)
    gains_row = jnp.concatenate(
        [mixer_gain, first_gain, attend_gain, second_gain, jnp.zeros((width - 4 * depth,), BF16)]
    )

    def my_part(rows):
        parts = rows.reshape(shards, members, part_rows, width)
        return lax.dynamic_index_in_dim(parts, own, 1, keepdims=False)[send_piece]

    outgoing = jnp.concatenate(
        [
            my_part(hidden_in),
            my_part(cotangent),
            jnp.broadcast_to(gains_row, (shards, 1, width)),
        ],
        axis=1,
    )
    arrived = lax.all_to_all(outgoing, TOKEN_AXES, split_axis=0, concat_axis=0, tiled=True)
    gains = (
        arrived[:, 2 * part_rows, : 4 * depth]
        .reshape(shards, 4, depth)
        .transpose(1, 0, 2)
        .reshape(4, width)
        .astype(F32)
    )
    gain_a, gain_f, gain_b, gain_s = gains[0], gains[1], gains[2], gains[3]
    parts = arrived[:, : 2 * part_rows][my_anchor].reshape(2 * shards * part_rows, width)
    parts = jnp.concatenate(tp_gather(parts)).reshape(members, shards, 2, part_rows, width)
    member_slot = (own - jnp.arange(members)) % members
    parts = jnp.stack(
        [lax.dynamic_index_in_dim(parts, member_slot[t], 0, keepdims=False) for t in range(members)],
        axis=2,
    )
    tokens = parts[:, 0].reshape(row_count, width)
    back_s = parts[:, 1].reshape(row_count, width)
    stream0 = lax.dynamic_slice_in_dim(tokens, own * chunk, chunk, 0).astype(F32)
    upstream = lax.dynamic_slice_in_dim(back_s, own * chunk, chunk, 0).astype(F32)
    back_s_chunks = [
        lax.dynamic_slice_in_dim(back_s, (own - k) % members * chunk, chunk, 0)
        for k in range(members)
    ]

    kernel_taps = mixer_kernel.shape[0]
    halo = kernel_taps - 1
    local_rows = device * row_count + jnp.arange(row_count)
    halo_segment, unused = locate(
        seq_lengths, local_rows[0] - halo + jnp.arange(row_count + halo)
    )
    offsets = reorder(jnp.arange(row_count))
    segment, places = locate(seq_lengths, device * row_count + offsets)
    ctx = lax.axis_index(CTX_AXES)
    group_rows = jnp.concatenate(
        [
            (lax.axis_index(GROUP_AXES) * contexts + (ctx ^ mask)) * row_count + offsets
            for mask in range(contexts)
        ]
    )
    key_segment, key_places = locate(seq_lengths, group_rows)
    allowed = (segment[:, None] == key_segment[None, :]) & (key_places[None, :] <= places[:, None])
    half_dim = HD // 2
    frequency = ROPE_BASE ** (-(jnp.arange(half_dim).astype(F32) * 2.0 / HD))
    angles = places.astype(F32)[:, None] * frequency[None, :]
    cosine = jnp.cos(angles)
    sine = jnp.sin(angles)

    kernel_local = lax.dynamic_slice_in_dim(mixer_kernel, own * channels, channels, 1).astype(F32)
    mixer_in = norm_rows(tokens.astype(F32), gain_a).astype(BF16)
    mixer_in_other = swap_core(mixer_in)
    halo_pad = 16
    halo_in = from_behind(mixer_in[row_count - halo_pad :], 1)
    proj_a = times(jnp.concatenate([halo_in, mixer_in]), project_a)
    proj_b_part = proj_a[:, :channels]
    proj_c_part = proj_a[halo_pad:, channels : 2 * channels]
    proj_x_part = proj_a[:, 2 * channels :]
    extended = (proj_b_part * proj_x_part)[halo_pad - halo :].astype(BF16).astype(F32)
    conv_out = shortconv(extended, kernel_local, halo_segment)
    gated_rows = reorder((proj_c_part * conv_out).astype(BF16))
    stream1 = stream0 + tp_reduce(tp_chunks(times_t(gated_rows, output_a_t)))

    normed_f = tp_gather(norm_rows(stream1, gain_f).astype(BF16))
    stream2 = stream1 + tp_reduce(ffn_forward(normed_f, first_all, steps))

    groups = H // KVH
    score_scale = HD ** (-0.5)
    qgain_f = query_gain.astype(F32)
    kgain_f = key_gain.astype(F32)

    def qk_maps(query_in, key_in, gain_q, gain_k):
        return (
            rotate(norm_rows(query_in, gain_q), cosine, sine),
            rotate(norm_rows(key_in, gain_k), cosine, sine),
        )

    attend_in = jnp.concatenate(tp_gather(norm_rows(stream2, gain_b).astype(BF16)))
    proj_b = times(attend_in, project_b).reshape(row_count, -1, groups + 2, HD)
    kv_heads = proj_b.shape[1]
    query_raw = proj_b[:, :, :groups]
    key_raw = proj_b[:, :, groups]
    query_f, key_f = qk_maps(query_raw, key_raw, qgain_f, kgain_f)
    query_b = query_f.astype(BF16)
    key_value = jnp.concatenate(
        [
            key_f.astype(BF16).reshape(row_count, -1),
            proj_b[:, :, groups + 1].astype(BF16).reshape(row_count, -1),
        ],
        axis=1,
    )
    key_value_all = jnp.concatenate(
        [key_value] + [swap_ctx(key_value, mask) for mask in range(1, contexts)], axis=0
    )
    key_all = key_value_all[:, : kv_heads * HD].reshape(-1, kv_heads, HD)
    value_all = key_value_all[:, kv_heads * HD :].reshape(-1, kv_heads, HD)
    scores = (
        jnp.einsum("tkgd,nkd->kgtn", query_b, key_all, preferred_element_type=F32) * score_scale
    )
    masked = jnp.where(allowed, scores, NEGATIVE)
    row_top = jnp.max(masked, axis=-1, keepdims=True)
    exponent = jnp.exp(masked - row_top)
    row_total = jnp.sum(exponent, axis=-1, keepdims=True)
    softmax_rows = exponent / row_total
    log_total = row_top + jnp.log(row_total)
    attended = (
        jnp.einsum(
            "kgtn,nkd->tkgd", softmax_rows.astype(BF16), value_all, preferred_element_type=F32
        )
        .astype(BF16)
        .reshape(row_count, -1)
    )
    stream3 = stream2 + tp_reduce(tp_chunks(times_t(attended, output_b_t)))

    normed_s = tp_gather(norm_rows(stream3, gain_s).astype(BF16))
    d_chunks, out_chunks, keep, side = ffn_backward(
        core_ref, normed_s, back_s_chunks, second_all, steps, True
    )
    unused, pullback = jax.vjp(norm_rows, stream3, gain_s)
    d_stream, gain_s_grad = pullback(tp_reduce(d_chunks))
    d_stream3 = upstream + d_stream
    stream4 = stream3 + tp_reduce(out_chunks)
    side_other = swap_core(side)
    ffn_lefts = [(side, 0), (side_other, 0), (side, 1), (side_other, 1)]
    ffn_cols = steps * block
    side_start = 2 * width // block
    second_grads = reduce_gradient(
        gradient(
            ffn_lefts, keep, side_other, side_start, block, steps, TILE, 0, width, ffn_cols, 0, None
        )
    )

    back_b = jnp.concatenate(tp_gather(d_stream3.astype(BF16)))
    back_b_other = swap_core(back_b)
    attend_in_other = swap_core(attend_in)
    d_attended_b = times(back_b, output_b_t).astype(BF16).reshape(row_count, -1, groups, HD)
    scores_again = (
        jnp.einsum("tkgd,nkd->kgtn", query_b, key_all, preferred_element_type=F32) * score_scale
    )
    probs_again = jnp.where(allowed, jnp.exp(scores_again - log_total), 0.0)
    d_probs = jnp.einsum("tkgd,nkd->kgtn", d_attended_b, value_all, preferred_element_type=F32)
    d_values = jnp.einsum(
        "kgtn,tkgd->nkd", probs_again.astype(BF16), d_attended_b, preferred_element_type=F32
    )
    inner_sum = jnp.sum(probs_again * d_probs, axis=-1, keepdims=True)
    d_scores = (probs_again * (d_probs - inner_sum)).astype(BF16)
    d_query = (
        jnp.einsum("kgtn,nkd->tkgd", d_scores, key_all, preferred_element_type=F32) * score_scale
    )
    d_keys = (
        jnp.einsum("kgtn,tkgd->nkd", d_scores, query_b, preferred_element_type=F32) * score_scale
    )
    d_key_value = jnp.concatenate(
        [d_keys.reshape(-1, kv_heads * HD), d_values.reshape(-1, kv_heads * HD)], axis=1
    )
    d_local = d_key_value[:row_count]
    for mask in range(1, contexts):
        part = d_key_value[mask * row_count : (mask + 1) * row_count].astype(BF16)
        d_local = d_local + swap_ctx(part, mask).astype(F32)
    d_key_local = d_local[:, : kv_heads * HD].reshape(row_count, kv_heads, HD)
    d_value_local = d_local[:, kv_heads * HD :].reshape(row_count, kv_heads, HD)
    unused, pullback = jax.vjp(qk_maps, query_raw, key_raw, qgain_f, kgain_f)
    d_query_raw, d_key_raw, qgain_grad, kgain_grad = pullback((d_query, d_key_local))
    d_proj_b = (
        jnp.concatenate([d_query_raw, d_key_raw[:, :, None], d_value_local[:, :, None]], axis=2)
        .astype(BF16)
        .reshape(row_count, -1)
    )
    d_attend_in = tp_reduce(tp_chunks(times_t(d_proj_b, project_b)))
    unused, pullback = jax.vjp(norm_rows, stream2, gain_b)
    d_norm_b, gain_b_grad = pullback(d_attend_in)
    d_stream2 = d_stream3 + d_norm_b
    keep, send = halves(d_proj_b, attended)
    first_core = core == 0
    attend_cols = keep.shape[1]
    small_tile = 2 * (heads_width + attend_project.shape[1]) // 16
    third = gradient(
        [
            (attend_in, 0),
            (attend_in_other, 0),
            (jnp.where(first_core, attend_in, back_b), 0),
            (jnp.where(first_core, attend_in_other, back_b_other), 0),
        ],
        keep,
        swap_core(send),
        0,
        small_tile,
        attend_cols // small_tile,
        0,
        (attend_project.shape[1] - attend_cols) // small_tile,
        width,
        ffn_cols + attend_cols,
        ffn_cols // small_tile,
        None,
    )

    back_f = tp_gather(d_stream2.astype(BF16))
    d_chunks, unused, keep, side = ffn_backward(
        core_ref, normed_f, back_f, first_all, steps, False
    )
    unused, pullback = jax.vjp(norm_rows, stream1, gain_f)
    d_stream, gain_f_grad = pullback(tp_reduce(d_chunks))
    d_stream1 = d_stream2 + d_stream
    side_other = swap_core(side)
    ffn_lefts = [(side, 0), (side_other, 0), (side, 1), (side_other, 1)]
    low, high = reduce_gradient(
        gradient(
            ffn_lefts,
            keep,
            side_other,
            side_start,
            block,
            steps,
            TILE,
            0,
            width,
            ffn_cols + attend_cols,
            0,
            third,
        )
    )
    first_grads = (low[:, :ffn_cols], high[:, :ffn_cols])
    attend_grads = jnp.concatenate([low[:, ffn_cols:], high[:, ffn_cols:]], axis=1)

    back_a = jnp.concatenate(tp_gather(d_stream1.astype(BF16)))
    back_a_other = swap_core(back_a)
    d_gated = reorder(times(back_a, output_a_t))
    d_cgate = d_gated * conv_out
    d_conv = d_gated * proj_c_part
    unused, pullback = jax.vjp(
        lambda ext_rows, kernel_in: shortconv(ext_rows, kernel_in, halo_segment),
        extended,
        kernel_local,
    )
    d_extended, kernel_grad = pullback(d_conv)
    returned = from_behind(d_extended[:halo], -1)
    d_product = d_extended[halo:] + jnp.concatenate(
        [jnp.zeros((row_count - halo, channels), F32), returned]
    )
    d_proj_a = jnp.concatenate(
        [
            d_product * proj_x_part[halo_pad:],
            d_cgate,
            d_product * proj_b_part[halo_pad:],
        ],
        axis=1,
    ).astype(BF16)
    d_mixer_in = tp_reduce(tp_chunks(times_t(reorder(d_proj_a), project_a)))
    unused, pullback = jax.vjp(norm_rows, stream0, gain_a)
    d_norm_a, gain_a_grad = pullback(d_mixer_in)
    d_stream0 = d_stream1 + d_norm_a
    keep, send = halves(d_proj_a, gated_rows)
    mixer_cols = keep.shape[1]
    low, high = reduce_gradient(
        gradient(
            [
                (mixer_in, 0),
                (mixer_in_other, 0),
                (jnp.where(first_core, mixer_in, back_a), 0),
                (jnp.where(first_core, mixer_in_other, back_a_other), 0),
            ],
            keep,
            swap_core(send),
            0,
            mixer_cols,
            1,
            3 * channels - mixer_cols,
            0,
            width,
            mixer_cols,
            0,
            None,
        )
    )
    mixer_grads = jnp.concatenate([low, high], axis=1)

    slot_for_anchor = jnp.sum(
        jnp.where(
            my_anchor[None, :] == jnp.arange(shards)[:, None], jnp.arange(shards)[None, :], 0
        ),
        axis=1,
    )
    dest_for_piece = jnp.sum(
        jnp.where(
            send_piece[None, :] == jnp.arange(shards)[:, None], jnp.arange(shards)[None, :], 0
        ),
        axis=1,
    )
    pieces = shards // members
    slot_place = (own - slot_for_anchor // pieces) % members * pieces + slot_for_anchor % pieces
    out_rows = jnp.concatenate(tp_gather(stream4.astype(BF16)))
    out_rows = out_rows.reshape(shards, piece_rows, width)[slot_place]
    out_home = lax.all_to_all(out_rows, TOKEN_AXES, split_axis=0, concat_axis=0, tiled=True)
    layer_out = out_home[dest_for_piece].reshape(row_count, width)

    def row_of(values):
        flat = values.reshape(-1)
        return jnp.concatenate([flat, jnp.zeros((width - flat.shape[0],), F32)])

    small = jnp.stack(
        [
            gain_a_grad,
            gain_f_grad,
            gain_b_grad,
            gain_s_grad,
            row_of(jnp.concatenate([qgain_grad, kgain_grad])),
            row_of(kernel_grad),
        ]
        + [jnp.zeros((width,), F32)] * 10
    )
    last = jnp.concatenate(
        tp_gather(jnp.concatenate([d_stream0.astype(BF16), small.astype(BF16)]))
    )
    last = last.reshape(members, chunk + 16, width)
    grad_rows = last[:, :chunk].reshape(shards, piece_rows, width)[slot_place]
    smalls = last[:, chunk:].astype(F32)
    summed = jnp.sum(smalls[:, :5], axis=0)
    gain_sums = summed[:4].reshape(4, shards, depth).transpose(1, 0, 2).reshape(shards, 4 * depth)
    head_sums = summed[4, : 2 * HD]
    kernel_rows = reorder(smalls[:, 5, : kernel_taps * channels])
    kernel_rows = kernel_rows.reshape(members, kernel_taps, channels).transpose(1, 0, 2)
    shared = jnp.concatenate([kernel_rows.reshape(-1), head_sums])
    fill = 4 * width - 4 * depth - shared.shape[0]
    small_rows = jnp.concatenate(
        [
            gain_sums,
            jnp.broadcast_to(shared, (shards, shared.shape[0])),
            jnp.zeros((shards, fill), F32),
        ],
        axis=1,
    ).astype(BF16)
    home = lax.all_to_all(
        jnp.concatenate([grad_rows, small_rows.reshape(shards, 4, width)], axis=1),
        TOKEN_AXES,
        split_axis=0,
        concat_axis=0,
        tiled=True,
    )
    input_gradient = home[:, :piece_rows][dest_for_piece].reshape(row_count, width)
    totals = jnp.sum(home[:, piece_rows:].astype(F32), axis=0).reshape(-1)
    gain_totals = totals[: 4 * depth].reshape(4, depth)
    kernel_end = 4 * depth + kernel_taps * width
    kernel_total = totals[4 * depth : kernel_end].reshape(kernel_taps, width)
    qgain_total = totals[kernel_end : kernel_end + HD]
    kgain_total = totals[kernel_end + HD : kernel_end + 2 * HD]

    gateup_s_grad, down_s_grad = ffn_gradients(*second_grads, steps, hidden)
    gateup_f_grad, down_f_grad = ffn_gradients(*first_grads, steps, hidden)
    proj_cols = attend_project.shape[1]
    return (
        layer_out,
        input_gradient,
        gain_totals[0],
        mixer_grads[:, : 3 * channels].reshape(depth, 3, channels),
        kernel_total,
        mixer_grads[:, 3 * channels :].T,
        gain_totals[1],
        gateup_f_grad,
        down_f_grad,
        gain_totals[2],
        attend_grads[:, :proj_cols],
        qgain_total,
        kgain_total,
        attend_grads[:, proj_cols:].T,
        gain_totals[3],
        gateup_s_grad,
        down_s_grad,
    )


def solution(mesh):
    names = TOKEN_AXES + ("tp",)
    rings = mesh.shape["fsdp"] // 2, 2, mesh.shape["ctx"] // 2, 2, mesh.shape["tp"]
    tokens = P(TOKEN_AXES, None)
    rows = P(TOKEN_AXES)
    three = P(TOKEN_AXES, None, "tp")
    two = P(TOKEN_AXES, "tp")
    turned = P("tp", TOKEN_AXES)
    return jax.shard_map(
        body,
        mesh=Mesh(mesh.devices.reshape(rings), names),
        in_specs=(
            tokens, tokens, P(), P(),
            rows, three, P(), turned,
            rows, three, turned,
            rows, two, P(), P(), turned,
            rows, three, turned,
        ),
        out_specs=(
            tokens, tokens,
            rows, three, P(), turned,
            rows, three, turned,
            rows, two, P(), P(), turned,
            rows, three, turned,
        ),
        check_vma=False,
    )
```

```python
import functools

import jax
import jax.numpy as jnp
from jax import lax
from jax.experimental import pallas as pl
from jax.experimental.pallas import tpu as pltpu
from jax.sharding import Mesh, PartitionSpec as P

H = 24
KVH = 8
HD = 64

EPSILON = 1e-05
ROPE_BASE = 1000000.0
NEGATIVE = -1e30

CHIP_AXES = ("x", "z_hi", "z_lo")
TOKEN_AXES = CHIP_AXES + ("core",)
GROUP_AXES = ("x", "z_hi")
CTX_AXES = ("z_lo", "core")
Z_AXES = ("z_hi", "z_lo")
CORES = 2
TILE = 256
VMEM_LIMIT = 48 * 1024 * 1024
F32 = jnp.float32
BF16 = jnp.bfloat16


def norm_rows(values, scales):
    return values * lax.rsqrt(jnp.mean(values * values, axis=-1, keepdims=True) + EPSILON) * scales


def rotate(values, cosine, sine):
    half_dim = values.shape[-1] // 2
    shape_out = (values.shape[0],) + (1,) * (values.ndim - 2) + (half_dim,)
    cosine = cosine.reshape(shape_out)
    sine = sine.reshape(shape_out)
    first_half = values[..., :half_dim]
    second_half = values[..., half_dim:]
    return jnp.concatenate(
        [
            first_half * cosine - second_half * sine,
            second_half * cosine + first_half * sine,
        ],
        axis=-1,
    )


def locate(lengths, positions):
    seq_ends = jnp.cumsum(lengths)
    segment = jnp.sum((positions[:, None] >= seq_ends[None, :]).astype(jnp.int32), axis=1)
    starts = seq_ends - lengths
    first_row = jnp.sum(
        jnp.where(segment[:, None] == jnp.arange(lengths.shape[0])[None, :], starts[None, :], 0),
        axis=1,
    )
    return (segment, positions - first_row)


def shortconv(extended, kernel_in, segment):
    kernel_taps = kernel_in.shape[0]
    out_rows = extended.shape[0] - kernel_taps + 1
    result = kernel_in[0] * extended[kernel_taps - 1 :]
    for t in range(1, kernel_taps):
        earlier = extended[kernel_taps - 1 - t : kernel_taps - 1 - t + out_rows]
        same_seq = (
            segment[kernel_taps - 1 - t : kernel_taps - 1 - t + out_rows]
            == segment[kernel_taps - 1 :]
        ).astype(F32)[:, None]
        result = result + kernel_in[t] * earlier * same_seq
    return result


def from_behind(block, distance):
    devices = range(lax.axis_size(CTX_AXES))
    route = [(i - distance, i) for i in devices if i - distance in devices]
    return lax.ppermute(block, CTX_AXES, route)


def swap_ctx(block, mask):
    return lax.ppermute(block, CTX_AXES, [(i, i ^ mask) for i in range(lax.axis_size(CTX_AXES))])


def swap_core(block):
    return lax.ppermute(block, "core", [(0, 1), (1, 0)])


def shift_ring(block, axis, distance):
    ring = lax.axis_size(axis)
    return lax.ppermute(block, axis, [(i, (i + distance) % ring) for i in range(ring)])


def shift_tp(block, distance):
    members = lax.axis_size("tp")
    return lax.ppermute(block, "tp", [(i, (i + distance) % members) for i in range(members)])


def tp_gather(shard):
    return [shard] + [shift_tp(shard, k) for k in range(1, lax.axis_size("tp"))]


def tp_chunks(partial):
    rows = partial.shape[0] // lax.axis_size("tp")
    return [
        partial[k * rows : (k + 1) * rows].astype(F32 if k == 0 else BF16)
        for k in range(lax.axis_size("tp"))
    ]


def tp_reduce(chunks):
    total = chunks[0]
    for k in range(1, len(chunks)):
        total = total + shift_tp(chunks[k], -k).astype(F32)
    return total


def reorder(rows):
    members = lax.axis_size("tp")
    own = lax.axis_index("tp")
    chunk = rows.shape[0] // members
    return jnp.concatenate(
        [
            lax.dynamic_slice_in_dim(rows, (own - k) % members * chunk, chunk, 0)
            for k in range(members)
        ],
        axis=0,
    )


def times(left, right):
    return lax.dot_general(left, right, (((1,), (0,)), ((), ())), preferred_element_type=F32)


def times_t(left, right):
    return lax.dot_general(left, right, (((1,), (1,)), ((), ())), preferred_element_type=F32)


def times_rows(left, right):
    return lax.dot_general(left, right, (((0,), (0,)), ((), ())), preferred_element_type=F32)


def assemble(chunk_refs, target):
    rows = chunk_refs[0].shape[0]
    for k, ref in enumerate(chunk_refs):
        target[k * rows : (k + 1) * rows, :] = ref[...]


def spread(total, chunk_refs):
    rows = chunk_refs[0].shape[0]
    for k, ref in enumerate(chunk_refs):
        ref[...] = total[k * rows : (k + 1) * rows, :].astype(ref.dtype)


def whole(shape):
    return pl.BlockSpec(shape, lambda *_: (0,) * len(shape))


def weight_specs(depth, steps):
    return [
        pl.BlockSpec((depth, 2 * TILE), lambda j: (0, j)),
        pl.BlockSpec((depth, TILE), lambda j: (0, 2 * steps + j)),
    ]


def chunk_shapes(count, rows, width):
    return [jax.ShapeDtypeStruct((rows, width), F32 if k == 0 else BF16) for k in range(count)]


def ffn_forward_kernel(count, *refs):
    x_refs, (gu_ref, dn_ref), outs = refs[:count], refs[count : count + 2], refs[count + 2 : -2]
    x_all, total = refs[-2:]
    step = pl.program_id(0)

    @pl.when(step == 0)
    def _():
        assemble(x_refs, x_all)
        total[...] = jnp.zeros_like(total)

    both = times(x_all[...], gu_ref[...])
    gate, up = both[:, :TILE], both[:, TILE:]
    active = (gate * jax.nn.sigmoid(gate) * up).astype(BF16)
    total[...] += times_t(active, dn_ref[...])

    @pl.when(step == pl.num_programs(0) - 1)
    def _():
        spread(total[...], outs)


def ffn_forward(chunks, pack, steps):
    count, (rows, width) = len(chunks), chunks[0].shape
    tokens = count * rows
    return pl.pallas_call(
        functools.partial(ffn_forward_kernel, count),
        grid=(steps,),
        in_specs=[whole((rows, width))] * count + weight_specs(width, steps),
        out_specs=[whole((rows, width))] * count,
        out_shape=chunk_shapes(count, rows, width),
        scratch_shapes=[pltpu.VMEM((tokens, width), BF16), pltpu.VMEM((tokens, width), F32)],
        compiler_params=pltpu.CompilerParams(vmem_limit_bytes=VMEM_LIMIT),
        cost_estimate=pl.CostEstimate(
            flops=2 * tokens * width * 3 * TILE * steps,
            bytes_accessed=2 * width * 3 * TILE * steps,
            transcendentals=tokens * TILE * steps,
        ),
        name="ffn_forward",
    )(*chunks, pack, pack)


def ffn_backward_kernel(count, forward, core_ref, *refs):
    x_refs, b_refs = refs[:count], refs[count : 2 * count]
    gu_ref, dn_ref = refs[2 * count : 2 * count + 2]
    place = 2 * count + 2
    back_outs = refs[place : place + count]
    place += count
    if forward:
        outs = refs[place : place + count]
        place += count
    keep_ref, side_ref = refs[place : place + 2]
    scratch = refs[place + 2 :]
    x_all, b_all, d_total = scratch[:3]
    step = pl.program_id(0)
    width = x_all.shape[1]

    @pl.when(step == 0)
    def _():
        assemble(x_refs, x_all)
        assemble(b_refs, b_all)
        side_ref[:, :width] = x_all[...]
        side_ref[:, width : 2 * width] = b_all[...]
        d_total[...] = jnp.zeros_like(d_total)
        if forward:
            scratch[3][...] = jnp.zeros_like(scratch[3])

    both = times(x_all[...], gu_ref[...])
    gate, up = both[:, :TILE], both[:, TILE:]
    d_active = times(b_all[...], dn_ref[...])
    sigmoid = jax.nn.sigmoid(gate)
    silu = gate * sigmoid
    active = (silu * up).astype(BF16)
    if forward:
        scratch[3][...] += times_t(active, dn_ref[...])
    d_gate = (d_active * up * (sigmoid * (1.0 + gate * (1.0 - sigmoid)))).astype(BF16)
    d_up = (d_active * silu).astype(BF16)
    d_total[...] += times_t(jnp.concatenate([d_gate, d_up], axis=1), gu_ref[...])
    first = core_ref[0] == 0
    half = TILE // 2
    low, high = active[:, :half], active[:, half:]
    start = pl.multiple_of(2 * width + step * (TILE + half), half)

    @pl.when(first)
    def _():
        keep_ref[:, :TILE] = d_gate
        keep_ref[:, TILE:] = low
        side_ref[:, pl.ds(start, TILE)] = d_up
        side_ref[:, pl.ds(start + TILE, half)] = high

    @pl.when(jnp.logical_not(first))
    def _():
        keep_ref[:, :TILE] = d_up
        keep_ref[:, TILE:] = high
        side_ref[:, pl.ds(start, TILE)] = d_gate
        side_ref[:, pl.ds(start + TILE, half)] = low

    @pl.when(step == pl.num_programs(0) - 1)
    def _():
        spread(d_total[...], back_outs)
        if forward:
            spread(scratch[3][...], outs)


def ffn_backward(core, chunks, back_chunks, pack, steps, forward):
    count, (rows, width) = len(chunks), chunks[0].shape
    tokens = count * rows
    block = TILE + TILE // 2
    ways = 2 if forward else 1
    side_width = 2 * width + steps * block
    results = pl.pallas_call(
        functools.partial(ffn_backward_kernel, count, forward),
        grid=(steps,),
        in_specs=[pl.BlockSpec(memory_space=pltpu.SMEM)]
        + [whole((rows, width))] * (2 * count)
        + weight_specs(width, steps),
        out_specs=[whole((rows, width))] * (ways * count)
        + [pl.BlockSpec((tokens, block), lambda j: (0, j)), whole((tokens, side_width))],
        out_shape=chunk_shapes(count, rows, width) * ways
        + [
            jax.ShapeDtypeStruct((tokens, steps * block), BF16),
            jax.ShapeDtypeStruct((tokens, side_width), BF16),
        ],
        scratch_shapes=[pltpu.VMEM((tokens, width), BF16)] * 2
        + [pltpu.VMEM((tokens, width), F32)] * ways,
        compiler_params=pltpu.CompilerParams(vmem_limit_bytes=VMEM_LIMIT),
        cost_estimate=pl.CostEstimate(
            flops=2 * tokens * width * (4 + ways) * TILE * steps,
            bytes_accessed=2 * width * 3 * TILE * steps + 4 * tokens * side_width,
            transcendentals=tokens * TILE * steps,
        ),
        name="ffn_both" if forward else "ffn_backward",
    )(core, *chunks, *back_chunks, pack, pack)
    return results[:count], results[count : ways * count], results[-2], results[-1]


def gradient_kernel(cut, whole_steps, *refs):
    one_own, one_other, two_own, two_other, own_ref, other_ref = refs[:6]
    out_ref = refs[-1]
    step = pl.program_id(0)

    def product(own_left, other_left, columns):
        total = times_rows(own_left[...], own_ref[:, columns])
        total += times_rows(other_left[...], other_ref[:, columns])
        out_ref[:, columns] = total.astype(BF16)

    if whole_steps:

        @pl.when(step < whole_steps)
        def _():
            product(one_own, one_other, slice(None))

        @pl.when(step >= whole_steps)
        def _():
            product(two_own, two_other, slice(None))

    else:
        product(one_own, one_other, slice(0, cut))
        product(two_own, two_other, slice(cut, None))


def gradient(lefts, own, other, other_start, block, steps, cut, whole_steps, width, out_width, out_start, target):
    tokens = own.shape[0]

    def left_spec(index):
        return pl.BlockSpec((tokens, width), lambda j: (0, index))

    in_specs = [left_spec(index) for unused, index in lefts] + [
        pl.BlockSpec((tokens, block), lambda j: (0, j)),
        pl.BlockSpec((tokens, block), lambda j: (0, other_start + j)),
    ]
    operands = [array for array, unused in lefts] + [own, other]
    aliases = {}
    if target is not None:
        in_specs.append(pl.BlockSpec(memory_space=pl.ANY))
        operands.append(target)
        aliases = {len(operands) - 1: 0}
    return pl.pallas_call(
        functools.partial(gradient_kernel, cut, whole_steps),
        grid=(steps,),
        in_specs=in_specs,
        out_specs=pl.BlockSpec((width, block), lambda j: (0, out_start + j)),
        out_shape=jax.ShapeDtypeStruct((width, out_width), BF16),
        input_output_aliases=aliases,
        compiler_params=pltpu.CompilerParams(vmem_limit_bytes=VMEM_LIMIT),
        cost_estimate=pl.CostEstimate(
            flops=4 * tokens * width * block * steps,
            bytes_accessed=2 * width * block * steps,
            transcendentals=0,
        ),
        name="weight_gradient",
    )(*operands)


def share_rows(summed):
    core = lax.axis_index("core")
    rows = summed.shape[0] // 2
    mine = lax.dynamic_slice_in_dim(summed, core * rows, rows, 0)
    other = swap_core(lax.dynamic_slice_in_dim(summed, (1 - core) * rows, rows, 0))
    first = core == 0
    return jnp.where(first, mine, other).astype(F32), jnp.where(first, other, mine).astype(F32)


def reduce_gradient(partial):
    return share_rows(lax.psum_scatter(partial, CHIP_AXES, scatter_dimension=0, tiled=True))


def exchange_gradient(partial):
    ring = lax.axis_size("x")
    blocks = partial.reshape(ring, ring, -1, partial.shape[1])
    half = partial.shape[1] // 2

    def along(values, axis, dimension):
        total = None
        place = lax.axis_index(axis)
        for k in range(ring):
            block = lax.dynamic_index_in_dim(values, (place + k) % ring, dimension, False)
            block = block if k == 0 else shift_ring(block.astype(BF16), axis, k)
            total = block.astype(F32) if k == 0 else total + block.astype(F32)
        return total

    low = along(along(blocks[..., :half], "x", 0), Z_AXES, 0)
    high = along(along(blocks[..., half:], Z_AXES, 1), "x", 0)
    return share_rows(jnp.concatenate([low, high], axis=1).astype(BF16))


def gather_pack(pack):
    rows, columns = pack.shape
    blocks = pack[None]
    for axis in ("x", Z_AXES):
        blocks = jnp.concatenate(
            [blocks] + [shift_ring(blocks, axis, k) for k in range(1, lax.axis_size(axis))]
        )
    blocks = jnp.concatenate([blocks, swap_core(blocks)])
    ring = lax.axis_size("x")
    index = jnp.arange(blocks.shape[0])
    step_core = (index % CORES - lax.axis_index("core")) % CORES
    step_z = (lax.axis_index(Z_AXES) - index // CORES % ring) % ring
    step_x = (lax.axis_index("x") - index // CORES // ring) % ring
    place = (step_core * ring + step_z) * ring + step_x
    return jnp.take(blocks, place, axis=0, mode="clip").reshape(-1, columns)


def ffn_gradients(low, high, steps, hidden):
    depth = low.shape[0]
    low = low.reshape(depth, steps, -1)
    high = high.reshape(depth, steps, -1)
    gate = low[:, :, :TILE].reshape(depth, -1)[:, :hidden]
    up = high[:, :, :TILE].reshape(depth, -1)[:, :hidden]
    down = jnp.concatenate([low[:, :, TILE:], high[:, :, TILE:]], axis=2)
    return jnp.stack([gate, up], axis=1), down.reshape(depth, -1)[:, :hidden].T


def halves(proj, out):
    first = lax.axis_index("core") == 0
    half = (proj.shape[1] + out.shape[1]) // 2
    late = jnp.concatenate([proj[:, half:], out], axis=1)
    early = proj[:, :half]
    return jnp.where(first, early, late), jnp.where(first, late, early)


def body(
    hidden_in,
    cotangent,
    seq_lengths,
    deal_order,
    mixer_gain,
    mixer_project,
    mixer_kernel,
    mixer_output,
    first_gain,
    first_gateup,
    first_down,
    attend_gain,
    attend_project,
    query_gain,
    key_gain,
    attend_output,
    second_gain,
    second_gateup,
    second_down,
):
    shards = lax.axis_size(TOKEN_AXES)
    contexts = lax.axis_size(CTX_AXES)
    members = lax.axis_size("tp")
    row_count, width = hidden_in.shape
    piece_rows = row_count // shards
    part_rows = piece_rows // members
    chunk = row_count // members
    device = lax.axis_index(TOKEN_AXES)
    own = lax.axis_index("tp")
    core = lax.axis_index("core")
    core_ref = core.reshape(1).astype(jnp.int32)
    depth = mixer_gain.shape[0]
    channels = mixer_output.shape[0]
    hidden = first_down.shape[0]
    heads_width = attend_output.shape[0]
    steps = -(-hidden // TILE)
    padded = steps * TILE
    ffn_width = 3 * padded
    block = TILE + TILE // 2

    def pack_ffn(gateup, down):
        wide = jnp.pad(gateup, ((0, 0), (0, 0), (0, padded - hidden)))
        wide = wide.reshape(depth, 2, steps, TILE).transpose(0, 2, 1, 3).reshape(depth, -1)
        return [wide, jnp.pad(down.T, ((0, 0), (0, padded - hidden)))]

    mixer_pack = jnp.concatenate([mixer_project.reshape(depth, -1), mixer_output.T], axis=1)
    first_pack = jnp.concatenate(
        pack_ffn(first_gateup, first_down) + [attend_project, attend_output.T], axis=1
    )
    second_pack = jnp.concatenate(pack_ffn(second_gateup, second_down), axis=1)
    first_all = lax.all_gather(first_pack, TOKEN_AXES, axis=0, tiled=True)
    second_all = lax.all_gather(second_pack, TOKEN_AXES, axis=0, tiled=True)
    mixer_all = gather_pack(mixer_pack)
    project_a = mixer_all[:, : 3 * channels]
    output_a_t = mixer_all[:, 3 * channels :]
    project_b = first_all[:, ffn_width : ffn_width + attend_project.shape[1]]
    output_b_t = first_all[:, ffn_width + attend_project.shape[1] :]

    piece_table = deal_order.reshape(shards, shards, piece_rows)[:, :, 0]
    anchor = piece_table // row_count
    anchor_piece = piece_table % row_count // piece_rows
    send_piece = jnp.sum(jnp.where(anchor == device, anchor_piece, 0), axis=1)
    my_anchor = lax.dynamic_index_in_dim(anchor, device, 0, keepdims=False)
    gains_row = jnp.concatenate(
        [mixer_gain, first_gain, attend_gain, second_gain, jnp.zeros((width - 4 * depth,), BF16)]
    )

    def my_part(rows):
        parts = rows.reshape(shards, members, part_rows, width)
        return lax.dynamic_index_in_dim(parts, own, 1, keepdims=False)[send_piece]

    outgoing = jnp.concatenate(
        [
            my_part(hidden_in),
            my_part(cotangent),
            jnp.broadcast_to(gains_row, (shards, 1, width)),
        ],
        axis=1,
    )
    arrived = lax.all_to_all(outgoing, TOKEN_AXES, split_axis=0, concat_axis=0, tiled=True)
    gains = (
        arrived[:, 2 * part_rows, : 4 * depth]
        .reshape(shards, 4, depth)
        .transpose(1, 0, 2)
        .reshape(4, width)
        .astype(F32)
    )
    gain_a, gain_f, gain_b, gain_s = gains[0], gains[1], gains[2], gains[3]
    parts = arrived[:, : 2 * part_rows][my_anchor].reshape(2 * shards * part_rows, width)
    parts = jnp.concatenate(tp_gather(parts)).reshape(members, shards, 2, part_rows, width)
    member_slot = (own - jnp.arange(members)) % members
    parts = jnp.stack(
        [lax.dynamic_index_in_dim(parts, member_slot[t], 0, keepdims=False) for t in range(members)],
        axis=2,
    )
    tokens = parts[:, 0].reshape(row_count, width)
    back_s = parts[:, 1].reshape(row_count, width)
    stream0 = lax.dynamic_slice_in_dim(tokens, own * chunk, chunk, 0).astype(F32)
    upstream = lax.dynamic_slice_in_dim(back_s, own * chunk, chunk, 0).astype(F32)
    back_s_chunks = [
        lax.dynamic_slice_in_dim(back_s, (own - k) % members * chunk, chunk, 0)
        for k in range(members)
    ]

    kernel_taps = mixer_kernel.shape[0]
    halo = kernel_taps - 1
    local_rows = device * row_count + jnp.arange(row_count)
    halo_segment, unused = locate(
        seq_lengths, local_rows[0] - halo + jnp.arange(row_count + halo)
    )
    offsets = reorder(jnp.arange(row_count))
    segment, places = locate(seq_lengths, device * row_count + offsets)
    ctx = lax.axis_index(CTX_AXES)
    group_rows = jnp.concatenate(
        [
            (lax.axis_index(GROUP_AXES) * contexts + (ctx ^ mask)) * row_count + offsets
            for mask in range(contexts)
        ]
    )
    key_segment, key_places = locate(seq_lengths, group_rows)
    allowed = (segment[:, None] == key_segment[None, :]) & (key_places[None, :] <= places[:, None])
    half_dim = HD // 2
    frequency = ROPE_BASE ** (-(jnp.arange(half_dim).astype(F32) * 2.0 / HD))
    angles = places.astype(F32)[:, None] * frequency[None, :]
    cosine = jnp.cos(angles)
    sine = jnp.sin(angles)

    kernel_local = lax.dynamic_slice_in_dim(mixer_kernel, own * channels, channels, 1).astype(F32)
    mixer_in = norm_rows(tokens.astype(F32), gain_a).astype(BF16)
    mixer_in_other = swap_core(mixer_in)
    halo_pad = 16
    halo_in = from_behind(mixer_in[row_count - halo_pad :], 1)
    proj_a = times(jnp.concatenate([halo_in, mixer_in]), project_a)
    proj_b_part = proj_a[:, :channels]
    proj_c_part = proj_a[halo_pad:, channels : 2 * channels]
    proj_x_part = proj_a[:, 2 * channels :]
    extended = (proj_b_part * proj_x_part)[halo_pad - halo :].astype(BF16).astype(F32)
    conv_out = shortconv(extended, kernel_local, halo_segment)
    gated_rows = reorder((proj_c_part * conv_out).astype(BF16))
    stream1 = stream0 + tp_reduce(tp_chunks(times_t(gated_rows, output_a_t)))

    normed_f = tp_gather(norm_rows(stream1, gain_f).astype(BF16))
    stream2 = stream1 + tp_reduce(ffn_forward(normed_f, first_all, steps))

    groups = H // KVH
    score_scale = HD ** (-0.5)
    qgain_f = query_gain.astype(F32)
    kgain_f = key_gain.astype(F32)

    def qk_maps(query_in, key_in, gain_q, gain_k):
        return (
            rotate(norm_rows(query_in, gain_q), cosine, sine),
            rotate(norm_rows(key_in, gain_k), cosine, sine),
        )

    attend_in = jnp.concatenate(tp_gather(norm_rows(stream2, gain_b).astype(BF16)))
    proj_b = times(attend_in, project_b).reshape(row_count, -1, groups + 2, HD)
    kv_heads = proj_b.shape[1]
    query_raw = proj_b[:, :, :groups]
    key_raw = proj_b[:, :, groups]
    query_f, key_f = qk_maps(query_raw, key_raw, qgain_f, kgain_f)
    query_b = query_f.astype(BF16)
    key_value = jnp.concatenate(
        [
            key_f.astype(BF16).reshape(row_count, -1),
            proj_b[:, :, groups + 1].astype(BF16).reshape(row_count, -1),
        ],
        axis=1,
    )
    key_value_all = jnp.concatenate(
        [key_value] + [swap_ctx(key_value, mask) for mask in range(1, contexts)], axis=0
    )
    key_all = key_value_all[:, : kv_heads * HD].reshape(-1, kv_heads, HD)
    value_all = key_value_all[:, kv_heads * HD :].reshape(-1, kv_heads, HD)
    scores = (
        jnp.einsum("tkgd,nkd->kgtn", query_b, key_all, preferred_element_type=F32) * score_scale
    )
    masked = jnp.where(allowed, scores, NEGATIVE)
    row_top = jnp.max(masked, axis=-1, keepdims=True)
    exponent = jnp.exp(masked - row_top)
    row_total = jnp.sum(exponent, axis=-1, keepdims=True)
    softmax_rows = exponent / row_total
    log_total = row_top + jnp.log(row_total)
    attended = (
        jnp.einsum(
            "kgtn,nkd->tkgd", softmax_rows.astype(BF16), value_all, preferred_element_type=F32
        )
        .astype(BF16)
        .reshape(row_count, -1)
    )
    stream3 = stream2 + tp_reduce(tp_chunks(times_t(attended, output_b_t)))

    normed_s = tp_gather(norm_rows(stream3, gain_s).astype(BF16))
    d_chunks, out_chunks, keep, side = ffn_backward(
        core_ref, normed_s, back_s_chunks, second_all, steps, True
    )
    unused, pullback = jax.vjp(norm_rows, stream3, gain_s)
    d_stream, gain_s_grad = pullback(tp_reduce(d_chunks))
    d_stream3 = upstream + d_stream
    stream4 = stream3 + tp_reduce(out_chunks)
    side_other = swap_core(side)
    ffn_lefts = [(side, 0), (side_other, 0), (side, 1), (side_other, 1)]
    ffn_cols = steps * block
    side_start = 2 * width // block
    partial = gradient(
        ffn_lefts, keep, side_other, side_start, block, steps, TILE, 0, width, ffn_cols, 0, None
    )

    back_b = tp_gather(d_stream3.astype(BF16))
    back_b, partial = lax.optimization_barrier((back_b, partial))
    second_grads = reduce_gradient(partial)
    back_b = jnp.concatenate(back_b)
    back_b_other = swap_core(back_b)
    attend_in_other = swap_core(attend_in)
    d_attended_b = times(back_b, output_b_t).astype(BF16).reshape(row_count, -1, groups, HD)
    scores_again = (
        jnp.einsum("tkgd,nkd->kgtn", query_b, key_all, preferred_element_type=F32) * score_scale
    )
    probs_again = jnp.where(allowed, jnp.exp(scores_again - log_total), 0.0)
    d_probs = jnp.einsum("tkgd,nkd->kgtn", d_attended_b, value_all, preferred_element_type=F32)
    d_values = jnp.einsum(
        "kgtn,tkgd->nkd", probs_again.astype(BF16), d_attended_b, preferred_element_type=F32
    )
    inner_sum = jnp.sum(probs_again * d_probs, axis=-1, keepdims=True)
    d_scores = (probs_again * (d_probs - inner_sum)).astype(BF16)
    d_query = (
        jnp.einsum("kgtn,nkd->tkgd", d_scores, key_all, preferred_element_type=F32) * score_scale
    )
    d_keys = (
        jnp.einsum("kgtn,tkgd->nkd", d_scores, query_b, preferred_element_type=F32) * score_scale
    )
    d_key_value = jnp.concatenate(
        [d_keys.reshape(-1, kv_heads * HD), d_values.reshape(-1, kv_heads * HD)], axis=1
    )
    d_local = d_key_value[:row_count]
    for mask in range(1, contexts):
        part = d_key_value[mask * row_count : (mask + 1) * row_count].astype(BF16)
        d_local = d_local + swap_ctx(part, mask).astype(F32)
    d_key_local = d_local[:, : kv_heads * HD].reshape(row_count, kv_heads, HD)
    d_value_local = d_local[:, kv_heads * HD :].reshape(row_count, kv_heads, HD)
    unused, pullback = jax.vjp(qk_maps, query_raw, key_raw, qgain_f, kgain_f)
    d_query_raw, d_key_raw, qgain_grad, kgain_grad = pullback((d_query, d_key_local))
    d_proj_b = (
        jnp.concatenate([d_query_raw, d_key_raw[:, :, None], d_value_local[:, :, None]], axis=2)
        .astype(BF16)
        .reshape(row_count, -1)
    )
    d_attend_in = tp_reduce(tp_chunks(times_t(d_proj_b, project_b)))
    unused, pullback = jax.vjp(norm_rows, stream2, gain_b)
    d_norm_b, gain_b_grad = pullback(d_attend_in)
    d_stream2 = d_stream3 + d_norm_b
    keep, send = halves(d_proj_b, attended)
    first_core = core == 0
    attend_cols = keep.shape[1]
    small_tile = 2 * (heads_width + attend_project.shape[1]) // 16
    third = gradient(
        [
            (attend_in, 0),
            (attend_in_other, 0),
            (jnp.where(first_core, attend_in, back_b), 0),
            (jnp.where(first_core, attend_in_other, back_b_other), 0),
        ],
        keep,
        swap_core(send),
        0,
        small_tile,
        attend_cols // small_tile,
        0,
        (attend_project.shape[1] - attend_cols) // small_tile,
        width,
        ffn_cols + attend_cols,
        ffn_cols // small_tile,
        None,
    )

    slot_for_anchor = jnp.sum(
        jnp.where(
            my_anchor[None, :] == jnp.arange(shards)[:, None], jnp.arange(shards)[None, :], 0
        ),
        axis=1,
    )
    dest_for_piece = jnp.sum(
        jnp.where(
            send_piece[None, :] == jnp.arange(shards)[:, None], jnp.arange(shards)[None, :], 0
        ),
        axis=1,
    )
    pieces = shards // members
    slot_place = (own - slot_for_anchor // pieces) % members * pieces + slot_for_anchor % pieces
    out_rows = jnp.concatenate(tp_gather(stream4.astype(BF16)))
    out_rows = out_rows.reshape(shards, piece_rows, width)[slot_place]
    out_home = lax.all_to_all(out_rows, TOKEN_AXES, split_axis=0, concat_axis=0, tiled=True)
    back_f = tp_gather(d_stream2.astype(BF16))
    back_f, third = lax.optimization_barrier((back_f, third))
    d_chunks, unused, keep, side = ffn_backward(
        core_ref, normed_f, back_f, first_all, steps, False
    )
    unused, pullback = jax.vjp(norm_rows, stream1, gain_f)
    d_stream, gain_f_grad = pullback(tp_reduce(d_chunks))
    d_stream1 = d_stream2 + d_stream
    side_other = swap_core(side)
    ffn_lefts = [(side, 0), (side_other, 0), (side, 1), (side_other, 1)]
    partial = gradient(
        ffn_lefts,
        keep,
        side_other,
        side_start,
        block,
        steps,
        TILE,
        0,
        width,
        ffn_cols + attend_cols,
        0,
        third,
    )

    back_a = tp_gather(d_stream1.astype(BF16))
    back_a, partial, out_home = lax.optimization_barrier((back_a, partial, out_home))
    low, high = reduce_gradient(partial)
    first_grads = (low[:, :ffn_cols], high[:, :ffn_cols])
    attend_grads = jnp.concatenate([low[:, ffn_cols:], high[:, ffn_cols:]], axis=1)
    back_a = jnp.concatenate(back_a)
    back_a_other = swap_core(back_a)
    d_gated = reorder(times(back_a, output_a_t))
    d_cgate = d_gated * conv_out
    d_conv = d_gated * proj_c_part
    unused, pullback = jax.vjp(
        lambda ext_rows, kernel_in: shortconv(ext_rows, kernel_in, halo_segment),
        extended,
        kernel_local,
    )
    d_extended, kernel_grad = pullback(d_conv)
    returned = from_behind(d_extended[:halo], -1)
    d_product = d_extended[halo:] + jnp.concatenate(
        [jnp.zeros((row_count - halo, channels), F32), returned]
    )
    d_proj_a = jnp.concatenate(
        [
            d_product * proj_x_part[halo_pad:],
            d_cgate,
            d_product * proj_b_part[halo_pad:],
        ],
        axis=1,
    ).astype(BF16)
    d_mixer_in = tp_reduce(tp_chunks(times_t(reorder(d_proj_a), project_a)))
    unused, pullback = jax.vjp(norm_rows, stream0, gain_a)
    d_norm_a, gain_a_grad = pullback(d_mixer_in)
    d_stream0 = d_stream1 + d_norm_a
    keep, send = halves(d_proj_a, gated_rows)
    mixer_cols = keep.shape[1]
    low, high = exchange_gradient(
        gradient(
            [
                (mixer_in, 0),
                (mixer_in_other, 0),
                (jnp.where(first_core, mixer_in, back_a), 0),
                (jnp.where(first_core, mixer_in_other, back_a_other), 0),
            ],
            keep,
            swap_core(send),
            0,
            mixer_cols,
            1,
            3 * channels - mixer_cols,
            0,
            width,
            mixer_cols,
            0,
            None,
        )
    )
    mixer_grads = jnp.concatenate([low, high], axis=1)

    def row_of(values):
        flat = values.reshape(-1)
        return jnp.concatenate([flat, jnp.zeros((width - flat.shape[0],), F32)])

    small = jnp.stack(
        [
            gain_a_grad,
            gain_f_grad,
            gain_b_grad,
            gain_s_grad,
            row_of(jnp.concatenate([qgain_grad, kgain_grad])),
            row_of(kernel_grad),
        ]
        + [jnp.zeros((width,), F32)] * 10
    )
    last = jnp.concatenate(
        tp_gather(jnp.concatenate([d_stream0.astype(BF16), small.astype(BF16)]))
    )
    last = last.reshape(members, chunk + 16, width)
    grad_rows = last[:, :chunk].reshape(shards, piece_rows, width)[slot_place]
    smalls = last[:, chunk:].astype(F32)
    summed = jnp.sum(smalls[:, :5], axis=0)
    gain_sums = summed[:4].reshape(4, shards, depth).transpose(1, 0, 2).reshape(shards, 4 * depth)
    head_sums = summed[4, : 2 * HD]
    kernel_rows = reorder(smalls[:, 5, : kernel_taps * channels])
    kernel_rows = kernel_rows.reshape(members, kernel_taps, channels).transpose(1, 0, 2)
    shared = jnp.concatenate([kernel_rows.reshape(-1), head_sums])
    fill = 4 * width - 4 * depth - shared.shape[0]
    small_rows = jnp.concatenate(
        [
            gain_sums,
            jnp.broadcast_to(shared, (shards, shared.shape[0])),
            jnp.zeros((shards, fill), F32),
        ],
        axis=1,
    ).astype(BF16)
    home = lax.all_to_all(
        jnp.concatenate([grad_rows, small_rows.reshape(shards, 4, width)], axis=1),
        TOKEN_AXES,
        split_axis=0,
        concat_axis=0,
        tiled=True,
    )
    layer_out = out_home[dest_for_piece].reshape(row_count, width)
    input_gradient = home[:, :piece_rows][dest_for_piece].reshape(row_count, width)
    totals = jnp.sum(home[:, piece_rows:].astype(F32), axis=0).reshape(-1)
    gain_totals = totals[: 4 * depth].reshape(4, depth)
    kernel_end = 4 * depth + kernel_taps * width
    kernel_total = totals[4 * depth : kernel_end].reshape(kernel_taps, width)
    qgain_total = totals[kernel_end : kernel_end + HD]
    kgain_total = totals[kernel_end + HD : kernel_end + 2 * HD]

    gateup_s_grad, down_s_grad = ffn_gradients(*second_grads, steps, hidden)
    gateup_f_grad, down_f_grad = ffn_gradients(*first_grads, steps, hidden)
    proj_cols = attend_project.shape[1]
    return (
        layer_out,
        input_gradient,
        gain_totals[0],
        mixer_grads[:, : 3 * channels].reshape(depth, 3, channels),
        kernel_total,
        mixer_grads[:, 3 * channels :].T,
        gain_totals[1],
        gateup_f_grad,
        down_f_grad,
        gain_totals[2],
        attend_grads[:, :proj_cols],
        qgain_total,
        kgain_total,
        attend_grads[:, proj_cols:].T,
        gain_totals[3],
        gateup_s_grad,
        down_s_grad,
    )


def solution(mesh):
    names = TOKEN_AXES + ("tp",)
    rings = mesh.shape["fsdp"] // 2, 2, mesh.shape["ctx"] // 2, 2, mesh.shape["tp"]
    tokens = P(TOKEN_AXES, None)
    rows = P(TOKEN_AXES)
    three = P(TOKEN_AXES, None, "tp")
    two = P(TOKEN_AXES, "tp")
    turned = P("tp", TOKEN_AXES)
    return jax.shard_map(
        body,
        mesh=Mesh(mesh.devices.reshape(rings), names),
        in_specs=(
            tokens, tokens, P(), P(),
            rows, three, P(), turned,
            rows, three, turned,
            rows, two, P(), P(), turned,
            rows, three, turned,
        ),
        out_specs=(
            tokens, tokens,
            rows, three, P(), turned,
            rows, three, turned,
            rows, two, P(), P(), turned,
            rows, three, turned,
        ),
        check_vma=False,
    )
```

```python
import functools

import jax
import jax.numpy as jnp
from jax import lax
from jax.experimental import pallas as pl
from jax.experimental.pallas import tpu as pltpu
from jax.sharding import Mesh, PartitionSpec as P

H = 24
KVH = 8
HD = 64

EPSILON = 1e-05
ROPE_BASE = 1000000.0
NEGATIVE = -1e30

CHIP_AXES = ("x", "z_hi", "z_lo")
TOKEN_AXES = CHIP_AXES + ("core",)
GROUP_AXES = ("x", "z_hi")
CTX_AXES = ("z_lo", "core")
Z_AXES = ("z_hi", "z_lo")
CORES = 2
TILE = 256
VMEM_LIMIT = 48 * 1024 * 1024
F32 = jnp.float32
BF16 = jnp.bfloat16


def norm_rows(values, scales):
    return values * lax.rsqrt(jnp.mean(values * values, axis=-1, keepdims=True) + EPSILON) * scales


def rotate(values, cosine, sine):
    half_dim = values.shape[-1] // 2
    shape_out = (values.shape[0],) + (1,) * (values.ndim - 2) + (half_dim,)
    cosine = cosine.reshape(shape_out)
    sine = sine.reshape(shape_out)
    first_half = values[..., :half_dim]
    second_half = values[..., half_dim:]
    return jnp.concatenate(
        [
            first_half * cosine - second_half * sine,
            second_half * cosine + first_half * sine,
        ],
        axis=-1,
    )


def locate(lengths, positions):
    seq_ends = jnp.cumsum(lengths)
    segment = jnp.sum((positions[:, None] >= seq_ends[None, :]).astype(jnp.int32), axis=1)
    starts = seq_ends - lengths
    first_row = jnp.sum(
        jnp.where(segment[:, None] == jnp.arange(lengths.shape[0])[None, :], starts[None, :], 0),
        axis=1,
    )
    return (segment, positions - first_row)


def shortconv(extended, kernel_in, segment):
    kernel_taps = kernel_in.shape[0]
    out_rows = extended.shape[0] - kernel_taps + 1
    result = kernel_in[0] * extended[kernel_taps - 1 :]
    for t in range(1, kernel_taps):
        earlier = extended[kernel_taps - 1 - t : kernel_taps - 1 - t + out_rows]
        same_seq = (
            segment[kernel_taps - 1 - t : kernel_taps - 1 - t + out_rows]
            == segment[kernel_taps - 1 :]
        ).astype(F32)[:, None]
        result = result + kernel_in[t] * earlier * same_seq
    return result


def from_behind(block, distance):
    devices = range(lax.axis_size(CTX_AXES))
    route = [(i - distance, i) for i in devices if i - distance in devices]
    return lax.ppermute(block, CTX_AXES, route)


def swap_ctx(block, mask):
    return lax.ppermute(block, CTX_AXES, [(i, i ^ mask) for i in range(lax.axis_size(CTX_AXES))])


def swap_core(block):
    return lax.ppermute(block, "core", [(0, 1), (1, 0)])


def shift_ring(block, axis, distance):
    ring = lax.axis_size(axis)
    return lax.ppermute(block, axis, [(i, (i + distance) % ring) for i in range(ring)])


def shift_tp(block, distance):
    members = lax.axis_size("tp")
    return lax.ppermute(block, "tp", [(i, (i + distance) % members) for i in range(members)])


def tp_gather(shard):
    return [shard] + [shift_tp(shard, k) for k in range(1, lax.axis_size("tp"))]


def tp_chunks(partial):
    rows = partial.shape[0] // lax.axis_size("tp")
    return [
        partial[k * rows : (k + 1) * rows].astype(F32 if k == 0 else BF16)
        for k in range(lax.axis_size("tp"))
    ]


def tp_reduce(chunks):
    total = chunks[0]
    for k in range(1, len(chunks)):
        total = total + shift_tp(chunks[k], -k).astype(F32)
    return total


def arrange(order, rows):
    return times(order, rows).astype(BF16)


def times(left, right):
    return lax.dot_general(left, right, (((1,), (0,)), ((), ())), preferred_element_type=F32)


def times_t(left, right):
    return lax.dot_general(left, right, (((1,), (1,)), ((), ())), preferred_element_type=F32)


def times_rows(left, right):
    return lax.dot_general(left, right, (((0,), (0,)), ((), ())), preferred_element_type=F32)


def assemble(chunk_refs, target):
    rows = chunk_refs[0].shape[0]
    for k, ref in enumerate(chunk_refs):
        target[k * rows : (k + 1) * rows, :] = ref[...]


def spread(total, chunk_refs):
    rows = chunk_refs[0].shape[0]
    for k, ref in enumerate(chunk_refs):
        ref[...] = total[k * rows : (k + 1) * rows, :].astype(ref.dtype)


def whole(shape):
    return pl.BlockSpec(shape, lambda *_: (0,) * len(shape))


def weight_specs(depth, steps):
    return [
        pl.BlockSpec((depth, 2 * TILE), lambda j: (0, j)),
        pl.BlockSpec((depth, TILE), lambda j: (0, 2 * steps + j)),
    ]


def chunk_shapes(count, rows, width):
    return [jax.ShapeDtypeStruct((rows, width), F32 if k == 0 else BF16) for k in range(count)]


def ffn_forward_kernel(count, *refs):
    x_refs, (gu_ref, dn_ref), outs = refs[:count], refs[count : count + 2], refs[count + 2 : -2]
    x_all, total = refs[-2:]
    step = pl.program_id(0)

    @pl.when(step == 0)
    def _():
        assemble(x_refs, x_all)
        total[...] = jnp.zeros_like(total)

    both = times(x_all[...], gu_ref[...])
    gate, up = both[:, :TILE], both[:, TILE:]
    active = (gate * jax.nn.sigmoid(gate) * up).astype(BF16)
    total[...] += times_t(active, dn_ref[...])

    @pl.when(step == pl.num_programs(0) - 1)
    def _():
        spread(total[...], outs)


def ffn_forward(chunks, pack, steps):
    count, (rows, width) = len(chunks), chunks[0].shape
    tokens = count * rows
    return pl.pallas_call(
        functools.partial(ffn_forward_kernel, count),
        grid=(steps,),
        in_specs=[whole((rows, width))] * count + weight_specs(width, steps),
        out_specs=[whole((rows, width))] * count,
        out_shape=chunk_shapes(count, rows, width),
        scratch_shapes=[pltpu.VMEM((tokens, width), BF16), pltpu.VMEM((tokens, width), F32)],
        compiler_params=pltpu.CompilerParams(vmem_limit_bytes=VMEM_LIMIT),
        cost_estimate=pl.CostEstimate(
            flops=2 * tokens * width * 3 * TILE * steps,
            bytes_accessed=2 * width * 3 * TILE * steps,
            transcendentals=tokens * TILE * steps,
        ),
        name="ffn_forward",
    )(*chunks, pack, pack)


def ffn_backward_kernel(count, forward, core_ref, *refs):
    x_refs, b_refs = refs[:count], refs[count : 2 * count]
    gu_ref, dn_ref = refs[2 * count : 2 * count + 2]
    place = 2 * count + 2
    back_outs = refs[place : place + count]
    place += count
    if forward:
        outs = refs[place : place + count]
        place += count
    keep_ref, side_ref = refs[place : place + 2]
    scratch = refs[place + 2 :]
    x_all, b_all, d_total = scratch[:3]
    step = pl.program_id(0)
    width = x_all.shape[1]

    @pl.when(step == 0)
    def _():
        assemble(x_refs, x_all)
        assemble(b_refs, b_all)
        side_ref[:, :width] = x_all[...]
        side_ref[:, width : 2 * width] = b_all[...]
        d_total[...] = jnp.zeros_like(d_total)
        if forward:
            scratch[3][...] = jnp.zeros_like(scratch[3])

    both = times(x_all[...], gu_ref[...])
    gate, up = both[:, :TILE], both[:, TILE:]
    d_active = times(b_all[...], dn_ref[...])
    sigmoid = jax.nn.sigmoid(gate)
    silu = gate * sigmoid
    active = (silu * up).astype(BF16)
    if forward:
        scratch[3][...] += times_t(active, dn_ref[...])
    d_gate = (d_active * up * (sigmoid * (1.0 + gate * (1.0 - sigmoid)))).astype(BF16)
    d_up = (d_active * silu).astype(BF16)
    d_total[...] += times_t(jnp.concatenate([d_gate, d_up], axis=1), gu_ref[...])
    first = core_ref[0] == 0
    half = TILE // 2
    low, high = active[:, :half], active[:, half:]
    start = pl.multiple_of(2 * width + step * (TILE + half), half)

    @pl.when(first)
    def _():
        keep_ref[:, :TILE] = d_gate
        keep_ref[:, TILE:] = low
        side_ref[:, pl.ds(start, TILE)] = d_up
        side_ref[:, pl.ds(start + TILE, half)] = high

    @pl.when(jnp.logical_not(first))
    def _():
        keep_ref[:, :TILE] = d_up
        keep_ref[:, TILE:] = high
        side_ref[:, pl.ds(start, TILE)] = d_gate
        side_ref[:, pl.ds(start + TILE, half)] = low

    @pl.when(step == pl.num_programs(0) - 1)
    def _():
        spread(d_total[...], back_outs)
        if forward:
            spread(scratch[3][...], outs)


def ffn_backward(core, chunks, back_chunks, pack, steps, forward):
    count, (rows, width) = len(chunks), chunks[0].shape
    tokens = count * rows
    block = TILE + TILE // 2
    ways = 2 if forward else 1
    side_width = 2 * width + steps * block
    results = pl.pallas_call(
        functools.partial(ffn_backward_kernel, count, forward),
        grid=(steps,),
        in_specs=[pl.BlockSpec(memory_space=pltpu.SMEM)]
        + [whole((rows, width))] * (2 * count)
        + weight_specs(width, steps),
        out_specs=[whole((rows, width))] * (ways * count)
        + [pl.BlockSpec((tokens, block), lambda j: (0, j)), whole((tokens, side_width))],
        out_shape=chunk_shapes(count, rows, width) * ways
        + [
            jax.ShapeDtypeStruct((tokens, steps * block), BF16),
            jax.ShapeDtypeStruct((tokens, side_width), BF16),
        ],
        scratch_shapes=[pltpu.VMEM((tokens, width), BF16)] * 2
        + [pltpu.VMEM((tokens, width), F32)] * ways,
        compiler_params=pltpu.CompilerParams(vmem_limit_bytes=VMEM_LIMIT),
        cost_estimate=pl.CostEstimate(
            flops=2 * tokens * width * (4 + ways) * TILE * steps,
            bytes_accessed=2 * width * 3 * TILE * steps + 4 * tokens * side_width,
            transcendentals=tokens * TILE * steps,
        ),
        name="ffn_both" if forward else "ffn_backward",
    )(core, *chunks, *back_chunks, pack, pack)
    return results[:count], results[count : ways * count], results[-2], results[-1]


def gradient_kernel(cut, whole_steps, *refs):
    one_own, one_other, two_own, two_other, own_ref, other_ref = refs[:6]
    out_ref = refs[-1]
    step = pl.program_id(0)

    def product(own_left, other_left, columns):
        total = times_rows(own_left[...], own_ref[:, columns])
        total += times_rows(other_left[...], other_ref[:, columns])
        out_ref[:, columns] = total.astype(BF16)

    if whole_steps:

        @pl.when(step < whole_steps)
        def _():
            product(one_own, one_other, slice(None))

        @pl.when(step >= whole_steps)
        def _():
            product(two_own, two_other, slice(None))

    else:
        product(one_own, one_other, slice(0, cut))
        product(two_own, two_other, slice(cut, None))


def gradient(lefts, own, other, other_start, block, steps, cut, whole_steps, width, out_width, out_start, target):
    tokens = own.shape[0]

    def left_spec(index):
        return pl.BlockSpec((tokens, width), lambda j: (0, index))

    in_specs = [left_spec(index) for unused, index in lefts] + [
        pl.BlockSpec((tokens, block), lambda j: (0, j)),
        pl.BlockSpec((tokens, block), lambda j: (0, other_start + j)),
    ]
    operands = [array for array, unused in lefts] + [own, other]
    aliases = {}
    if target is not None:
        in_specs.append(pl.BlockSpec(memory_space=pl.ANY))
        operands.append(target)
        aliases = {len(operands) - 1: 0}
    return pl.pallas_call(
        functools.partial(gradient_kernel, cut, whole_steps),
        grid=(steps,),
        in_specs=in_specs,
        out_specs=pl.BlockSpec((width, block), lambda j: (0, out_start + j)),
        out_shape=jax.ShapeDtypeStruct((width, out_width), BF16),
        input_output_aliases=aliases,
        compiler_params=pltpu.CompilerParams(vmem_limit_bytes=VMEM_LIMIT),
        cost_estimate=pl.CostEstimate(
            flops=4 * tokens * width * block * steps,
            bytes_accessed=2 * width * block * steps,
            transcendentals=0,
        ),
        name="weight_gradient",
    )(*operands)


def share_rows(summed):
    core = lax.axis_index("core")
    rows = summed.shape[0] // 2
    mine = lax.dynamic_slice_in_dim(summed, core * rows, rows, 0)
    other = swap_core(lax.dynamic_slice_in_dim(summed, (1 - core) * rows, rows, 0))
    first = core == 0
    return jnp.where(first, mine, other).astype(F32), jnp.where(first, other, mine).astype(F32)


def reduce_gradient(partial):
    return share_rows(lax.psum_scatter(partial, CHIP_AXES, scatter_dimension=0, tiled=True))


def exchange_gradient(partial):
    ring = lax.axis_size("x")
    blocks = partial.reshape(ring, ring, -1, partial.shape[1])
    half = partial.shape[1] // 2

    def along(values, axis, dimension):
        total = None
        place = lax.axis_index(axis)
        for k in range(ring):
            block = lax.dynamic_index_in_dim(values, (place + k) % ring, dimension, False)
            block = block if k == 0 else shift_ring(block.astype(BF16), axis, k)
            total = block.astype(F32) if k == 0 else total + block.astype(F32)
        return total

    low = along(along(blocks[..., :half], "x", 0), Z_AXES, 0)
    high = along(along(blocks[..., half:], Z_AXES, 1), "x", 0)
    return share_rows(jnp.concatenate([low, high], axis=1).astype(BF16))


def ffn_gradients(low, high, steps, hidden):
    depth = low.shape[0]
    low = low.reshape(depth, steps, -1)
    high = high.reshape(depth, steps, -1)
    gate = low[:, :, :TILE].reshape(depth, -1)[:, :hidden]
    up = high[:, :, :TILE].reshape(depth, -1)[:, :hidden]
    down = jnp.concatenate([low[:, :, TILE:], high[:, :, TILE:]], axis=2)
    return jnp.stack([gate, up], axis=1), down.reshape(depth, -1)[:, :hidden].T


def halves(proj, out):
    first = lax.axis_index("core") == 0
    half = (proj.shape[1] + out.shape[1]) // 2
    late = jnp.concatenate([proj[:, half:], out], axis=1)
    early = proj[:, :half]
    return jnp.where(first, early, late), jnp.where(first, late, early)


def body(
    hidden_in,
    cotangent,
    seq_lengths,
    deal_order,
    mixer_gain,
    mixer_project,
    mixer_kernel,
    mixer_output,
    first_gain,
    first_gateup,
    first_down,
    attend_gain,
    attend_project,
    query_gain,
    key_gain,
    attend_output,
    second_gain,
    second_gateup,
    second_down,
):
    shards = lax.axis_size(TOKEN_AXES)
    contexts = lax.axis_size(CTX_AXES)
    members = lax.axis_size("tp")
    row_count, width = hidden_in.shape
    piece_rows = row_count // shards
    part_rows = piece_rows // members
    chunk = row_count // members
    device = lax.axis_index(TOKEN_AXES)
    own = lax.axis_index("tp")
    core = lax.axis_index("core")
    core_ref = core.reshape(1).astype(jnp.int32)
    depth = mixer_gain.shape[0]
    channels = mixer_output.shape[0]
    hidden = first_down.shape[0]
    heads_width = attend_output.shape[0]
    steps = -(-hidden // TILE)
    padded = steps * TILE
    ffn_width = 3 * padded
    block = TILE + TILE // 2

    def pack_ffn(gateup, down):
        wide = jnp.pad(gateup, ((0, 0), (0, 0), (0, padded - hidden)))
        wide = wide.reshape(depth, 2, steps, TILE).transpose(0, 2, 1, 3).reshape(depth, -1)
        return [wide, jnp.pad(down.T, ((0, 0), (0, padded - hidden)))]

    mixer_pack = jnp.concatenate([mixer_project.reshape(depth, -1), mixer_output.T], axis=1)
    mixer_all = lax.all_gather(mixer_pack, TOKEN_AXES, axis=0, tiled=True)
    first_pack = jnp.concatenate(
        pack_ffn(first_gateup, first_down) + [attend_project, attend_output.T], axis=1
    )
    second_pack = jnp.concatenate(pack_ffn(second_gateup, second_down), axis=1)
    first_all = lax.all_gather(first_pack, TOKEN_AXES, axis=0, tiled=True)
    second_all = lax.all_gather(second_pack, TOKEN_AXES, axis=0, tiled=True)
    project_a = mixer_all[:, : 3 * channels]
    output_a_t = mixer_all[:, 3 * channels :]
    project_b = first_all[:, ffn_width : ffn_width + attend_project.shape[1]]
    output_b_t = first_all[:, ffn_width + attend_project.shape[1] :]

    piece_table = deal_order.reshape(shards, shards, piece_rows)[:, :, 0]
    anchor = piece_table // row_count
    anchor_piece = piece_table % row_count // piece_rows
    send_piece = jnp.sum(jnp.where(anchor == device, anchor_piece, 0), axis=1)
    my_anchor = lax.dynamic_index_in_dim(anchor, device, 0, keepdims=False)
    gains_row = jnp.concatenate(
        [mixer_gain, first_gain, attend_gain, second_gain, jnp.zeros((width - 4 * depth,), BF16)]
    )

    def my_part(rows):
        parts = rows.reshape(shards, members, part_rows, width)
        return lax.dynamic_index_in_dim(parts, own, 1, keepdims=False)[send_piece]

    outgoing = jnp.concatenate(
        [
            my_part(hidden_in),
            my_part(cotangent),
            jnp.broadcast_to(gains_row, (shards, 1, width)),
        ],
        axis=1,
    )
    arrived = lax.all_to_all(outgoing, TOKEN_AXES, split_axis=0, concat_axis=0, tiled=True)
    gains = (
        arrived[:, 2 * part_rows, : 4 * depth]
        .reshape(shards, 4, depth)
        .transpose(1, 0, 2)
        .reshape(4, width)
        .astype(F32)
    )
    gain_a, gain_f, gain_b, gain_s = gains[0], gains[1], gains[2], gains[3]
    parts = arrived[:, : 2 * part_rows][my_anchor]
    own_tokens = parts[:, :part_rows].reshape(chunk, width)
    own_back = parts[:, part_rows:].reshape(chunk, width)
    stream0 = own_tokens.astype(F32)
    upstream = own_back.astype(F32)
    both = tp_gather(jnp.concatenate([own_tokens, own_back]))
    back_s_chunks = [slot[chunk:] for slot in both]

    gathered = jnp.arange(row_count)
    member_of = (own - gathered // chunk) % members
    offsets = (
        gathered % chunk // part_rows * piece_rows + member_of * part_rows + gathered % part_rows
    )
    to_gathered = (offsets[:, None] == gathered[None, :]).astype(BF16)
    to_dealt = (offsets[None, :] == gathered[:, None]).astype(BF16)
    tokens = times(to_dealt, jnp.concatenate([slot[:chunk] for slot in both]))

    kernel_taps = mixer_kernel.shape[0]
    halo = kernel_taps - 1
    local_rows = device * row_count + jnp.arange(row_count)
    halo_segment, unused = locate(
        seq_lengths, local_rows[0] - halo + jnp.arange(row_count + halo)
    )
    segment, places = locate(seq_lengths, device * row_count + offsets)
    ctx = lax.axis_index(CTX_AXES)
    group_rows = jnp.concatenate(
        [
            (lax.axis_index(GROUP_AXES) * contexts + (ctx ^ mask)) * row_count + offsets
            for mask in range(contexts)
        ]
    )
    key_segment, key_places = locate(seq_lengths, group_rows)
    allowed = (segment[:, None] == key_segment[None, :]) & (key_places[None, :] <= places[:, None])
    half_dim = HD // 2
    frequency = ROPE_BASE ** (-(jnp.arange(half_dim).astype(F32) * 2.0 / HD))
    angles = places.astype(F32)[:, None] * frequency[None, :]
    cosine = jnp.cos(angles)
    sine = jnp.sin(angles)

    kernel_local = lax.dynamic_slice_in_dim(mixer_kernel, own * channels, channels, 1).astype(F32)
    mixer_in = norm_rows(tokens, gain_a).astype(BF16)
    mixer_in_other = swap_core(mixer_in)
    halo_pad = 16
    halo_in = from_behind(mixer_in[row_count - halo_pad :], 1)
    proj_a = times(jnp.concatenate([halo_in, mixer_in]), project_a)
    proj_b_part = proj_a[:, :channels]
    proj_c_part = proj_a[halo_pad:, channels : 2 * channels]
    proj_x_part = proj_a[:, 2 * channels :]
    extended = (proj_b_part * proj_x_part)[halo_pad - halo :].astype(BF16).astype(F32)
    conv_out = shortconv(extended, kernel_local, halo_segment)
    gated_rows = (proj_c_part * conv_out).astype(BF16)
    gated_parts = arrange(to_gathered, gated_rows)
    stream1 = stream0 + tp_reduce(tp_chunks(times_t(gated_parts, output_a_t)))

    normed_f = tp_gather(norm_rows(stream1, gain_f).astype(BF16))
    stream2 = stream1 + tp_reduce(ffn_forward(normed_f, first_all, steps))

    groups = H // KVH
    score_scale = HD ** (-0.5)
    qgain_f = query_gain.astype(F32)
    kgain_f = key_gain.astype(F32)

    def qk_maps(query_in, key_in, gain_q, gain_k):
        return (
            rotate(norm_rows(query_in, gain_q), cosine, sine),
            rotate(norm_rows(key_in, gain_k), cosine, sine),
        )

    attend_in = jnp.concatenate(tp_gather(norm_rows(stream2, gain_b).astype(BF16)))
    proj_b = times(attend_in, project_b).reshape(row_count, -1, groups + 2, HD)
    kv_heads = proj_b.shape[1]
    query_raw = proj_b[:, :, :groups]
    key_raw = proj_b[:, :, groups]
    query_f, key_f = qk_maps(query_raw, key_raw, qgain_f, kgain_f)
    query_b = query_f.astype(BF16)
    key_value = jnp.concatenate(
        [
            key_f.astype(BF16).reshape(row_count, -1),
            proj_b[:, :, groups + 1].astype(BF16).reshape(row_count, -1),
        ],
        axis=1,
    )
    key_value_all = jnp.concatenate(
        [key_value] + [swap_ctx(key_value, mask) for mask in range(1, contexts)], axis=0
    )
    key_all = key_value_all[:, : kv_heads * HD].reshape(-1, kv_heads, HD)
    value_all = key_value_all[:, kv_heads * HD :].reshape(-1, kv_heads, HD)
    scores = (
        jnp.einsum("tkgd,nkd->kgtn", query_b, key_all, preferred_element_type=F32) * score_scale
    )
    masked = jnp.where(allowed, scores, NEGATIVE)
    row_top = jnp.max(masked, axis=-1, keepdims=True)
    exponent = jnp.exp(masked - row_top)
    row_total = jnp.sum(exponent, axis=-1, keepdims=True)
    softmax_rows = exponent / row_total
    log_total = row_top + jnp.log(row_total)
    attended = (
        jnp.einsum(
            "kgtn,nkd->tkgd", softmax_rows.astype(BF16), value_all, preferred_element_type=F32
        )
        .astype(BF16)
        .reshape(row_count, -1)
    )
    stream3 = stream2 + tp_reduce(tp_chunks(times_t(attended, output_b_t)))

    normed_s = tp_gather(norm_rows(stream3, gain_s).astype(BF16))
    d_chunks, out_chunks, keep, side = ffn_backward(
        core_ref, normed_s, back_s_chunks, second_all, steps, True
    )
    unused, pullback = jax.vjp(norm_rows, stream3, gain_s)
    d_stream, gain_s_grad = pullback(tp_reduce(d_chunks))
    d_stream3 = upstream + d_stream
    stream4 = stream3 + tp_reduce(out_chunks)
    side_other = swap_core(side)
    ffn_lefts = [(side, 0), (side_other, 0), (side, 1), (side_other, 1)]
    ffn_cols = steps * block
    side_start = 2 * width // block
    partial = gradient(
        ffn_lefts, keep, side_other, side_start, block, steps, TILE, 0, width, ffn_cols, 0, None
    )

    back_b = tp_gather(d_stream3.astype(BF16))
    back_b, partial = lax.optimization_barrier((back_b, partial))
    second_grads = reduce_gradient(partial)
    back_b = jnp.concatenate(back_b)
    back_b_other = swap_core(back_b)
    attend_in_other = swap_core(attend_in)
    d_attended_b = times(back_b, output_b_t).astype(BF16).reshape(row_count, -1, groups, HD)
    scores_again = (
        jnp.einsum("tkgd,nkd->kgtn", query_b, key_all, preferred_element_type=F32) * score_scale
    )
    probs_again = jnp.where(allowed, jnp.exp(scores_again - log_total), 0.0)
    d_probs = jnp.einsum("tkgd,nkd->kgtn", d_attended_b, value_all, preferred_element_type=F32)
    d_values = jnp.einsum(
        "kgtn,tkgd->nkd", probs_again.astype(BF16), d_attended_b, preferred_element_type=F32
    )
    inner_sum = jnp.sum(probs_again * d_probs, axis=-1, keepdims=True)
    d_scores = (probs_again * (d_probs - inner_sum)).astype(BF16)
    d_query = (
        jnp.einsum("kgtn,nkd->tkgd", d_scores, key_all, preferred_element_type=F32) * score_scale
    )
    d_keys = (
        jnp.einsum("kgtn,tkgd->nkd", d_scores, query_b, preferred_element_type=F32) * score_scale
    )
    d_key_value = jnp.concatenate(
        [d_keys.reshape(-1, kv_heads * HD), d_values.reshape(-1, kv_heads * HD)], axis=1
    )
    d_local = d_key_value[:row_count]
    for mask in range(1, contexts):
        part = d_key_value[mask * row_count : (mask + 1) * row_count].astype(BF16)
        d_local = d_local + swap_ctx(part, mask).astype(F32)
    d_key_local = d_local[:, : kv_heads * HD].reshape(row_count, kv_heads, HD)
    d_value_local = d_local[:, kv_heads * HD :].reshape(row_count, kv_heads, HD)
    unused, pullback = jax.vjp(qk_maps, query_raw, key_raw, qgain_f, kgain_f)
    d_query_raw, d_key_raw, qgain_grad, kgain_grad = pullback((d_query, d_key_local))
    d_proj_b = (
        jnp.concatenate([d_query_raw, d_key_raw[:, :, None], d_value_local[:, :, None]], axis=2)
        .astype(BF16)
        .reshape(row_count, -1)
    )
    d_attend_in = tp_reduce(tp_chunks(times_t(d_proj_b, project_b)))
    unused, pullback = jax.vjp(norm_rows, stream2, gain_b)
    d_norm_b, gain_b_grad = pullback(d_attend_in)
    d_stream2 = d_stream3 + d_norm_b
    keep, send = halves(d_proj_b, attended)
    first_core = core == 0
    attend_cols = keep.shape[1]
    small_tile = 2 * (heads_width + attend_project.shape[1]) // 16
    third = gradient(
        [
            (attend_in, 0),
            (attend_in_other, 0),
            (jnp.where(first_core, attend_in, back_b), 0),
            (jnp.where(first_core, attend_in_other, back_b_other), 0),
        ],
        keep,
        swap_core(send),
        0,
        small_tile,
        attend_cols // small_tile,
        0,
        (attend_project.shape[1] - attend_cols) // small_tile,
        width,
        ffn_cols + attend_cols,
        ffn_cols // small_tile,
        None,
    )

    back_f = tp_gather(d_stream2.astype(BF16))
    back_f, third, stream4 = lax.optimization_barrier((back_f, third, stream4))
    d_chunks, unused, keep, side = ffn_backward(
        core_ref, normed_f, back_f, first_all, steps, False
    )
    side_other = swap_core(side)
    ffn_lefts = [(side, 0), (side_other, 0), (side, 1), (side_other, 1)]
    partial = gradient(
        ffn_lefts,
        keep,
        side_other,
        side_start,
        block,
        steps,
        TILE,
        0,
        width,
        ffn_cols + attend_cols,
        0,
        third,
    )

    d_normed, partial = lax.optimization_barrier((tp_reduce(d_chunks), partial))
    unused, pullback = jax.vjp(norm_rows, stream1, gain_f)
    d_stream, gain_f_grad = pullback(d_normed)
    d_stream1 = d_stream2 + d_stream

    back_a = tp_gather(d_stream1.astype(BF16))
    low, high = reduce_gradient(partial)
    first_grads = (low[:, :ffn_cols], high[:, :ffn_cols])
    attend_grads = jnp.concatenate([low[:, ffn_cols:], high[:, ffn_cols:]], axis=1)
    back_a = arrange(to_dealt, jnp.concatenate(back_a))
    back_a_other = swap_core(back_a)
    d_gated = times(back_a, output_a_t)
    d_cgate = d_gated * conv_out
    d_conv = d_gated * proj_c_part
    unused, pullback = jax.vjp(
        lambda ext_rows, kernel_in: shortconv(ext_rows, kernel_in, halo_segment),
        extended,
        kernel_local,
    )
    d_extended, kernel_grad = pullback(d_conv)
    returned = from_behind(d_extended[:halo], -1)
    d_product = d_extended[halo:] + jnp.concatenate(
        [jnp.zeros((row_count - halo, channels), F32), returned]
    )
    d_proj_a = jnp.concatenate(
        [
            d_product * proj_x_part[halo_pad:],
            d_cgate,
            d_product * proj_b_part[halo_pad:],
        ],
        axis=1,
    ).astype(BF16)
    d_chunks = tp_chunks(times_t(arrange(to_gathered, d_proj_a), project_a))
    keep, send = halves(d_proj_a, gated_rows)
    mixer_cols = keep.shape[1]
    partial = gradient(
        [
            (mixer_in, 0),
            (mixer_in_other, 0),
            (jnp.where(first_core, mixer_in, back_a), 0),
            (jnp.where(first_core, mixer_in_other, back_a_other), 0),
        ],
        keep,
        swap_core(send),
        0,
        mixer_cols,
        1,
        3 * channels - mixer_cols,
        0,
        width,
        mixer_cols,
        0,
        None,
    )
    d_mixer_in, partial = lax.optimization_barrier((tp_reduce(d_chunks), partial))
    unused, pullback = jax.vjp(norm_rows, stream0, gain_a)
    d_norm_a, gain_a_grad = pullback(d_mixer_in)
    d_stream0 = d_stream1 + d_norm_a
    low, high = exchange_gradient(partial)
    mixer_grads = jnp.concatenate([low, high], axis=1)

    slot_for_anchor = jnp.sum(
        jnp.where(
            my_anchor[None, :] == jnp.arange(shards)[:, None], jnp.arange(shards)[None, :], 0
        ),
        axis=1,
    )
    gain_rows = jnp.concatenate(
        [
            grad.reshape(shards, depth)
            for grad in (gain_f_grad, gain_b_grad, gain_s_grad, gain_a_grad)
        ],
        axis=1,
    )
    kernel_cols = kernel_taps * channels
    shared = jnp.concatenate([kernel_grad.reshape(-1), qgain_grad, kgain_grad])
    fill = width - shared.shape[0] - 4 * depth
    small_row = jnp.concatenate(
        [
            jnp.broadcast_to(shared, (shards, shared.shape[0])),
            jnp.pad(gain_rows, ((0, 0), (0, fill))),
        ],
        axis=1,
    ).astype(BF16)

    def by_anchor(rows):
        return rows.astype(BF16).reshape(shards, part_rows, width)[slot_for_anchor]

    home = lax.all_to_all(
        jnp.concatenate(
            [by_anchor(d_stream0), by_anchor(stream4), small_row[:, None]], axis=1
        ),
        TOKEN_AXES,
        split_axis=0,
        concat_axis=0,
        tiled=True,
    )
    small_sum = jnp.sum(home[:, 2 * part_rows].astype(F32), axis=0)
    small_high = small_sum.astype(BF16)
    small_low = (small_sum - small_high.astype(F32)).astype(BF16)
    last = tp_gather(
        jnp.concatenate(
            [
                home[:, :part_rows].reshape(chunk, width),
                home[:, part_rows : 2 * part_rows].reshape(chunk, width),
                jnp.pad(jnp.stack([small_high, small_low]), ((0, 6), (0, 0))),
            ]
        )
    )
    home_rows = (
        jnp.repeat(jnp.tile(send_piece, members), part_rows) * piece_rows
        + member_of * part_rows
        + gathered % part_rows
    )
    to_arrival = (home_rows[None, :] == gathered[:, None]).astype(BF16)
    input_gradient = arrange(to_arrival, jnp.concatenate([slot[:chunk] for slot in last]))
    layer_out = arrange(to_arrival, jnp.concatenate([slot[chunk : 2 * chunk] for slot in last]))
    smalls = [
        slot[2 * chunk].astype(F32) + slot[2 * chunk + 1].astype(F32) for slot in last
    ]
    totals = sum(smalls)
    kernel_rows = jnp.stack([small[:kernel_cols].reshape(kernel_taps, channels) for small in smalls])
    kernel_total = jnp.concatenate(
        [
            lax.dynamic_index_in_dim(kernel_rows, (own - member) % members, 0, keepdims=False)
            for member in range(members)
        ],
        axis=1,
    )
    qgain_total = totals[kernel_cols : kernel_cols + HD]
    kgain_total = totals[kernel_cols + HD : kernel_cols + 2 * HD]
    gain_start = kernel_cols + 2 * HD
    gain_totals = totals[gain_start : gain_start + 4 * depth].reshape(4, depth)

    gateup_s_grad, down_s_grad = ffn_gradients(*second_grads, steps, hidden)
    gateup_f_grad, down_f_grad = ffn_gradients(*first_grads, steps, hidden)
    proj_cols = attend_project.shape[1]
    return (
        layer_out,
        input_gradient,
        gain_totals[3],
        mixer_grads[:, : 3 * channels].reshape(depth, 3, channels),
        kernel_total,
        mixer_grads[:, 3 * channels :].T,
        gain_totals[0],
        gateup_f_grad,
        down_f_grad,
        gain_totals[1],
        attend_grads[:, :proj_cols],
        qgain_total,
        kgain_total,
        attend_grads[:, proj_cols:].T,
        gain_totals[2],
        gateup_s_grad,
        down_s_grad,
    )


def solution(mesh):
    names = TOKEN_AXES + ("tp",)
    rings = mesh.shape["fsdp"] // 2, 2, mesh.shape["ctx"] // 2, 2, mesh.shape["tp"]
    tokens = P(TOKEN_AXES, None)
    rows = P(TOKEN_AXES)
    three = P(TOKEN_AXES, None, "tp")
    two = P(TOKEN_AXES, "tp")
    turned = P("tp", TOKEN_AXES)
    return jax.shard_map(
        body,
        mesh=Mesh(mesh.devices.reshape(rings), names),
        in_specs=(
            tokens, tokens, P(), P(),
            rows, three, P(), turned,
            rows, three, turned,
            rows, two, P(), P(), turned,
            rows, three, turned,
        ),
        out_specs=(
            tokens, tokens,
            rows, three, P(), turned,
            rows, three, turned,
            rows, two, P(), P(), turned,
            rows, three, turned,
        ),
        check_vma=False,
    )
```

```python
import functools

import jax
import jax.numpy as jnp
from jax import lax
from jax.experimental import pallas as pl
from jax.experimental.pallas import tpu as pltpu
from jax.sharding import Mesh, PartitionSpec as P

H = 24
KVH = 8
HD = 64

EPSILON = 1e-05
ROPE_BASE = 1000000.0
NEGATIVE = -1e30

CHIP_AXES = ("x", "z_hi", "z_lo")
TOKEN_AXES = CHIP_AXES + ("core",)
GROUP_AXES = ("x", "z_hi")
CTX_AXES = ("z_lo", "core")
Z_AXES = ("z_hi", "z_lo")
CORES = 2
TILE = 256
VMEM_LIMIT = 48 * 1024 * 1024
F32 = jnp.float32
BF16 = jnp.bfloat16


def norm_rows(values, scales):
    return values * lax.rsqrt(jnp.mean(values * values, axis=-1, keepdims=True) + EPSILON) * scales


def rotate(values, cosine, sine):
    half_dim = values.shape[-1] // 2
    shape_out = (values.shape[0],) + (1,) * (values.ndim - 2) + (half_dim,)
    cosine = cosine.reshape(shape_out)
    sine = sine.reshape(shape_out)
    first_half = values[..., :half_dim]
    second_half = values[..., half_dim:]
    return jnp.concatenate(
        [
            first_half * cosine - second_half * sine,
            second_half * cosine + first_half * sine,
        ],
        axis=-1,
    )


def locate(lengths, positions):
    seq_ends = jnp.cumsum(lengths)
    segment = jnp.sum((positions[:, None] >= seq_ends[None, :]).astype(jnp.int32), axis=1)
    starts = seq_ends - lengths
    first_row = jnp.sum(
        jnp.where(segment[:, None] == jnp.arange(lengths.shape[0])[None, :], starts[None, :], 0),
        axis=1,
    )
    return (segment, positions - first_row)


def shortconv(extended, kernel_in, segment):
    kernel_taps = kernel_in.shape[0]
    out_rows = extended.shape[0] - kernel_taps + 1
    result = kernel_in[0] * extended[kernel_taps - 1 :]
    for t in range(1, kernel_taps):
        earlier = extended[kernel_taps - 1 - t : kernel_taps - 1 - t + out_rows]
        same_seq = (
            segment[kernel_taps - 1 - t : kernel_taps - 1 - t + out_rows]
            == segment[kernel_taps - 1 :]
        ).astype(F32)[:, None]
        result = result + kernel_in[t] * earlier * same_seq
    return result


def from_behind(block, distance):
    devices = range(lax.axis_size(CTX_AXES))
    route = [(i - distance, i) for i in devices if i - distance in devices]
    return lax.ppermute(block, CTX_AXES, route)


def swap_ctx(block, mask):
    return lax.ppermute(block, CTX_AXES, [(i, i ^ mask) for i in range(lax.axis_size(CTX_AXES))])


def swap_core(block):
    return lax.ppermute(block, "core", [(0, 1), (1, 0)])


def shift_ring(block, axis, distance):
    ring = lax.axis_size(axis)
    return lax.ppermute(block, axis, [(i, (i + distance) % ring) for i in range(ring)])


def shift_tp(block, distance):
    members = lax.axis_size("tp")
    return lax.ppermute(block, "tp", [(i, (i + distance) % members) for i in range(members)])


def tp_gather(shard):
    return [shard] + [shift_tp(shard, k) for k in range(1, lax.axis_size("tp"))]


def tp_chunks(partial):
    rows = partial.shape[0] // lax.axis_size("tp")
    return [
        partial[k * rows : (k + 1) * rows].astype(F32 if k == 0 else BF16)
        for k in range(lax.axis_size("tp"))
    ]


def tp_reduce(chunks):
    total = chunks[0]
    for k in range(1, len(chunks)):
        total = total + shift_tp(chunks[k], -k).astype(F32)
    return total


def arrange(order, rows):
    return times(order, rows).astype(BF16)


def times(left, right):
    return lax.dot_general(left, right, (((1,), (0,)), ((), ())), preferred_element_type=F32)


def times_t(left, right):
    return lax.dot_general(left, right, (((1,), (1,)), ((), ())), preferred_element_type=F32)


def times_rows(left, right):
    return lax.dot_general(left, right, (((0,), (0,)), ((), ())), preferred_element_type=F32)


def assemble(chunk_refs, target):
    rows = chunk_refs[0].shape[0]
    for k, ref in enumerate(chunk_refs):
        target[k * rows : (k + 1) * rows, :] = ref[...]


def spread(total, chunk_refs):
    rows = chunk_refs[0].shape[0]
    for k, ref in enumerate(chunk_refs):
        ref[...] = total[k * rows : (k + 1) * rows, :].astype(ref.dtype)


def whole(shape):
    return pl.BlockSpec(shape, lambda *_: (0,) * len(shape))


def weight_specs(depth, steps):
    return [
        pl.BlockSpec((depth, 2 * TILE), lambda j: (0, j)),
        pl.BlockSpec((depth, TILE), lambda j: (0, 2 * steps + j)),
    ]


def chunk_shapes(count, rows, width):
    return [jax.ShapeDtypeStruct((rows, width), F32 if k == 0 else BF16) for k in range(count)]


def ffn_forward_kernel(count, *refs):
    x_refs, (gu_ref, dn_ref), outs = refs[:count], refs[count : count + 2], refs[count + 2 : -2]
    x_all, total = refs[-2:]
    step = pl.program_id(0)

    @pl.when(step == 0)
    def _():
        assemble(x_refs, x_all)
        total[...] = jnp.zeros_like(total)

    both = times(x_all[...], gu_ref[...])
    gate, up = both[:, :TILE], both[:, TILE:]
    active = (gate * jax.nn.sigmoid(gate) * up).astype(BF16)
    total[...] += times_t(active, dn_ref[...])

    @pl.when(step == pl.num_programs(0) - 1)
    def _():
        spread(total[...], outs)


def ffn_forward(chunks, pack, steps):
    count, (rows, width) = len(chunks), chunks[0].shape
    tokens = count * rows
    return pl.pallas_call(
        functools.partial(ffn_forward_kernel, count),
        grid=(steps,),
        in_specs=[whole((rows, width))] * count + weight_specs(width, steps),
        out_specs=[whole((rows, width))] * count,
        out_shape=chunk_shapes(count, rows, width),
        scratch_shapes=[pltpu.VMEM((tokens, width), BF16), pltpu.VMEM((tokens, width), F32)],
        compiler_params=pltpu.CompilerParams(vmem_limit_bytes=VMEM_LIMIT),
        cost_estimate=pl.CostEstimate(
            flops=2 * tokens * width * 3 * TILE * steps,
            bytes_accessed=2 * width * 3 * TILE * steps,
            transcendentals=tokens * TILE * steps,
        ),
        name="ffn_forward",
    )(*chunks, pack, pack)


def ffn_backward_kernel(count, forward, core_ref, *refs):
    x_refs, b_refs = refs[:count], refs[count : 2 * count]
    gu_ref, dn_ref = refs[2 * count : 2 * count + 2]
    place = 2 * count + 2
    back_outs = refs[place : place + count]
    place += count
    if forward:
        outs = refs[place : place + count]
        place += count
    keep_ref, side_ref = refs[place : place + 2]
    scratch = refs[place + 2 :]
    x_all, b_all, d_total = scratch[:3]
    step = pl.program_id(0)
    width = x_all.shape[1]

    @pl.when(step == 0)
    def _():
        assemble(x_refs, x_all)
        assemble(b_refs, b_all)
        if forward:
            side_ref[:, :width] = x_all[...]
            side_ref[:, width : 2 * width] = b_all[...]
        d_total[...] = jnp.zeros_like(d_total)
        if forward:
            scratch[3][...] = jnp.zeros_like(scratch[3])

    both = times(x_all[...], gu_ref[...])
    gate, up = both[:, :TILE], both[:, TILE:]
    d_active = times(b_all[...], dn_ref[...])
    sigmoid = jax.nn.sigmoid(gate)
    silu = gate * sigmoid
    active = (silu * up).astype(BF16)
    if forward:
        scratch[3][...] += times_t(active, dn_ref[...])
    d_gate = (d_active * up * (sigmoid * (1.0 + gate * (1.0 - sigmoid)))).astype(BF16)
    d_up = (d_active * silu).astype(BF16)
    d_total[...] += times_t(jnp.concatenate([d_gate, d_up], axis=1), gu_ref[...])
    first = core_ref[0] == 0
    half = TILE // 2
    low, high = active[:, :half], active[:, half:]
    start = (2 * width if forward else 0) + step * (TILE + half)
    start = pl.multiple_of(start, half)

    @pl.when(first)
    def _():
        keep_ref[:, :TILE] = d_gate
        keep_ref[:, TILE:] = low
        side_ref[:, pl.ds(start, TILE)] = d_up
        side_ref[:, pl.ds(start + TILE, half)] = high

    @pl.when(jnp.logical_not(first))
    def _():
        keep_ref[:, :TILE] = d_up
        keep_ref[:, TILE:] = high
        side_ref[:, pl.ds(start, TILE)] = d_gate
        side_ref[:, pl.ds(start + TILE, half)] = low

    @pl.when(step == pl.num_programs(0) - 1)
    def _():
        spread(d_total[...], back_outs)
        if forward:
            spread(scratch[3][...], outs)


def ffn_backward(core, chunks, back_chunks, pack, steps, forward):
    count, (rows, width) = len(chunks), chunks[0].shape
    tokens = count * rows
    block = TILE + TILE // 2
    ways = 2 if forward else 1
    side_width = (2 * width if forward else 0) + steps * block
    results = pl.pallas_call(
        functools.partial(ffn_backward_kernel, count, forward),
        grid=(steps,),
        in_specs=[pl.BlockSpec(memory_space=pltpu.SMEM)]
        + [whole((rows, width))] * (2 * count)
        + weight_specs(width, steps),
        out_specs=[whole((rows, width))] * (ways * count)
        + [pl.BlockSpec((tokens, block), lambda j: (0, j)), whole((tokens, side_width))],
        out_shape=chunk_shapes(count, rows, width) * ways
        + [
            jax.ShapeDtypeStruct((tokens, steps * block), BF16),
            jax.ShapeDtypeStruct((tokens, side_width), BF16),
        ],
        scratch_shapes=[pltpu.VMEM((tokens, width), BF16)] * 2
        + [pltpu.VMEM((tokens, width), F32)] * ways,
        compiler_params=pltpu.CompilerParams(vmem_limit_bytes=VMEM_LIMIT),
        cost_estimate=pl.CostEstimate(
            flops=2 * tokens * width * (4 + ways) * TILE * steps,
            bytes_accessed=2 * width * 3 * TILE * steps + 4 * tokens * side_width,
            transcendentals=tokens * TILE * steps,
        ),
        name="ffn_both" if forward else "ffn_backward",
    )(core, *chunks, *back_chunks, pack, pack)
    return results[:count], results[count : ways * count], results[-2], results[-1]


def gradient_kernel(cut, whole_steps, *refs):
    one_own, one_other, two_own, two_other, own_ref, other_ref = refs[:6]
    out_ref = refs[-1]
    step = pl.program_id(0)

    def product(own_left, other_left, columns):
        total = times_rows(own_left[...], own_ref[:, columns])
        total += times_rows(other_left[...], other_ref[:, columns])
        out_ref[:, columns] = total.astype(BF16)

    if whole_steps:

        @pl.when(step < whole_steps)
        def _():
            product(one_own, one_other, slice(None))

        @pl.when(step >= whole_steps)
        def _():
            product(two_own, two_other, slice(None))

    else:
        product(one_own, one_other, slice(0, cut))
        product(two_own, two_other, slice(cut, None))


def gradient(lefts, own, other, other_start, block, steps, cut, whole_steps, width, out_width, out_start, target):
    tokens = own.shape[0]

    def left_spec(index):
        return pl.BlockSpec((tokens, width), lambda j: (0, index))

    in_specs = [left_spec(index) for unused, index in lefts] + [
        pl.BlockSpec((tokens, block), lambda j: (0, j)),
        pl.BlockSpec((tokens, block), lambda j: (0, other_start + j)),
    ]
    operands = [array for array, unused in lefts] + [own, other]
    aliases = {}
    if target is not None:
        in_specs.append(pl.BlockSpec(memory_space=pl.ANY))
        operands.append(target)
        aliases = {len(operands) - 1: 0}
    return pl.pallas_call(
        functools.partial(gradient_kernel, cut, whole_steps),
        grid=(steps,),
        in_specs=in_specs,
        out_specs=pl.BlockSpec((width, block), lambda j: (0, out_start + j)),
        out_shape=jax.ShapeDtypeStruct((width, out_width), BF16),
        input_output_aliases=aliases,
        compiler_params=pltpu.CompilerParams(vmem_limit_bytes=VMEM_LIMIT),
        cost_estimate=pl.CostEstimate(
            flops=4 * tokens * width * block * steps,
            bytes_accessed=2 * width * block * steps,
            transcendentals=0,
        ),
        name="weight_gradient",
    )(*operands)


def share_rows(summed):
    core = lax.axis_index("core")
    rows = summed.shape[0] // 2
    mine = lax.dynamic_slice_in_dim(summed, core * rows, rows, 0)
    other = swap_core(lax.dynamic_slice_in_dim(summed, (1 - core) * rows, rows, 0))
    first = core == 0
    return jnp.where(first, mine, other).astype(F32), jnp.where(first, other, mine).astype(F32)


def reduce_gradient(partial):
    return share_rows(lax.psum_scatter(partial, CHIP_AXES, scatter_dimension=0, tiled=True))


def along(values, axis, dimension):
    ring = lax.axis_size(axis)
    place = lax.axis_index(axis)
    total = None
    for k in range(ring):
        block = lax.dynamic_index_in_dim(values, (place + k) % ring, dimension, False)
        block = block if k == 0 else shift_ring(block.astype(BF16), axis, k)
        total = block.astype(F32) if k == 0 else total + block.astype(F32)
    return total


def exchange_first(partial):
    ring = lax.axis_size("x")
    blocks = partial.reshape(ring, ring, -1, partial.shape[1])
    half = partial.shape[1] // 2
    return along(blocks[..., :half], "x", 0), along(blocks[..., half:], Z_AXES, 1)


def exchange_second(low, high):
    total = jnp.concatenate([along(low, Z_AXES, 0), along(high, "x", 0)], axis=1)
    return share_rows(total.astype(BF16))


def gather_pack(pack):
    rows, columns = pack.shape
    half = columns // 2
    ring = lax.axis_size("x")
    x, z, core = lax.axis_index("x"), lax.axis_index(Z_AXES), lax.axis_index("core")

    def fill(shape, parts):
        result = jnp.zeros(shape, pack.dtype)
        for part, place in parts:
            result = lax.dynamic_update_slice(result, part, place)
        return result

    low, high = pack[:, :half], pack[:, half:]
    low_parts = [(shift_ring(low, "x", k)[None] if k else low[None], k) for k in range(ring)]
    high_parts = [(shift_ring(high, Z_AXES, k)[None] if k else high[None], k) for k in range(ring)]
    low = fill((ring, rows, half), [(v, ((x - k) % ring, 0, 0)) for v, k in low_parts])
    high = fill((ring, rows, half), [(v, ((z - k) % ring, 0, 0)) for v, k in high_parts])
    parts = []
    for k in range(ring):
        part = shift_ring(low, Z_AXES, k) if k else low
        parts.append((part[:, None], (0, (z - k) % ring, 0, 0)))
        part = shift_ring(high, "x", k) if k else high
        parts.append((part[None], ((x - k) % ring, 0, 0, half)))
    plane = fill((ring, ring, rows, columns), parts)
    other = swap_core(plane)
    both = fill(
        (ring, ring, CORES, rows, columns),
        [
            (plane[:, :, None], (0, 0, core, 0, 0)),
            (other[:, :, None], (0, 0, 1 - core, 0, 0)),
        ],
    )
    return both.reshape(-1, columns)


def ffn_gradients(low, high, steps, hidden):
    depth = low.shape[0]
    low = low.reshape(depth, steps, -1)
    high = high.reshape(depth, steps, -1)
    gate = low[:, :, :TILE].reshape(depth, -1)[:, :hidden]
    up = high[:, :, :TILE].reshape(depth, -1)[:, :hidden]
    down = jnp.concatenate([low[:, :, TILE:], high[:, :, TILE:]], axis=2)
    return jnp.stack([gate, up], axis=1), down.reshape(depth, -1)[:, :hidden].T


def halves(proj, out):
    first = lax.axis_index("core") == 0
    half = (proj.shape[1] + out.shape[1]) // 2
    late = jnp.concatenate([proj[:, half:], out], axis=1)
    early = proj[:, :half]
    return jnp.where(first, early, late), jnp.where(first, late, early)


def body(
    hidden_in,
    cotangent,
    seq_lengths,
    deal_order,
    mixer_gain,
    mixer_project,
    mixer_kernel,
    mixer_output,
    first_gain,
    first_gateup,
    first_down,
    attend_gain,
    attend_project,
    query_gain,
    key_gain,
    attend_output,
    second_gain,
    second_gateup,
    second_down,
):
    shards = lax.axis_size(TOKEN_AXES)
    contexts = lax.axis_size(CTX_AXES)
    members = lax.axis_size("tp")
    row_count, width = hidden_in.shape
    piece_rows = row_count // shards
    part_rows = piece_rows // members
    chunk = row_count // members
    device = lax.axis_index(TOKEN_AXES)
    own = lax.axis_index("tp")
    core = lax.axis_index("core")
    core_ref = core.reshape(1).astype(jnp.int32)
    depth = mixer_gain.shape[0]
    channels = mixer_output.shape[0]
    hidden = first_down.shape[0]
    heads_width = attend_output.shape[0]
    steps = -(-hidden // TILE)
    padded = steps * TILE
    ffn_width = 3 * padded
    block = TILE + TILE // 2

    def pack_ffn(gateup, down):
        wide = jnp.pad(gateup, ((0, 0), (0, 0), (0, padded - hidden)))
        wide = wide.reshape(depth, 2, steps, TILE).transpose(0, 2, 1, 3).reshape(depth, -1)
        return [wide, jnp.pad(down.T, ((0, 0), (0, padded - hidden)))]

    mixer_pack = jnp.concatenate([mixer_project.reshape(depth, -1), mixer_output.T], axis=1)
    first_pack = jnp.concatenate(
        pack_ffn(first_gateup, first_down) + [attend_project, attend_output.T], axis=1
    )
    second_pack = jnp.concatenate(pack_ffn(second_gateup, second_down), axis=1)
    first_all = lax.all_gather(first_pack, TOKEN_AXES, axis=0, tiled=True)
    mixer_all = gather_pack(mixer_pack)
    second_all = lax.all_gather(second_pack, TOKEN_AXES, axis=0, tiled=True)
    project_a = mixer_all[:, : 3 * channels]
    output_a_t = mixer_all[:, 3 * channels :]
    project_b = first_all[:, ffn_width : ffn_width + attend_project.shape[1]]
    output_b_t = first_all[:, ffn_width + attend_project.shape[1] :]

    piece_table = deal_order.reshape(shards, shards, piece_rows)[:, :, 0]
    anchor = piece_table // row_count
    anchor_piece = piece_table % row_count // piece_rows
    send_piece = jnp.sum(jnp.where(anchor == device, anchor_piece, 0), axis=1)
    my_anchor = lax.dynamic_index_in_dim(anchor, device, 0, keepdims=False)
    gains_row = jnp.concatenate(
        [mixer_gain, first_gain, attend_gain, second_gain, jnp.zeros((width - 4 * depth,), BF16)]
    )

    def my_part(rows):
        parts = rows.reshape(shards, members, part_rows, width)
        return lax.dynamic_index_in_dim(parts, own, 1, keepdims=False)[send_piece]

    outgoing = jnp.concatenate(
        [
            my_part(hidden_in),
            my_part(cotangent),
            jnp.broadcast_to(gains_row, (shards, 1, width)),
        ],
        axis=1,
    )
    arrived = lax.all_to_all(outgoing, TOKEN_AXES, split_axis=0, concat_axis=0, tiled=True)
    gains = (
        arrived[:, 2 * part_rows, : 4 * depth]
        .reshape(shards, 4, depth)
        .transpose(1, 0, 2)
        .reshape(4, width)
        .astype(F32)
    )
    gain_a, gain_f, gain_b, gain_s = gains[0], gains[1], gains[2], gains[3]
    parts = arrived[:, : 2 * part_rows][my_anchor]
    own_tokens = parts[:, :part_rows].reshape(chunk, width)
    own_back = parts[:, part_rows:].reshape(chunk, width)
    stream0 = own_tokens.astype(F32)
    upstream = own_back.astype(F32)
    both = tp_gather(jnp.concatenate([own_tokens, own_back]))
    back_s_chunks = [slot[chunk:] for slot in both]

    gathered = jnp.arange(row_count)
    member_of = (own - gathered // chunk) % members
    offsets = (
        gathered % chunk // part_rows * piece_rows + member_of * part_rows + gathered % part_rows
    )
    to_gathered = (offsets[:, None] == gathered[None, :]).astype(BF16)
    to_dealt = (offsets[None, :] == gathered[:, None]).astype(BF16)
    tokens = times(to_dealt, jnp.concatenate([slot[:chunk] for slot in both]))

    kernel_taps = mixer_kernel.shape[0]
    halo = kernel_taps - 1
    local_rows = device * row_count + jnp.arange(row_count)
    halo_segment, unused = locate(
        seq_lengths, local_rows[0] - halo + jnp.arange(row_count + halo)
    )
    segment, places = locate(seq_lengths, device * row_count + offsets)
    ctx = lax.axis_index(CTX_AXES)
    group_rows = jnp.concatenate(
        [
            (lax.axis_index(GROUP_AXES) * contexts + (ctx ^ mask)) * row_count + offsets
            for mask in range(contexts)
        ]
    )
    key_segment, key_places = locate(seq_lengths, group_rows)
    allowed = (segment[:, None] == key_segment[None, :]) & (key_places[None, :] <= places[:, None])
    half_dim = HD // 2
    frequency = ROPE_BASE ** (-(jnp.arange(half_dim).astype(F32) * 2.0 / HD))
    angles = places.astype(F32)[:, None] * frequency[None, :]
    cosine = jnp.cos(angles)
    sine = jnp.sin(angles)

    kernel_local = lax.dynamic_slice_in_dim(mixer_kernel, own * channels, channels, 1).astype(F32)
    mixer_in = norm_rows(tokens, gain_a).astype(BF16)
    mixer_in_other = swap_core(mixer_in)
    halo_pad = 16
    halo_in = from_behind(mixer_in[row_count - halo_pad :], 1)
    proj_a = times(jnp.concatenate([halo_in, mixer_in]), project_a)
    proj_b_part = proj_a[:, :channels]
    proj_c_part = proj_a[halo_pad:, channels : 2 * channels]
    proj_x_part = proj_a[:, 2 * channels :]
    extended = (proj_b_part * proj_x_part)[halo_pad - halo :].astype(BF16).astype(F32)
    conv_out = shortconv(extended, kernel_local, halo_segment)
    gated_rows = (proj_c_part * conv_out).astype(BF16)
    gated_parts = arrange(to_gathered, gated_rows)
    stream1 = stream0 + tp_reduce(tp_chunks(times_t(gated_parts, output_a_t)))

    normed_f = tp_gather(norm_rows(stream1, gain_f).astype(BF16))
    stream2 = stream1 + tp_reduce(ffn_forward(normed_f, first_all, steps))

    groups = H // KVH
    score_scale = HD ** (-0.5)
    qgain_f = query_gain.astype(F32)
    kgain_f = key_gain.astype(F32)

    def qk_maps(query_in, key_in, gain_q, gain_k):
        return (
            rotate(norm_rows(query_in, gain_q), cosine, sine),
            rotate(norm_rows(key_in, gain_k), cosine, sine),
        )

    attend_in = jnp.concatenate(tp_gather(norm_rows(stream2, gain_b).astype(BF16)))
    proj_b = times(attend_in, project_b).reshape(row_count, -1, groups + 2, HD)
    kv_heads = proj_b.shape[1]
    query_raw = proj_b[:, :, :groups]
    key_raw = proj_b[:, :, groups]
    query_f, key_f = qk_maps(query_raw, key_raw, qgain_f, kgain_f)
    query_b = query_f.astype(BF16)
    key_value = jnp.concatenate(
        [
            key_f.astype(BF16).reshape(row_count, -1),
            proj_b[:, :, groups + 1].astype(BF16).reshape(row_count, -1),
        ],
        axis=1,
    )
    key_value_all = jnp.concatenate(
        [key_value] + [swap_ctx(key_value, mask) for mask in range(1, contexts)], axis=0
    )
    key_all = key_value_all[:, : kv_heads * HD].reshape(-1, kv_heads, HD)
    value_all = key_value_all[:, kv_heads * HD :].reshape(-1, kv_heads, HD)
    scores = (
        jnp.einsum("tkgd,nkd->kgtn", query_b, key_all, preferred_element_type=F32) * score_scale
    )
    masked = jnp.where(allowed, scores, NEGATIVE)
    row_top = jnp.max(masked, axis=-1, keepdims=True)
    exponent = jnp.exp(masked - row_top)
    row_total = jnp.sum(exponent, axis=-1, keepdims=True)
    softmax_rows = exponent / row_total
    log_total = row_top + jnp.log(row_total)
    attended = (
        jnp.einsum(
            "kgtn,nkd->tkgd", softmax_rows.astype(BF16), value_all, preferred_element_type=F32
        )
        .astype(BF16)
        .reshape(row_count, -1)
    )
    stream3 = stream2 + tp_reduce(tp_chunks(times_t(attended, output_b_t)))

    normed_s = tp_gather(norm_rows(stream3, gain_s).astype(BF16))
    d_chunks, out_chunks, keep, side = ffn_backward(
        core_ref, normed_s, back_s_chunks, second_all, steps, True
    )
    unused, pullback = jax.vjp(norm_rows, stream3, gain_s)
    d_stream, gain_s_grad = pullback(tp_reduce(d_chunks))
    d_stream3 = upstream + d_stream
    out_others = [shift_tp(out_chunks[k], -k) for k in range(1, members)]
    side_other = swap_core(side)
    ffn_lefts = [(side, 0), (side_other, 0), (side, 1), (side_other, 1)]
    ffn_cols = steps * block
    side_start = 2 * width // block
    partial = gradient(
        ffn_lefts, keep, side_other, side_start, block, steps, TILE, 0, width, ffn_cols, 0, None
    )

    back_b = tp_gather(d_stream3.astype(BF16))
    back_b, partial = lax.optimization_barrier((back_b, partial))
    second_grads = reduce_gradient(partial)
    back_b = jnp.concatenate(back_b)
    back_b_other = swap_core(back_b)
    attend_in_other = swap_core(attend_in)
    d_attended_b = times(back_b, output_b_t).astype(BF16).reshape(row_count, -1, groups, HD)
    scores_again = (
        jnp.einsum("tkgd,nkd->kgtn", query_b, key_all, preferred_element_type=F32) * score_scale
    )
    probs_again = jnp.where(allowed, jnp.exp(scores_again - log_total), 0.0)
    d_probs = jnp.einsum("tkgd,nkd->kgtn", d_attended_b, value_all, preferred_element_type=F32)
    d_values = jnp.einsum(
        "kgtn,tkgd->nkd", probs_again.astype(BF16), d_attended_b, preferred_element_type=F32
    )
    inner_sum = jnp.sum(probs_again * d_probs, axis=-1, keepdims=True)
    d_scores = (probs_again * (d_probs - inner_sum)).astype(BF16)
    d_query = (
        jnp.einsum("kgtn,nkd->tkgd", d_scores, key_all, preferred_element_type=F32) * score_scale
    )
    d_keys = (
        jnp.einsum("kgtn,tkgd->nkd", d_scores, query_b, preferred_element_type=F32) * score_scale
    )
    d_key_value = jnp.concatenate(
        [d_keys.reshape(-1, kv_heads * HD), d_values.reshape(-1, kv_heads * HD)], axis=1
    )
    d_local = d_key_value[:row_count]
    for mask in range(1, contexts):
        part = d_key_value[mask * row_count : (mask + 1) * row_count].astype(BF16)
        d_local = d_local + swap_ctx(part, mask).astype(F32)
    d_key_local = d_local[:, : kv_heads * HD].reshape(row_count, kv_heads, HD)
    d_value_local = d_local[:, kv_heads * HD :].reshape(row_count, kv_heads, HD)
    unused, pullback = jax.vjp(qk_maps, query_raw, key_raw, qgain_f, kgain_f)
    d_query_raw, d_key_raw, qgain_grad, kgain_grad = pullback((d_query, d_key_local))
    d_proj_b = (
        jnp.concatenate([d_query_raw, d_key_raw[:, :, None], d_value_local[:, :, None]], axis=2)
        .astype(BF16)
        .reshape(row_count, -1)
    )
    d_attend_in = tp_reduce(tp_chunks(times_t(d_proj_b, project_b)))
    unused, pullback = jax.vjp(norm_rows, stream2, gain_b)
    d_norm_b, gain_b_grad = pullback(d_attend_in)
    d_stream2 = d_stream3 + d_norm_b
    keep, send = halves(d_proj_b, attended)
    first_core = core == 0
    attend_cols = keep.shape[1]
    small_tile = 2 * (heads_width + attend_project.shape[1]) // 16
    third = gradient(
        [
            (attend_in, 0),
            (attend_in_other, 0),
            (jnp.where(first_core, attend_in, back_b), 0),
            (jnp.where(first_core, attend_in_other, back_b_other), 0),
        ],
        keep,
        swap_core(send),
        0,
        small_tile,
        attend_cols // small_tile,
        0,
        (attend_project.shape[1] - attend_cols) // small_tile,
        width,
        ffn_cols + attend_cols,
        ffn_cols // small_tile,
        None,
    )

    back_f = tp_gather(d_stream2.astype(BF16))
    back_f, third = lax.optimization_barrier((back_f, third))
    left_x, left_b = jnp.concatenate(normed_f), jnp.concatenate(back_f)
    ffn_lefts = [(left_x, 0), (swap_core(left_x), 0), (left_b, 0), (swap_core(left_b), 0)]
    d_chunks, unused, keep, side = ffn_backward(
        core_ref, normed_f, back_f, first_all, steps, False
    )
    d_chunks, out_others = lax.optimization_barrier((d_chunks, out_others))
    stream4 = stream3 + out_chunks[0]
    for part in out_others:
        stream4 = stream4 + part.astype(F32)
    partial = gradient(
        ffn_lefts,
        keep,
        swap_core(side),
        0,
        block,
        steps,
        TILE,
        0,
        width,
        ffn_cols + attend_cols,
        0,
        third,
    )

    d_normed, partial = lax.optimization_barrier((tp_reduce(d_chunks), partial))
    unused, pullback = jax.vjp(norm_rows, stream1, gain_f)
    d_stream, gain_f_grad = pullback(d_normed)
    d_stream1 = d_stream2 + d_stream

    back_a = tp_gather(d_stream1.astype(BF16))
    low, high = reduce_gradient(partial)
    first_grads = (low[:, :ffn_cols], high[:, :ffn_cols])
    attend_grads = jnp.concatenate([low[:, ffn_cols:], high[:, ffn_cols:]], axis=1)
    back_a = arrange(to_dealt, jnp.concatenate(back_a))
    back_a_other = swap_core(back_a)
    d_gated = times(back_a, output_a_t)
    d_cgate = d_gated * conv_out
    d_conv = d_gated * proj_c_part
    unused, pullback = jax.vjp(
        lambda ext_rows, kernel_in: shortconv(ext_rows, kernel_in, halo_segment),
        extended,
        kernel_local,
    )
    d_extended, kernel_grad = pullback(d_conv)
    returned = from_behind(d_extended[:halo], -1)
    d_product = d_extended[halo:] + jnp.concatenate(
        [jnp.zeros((row_count - halo, channels), F32), returned]
    )
    d_proj_a = jnp.concatenate(
        [
            d_product * proj_x_part[halo_pad:],
            d_cgate,
            d_product * proj_b_part[halo_pad:],
        ],
        axis=1,
    ).astype(BF16)
    d_chunks = tp_chunks(times_t(arrange(to_gathered, d_proj_a), project_a))
    keep, send = halves(d_proj_a, gated_rows)
    mixer_cols = keep.shape[1]
    partial = gradient(
        [
            (mixer_in, 0),
            (mixer_in_other, 0),
            (jnp.where(first_core, mixer_in, back_a), 0),
            (jnp.where(first_core, mixer_in_other, back_a_other), 0),
        ],
        keep,
        swap_core(send),
        0,
        mixer_cols,
        1,
        3 * channels - mixer_cols,
        0,
        width,
        mixer_cols,
        0,
        None,
    )
    d_mixer_in, partial = lax.optimization_barrier((tp_reduce(d_chunks), partial))
    unused, pullback = jax.vjp(norm_rows, stream0, gain_a)
    d_norm_a, gain_a_grad = pullback(d_mixer_in)
    d_stream0 = d_stream1 + d_norm_a
    mixer_partial = exchange_first(partial)

    slot_for_anchor = jnp.sum(
        jnp.where(
            my_anchor[None, :] == jnp.arange(shards)[:, None], jnp.arange(shards)[None, :], 0
        ),
        axis=1,
    )
    gain_rows = jnp.concatenate(
        [
            grad.reshape(shards, depth)
            for grad in (gain_f_grad, gain_b_grad, gain_s_grad, gain_a_grad)
        ],
        axis=1,
    )
    kernel_cols = kernel_taps * channels
    shared = jnp.concatenate([kernel_grad.reshape(-1), qgain_grad, kgain_grad])
    fill = width - shared.shape[0] - 4 * depth
    small_row = jnp.concatenate(
        [
            jnp.broadcast_to(shared, (shards, shared.shape[0])),
            jnp.pad(gain_rows, ((0, 0), (0, fill))),
        ],
        axis=1,
    ).astype(BF16)

    def by_anchor(rows):
        return rows.astype(BF16).reshape(shards, part_rows, width)[slot_for_anchor]

    home = lax.all_to_all(
        jnp.concatenate(
            [by_anchor(d_stream0), by_anchor(stream4), small_row[:, None]], axis=1
        ),
        TOKEN_AXES,
        split_axis=0,
        concat_axis=0,
        tiled=True,
    )
    small_sum = jnp.sum(home[:, 2 * part_rows].astype(F32), axis=0)
    small_high = small_sum.astype(BF16)
    small_low = (small_sum - small_high.astype(F32)).astype(BF16)
    last = tp_gather(
        jnp.concatenate(
            [
                home[:, :part_rows].reshape(chunk, width),
                home[:, part_rows : 2 * part_rows].reshape(chunk, width),
                jnp.pad(jnp.stack([small_high, small_low]), ((0, 6), (0, 0))),
            ]
        )
    )
    last, mixer_partial = lax.optimization_barrier((last, mixer_partial))
    mixer_grads = jnp.concatenate(exchange_second(*mixer_partial), axis=1)
    home_rows = (
        jnp.repeat(jnp.tile(send_piece, members), part_rows) * piece_rows
        + member_of * part_rows
        + gathered % part_rows
    )
    to_arrival = (home_rows[None, :] == gathered[:, None]).astype(BF16)
    input_gradient = arrange(to_arrival, jnp.concatenate([slot[:chunk] for slot in last]))
    layer_out = arrange(to_arrival, jnp.concatenate([slot[chunk : 2 * chunk] for slot in last]))
    smalls = [
        slot[2 * chunk].astype(F32) + slot[2 * chunk + 1].astype(F32) for slot in last
    ]
    totals = sum(smalls)
    kernel_rows = jnp.stack([small[:kernel_cols].reshape(kernel_taps, channels) for small in smalls])
    kernel_total = jnp.concatenate(
        [
            lax.dynamic_index_in_dim(kernel_rows, (own - member) % members, 0, keepdims=False)
            for member in range(members)
        ],
        axis=1,
    )
    qgain_total = totals[kernel_cols : kernel_cols + HD]
    kgain_total = totals[kernel_cols + HD : kernel_cols + 2 * HD]
    gain_start = kernel_cols + 2 * HD
    gain_totals = totals[gain_start : gain_start + 4 * depth].reshape(4, depth)

    gateup_s_grad, down_s_grad = ffn_gradients(*second_grads, steps, hidden)
    gateup_f_grad, down_f_grad = ffn_gradients(*first_grads, steps, hidden)
    proj_cols = attend_project.shape[1]
    return (
        layer_out,
        input_gradient,
        gain_totals[3],
        mixer_grads[:, : 3 * channels].reshape(depth, 3, channels),
        kernel_total,
        mixer_grads[:, 3 * channels :].T,
        gain_totals[0],
        gateup_f_grad,
        down_f_grad,
        gain_totals[1],
        attend_grads[:, :proj_cols],
        qgain_total,
        kgain_total,
        attend_grads[:, proj_cols:].T,
        gain_totals[2],
        gateup_s_grad,
        down_s_grad,
    )


def solution(mesh):
    names = TOKEN_AXES + ("tp",)
    rings = mesh.shape["fsdp"] // 2, 2, mesh.shape["ctx"] // 2, 2, mesh.shape["tp"]
    tokens = P(TOKEN_AXES, None)
    rows = P(TOKEN_AXES)
    three = P(TOKEN_AXES, None, "tp")
    two = P(TOKEN_AXES, "tp")
    turned = P("tp", TOKEN_AXES)
    return jax.shard_map(
        body,
        mesh=Mesh(mesh.devices.reshape(rings), names),
        in_specs=(
            tokens, tokens, P(), P(),
            rows, three, P(), turned,
            rows, three, turned,
            rows, two, P(), P(), turned,
            rows, three, turned,
        ),
        out_specs=(
            tokens, tokens,
            rows, three, P(), turned,
            rows, three, turned,
            rows, two, P(), P(), turned,
            rows, three, turned,
        ),
        check_vma=False,
    )
```

```python
import functools

import jax
import jax.numpy as jnp
from jax import lax
from jax.experimental import pallas as pl
from jax.experimental.pallas import tpu as pltpu
from jax.sharding import Mesh, PartitionSpec as P

H = 24
KVH = 8
HD = 64

EPSILON = 1e-05
ROPE_BASE = 1000000.0
NEGATIVE = -1e30

CHIP_AXES = ("x", "z_hi", "z_lo")
TOKEN_AXES = CHIP_AXES + ("core",)
GROUP_AXES = ("x", "z_hi")
CTX_AXES = ("z_lo", "core")
Z_AXES = ("z_hi", "z_lo")
CORES = 2
TILE = 256
VMEM_LIMIT = 48 * 1024 * 1024
F32 = jnp.float32
BF16 = jnp.bfloat16


def norm_rows(values, scales):
    return values * lax.rsqrt(jnp.mean(values * values, axis=-1, keepdims=True) + EPSILON) * scales


def rotate(values, cosine, sine):
    half_dim = values.shape[-1] // 2
    shape_out = (values.shape[0],) + (1,) * (values.ndim - 2) + (half_dim,)
    cosine = cosine.reshape(shape_out)
    sine = sine.reshape(shape_out)
    first_half = values[..., :half_dim]
    second_half = values[..., half_dim:]
    return jnp.concatenate(
        [
            first_half * cosine - second_half * sine,
            second_half * cosine + first_half * sine,
        ],
        axis=-1,
    )


def locate(lengths, positions):
    seq_ends = jnp.cumsum(lengths)
    segment = jnp.sum((positions[:, None] >= seq_ends[None, :]).astype(jnp.int32), axis=1)
    starts = seq_ends - lengths
    first_row = jnp.sum(
        jnp.where(segment[:, None] == jnp.arange(lengths.shape[0])[None, :], starts[None, :], 0),
        axis=1,
    )
    return (segment, positions - first_row)


def shortconv(extended, kernel_in, segment):
    kernel_taps = kernel_in.shape[0]
    out_rows = extended.shape[0] - kernel_taps + 1
    result = kernel_in[0] * extended[kernel_taps - 1 :]
    for t in range(1, kernel_taps):
        earlier = extended[kernel_taps - 1 - t : kernel_taps - 1 - t + out_rows]
        same_seq = (
            segment[kernel_taps - 1 - t : kernel_taps - 1 - t + out_rows]
            == segment[kernel_taps - 1 :]
        ).astype(F32)[:, None]
        result = result + kernel_in[t] * earlier * same_seq
    return result


def from_behind(block, distance):
    devices = range(lax.axis_size(CTX_AXES))
    route = [(i - distance, i) for i in devices if i - distance in devices]
    return lax.ppermute(block, CTX_AXES, route)


def swap_ctx(block, mask):
    return lax.ppermute(block, CTX_AXES, [(i, i ^ mask) for i in range(lax.axis_size(CTX_AXES))])


def swap_core(block):
    return lax.ppermute(block, "core", [(0, 1), (1, 0)])


def shift_ring(block, axis, distance):
    ring = lax.axis_size(axis)
    return lax.ppermute(block, axis, [(i, (i + distance) % ring) for i in range(ring)])


def shift_tp(block, distance):
    members = lax.axis_size("tp")
    return lax.ppermute(block, "tp", [(i, (i + distance) % members) for i in range(members)])


def tp_gather(shard):
    return [shard] + [shift_tp(shard, k) for k in range(1, lax.axis_size("tp"))]


def tp_chunks(partial):
    rows = partial.shape[0] // lax.axis_size("tp")
    return [
        partial[k * rows : (k + 1) * rows].astype(F32 if k == 0 else BF16)
        for k in range(lax.axis_size("tp"))
    ]


def tp_reduce(chunks):
    total = chunks[0]
    for k in range(1, len(chunks)):
        total = total + shift_tp(chunks[k], -k).astype(F32)
    return total


def arrange(order, rows):
    return times(order, rows).astype(BF16)


def times(left, right):
    return lax.dot_general(left, right, (((1,), (0,)), ((), ())), preferred_element_type=F32)


def times_t(left, right):
    return lax.dot_general(left, right, (((1,), (1,)), ((), ())), preferred_element_type=F32)


def times_rows(left, right):
    return lax.dot_general(left, right, (((0,), (0,)), ((), ())), preferred_element_type=F32)


def assemble(chunk_refs, target):
    rows = chunk_refs[0].shape[0]
    for k, ref in enumerate(chunk_refs):
        target[k * rows : (k + 1) * rows, :] = ref[...]


def spread(total, chunk_refs):
    rows = chunk_refs[0].shape[0]
    for k, ref in enumerate(chunk_refs):
        ref[...] = total[k * rows : (k + 1) * rows, :].astype(ref.dtype)


def whole(shape):
    return pl.BlockSpec(shape, lambda *_: (0,) * len(shape))


def weight_specs(depth, steps):
    return [
        pl.BlockSpec((depth, 2 * TILE), lambda j: (0, j)),
        pl.BlockSpec((depth, TILE), lambda j: (0, 2 * steps + j)),
    ]


def chunk_shapes(count, rows, width):
    return [jax.ShapeDtypeStruct((rows, width), F32 if k == 0 else BF16) for k in range(count)]


def ffn_forward_kernel(count, *refs):
    x_refs, (gu_ref, dn_ref), outs = refs[:count], refs[count : count + 2], refs[count + 2 : -2]
    x_all, total = refs[-2:]
    step = pl.program_id(0)

    @pl.when(step == 0)
    def _():
        assemble(x_refs, x_all)
        total[...] = jnp.zeros_like(total)

    both = times(x_all[...], gu_ref[...])
    gate, up = both[:, :TILE], both[:, TILE:]
    active = (gate * jax.nn.sigmoid(gate) * up).astype(BF16)
    total[...] += times_t(active, dn_ref[...])

    @pl.when(step == pl.num_programs(0) - 1)
    def _():
        spread(total[...], outs)


def ffn_forward(chunks, pack, steps):
    count, (rows, width) = len(chunks), chunks[0].shape
    tokens = count * rows
    return pl.pallas_call(
        functools.partial(ffn_forward_kernel, count),
        grid=(steps,),
        in_specs=[whole((rows, width))] * count + weight_specs(width, steps),
        out_specs=[whole((rows, width))] * count,
        out_shape=chunk_shapes(count, rows, width),
        scratch_shapes=[pltpu.VMEM((tokens, width), BF16), pltpu.VMEM((tokens, width), F32)],
        compiler_params=pltpu.CompilerParams(vmem_limit_bytes=VMEM_LIMIT),
        cost_estimate=pl.CostEstimate(
            flops=2 * tokens * width * 3 * TILE * steps,
            bytes_accessed=2 * width * 3 * TILE * steps,
            transcendentals=tokens * TILE * steps,
        ),
        name="ffn_forward",
    )(*chunks, pack, pack)


def ffn_backward_kernel(count, forward, core_ref, *refs):
    x_refs, b_refs = refs[:count], refs[count : 2 * count]
    gu_ref, dn_ref = refs[2 * count : 2 * count + 2]
    place = 2 * count + 2
    back_outs = refs[place : place + count]
    place += count
    if forward:
        outs = refs[place : place + count]
        place += count
    keep_ref, side_ref = refs[place : place + 2]
    scratch = refs[place + 2 :]
    x_all, b_all, d_total = scratch[:3]
    step = pl.program_id(0)
    width = x_all.shape[1]

    @pl.when(step == 0)
    def _():
        assemble(x_refs, x_all)
        assemble(b_refs, b_all)
        if forward:
            side_ref[:, :width] = x_all[...]
            side_ref[:, width : 2 * width] = b_all[...]
        d_total[...] = jnp.zeros_like(d_total)
        if forward:
            scratch[3][...] = jnp.zeros_like(scratch[3])

    both = times(x_all[...], gu_ref[...])
    gate, up = both[:, :TILE], both[:, TILE:]
    d_active = times(b_all[...], dn_ref[...])
    sigmoid = jax.nn.sigmoid(gate)
    silu = gate * sigmoid
    active = (silu * up).astype(BF16)
    if forward:
        scratch[3][...] += times_t(active, dn_ref[...])
    d_gate = (d_active * up * (sigmoid * (1.0 + gate * (1.0 - sigmoid)))).astype(BF16)
    d_up = (d_active * silu).astype(BF16)
    d_total[...] += times_t(jnp.concatenate([d_gate, d_up], axis=1), gu_ref[...])
    first = core_ref[0] == 0
    half = TILE // 2
    low, high = active[:, :half], active[:, half:]
    start = (2 * width if forward else 0) + step * (TILE + half)
    start = pl.multiple_of(start, half)

    @pl.when(first)
    def _():
        keep_ref[:, :TILE] = d_gate
        keep_ref[:, TILE:] = low
        side_ref[:, pl.ds(start, TILE)] = d_up
        side_ref[:, pl.ds(start + TILE, half)] = high

    @pl.when(jnp.logical_not(first))
    def _():
        keep_ref[:, :TILE] = d_up
        keep_ref[:, TILE:] = high
        side_ref[:, pl.ds(start, TILE)] = d_gate
        side_ref[:, pl.ds(start + TILE, half)] = low

    @pl.when(step == pl.num_programs(0) - 1)
    def _():
        spread(d_total[...], back_outs)
        if forward:
            spread(scratch[3][...], outs)


def ffn_backward(core, chunks, back_chunks, pack, steps, forward):
    count, (rows, width) = len(chunks), chunks[0].shape
    tokens = count * rows
    block = TILE + TILE // 2
    ways = 2 if forward else 1
    side_width = (2 * width if forward else 0) + steps * block
    results = pl.pallas_call(
        functools.partial(ffn_backward_kernel, count, forward),
        grid=(steps,),
        in_specs=[pl.BlockSpec(memory_space=pltpu.SMEM)]
        + [whole((rows, width))] * (2 * count)
        + weight_specs(width, steps),
        out_specs=[whole((rows, width))] * (ways * count)
        + [pl.BlockSpec((tokens, block), lambda j: (0, j)), whole((tokens, side_width))],
        out_shape=chunk_shapes(count, rows, width) * ways
        + [
            jax.ShapeDtypeStruct((tokens, steps * block), BF16),
            jax.ShapeDtypeStruct((tokens, side_width), BF16),
        ],
        scratch_shapes=[pltpu.VMEM((tokens, width), BF16)] * 2
        + [pltpu.VMEM((tokens, width), F32)] * ways,
        compiler_params=pltpu.CompilerParams(vmem_limit_bytes=VMEM_LIMIT),
        cost_estimate=pl.CostEstimate(
            flops=2 * tokens * width * (4 + ways) * TILE * steps,
            bytes_accessed=2 * width * 3 * TILE * steps + 4 * tokens * side_width,
            transcendentals=tokens * TILE * steps,
        ),
        name="ffn_both" if forward else "ffn_backward",
    )(core, *chunks, *back_chunks, pack, pack)
    return results[:count], results[count : ways * count], results[-2], results[-1]


def gradient_kernel(cut, whole_steps, *refs):
    one_own, one_other, two_own, two_other, own_ref, other_ref = refs[:6]
    out_ref = refs[-1]
    step = pl.program_id(0)

    def product(own_left, other_left, columns):
        total = times_rows(own_left[...], own_ref[:, columns])
        total += times_rows(other_left[...], other_ref[:, columns])
        out_ref[:, columns] = total.astype(BF16)

    if whole_steps:

        @pl.when(step < whole_steps)
        def _():
            product(one_own, one_other, slice(None))

        @pl.when(step >= whole_steps)
        def _():
            product(two_own, two_other, slice(None))

    else:
        product(one_own, one_other, slice(0, cut))
        product(two_own, two_other, slice(cut, None))


def gradient(lefts, own, other, other_start, block, steps, cut, whole_steps, width, out_width, out_start, target):
    tokens = own.shape[0]

    def left_spec(index):
        return pl.BlockSpec((tokens, width), lambda j: (0, index))

    in_specs = [left_spec(index) for unused, index in lefts] + [
        pl.BlockSpec((tokens, block), lambda j: (0, j)),
        pl.BlockSpec((tokens, block), lambda j: (0, other_start + j)),
    ]
    operands = [array for array, unused in lefts] + [own, other]
    aliases = {}
    if target is not None:
        in_specs.append(pl.BlockSpec(memory_space=pl.ANY))
        operands.append(target)
        aliases = {len(operands) - 1: 0}
    return pl.pallas_call(
        functools.partial(gradient_kernel, cut, whole_steps),
        grid=(steps,),
        in_specs=in_specs,
        out_specs=pl.BlockSpec((width, block), lambda j: (0, out_start + j)),
        out_shape=jax.ShapeDtypeStruct((width, out_width), BF16),
        input_output_aliases=aliases,
        compiler_params=pltpu.CompilerParams(vmem_limit_bytes=VMEM_LIMIT),
        cost_estimate=pl.CostEstimate(
            flops=4 * tokens * width * block * steps,
            bytes_accessed=2 * width * block * steps,
            transcendentals=0,
        ),
        name="weight_gradient",
    )(*operands)


def share_rows(summed):
    core = lax.axis_index("core")
    rows = summed.shape[0] // 2
    mine = lax.dynamic_slice_in_dim(summed, core * rows, rows, 0)
    other = swap_core(lax.dynamic_slice_in_dim(summed, (1 - core) * rows, rows, 0))
    first = core == 0
    return jnp.where(first, mine, other).astype(F32), jnp.where(first, other, mine).astype(F32)


def reduce_gradient(partial):
    return share_rows(lax.psum_scatter(partial, CHIP_AXES, scatter_dimension=0, tiled=True))


def along(blocks, axis):
    ring = lax.axis_size(axis)
    place = lax.axis_index(axis)
    return [lax.dynamic_index_in_dim(blocks, place, 0, False)] + [
        shift_ring(lax.dynamic_index_in_dim(blocks, (place + k) % ring, 0, False), axis, k)
        for k in range(1, ring)
    ]


def add_parts(parts):
    total = parts[0].astype(F32)
    for part in parts[1:]:
        total = total + part.astype(F32)
    return total


def fill(shape, parts):
    result = jnp.zeros(shape, BF16)
    for part, place in parts:
        result = lax.dynamic_update_slice(result, part, place)
    return result


def gather_first(pack):
    rows, columns = pack.shape
    half = columns // 2
    ring = lax.axis_size("x")
    x, z = lax.axis_index("x"), lax.axis_index(Z_AXES)
    low, high = pack[:, :half], pack[:, half:]
    low_parts = [(shift_ring(low, "x", k)[None] if k else low[None], k) for k in range(ring)]
    high_parts = [(shift_ring(high, Z_AXES, k)[None] if k else high[None], k) for k in range(ring)]
    low = fill((ring, rows, half), [(v, ((x - k) % ring, 0, 0)) for v, k in low_parts])
    high = fill((ring, rows, half), [(v, ((z - k) % ring, 0, 0)) for v, k in high_parts])
    return low, high


def gather_second(low, high):
    ring, rows, half = low.shape
    columns = 2 * half
    x, z, core = lax.axis_index("x"), lax.axis_index(Z_AXES), lax.axis_index("core")
    parts = []
    for k in range(ring):
        part = shift_ring(low, Z_AXES, k) if k else low
        parts.append((part[:, None], (0, (z - k) % ring, 0, 0)))
        part = shift_ring(high, "x", k) if k else high
        parts.append((part[None], ((x - k) % ring, 0, 0, half)))
    plane = fill((ring, ring, rows, columns), parts)
    other = swap_core(plane)
    both = fill(
        (ring, ring, CORES, rows, columns),
        [
            (plane[:, :, None], (0, 0, core, 0, 0)),
            (other[:, :, None], (0, 0, 1 - core, 0, 0)),
        ],
    )
    return both.reshape(-1, columns)


def ffn_gradients(low, high, steps, hidden):
    depth = low.shape[0]
    low = low.reshape(depth, steps, -1)
    high = high.reshape(depth, steps, -1)
    gate = low[:, :, :TILE].reshape(depth, -1)[:, :hidden]
    up = high[:, :, :TILE].reshape(depth, -1)[:, :hidden]
    down = jnp.concatenate([low[:, :, TILE:], high[:, :, TILE:]], axis=2)
    return jnp.stack([gate, up], axis=1), down.reshape(depth, -1)[:, :hidden].T


def halves(proj, out):
    first = lax.axis_index("core") == 0
    half = (proj.shape[1] + out.shape[1]) // 2
    late = jnp.concatenate([proj[:, half:], out], axis=1)
    early = proj[:, :half]
    return jnp.where(first, early, late), jnp.where(first, late, early)


def body(
    hidden_in,
    cotangent,
    seq_lengths,
    deal_order,
    mixer_gain,
    mixer_project,
    mixer_kernel,
    mixer_output,
    first_gain,
    first_gateup,
    first_down,
    attend_gain,
    attend_project,
    query_gain,
    key_gain,
    attend_output,
    second_gain,
    second_gateup,
    second_down,
):
    shards = lax.axis_size(TOKEN_AXES)
    contexts = lax.axis_size(CTX_AXES)
    members = lax.axis_size("tp")
    row_count, width = hidden_in.shape
    piece_rows = row_count // shards
    part_rows = piece_rows // members
    chunk = row_count // members
    device = lax.axis_index(TOKEN_AXES)
    own = lax.axis_index("tp")
    core = lax.axis_index("core")
    core_ref = core.reshape(1).astype(jnp.int32)
    depth = mixer_gain.shape[0]
    channels = mixer_output.shape[0]
    hidden = first_down.shape[0]
    heads_width = attend_output.shape[0]
    steps = -(-hidden // TILE)
    padded = steps * TILE
    ffn_width = 3 * padded
    block = TILE + TILE // 2

    def pack_ffn(gateup, down):
        wide = jnp.pad(gateup, ((0, 0), (0, 0), (0, padded - hidden)))
        wide = wide.reshape(depth, 2, steps, TILE).transpose(0, 2, 1, 3).reshape(depth, -1)
        return [wide, jnp.pad(down.T, ((0, 0), (0, padded - hidden)))]

    mixer_pack = jnp.concatenate([mixer_project.reshape(depth, -1), mixer_output.T], axis=1)
    first_pack = jnp.concatenate(
        pack_ffn(first_gateup, first_down) + [attend_project, attend_output.T], axis=1
    )
    second_pack = jnp.concatenate(pack_ffn(second_gateup, second_down), axis=1)
    first_all = lax.all_gather(first_pack, TOKEN_AXES, axis=0, tiled=True)
    second_all = lax.all_gather(second_pack, TOKEN_AXES, axis=0, tiled=True)
    project_b = first_all[:, ffn_width : ffn_width + attend_project.shape[1]]
    output_b_t = first_all[:, ffn_width + attend_project.shape[1] :]

    piece_table = deal_order.reshape(shards, shards, piece_rows)[:, :, 0]
    anchor = piece_table // row_count
    anchor_piece = piece_table % row_count // piece_rows
    send_piece = jnp.sum(jnp.where(anchor == device, anchor_piece, 0), axis=1)
    my_anchor = lax.dynamic_index_in_dim(anchor, device, 0, keepdims=False)
    gains_row = jnp.concatenate(
        [mixer_gain, first_gain, attend_gain, second_gain, jnp.zeros((width - 4 * depth,), BF16)]
    )

    def my_part(rows):
        parts = rows.reshape(shards, members, part_rows, width)
        return lax.dynamic_index_in_dim(parts, own, 1, keepdims=False)[send_piece]

    outgoing = jnp.concatenate(
        [
            my_part(hidden_in),
            my_part(cotangent),
            jnp.broadcast_to(gains_row, (shards, 1, width)),
        ],
        axis=1,
    )
    outgoing, mixer_pack = lax.optimization_barrier((outgoing, mixer_pack))
    mixer_low, mixer_high = gather_first(mixer_pack)
    arrived = lax.all_to_all(outgoing, TOKEN_AXES, split_axis=0, concat_axis=0, tiled=True)
    gains = (
        arrived[:, 2 * part_rows, : 4 * depth]
        .reshape(shards, 4, depth)
        .transpose(1, 0, 2)
        .reshape(4, width)
        .astype(F32)
    )
    gain_a, gain_f, gain_b, gain_s = gains[0], gains[1], gains[2], gains[3]
    parts = arrived[:, : 2 * part_rows][my_anchor]
    own_tokens = parts[:, :part_rows].reshape(chunk, width)
    own_back = parts[:, part_rows:].reshape(chunk, width)
    stream0 = own_tokens.astype(F32)
    upstream = own_back.astype(F32)
    both = tp_gather(jnp.concatenate([own_tokens, own_back]))
    both, mixer_low, mixer_high = lax.optimization_barrier((both, mixer_low, mixer_high))
    mixer_all = gather_second(mixer_low, mixer_high)
    project_a = mixer_all[:, : 3 * channels]
    output_a_t = mixer_all[:, 3 * channels :]
    back_s_chunks = [slot[chunk:] for slot in both]

    gathered = jnp.arange(row_count)
    member_of = (own - gathered // chunk) % members
    offsets = (
        gathered % chunk // part_rows * piece_rows + member_of * part_rows + gathered % part_rows
    )
    to_gathered = (offsets[:, None] == gathered[None, :]).astype(BF16)
    to_dealt = (offsets[None, :] == gathered[:, None]).astype(BF16)
    tokens = times(to_dealt, jnp.concatenate([slot[:chunk] for slot in both]))

    kernel_taps = mixer_kernel.shape[0]
    halo = kernel_taps - 1
    local_rows = device * row_count + jnp.arange(row_count)
    halo_segment, unused = locate(
        seq_lengths, local_rows[0] - halo + jnp.arange(row_count + halo)
    )
    segment, places = locate(seq_lengths, device * row_count + offsets)
    ctx = lax.axis_index(CTX_AXES)
    group_rows = jnp.concatenate(
        [
            (lax.axis_index(GROUP_AXES) * contexts + (ctx ^ mask)) * row_count + offsets
            for mask in range(contexts)
        ]
    )
    key_segment, key_places = locate(seq_lengths, group_rows)
    allowed = (segment[:, None] == key_segment[None, :]) & (key_places[None, :] <= places[:, None])
    half_dim = HD // 2
    frequency = ROPE_BASE ** (-(jnp.arange(half_dim).astype(F32) * 2.0 / HD))
    angles = places.astype(F32)[:, None] * frequency[None, :]
    cosine = jnp.cos(angles)
    sine = jnp.sin(angles)

    kernel_local = lax.dynamic_slice_in_dim(mixer_kernel, own * channels, channels, 1).astype(F32)
    mixer_in = norm_rows(tokens, gain_a).astype(BF16)
    mixer_in_other = swap_core(mixer_in)
    halo_pad = 16
    halo_in = from_behind(mixer_in[row_count - halo_pad :], 1)
    proj_a = times(jnp.concatenate([halo_in, mixer_in]), project_a)
    proj_b_part = proj_a[:, :channels]
    proj_c_part = proj_a[halo_pad:, channels : 2 * channels]
    proj_x_part = proj_a[:, 2 * channels :]
    extended = (proj_b_part * proj_x_part)[halo_pad - halo :].astype(BF16).astype(F32)
    conv_out = shortconv(extended, kernel_local, halo_segment)
    gated_rows = (proj_c_part * conv_out).astype(BF16)
    gated_parts = arrange(to_gathered, gated_rows)
    stream1 = stream0 + tp_reduce(tp_chunks(times_t(gated_parts, output_a_t)))

    normed_f = tp_gather(norm_rows(stream1, gain_f).astype(BF16))
    stream2 = stream1 + tp_reduce(ffn_forward(normed_f, first_all, steps))

    groups = H // KVH
    score_scale = HD ** (-0.5)
    qgain_f = query_gain.astype(F32)
    kgain_f = key_gain.astype(F32)

    def qk_maps(query_in, key_in, gain_q, gain_k):
        return (
            rotate(norm_rows(query_in, gain_q), cosine, sine),
            rotate(norm_rows(key_in, gain_k), cosine, sine),
        )

    attend_in = jnp.concatenate(tp_gather(norm_rows(stream2, gain_b).astype(BF16)))
    proj_b = times(attend_in, project_b).reshape(row_count, -1, groups + 2, HD)
    kv_heads = proj_b.shape[1]
    query_raw = proj_b[:, :, :groups]
    key_raw = proj_b[:, :, groups]
    query_f, key_f = qk_maps(query_raw, key_raw, qgain_f, kgain_f)
    query_b = query_f.astype(BF16)
    key_value = jnp.concatenate(
        [
            key_f.astype(BF16).reshape(row_count, -1),
            proj_b[:, :, groups + 1].astype(BF16).reshape(row_count, -1),
        ],
        axis=1,
    )
    key_value_all = jnp.concatenate(
        [key_value] + [swap_ctx(key_value, mask) for mask in range(1, contexts)], axis=0
    )
    key_all = key_value_all[:, : kv_heads * HD].reshape(-1, kv_heads, HD)
    value_all = key_value_all[:, kv_heads * HD :].reshape(-1, kv_heads, HD)
    scores = (
        jnp.einsum("tkgd,nkd->kgtn", query_b, key_all, preferred_element_type=F32) * score_scale
    )
    masked = jnp.where(allowed, scores, NEGATIVE)
    row_top = jnp.max(masked, axis=-1, keepdims=True)
    exponent = jnp.exp(masked - row_top)
    row_total = jnp.sum(exponent, axis=-1, keepdims=True)
    softmax_rows = exponent / row_total
    log_total = row_top + jnp.log(row_total)
    attended = (
        jnp.einsum(
            "kgtn,nkd->tkgd", softmax_rows.astype(BF16), value_all, preferred_element_type=F32
        )
        .astype(BF16)
        .reshape(row_count, -1)
    )
    stream3 = stream2 + tp_reduce(tp_chunks(times_t(attended, output_b_t)))

    normed_s = tp_gather(norm_rows(stream3, gain_s).astype(BF16))
    d_chunks, out_chunks, keep, side = ffn_backward(
        core_ref, normed_s, back_s_chunks, second_all, steps, True
    )
    unused, pullback = jax.vjp(norm_rows, stream3, gain_s)
    d_stream, gain_s_grad = pullback(tp_reduce(d_chunks))
    d_stream3 = upstream + d_stream
    out_others = [shift_tp(out_chunks[k], -k) for k in range(1, members)]
    side_other = swap_core(side)
    ffn_lefts = [(side, 0), (side_other, 0), (side, 1), (side_other, 1)]
    ffn_cols = steps * block
    side_start = 2 * width // block
    partial = gradient(
        ffn_lefts, keep, side_other, side_start, block, steps, TILE, 0, width, ffn_cols, 0, None
    )

    back_b = tp_gather(d_stream3.astype(BF16))
    back_b, partial = lax.optimization_barrier((back_b, partial))
    second_grads = reduce_gradient(partial)
    back_b = jnp.concatenate(back_b)
    back_b_other = swap_core(back_b)
    attend_in_other = swap_core(attend_in)
    d_attended_b = times(back_b, output_b_t).astype(BF16).reshape(row_count, -1, groups, HD)
    scores_again = (
        jnp.einsum("tkgd,nkd->kgtn", query_b, key_all, preferred_element_type=F32) * score_scale
    )
    probs_again = jnp.where(allowed, jnp.exp(scores_again - log_total), 0.0)
    d_probs = jnp.einsum("tkgd,nkd->kgtn", d_attended_b, value_all, preferred_element_type=F32)
    d_values = jnp.einsum(
        "kgtn,tkgd->nkd", probs_again.astype(BF16), d_attended_b, preferred_element_type=F32
    )
    inner_sum = jnp.sum(probs_again * d_probs, axis=-1, keepdims=True)
    d_scores = (probs_again * (d_probs - inner_sum)).astype(BF16)
    d_query = (
        jnp.einsum("kgtn,nkd->tkgd", d_scores, key_all, preferred_element_type=F32) * score_scale
    )
    d_keys = (
        jnp.einsum("kgtn,tkgd->nkd", d_scores, query_b, preferred_element_type=F32) * score_scale
    )
    d_key_value = jnp.concatenate(
        [d_keys.reshape(-1, kv_heads * HD), d_values.reshape(-1, kv_heads * HD)], axis=1
    )
    d_local = d_key_value[:row_count]
    for mask in range(1, contexts):
        part = d_key_value[mask * row_count : (mask + 1) * row_count].astype(BF16)
        d_local = d_local + swap_ctx(part, mask).astype(F32)
    d_key_local = d_local[:, : kv_heads * HD].reshape(row_count, kv_heads, HD)
    d_value_local = d_local[:, kv_heads * HD :].reshape(row_count, kv_heads, HD)
    unused, pullback = jax.vjp(qk_maps, query_raw, key_raw, qgain_f, kgain_f)
    d_query_raw, d_key_raw, qgain_grad, kgain_grad = pullback((d_query, d_key_local))
    d_proj_b = (
        jnp.concatenate([d_query_raw, d_key_raw[:, :, None], d_value_local[:, :, None]], axis=2)
        .astype(BF16)
        .reshape(row_count, -1)
    )
    d_attend_in = tp_reduce(tp_chunks(times_t(d_proj_b, project_b)))
    unused, pullback = jax.vjp(norm_rows, stream2, gain_b)
    d_norm_b, gain_b_grad = pullback(d_attend_in)
    d_stream2 = d_stream3 + d_norm_b
    keep, send = halves(d_proj_b, attended)
    first_core = core == 0
    attend_cols = keep.shape[1]
    small_tile = 2 * (heads_width + attend_project.shape[1]) // 16
    third = gradient(
        [
            (attend_in, 0),
            (attend_in_other, 0),
            (jnp.where(first_core, attend_in, back_b), 0),
            (jnp.where(first_core, attend_in_other, back_b_other), 0),
        ],
        keep,
        swap_core(send),
        0,
        small_tile,
        attend_cols // small_tile,
        0,
        (attend_project.shape[1] - attend_cols) // small_tile,
        width,
        ffn_cols + attend_cols,
        ffn_cols // small_tile,
        None,
    )

    back_f = tp_gather(d_stream2.astype(BF16))
    back_f, third = lax.optimization_barrier((back_f, third))
    left_x, left_b = jnp.concatenate(normed_f), jnp.concatenate(back_f)
    ffn_lefts = [(left_x, 0), (swap_core(left_x), 0), (left_b, 0), (swap_core(left_b), 0)]
    d_chunks, unused, keep, side = ffn_backward(
        core_ref, normed_f, back_f, first_all, steps, False
    )
    d_chunks, out_others = lax.optimization_barrier((d_chunks, out_others))
    stream4 = stream3 + out_chunks[0]
    for part in out_others:
        stream4 = stream4 + part.astype(F32)
    partial = gradient(
        ffn_lefts,
        keep,
        swap_core(side),
        0,
        block,
        steps,
        TILE,
        0,
        width,
        ffn_cols + attend_cols,
        0,
        third,
    )

    unused, pullback = jax.vjp(norm_rows, stream1, gain_f)
    d_stream, gain_f_grad = pullback(tp_reduce(d_chunks))
    d_stream1 = d_stream2 + d_stream

    back_a = tp_gather(d_stream1.astype(BF16))
    back_a, partial = lax.optimization_barrier((back_a, partial))
    low, high = reduce_gradient(partial)
    first_grads = (low[:, :ffn_cols], high[:, :ffn_cols])
    attend_grads = jnp.concatenate([low[:, ffn_cols:], high[:, ffn_cols:]], axis=1)
    back_a = arrange(to_dealt, jnp.concatenate(back_a))
    back_a_other = swap_core(back_a)
    d_gated = times(back_a, output_a_t)
    d_cgate = d_gated * conv_out
    d_conv = d_gated * proj_c_part
    unused, pullback = jax.vjp(
        lambda ext_rows, kernel_in: shortconv(ext_rows, kernel_in, halo_segment),
        extended,
        kernel_local,
    )
    d_extended, kernel_grad = pullback(d_conv)
    returned = from_behind(d_extended[:halo], -1)
    d_product = d_extended[halo:] + jnp.concatenate(
        [jnp.zeros((row_count - halo, channels), F32), returned]
    )
    d_proj_a = jnp.concatenate(
        [
            d_product * proj_x_part[halo_pad:],
            d_cgate,
            d_product * proj_b_part[halo_pad:],
        ],
        axis=1,
    ).astype(BF16)
    d_chunks = tp_chunks(times_t(arrange(to_gathered, d_proj_a), project_a))
    keep, send = halves(d_proj_a, gated_rows)
    mixer_cols = keep.shape[1]
    partial = gradient(
        [
            (mixer_in, 0),
            (mixer_in_other, 0),
            (jnp.where(first_core, mixer_in, back_a), 0),
            (jnp.where(first_core, mixer_in_other, back_a_other), 0),
        ],
        keep,
        swap_core(send),
        0,
        mixer_cols,
        1,
        3 * channels - mixer_cols,
        0,
        width,
        mixer_cols,
        0,
        None,
    )
    second_grads = ffn_gradients(*second_grads, steps, hidden)
    d_mixer_in, second_grads = lax.optimization_barrier((tp_reduce(d_chunks), second_grads))
    unused, pullback = jax.vjp(norm_rows, stream0, gain_a)
    d_norm_a, gain_a_grad = pullback(d_mixer_in)
    d_stream0 = d_stream1 + d_norm_a

    slot_for_anchor = jnp.sum(
        jnp.where(
            my_anchor[None, :] == jnp.arange(shards)[:, None], jnp.arange(shards)[None, :], 0
        ),
        axis=1,
    )
    gain_rows = jnp.concatenate(
        [
            grad.reshape(shards, depth)
            for grad in (gain_f_grad, gain_b_grad, gain_s_grad, gain_a_grad)
        ],
        axis=1,
    )
    kernel_cols = kernel_taps * channels
    shared = jnp.concatenate([kernel_grad.reshape(-1), qgain_grad, kgain_grad])
    fill = width - shared.shape[0] - 4 * depth
    small_row = jnp.concatenate(
        [
            jnp.broadcast_to(shared, (shards, shared.shape[0])),
            jnp.pad(gain_rows, ((0, 0), (0, fill))),
        ],
        axis=1,
    ).astype(BF16)

    def by_anchor(rows):
        return rows.astype(BF16).reshape(shards, part_rows, width)[slot_for_anchor]

    home = lax.all_to_all(
        jnp.concatenate(
            [by_anchor(d_stream0), by_anchor(stream4), small_row[:, None]], axis=1
        ),
        TOKEN_AXES,
        split_axis=0,
        concat_axis=0,
        tiled=True,
    )
    home, partial = lax.optimization_barrier((home, partial))
    ring = lax.axis_size("x")
    mixer_parts = along(partial.reshape(ring, -1, mixer_cols), "x")
    small_sum = jnp.sum(home[:, 2 * part_rows].astype(F32), axis=0)
    small_high = small_sum.astype(BF16)
    small_low = (small_sum - small_high.astype(F32)).astype(BF16)
    last = tp_gather(
        jnp.concatenate(
            [
                home[:, :part_rows].reshape(chunk, width),
                home[:, part_rows : 2 * part_rows].reshape(chunk, width),
                jnp.pad(jnp.stack([small_high, small_low]), ((0, 6), (0, 0))),
            ]
        )
    )
    last, mixer_parts = lax.optimization_barrier((last, mixer_parts))
    mixer_parts = add_parts(mixer_parts).astype(BF16).reshape(ring, -1, mixer_cols)
    mixer_parts = along(mixer_parts, Z_AXES)
    first_grads = ffn_gradients(*first_grads, steps, hidden)
    mixer_parts, first_grads = lax.optimization_barrier((mixer_parts, first_grads))
    mixer_grads = jnp.concatenate(share_rows(add_parts(mixer_parts).astype(BF16)), axis=1)
    home_rows = (
        jnp.repeat(jnp.tile(send_piece, members), part_rows) * piece_rows
        + member_of * part_rows
        + gathered % part_rows
    )
    to_arrival = (home_rows[None, :] == gathered[:, None]).astype(BF16)
    input_gradient = arrange(to_arrival, jnp.concatenate([slot[:chunk] for slot in last]))
    layer_out = arrange(to_arrival, jnp.concatenate([slot[chunk : 2 * chunk] for slot in last]))
    smalls = [
        slot[2 * chunk].astype(F32) + slot[2 * chunk + 1].astype(F32) for slot in last
    ]
    totals = sum(smalls)
    kernel_rows = jnp.stack([small[:kernel_cols].reshape(kernel_taps, channels) for small in smalls])
    kernel_total = jnp.concatenate(
        [
            lax.dynamic_index_in_dim(kernel_rows, (own - member) % members, 0, keepdims=False)
            for member in range(members)
        ],
        axis=1,
    )
    qgain_total = totals[kernel_cols : kernel_cols + HD]
    kgain_total = totals[kernel_cols + HD : kernel_cols + 2 * HD]
    gain_start = kernel_cols + 2 * HD
    gain_totals = totals[gain_start : gain_start + 4 * depth].reshape(4, depth)

    gateup_s_grad, down_s_grad = second_grads
    gateup_f_grad, down_f_grad = first_grads
    proj_cols = attend_project.shape[1]
    return (
        layer_out,
        input_gradient,
        gain_totals[3],
        mixer_grads[:, : 3 * channels].reshape(depth, 3, channels),
        kernel_total,
        mixer_grads[:, 3 * channels :].T,
        gain_totals[0],
        gateup_f_grad,
        down_f_grad,
        gain_totals[1],
        attend_grads[:, :proj_cols],
        qgain_total,
        kgain_total,
        attend_grads[:, proj_cols:].T,
        gain_totals[2],
        gateup_s_grad,
        down_s_grad,
    )


def solution(mesh):
    names = TOKEN_AXES + ("tp",)
    rings = mesh.shape["fsdp"] // 2, 2, mesh.shape["ctx"] // 2, 2, mesh.shape["tp"]
    tokens = P(TOKEN_AXES, None)
    rows = P(TOKEN_AXES)
    three = P(TOKEN_AXES, None, "tp")
    two = P(TOKEN_AXES, "tp")
    turned = P("tp", TOKEN_AXES)
    return jax.shard_map(
        body,
        mesh=Mesh(mesh.devices.reshape(rings), names),
        in_specs=(
            tokens, tokens, P(), P(),
            rows, three, P(), turned,
            rows, three, turned,
            rows, two, P(), P(), turned,
            rows, three, turned,
        ),
        out_specs=(
            tokens, tokens,
            rows, three, P(), turned,
            rows, three, turned,
            rows, two, P(), P(), turned,
            rows, three, turned,
        ),
        check_vma=False,
    )
```

```python
import functools

import jax
import jax.numpy as jnp
from jax import lax
from jax.experimental import pallas as pl
from jax.experimental.pallas import tpu as pltpu
from jax.sharding import Mesh, PartitionSpec as P

H = 24
KVH = 8
HD = 64

EPSILON = 1e-05
ROPE_BASE = 1000000.0
NEGATIVE = -1e30

CHIP_AXES = ("x", "z_hi", "z_lo")
TOKEN_AXES = CHIP_AXES + ("core",)
GROUP_AXES = ("x", "z_hi")
CTX_AXES = ("z_lo", "core")
Z_AXES = ("z_hi", "z_lo")
CORES = 2
TILE = 256
VMEM_LIMIT = 48 * 1024 * 1024
F32 = jnp.float32
BF16 = jnp.bfloat16


def norm_rows(values, scales):
    return values * lax.rsqrt(jnp.mean(values * values, axis=-1, keepdims=True) + EPSILON) * scales


def rotate(values, cosine, sine):
    half_dim = values.shape[-1] // 2
    shape_out = (values.shape[0],) + (1,) * (values.ndim - 2) + (half_dim,)
    cosine = cosine.reshape(shape_out)
    sine = sine.reshape(shape_out)
    first_half = values[..., :half_dim]
    second_half = values[..., half_dim:]
    return jnp.concatenate(
        [
            first_half * cosine - second_half * sine,
            second_half * cosine + first_half * sine,
        ],
        axis=-1,
    )


def locate(lengths, positions):
    seq_ends = jnp.cumsum(lengths)
    segment = jnp.sum((positions[:, None] >= seq_ends[None, :]).astype(jnp.int32), axis=1)
    starts = seq_ends - lengths
    first_row = jnp.sum(
        jnp.where(segment[:, None] == jnp.arange(lengths.shape[0])[None, :], starts[None, :], 0),
        axis=1,
    )
    return (segment, positions - first_row)


def shortconv(extended, kernel_in, segment):
    kernel_taps = kernel_in.shape[0]
    out_rows = extended.shape[0] - kernel_taps + 1
    result = kernel_in[0] * extended[kernel_taps - 1 :]
    for t in range(1, kernel_taps):
        earlier = extended[kernel_taps - 1 - t : kernel_taps - 1 - t + out_rows]
        same_seq = (
            segment[kernel_taps - 1 - t : kernel_taps - 1 - t + out_rows]
            == segment[kernel_taps - 1 :]
        ).astype(F32)[:, None]
        result = result + kernel_in[t] * earlier * same_seq
    return result


def from_behind(block, distance):
    devices = range(lax.axis_size(CTX_AXES))
    route = [(i - distance, i) for i in devices if i - distance in devices]
    return lax.ppermute(block, CTX_AXES, route)


def swap_ctx(block, mask):
    return lax.ppermute(block, CTX_AXES, [(i, i ^ mask) for i in range(lax.axis_size(CTX_AXES))])


def swap_core(block):
    return lax.ppermute(block, "core", [(0, 1), (1, 0)])


def shift_ring(block, axis, distance):
    ring = lax.axis_size(axis)
    return lax.ppermute(block, axis, [(i, (i + distance) % ring) for i in range(ring)])


def shift_tp(block, distance):
    members = lax.axis_size("tp")
    return lax.ppermute(block, "tp", [(i, (i + distance) % members) for i in range(members)])


def tp_gather(shard):
    return [shard] + [shift_tp(shard, k) for k in range(1, lax.axis_size("tp"))]


def tp_chunks(partial):
    rows = partial.shape[0] // lax.axis_size("tp")
    return [
        partial[k * rows : (k + 1) * rows].astype(F32 if k == 0 else BF16)
        for k in range(lax.axis_size("tp"))
    ]


def tp_reduce(chunks):
    total = chunks[0]
    for k in range(1, len(chunks)):
        total = total + shift_tp(chunks[k], -k).astype(F32)
    return total


def arrange(order, rows):
    return times(order, rows).astype(BF16)


def times(left, right):
    return lax.dot_general(left, right, (((1,), (0,)), ((), ())), preferred_element_type=F32)


def times_t(left, right):
    return lax.dot_general(left, right, (((1,), (1,)), ((), ())), preferred_element_type=F32)


def times_rows(left, right):
    return lax.dot_general(left, right, (((0,), (0,)), ((), ())), preferred_element_type=F32)


def assemble(chunk_refs, target):
    rows = chunk_refs[0].shape[0]
    for k, ref in enumerate(chunk_refs):
        target[k * rows : (k + 1) * rows, :] = ref[...]


def spread(total, chunk_refs):
    rows = chunk_refs[0].shape[0]
    for k, ref in enumerate(chunk_refs):
        ref[...] = total[k * rows : (k + 1) * rows, :].astype(ref.dtype)


def whole(shape):
    return pl.BlockSpec(shape, lambda *_: (0,) * len(shape))


def weight_specs(depth, steps):
    return [
        pl.BlockSpec((depth, 2 * TILE), lambda j: (0, j)),
        pl.BlockSpec((depth, TILE), lambda j: (0, 2 * steps + j)),
    ]


def chunk_shapes(count, rows, width):
    return [jax.ShapeDtypeStruct((rows, width), F32 if k == 0 else BF16) for k in range(count)]


def ffn_forward_kernel(count, *refs):
    x_refs, (gu_ref, dn_ref), outs = refs[:count], refs[count : count + 2], refs[count + 2 : -2]
    x_all, total = refs[-2:]
    step = pl.program_id(0)

    @pl.when(step == 0)
    def _():
        assemble(x_refs, x_all)
        total[...] = jnp.zeros_like(total)

    both = times(x_all[...], gu_ref[...])
    gate, up = both[:, :TILE], both[:, TILE:]
    active = (gate * jax.nn.sigmoid(gate) * up).astype(BF16)
    total[...] += times_t(active, dn_ref[...])

    @pl.when(step == pl.num_programs(0) - 1)
    def _():
        spread(total[...], outs)


def ffn_forward(chunks, pack, steps):
    count, (rows, width) = len(chunks), chunks[0].shape
    tokens = count * rows
    return pl.pallas_call(
        functools.partial(ffn_forward_kernel, count),
        grid=(steps,),
        in_specs=[whole((rows, width))] * count + weight_specs(width, steps),
        out_specs=[whole((rows, width))] * count,
        out_shape=chunk_shapes(count, rows, width),
        scratch_shapes=[pltpu.VMEM((tokens, width), BF16), pltpu.VMEM((tokens, width), F32)],
        compiler_params=pltpu.CompilerParams(vmem_limit_bytes=VMEM_LIMIT),
        cost_estimate=pl.CostEstimate(
            flops=2 * tokens * width * 3 * TILE * steps,
            bytes_accessed=2 * width * 3 * TILE * steps,
            transcendentals=tokens * TILE * steps,
        ),
        name="ffn_forward",
    )(*chunks, pack, pack)


def ffn_backward_kernel(count, forward, core_ref, *refs):
    x_refs, b_refs = refs[:count], refs[count : 2 * count]
    gu_ref, dn_ref = refs[2 * count : 2 * count + 2]
    place = 2 * count + 2
    back_outs = refs[place : place + count]
    place += count
    if forward:
        outs = refs[place : place + count]
        place += count
    keep_ref, side_ref = refs[place : place + 2]
    scratch = refs[place + 2 :]
    x_all, b_all, d_total = scratch[:3]
    step = pl.program_id(0)
    width = x_all.shape[1]

    @pl.when(step == 0)
    def _():
        assemble(x_refs, x_all)
        assemble(b_refs, b_all)
        if forward:
            side_ref[:, :width] = x_all[...]
            side_ref[:, width : 2 * width] = b_all[...]
        d_total[...] = jnp.zeros_like(d_total)
        if forward:
            scratch[3][...] = jnp.zeros_like(scratch[3])

    both = times(x_all[...], gu_ref[...])
    gate, up = both[:, :TILE], both[:, TILE:]
    d_active = times(b_all[...], dn_ref[...])
    sigmoid = jax.nn.sigmoid(gate)
    silu = gate * sigmoid
    active = (silu * up).astype(BF16)
    if forward:
        scratch[3][...] += times_t(active, dn_ref[...])
    d_gate = (d_active * up * (sigmoid * (1.0 + gate * (1.0 - sigmoid)))).astype(BF16)
    d_up = (d_active * silu).astype(BF16)
    d_total[...] += times_t(jnp.concatenate([d_gate, d_up], axis=1), gu_ref[...])
    first = core_ref[0] == 0
    half = TILE // 2
    low, high = active[:, :half], active[:, half:]
    offset = 2 * width if forward else 0
    wide = pl.multiple_of(step * TILE, TILE)
    narrow = pl.multiple_of(pl.num_programs(0) * TILE + step * half, half)
    side_wide = pl.multiple_of(offset + wide, TILE)
    side_narrow = pl.multiple_of(offset + narrow, half)

    @pl.when(first)
    def _():
        keep_ref[:, pl.ds(wide, TILE)] = d_gate
        keep_ref[:, pl.ds(narrow, half)] = low
        side_ref[:, pl.ds(side_wide, TILE)] = d_up
        side_ref[:, pl.ds(side_narrow, half)] = high

    @pl.when(jnp.logical_not(first))
    def _():
        keep_ref[:, pl.ds(wide, TILE)] = d_up
        keep_ref[:, pl.ds(narrow, half)] = high
        side_ref[:, pl.ds(side_wide, TILE)] = d_gate
        side_ref[:, pl.ds(side_narrow, half)] = low

    @pl.when(step == pl.num_programs(0) - 1)
    def _():
        spread(d_total[...], back_outs)
        if forward:
            spread(scratch[3][...], outs)


def ffn_backward(core, chunks, back_chunks, pack, steps, forward):
    count, (rows, width) = len(chunks), chunks[0].shape
    tokens = count * rows
    block = TILE + TILE // 2
    ways = 2 if forward else 1
    side_width = (2 * width if forward else 0) + steps * block
    results = pl.pallas_call(
        functools.partial(ffn_backward_kernel, count, forward),
        grid=(steps,),
        in_specs=[pl.BlockSpec(memory_space=pltpu.SMEM)]
        + [whole((rows, width))] * (2 * count)
        + weight_specs(width, steps),
        out_specs=[whole((rows, width))] * (ways * count)
        + [whole((tokens, steps * block)), whole((tokens, side_width))],
        out_shape=chunk_shapes(count, rows, width) * ways
        + [
            jax.ShapeDtypeStruct((tokens, steps * block), BF16),
            jax.ShapeDtypeStruct((tokens, side_width), BF16),
        ],
        scratch_shapes=[pltpu.VMEM((tokens, width), BF16)] * 2
        + [pltpu.VMEM((tokens, width), F32)] * ways,
        compiler_params=pltpu.CompilerParams(vmem_limit_bytes=VMEM_LIMIT),
        cost_estimate=pl.CostEstimate(
            flops=2 * tokens * width * (4 + ways) * TILE * steps,
            bytes_accessed=2 * width * 3 * TILE * steps + 4 * tokens * side_width,
            transcendentals=tokens * TILE * steps,
        ),
        name="ffn_both" if forward else "ffn_backward",
    )(core, *chunks, *back_chunks, pack, pack)
    return results[:count], results[count : ways * count], results[-2], results[-1]


def gradient_kernel(edge, cut, *refs):
    one_own, one_other, two_own, two_other, own_ref, other_ref = refs[:6]
    out_ref = refs[-1]
    step = pl.program_id(0)

    def product(own_left, other_left, columns):
        total = times_rows(own_left[...], own_ref[:, columns])
        total += times_rows(other_left[...], other_ref[:, columns])
        out_ref[:, columns] = total.astype(BF16)

    @pl.when(step < edge)
    def _():
        product(one_own, one_other, slice(None))

    @pl.when(step > edge if cut else step >= edge)
    def _():
        product(two_own, two_other, slice(None))

    if cut:

        @pl.when(step == edge)
        def _():
            product(one_own, one_other, slice(0, cut))
            product(two_own, two_other, slice(cut, None))


def gradient(lefts, own, other, other_start, block, steps, columns, width, out_width, out_start, target):
    tokens = own.shape[0]
    edge, cut = divmod(columns, block)

    def left_spec(index):
        return pl.BlockSpec((tokens, width), lambda j: (0, index))

    in_specs = [left_spec(index) for unused, index in lefts] + [
        pl.BlockSpec((tokens, block), lambda j: (0, j)),
        pl.BlockSpec((tokens, block), lambda j: (0, other_start + j)),
    ]
    operands = [array for array, unused in lefts] + [own, other]
    aliases = {}
    if target is not None:
        in_specs.append(pl.BlockSpec(memory_space=pl.ANY))
        operands.append(target)
        aliases = {len(operands) - 1: 0}
    return pl.pallas_call(
        functools.partial(gradient_kernel, edge, cut),
        grid=(steps,),
        in_specs=in_specs,
        out_specs=pl.BlockSpec((width, block), lambda j: (0, out_start + j)),
        out_shape=jax.ShapeDtypeStruct((width, out_width), BF16),
        input_output_aliases=aliases,
        compiler_params=pltpu.CompilerParams(vmem_limit_bytes=VMEM_LIMIT),
        cost_estimate=pl.CostEstimate(
            flops=4 * tokens * width * block * steps,
            bytes_accessed=2 * width * block * steps,
            transcendentals=0,
        ),
        name="weight_gradient",
    )(*operands)


def share_rows(summed):
    core = lax.axis_index("core")
    rows = summed.shape[0] // 2
    mine = lax.dynamic_slice_in_dim(summed, core * rows, rows, 0)
    other = swap_core(lax.dynamic_slice_in_dim(summed, (1 - core) * rows, rows, 0))
    first = core == 0
    return jnp.where(first, mine, other).astype(F32), jnp.where(first, other, mine).astype(F32)


def sum_chips(partial):
    return lax.psum_scatter(partial, CHIP_AXES, scatter_dimension=0, tiled=True)


def along(blocks, axis):
    ring = lax.axis_size(axis)
    place = lax.axis_index(axis)
    return [lax.dynamic_index_in_dim(blocks, place, 0, False)] + [
        shift_ring(lax.dynamic_index_in_dim(blocks, (place + k) % ring, 0, False), axis, k)
        for k in range(1, ring)
    ]


def add_parts(parts):
    total = parts[0].astype(F32)
    for part in parts[1:]:
        total = total + part.astype(F32)
    return total


def fill(shape, parts):
    result = jnp.zeros(shape, BF16)
    for part, place in parts:
        result = lax.dynamic_update_slice(result, part, place)
    return result


def gather_first(pack):
    rows, columns = pack.shape
    half = columns // 2
    ring = lax.axis_size("x")
    x, z = lax.axis_index("x"), lax.axis_index(Z_AXES)
    low, high = pack[:, :half], pack[:, half:]
    low_parts = [(shift_ring(low, "x", k)[None] if k else low[None], k) for k in range(ring)]
    high_parts = [(shift_ring(high, Z_AXES, k)[None] if k else high[None], k) for k in range(ring)]
    low = fill((ring, rows, half), [(v, ((x - k) % ring, 0, 0)) for v, k in low_parts])
    high = fill((ring, rows, half), [(v, ((z - k) % ring, 0, 0)) for v, k in high_parts])
    return low, high


def gather_second(low, high):
    ring, rows, half = low.shape
    columns = 2 * half
    x, z, core = lax.axis_index("x"), lax.axis_index(Z_AXES), lax.axis_index("core")
    parts = []
    for k in range(ring):
        part = shift_ring(low, Z_AXES, k) if k else low
        parts.append((part[:, None], (0, (z - k) % ring, 0, 0)))
        part = shift_ring(high, "x", k) if k else high
        parts.append((part[None], ((x - k) % ring, 0, 0, half)))
    plane = fill((ring, ring, rows, columns), parts)
    other = swap_core(plane)
    both = fill(
        (ring, ring, CORES, rows, columns),
        [
            (plane[:, :, None], (0, 0, core, 0, 0)),
            (other[:, :, None], (0, 0, 1 - core, 0, 0)),
        ],
    )
    return both.reshape(-1, columns)


def ffn_gradients(low, high, steps, hidden):
    depth = low.shape[0]
    padded = steps * TILE
    gateup = jnp.stack([low[:, :hidden], high[:, :hidden]], axis=1)
    down = jnp.concatenate(
        [part[:, padded:].reshape(depth, steps, TILE // 2) for part in (low, high)], axis=2
    )
    return gateup, down.reshape(depth, padded)[:, :hidden].T


def halves(proj, out):
    first = lax.axis_index("core") == 0
    half = (proj.shape[1] + out.shape[1]) // 2
    late = jnp.concatenate([proj[:, half:], out], axis=1)
    early = proj[:, :half]
    return jnp.where(first, early, late), jnp.where(first, late, early)


def body(
    hidden_in,
    cotangent,
    seq_lengths,
    deal_order,
    mixer_gain,
    mixer_project,
    mixer_kernel,
    mixer_output,
    first_gain,
    first_gateup,
    first_down,
    attend_gain,
    attend_project,
    query_gain,
    key_gain,
    attend_output,
    second_gain,
    second_gateup,
    second_down,
):
    shards = lax.axis_size(TOKEN_AXES)
    contexts = lax.axis_size(CTX_AXES)
    members = lax.axis_size("tp")
    row_count, width = hidden_in.shape
    piece_rows = row_count // shards
    part_rows = piece_rows // members
    chunk = row_count // members
    device = lax.axis_index(TOKEN_AXES)
    own = lax.axis_index("tp")
    core = lax.axis_index("core")
    core_ref = core.reshape(1).astype(jnp.int32)
    depth = mixer_gain.shape[0]
    channels = mixer_output.shape[0]
    hidden = first_down.shape[0]
    heads_width = attend_output.shape[0]
    steps = -(-hidden // TILE)
    padded = steps * TILE
    ffn_width = 3 * padded
    block = TILE + TILE // 2

    def pack_ffn(gateup, down):
        wide = jnp.pad(gateup, ((0, 0), (0, 0), (0, padded - hidden)))
        wide = wide.reshape(depth, 2, steps, TILE).transpose(0, 2, 1, 3).reshape(depth, -1)
        return [wide, jnp.pad(down.T, ((0, 0), (0, padded - hidden)))]

    mixer_pack = jnp.concatenate([mixer_project.reshape(depth, -1), mixer_output.T], axis=1)
    first_pack = jnp.concatenate(
        pack_ffn(first_gateup, first_down) + [attend_project, attend_output.T], axis=1
    )
    second_pack = jnp.concatenate(pack_ffn(second_gateup, second_down), axis=1)
    first_all = lax.all_gather(first_pack, TOKEN_AXES, axis=0, tiled=True)
    second_all = lax.all_gather(second_pack, TOKEN_AXES, axis=0, tiled=True)
    project_b = first_all[:, ffn_width : ffn_width + attend_project.shape[1]]
    output_b_t = first_all[:, ffn_width + attend_project.shape[1] :]

    piece_table = deal_order.reshape(shards, shards, piece_rows)[:, :, 0]
    anchor = piece_table // row_count
    anchor_piece = piece_table % row_count // piece_rows
    send_piece = jnp.sum(jnp.where(anchor == device, anchor_piece, 0), axis=1)
    my_anchor = lax.dynamic_index_in_dim(anchor, device, 0, keepdims=False)
    gains_row = jnp.concatenate(
        [mixer_gain, first_gain, attend_gain, second_gain, jnp.zeros((width - 4 * depth,), BF16)]
    )

    def my_part(rows):
        parts = rows.reshape(shards, members, part_rows, width)
        return lax.dynamic_index_in_dim(parts, own, 1, keepdims=False)[send_piece]

    outgoing = jnp.concatenate(
        [
            my_part(hidden_in),
            my_part(cotangent),
            jnp.broadcast_to(gains_row, (shards, 1, width)),
        ],
        axis=1,
    )
    arrived = lax.all_to_all(outgoing, TOKEN_AXES, split_axis=0, concat_axis=0, tiled=True)
    arrived, mixer_pack = lax.optimization_barrier((arrived, mixer_pack))
    mixer_low, mixer_high = gather_first(mixer_pack)
    gains = (
        arrived[:, 2 * part_rows, : 4 * depth]
        .reshape(shards, 4, depth)
        .transpose(1, 0, 2)
        .reshape(4, width)
        .astype(F32)
    )
    gain_a, gain_f, gain_b, gain_s = gains[0], gains[1], gains[2], gains[3]
    parts = arrived[:, : 2 * part_rows][my_anchor]
    own_tokens = parts[:, :part_rows].reshape(chunk, width)
    own_back = parts[:, part_rows:].reshape(chunk, width)
    stream0 = own_tokens.astype(F32)
    upstream = own_back.astype(F32)
    both = tp_gather(jnp.concatenate([own_tokens, own_back]))
    both, mixer_low, mixer_high = lax.optimization_barrier((both, mixer_low, mixer_high))
    mixer_all = gather_second(mixer_low, mixer_high)
    project_a = mixer_all[:, : 3 * channels]
    output_a_t = mixer_all[:, 3 * channels :]
    back_s_chunks = [slot[chunk:] for slot in both]

    gathered = jnp.arange(row_count)
    member_of = (own - gathered // chunk) % members
    offsets = (
        gathered % chunk // part_rows * piece_rows + member_of * part_rows + gathered % part_rows
    )
    to_gathered = (offsets[:, None] == gathered[None, :]).astype(BF16)
    to_dealt = (offsets[None, :] == gathered[:, None]).astype(BF16)
    tokens = times(to_dealt, jnp.concatenate([slot[:chunk] for slot in both]))

    kernel_taps = mixer_kernel.shape[0]
    halo = kernel_taps - 1
    local_rows = device * row_count + jnp.arange(row_count)
    halo_segment, unused = locate(
        seq_lengths, local_rows[0] - halo + jnp.arange(row_count + halo)
    )
    segment, places = locate(seq_lengths, device * row_count + offsets)
    ctx = lax.axis_index(CTX_AXES)
    group_rows = jnp.concatenate(
        [
            (lax.axis_index(GROUP_AXES) * contexts + (ctx ^ mask)) * row_count + offsets
            for mask in range(contexts)
        ]
    )
    key_segment, key_places = locate(seq_lengths, group_rows)
    allowed = (segment[:, None] == key_segment[None, :]) & (key_places[None, :] <= places[:, None])
    half_dim = HD // 2
    frequency = ROPE_BASE ** (-(jnp.arange(half_dim).astype(F32) * 2.0 / HD))
    angles = places.astype(F32)[:, None] * frequency[None, :]
    cosine = jnp.cos(angles)
    sine = jnp.sin(angles)

    kernel_local = lax.dynamic_slice_in_dim(mixer_kernel, own * channels, channels, 1).astype(F32)
    mixer_in = norm_rows(tokens, gain_a).astype(BF16)
    mixer_in_other = swap_core(mixer_in)
    halo_pad = 16
    halo_in = from_behind(mixer_in[row_count - halo_pad :], 1)
    proj_a = times(jnp.concatenate([halo_in, mixer_in]), project_a)
    proj_b_part = proj_a[:, :channels]
    proj_c_part = proj_a[halo_pad:, channels : 2 * channels]
    proj_x_part = proj_a[:, 2 * channels :]
    extended = (proj_b_part * proj_x_part)[halo_pad - halo :].astype(BF16).astype(F32)
    conv_out = shortconv(extended, kernel_local, halo_segment)
    gated_rows = (proj_c_part * conv_out).astype(BF16)
    gated_parts = arrange(to_gathered, gated_rows)
    stream1 = stream0 + tp_reduce(tp_chunks(times_t(gated_parts, output_a_t)))

    normed_f = tp_gather(norm_rows(stream1, gain_f).astype(BF16))
    stream2 = stream1 + tp_reduce(ffn_forward(normed_f, first_all, steps))

    groups = H // KVH
    score_scale = HD ** (-0.5)
    qgain_f = query_gain.astype(F32)
    kgain_f = key_gain.astype(F32)

    def qk_maps(query_in, key_in, gain_q, gain_k):
        return (
            rotate(norm_rows(query_in, gain_q), cosine, sine),
            rotate(norm_rows(key_in, gain_k), cosine, sine),
        )

    attend_in = jnp.concatenate(tp_gather(norm_rows(stream2, gain_b).astype(BF16)))
    proj_b = times(attend_in, project_b).reshape(row_count, -1, groups + 2, HD)
    kv_heads = proj_b.shape[1]
    query_raw = proj_b[:, :, :groups]
    key_raw = proj_b[:, :, groups]
    query_f, key_f = qk_maps(query_raw, key_raw, qgain_f, kgain_f)
    query_b = query_f.astype(BF16)
    key_value = jnp.concatenate(
        [
            key_f.astype(BF16).reshape(row_count, -1),
            proj_b[:, :, groups + 1].astype(BF16).reshape(row_count, -1),
        ],
        axis=1,
    )
    key_value_z = swap_ctx(key_value, 2)
    key_value_core = swap_core(jnp.concatenate([key_value, key_value_z]))
    key_value_all = jnp.concatenate(
        [key_value, key_value_core[:row_count], key_value_z, key_value_core[row_count:]]
    )
    key_all = key_value_all[:, : kv_heads * HD].reshape(-1, kv_heads, HD)
    value_all = key_value_all[:, kv_heads * HD :].reshape(-1, kv_heads, HD)
    scores = (
        jnp.einsum("tkgd,nkd->kgtn", query_b, key_all, preferred_element_type=F32) * score_scale
    )
    masked = jnp.where(allowed, scores, NEGATIVE)
    row_top = jnp.max(masked, axis=-1, keepdims=True)
    exponent = jnp.exp(masked - row_top)
    row_total = jnp.sum(exponent, axis=-1, keepdims=True)
    softmax_rows = exponent / row_total
    log_total = row_top + jnp.log(row_total)
    attended = (
        jnp.einsum(
            "kgtn,nkd->tkgd", softmax_rows.astype(BF16), value_all, preferred_element_type=F32
        )
        .astype(BF16)
        .reshape(row_count, -1)
    )
    stream3 = stream2 + tp_reduce(tp_chunks(times_t(attended, output_b_t)))

    normed_s = tp_gather(norm_rows(stream3, gain_s).astype(BF16))
    d_chunks, out_chunks, keep, side = ffn_backward(
        core_ref, normed_s, back_s_chunks, second_all, steps, True
    )
    unused, pullback = jax.vjp(norm_rows, stream3, gain_s)
    d_stream, gain_s_grad = pullback(tp_reduce(d_chunks))
    d_stream3 = upstream + d_stream
    out_others = [shift_tp(out_chunks[k], -k) for k in range(1, members)]
    side_other = swap_core(side)
    ffn_lefts = [(side, 0), (side_other, 0), (side, 1), (side_other, 1)]
    ffn_cols = steps * block
    side_start = 2 * width // block
    partial = gradient(
        ffn_lefts, keep, side_other, side_start, block, steps, padded, width, ffn_cols, 0, None
    )

    back_b = tp_gather(d_stream3.astype(BF16))
    back_b, partial = lax.optimization_barrier((back_b, partial))
    second_grads = share_rows(sum_chips(partial))
    back_b = jnp.concatenate(back_b)
    back_b_other = swap_core(back_b)
    attend_in_other = swap_core(attend_in)
    d_attended_b = times(back_b, output_b_t).astype(BF16).reshape(row_count, -1, groups, HD)
    scores_again = (
        jnp.einsum("tkgd,nkd->kgtn", query_b, key_all, preferred_element_type=F32) * score_scale
    )
    probs_again = jnp.where(allowed, jnp.exp(scores_again - log_total), 0.0)
    d_probs = jnp.einsum("tkgd,nkd->kgtn", d_attended_b, value_all, preferred_element_type=F32)
    d_values = jnp.einsum(
        "kgtn,tkgd->nkd", probs_again.astype(BF16), d_attended_b, preferred_element_type=F32
    )
    inner_sum = jnp.sum(probs_again * d_probs, axis=-1, keepdims=True)
    d_scores = (probs_again * (d_probs - inner_sum)).astype(BF16)
    d_query = (
        jnp.einsum("kgtn,nkd->tkgd", d_scores, key_all, preferred_element_type=F32) * score_scale
    )
    d_keys = (
        jnp.einsum("kgtn,tkgd->nkd", d_scores, query_b, preferred_element_type=F32) * score_scale
    )
    d_key_value = jnp.concatenate(
        [d_keys.reshape(-1, kv_heads * HD), d_values.reshape(-1, kv_heads * HD)], axis=1
    )
    d_slots = d_key_value.reshape(contexts, row_count, -1)
    d_others = jnp.concatenate([d_slots[1], d_slots[3]]).astype(BF16)
    d_others = swap_core(d_others).astype(F32)
    d_far = (d_slots[2] + d_others[row_count:]).astype(BF16)
    d_local = d_slots[0] + d_others[:row_count] + swap_ctx(d_far, 2).astype(F32)
    d_key_local = d_local[:, : kv_heads * HD].reshape(row_count, kv_heads, HD)
    d_value_local = d_local[:, kv_heads * HD :].reshape(row_count, kv_heads, HD)
    unused, pullback = jax.vjp(qk_maps, query_raw, key_raw, qgain_f, kgain_f)
    d_query_raw, d_key_raw, qgain_grad, kgain_grad = pullback((d_query, d_key_local))
    d_proj_b = (
        jnp.concatenate([d_query_raw, d_key_raw[:, :, None], d_value_local[:, :, None]], axis=2)
        .astype(BF16)
        .reshape(row_count, -1)
    )
    d_attend_in = tp_reduce(tp_chunks(times_t(d_proj_b, project_b)))
    unused, pullback = jax.vjp(norm_rows, stream2, gain_b)
    d_norm_b, gain_b_grad = pullback(d_attend_in)
    d_stream2 = d_stream3 + d_norm_b
    keep, send = halves(d_proj_b, attended)
    first_core = core == 0
    attend_cols = keep.shape[1]
    small_tile = 2 * (heads_width + attend_project.shape[1]) // 16
    third = gradient(
        [
            (attend_in, 0),
            (attend_in_other, 0),
            (jnp.where(first_core, attend_in, back_b), 0),
            (jnp.where(first_core, attend_in_other, back_b_other), 0),
        ],
        keep,
        swap_core(send),
        0,
        small_tile,
        attend_cols // small_tile,
        attend_project.shape[1] - attend_cols,
        width,
        ffn_cols + attend_cols,
        ffn_cols // small_tile,
        None,
    )

    back_f = tp_gather(d_stream2.astype(BF16))
    back_f, third = lax.optimization_barrier((back_f, third))
    left_x, left_b = jnp.concatenate(normed_f), jnp.concatenate(back_f)
    ffn_lefts = [(left_x, 0), (swap_core(left_x), 0), (left_b, 0), (swap_core(left_b), 0)]
    d_chunks, unused, keep, side = ffn_backward(
        core_ref, normed_f, back_f, first_all, steps, False
    )
    d_chunks, out_others = lax.optimization_barrier((d_chunks, out_others))
    stream4 = stream3 + out_chunks[0]
    for part in out_others:
        stream4 = stream4 + part.astype(F32)
    partial = gradient(
        ffn_lefts,
        keep,
        swap_core(side),
        0,
        block,
        steps,
        padded,
        width,
        ffn_cols + attend_cols,
        0,
        third,
    )

    unused, pullback = jax.vjp(norm_rows, stream1, gain_f)
    d_stream, gain_f_grad = pullback(tp_reduce(d_chunks))
    d_stream1 = d_stream2 + d_stream

    back_a = tp_gather(d_stream1.astype(BF16))
    back_a, partial = lax.optimization_barrier((back_a, partial))
    first_sums = sum_chips(partial)
    back_a = arrange(to_dealt, jnp.concatenate(back_a))
    back_a_other = swap_core(back_a)
    d_gated = times(back_a, output_a_t)
    d_cgate = d_gated * conv_out
    d_conv = d_gated * proj_c_part
    unused, pullback = jax.vjp(
        lambda ext_rows, kernel_in: shortconv(ext_rows, kernel_in, halo_segment),
        extended,
        kernel_local,
    )
    d_extended, kernel_grad = pullback(d_conv)
    returned = from_behind(d_extended[:halo], -1)
    d_product = d_extended[halo:] + jnp.concatenate(
        [jnp.zeros((row_count - halo, channels), F32), returned]
    )
    d_proj_a = jnp.concatenate(
        [
            d_product * proj_x_part[halo_pad:],
            d_cgate,
            d_product * proj_b_part[halo_pad:],
        ],
        axis=1,
    ).astype(BF16)
    d_chunks = tp_chunks(times_t(arrange(to_gathered, d_proj_a), project_a))
    keep, send = halves(d_proj_a, gated_rows)
    mixer_cols = keep.shape[1]
    partial = gradient(
        [
            (mixer_in, 0),
            (mixer_in_other, 0),
            (jnp.where(first_core, mixer_in, back_a), 0),
            (jnp.where(first_core, mixer_in_other, back_a_other), 0),
        ],
        keep,
        swap_core(send),
        0,
        mixer_cols,
        1,
        3 * channels - mixer_cols,
        width,
        mixer_cols,
        0,
        None,
    )
    kernel_cols = kernel_taps * channels
    gain_start = kernel_cols + 2 * HD
    shared = jnp.concatenate([kernel_grad.reshape(-1), qgain_grad, kgain_grad])
    early_gains = [
        grad.reshape(shards, depth) for grad in (gain_f_grad, gain_b_grad, gain_s_grad)
    ]
    early_row = jnp.concatenate(
        [
            jnp.broadcast_to(shared, (shards, gain_start)),
            jnp.pad(
                jnp.concatenate(early_gains, axis=1),
                ((0, 0), (0, width - gain_start - 3 * depth)),
            ),
        ],
        axis=1,
    )
    d_mixer_in, early_row = lax.optimization_barrier((tp_reduce(d_chunks), early_row))
    unused, pullback = jax.vjp(norm_rows, stream0, gain_a)
    d_norm_a, gain_a_grad = pullback(d_mixer_in)
    d_stream0 = d_stream1 + d_norm_a

    slot_for_anchor = jnp.sum(
        jnp.where(
            my_anchor[None, :] == jnp.arange(shards)[:, None], jnp.arange(shards)[None, :], 0
        ),
        axis=1,
    )
    late_start = gain_start + 3 * depth
    late_row = jnp.pad(
        gain_a_grad.reshape(shards, depth), ((0, 0), (late_start, width - late_start - depth))
    )
    leaving = jnp.concatenate(
        [d_stream0.astype(BF16), stream4.astype(BF16), (early_row + late_row).astype(BF16)]
    )
    line = jnp.arange(shards * piece_rows)
    target, item = line // piece_rows, line % piece_rows
    source = jnp.where(
        item < 2 * part_rows,
        item // part_rows * chunk
        + jnp.repeat(slot_for_anchor, piece_rows) * part_rows
        + item % part_rows,
        jnp.where(item == 2 * part_rows, 2 * chunk + target, -1),
    )
    to_leaving = (source[:, None] == jnp.arange(leaving.shape[0])[None, :]).astype(BF16)
    leaving = arrange(to_leaving, leaving)
    leaving, partial = lax.optimization_barrier((leaving, partial))
    home = lax.all_to_all(
        leaving.reshape(shards, piece_rows, width),
        TOKEN_AXES,
        split_axis=0,
        concat_axis=0,
        tiled=True,
    )
    ring = lax.axis_size("x")
    mixer_parts = along(partial.reshape(ring, -1, mixer_cols), "x")
    second_grads = ffn_gradients(*second_grads, steps, hidden)
    home, mixer_parts, second_grads = lax.optimization_barrier((home, mixer_parts, second_grads))
    place = jnp.arange(2 * chunk + 8)
    small_line = (place == 2 * chunk) | (place == 2 * chunk + 1)
    wanted = (
        place % chunk // part_rows * piece_rows
        + place // chunk * part_rows
        + place % part_rows
    )
    to_payload = jnp.where(
        (place < 2 * chunk)[:, None],
        wanted[:, None] == line[None, :],
        small_line[:, None] & (item == 2 * part_rows)[None, :],
    ).astype(BF16)
    payload = times(to_payload, home.reshape(shards * piece_rows, width))
    rounded = payload.astype(BF16).astype(F32)
    payload = jnp.where((place == 2 * chunk + 1)[:, None], payload - rounded, payload)
    last = tp_gather(payload.astype(BF16))
    mixer_parts = add_parts(mixer_parts).astype(BF16).reshape(ring, -1, mixer_cols)
    last[1], mixer_parts = lax.optimization_barrier((last[1], mixer_parts))
    mixer_parts = along(mixer_parts, Z_AXES)
    last, first_sums = lax.optimization_barrier((last, first_sums))
    low, high = share_rows(first_sums)
    first_grads = ffn_gradients(low[:, :ffn_cols], high[:, :ffn_cols], steps, hidden)
    attend_grads = jnp.concatenate([low[:, ffn_cols:], high[:, ffn_cols:]], axis=1)
    mixer_grads = jnp.concatenate(share_rows(add_parts(mixer_parts).astype(BF16)), axis=1)
    home_rows = (
        jnp.repeat(jnp.tile(send_piece, members), part_rows) * piece_rows
        + member_of * part_rows
        + gathered % part_rows
    )
    to_arrival = (home_rows[None, :] == gathered[:, None]).astype(BF16)
    input_gradient = arrange(to_arrival, jnp.concatenate([slot[:chunk] for slot in last]))
    layer_out = arrange(to_arrival, jnp.concatenate([slot[chunk : 2 * chunk] for slot in last]))
    smalls = [
        slot[2 * chunk].astype(F32) + slot[2 * chunk + 1].astype(F32) for slot in last
    ]
    totals = sum(smalls)
    kernel_rows = jnp.stack([small[:kernel_cols].reshape(kernel_taps, channels) for small in smalls])
    kernel_total = jnp.concatenate(
        [
            lax.dynamic_index_in_dim(kernel_rows, (own - member) % members, 0, keepdims=False)
            for member in range(members)
        ],
        axis=1,
    )
    qgain_total = totals[kernel_cols : kernel_cols + HD]
    kgain_total = totals[kernel_cols + HD : kernel_cols + 2 * HD]
    gain_totals = totals[gain_start : gain_start + 4 * depth].reshape(4, depth)

    gateup_s_grad, down_s_grad = second_grads
    gateup_f_grad, down_f_grad = first_grads
    proj_cols = attend_project.shape[1]
    return (
        layer_out,
        input_gradient,
        gain_totals[3],
        mixer_grads[:, : 3 * channels].reshape(depth, 3, channels),
        kernel_total,
        mixer_grads[:, 3 * channels :].T,
        gain_totals[0],
        gateup_f_grad,
        down_f_grad,
        gain_totals[1],
        attend_grads[:, :proj_cols],
        qgain_total,
        kgain_total,
        attend_grads[:, proj_cols:].T,
        gain_totals[2],
        gateup_s_grad,
        down_s_grad,
    )


def solution(mesh):
    names = TOKEN_AXES + ("tp",)
    rings = mesh.shape["fsdp"] // 2, 2, mesh.shape["ctx"] // 2, 2, mesh.shape["tp"]
    tokens = P(TOKEN_AXES, None)
    rows = P(TOKEN_AXES)
    three = P(TOKEN_AXES, None, "tp")
    two = P(TOKEN_AXES, "tp")
    turned = P("tp", TOKEN_AXES)
    return jax.shard_map(
        body,
        mesh=Mesh(mesh.devices.reshape(rings), names),
        in_specs=(
            tokens, tokens, P(), P(),
            rows, three, P(), turned,
            rows, three, turned,
            rows, two, P(), P(), turned,
            rows, three, turned,
        ),
        out_specs=(
            tokens, tokens,
            rows, three, P(), turned,
            rows, three, turned,
            rows, two, P(), P(), turned,
            rows, three, turned,
        ),
        check_vma=False,
    )
```

```python
import functools

import jax
import jax.numpy as jnp
from jax import lax
from jax.experimental import pallas as pl
from jax.experimental.pallas import tpu as pltpu
from jax.sharding import Mesh, PartitionSpec as P

H = 24
KVH = 8
HD = 64

EPSILON = 1e-05
ROPE_BASE = 1000000.0
NEGATIVE = -1e30

CHIP_AXES = ("x", "z_hi", "z_lo")
TOKEN_AXES = CHIP_AXES + ("core",)
GROUP_AXES = ("x", "z_hi")
CTX_AXES = ("z_lo", "core")
Z_AXES = ("z_hi", "z_lo")
CORES = 2
TILE = 256
VMEM_LIMIT = 48 * 1024 * 1024
F32 = jnp.float32
BF16 = jnp.bfloat16


def norm_rows(values, scales):
    return values * lax.rsqrt(jnp.mean(values * values, axis=-1, keepdims=True) + EPSILON) * scales


def rotate(values, cosine, sine):
    half_dim = values.shape[-1] // 2
    shape_out = (values.shape[0],) + (1,) * (values.ndim - 2) + (half_dim,)
    cosine = cosine.reshape(shape_out)
    sine = sine.reshape(shape_out)
    first_half = values[..., :half_dim]
    second_half = values[..., half_dim:]
    return jnp.concatenate(
        [
            first_half * cosine - second_half * sine,
            second_half * cosine + first_half * sine,
        ],
        axis=-1,
    )


def locate(lengths, positions):
    seq_ends = jnp.cumsum(lengths)
    segment = jnp.sum((positions[:, None] >= seq_ends[None, :]).astype(jnp.int32), axis=1)
    starts = seq_ends - lengths
    first_row = jnp.sum(
        jnp.where(segment[:, None] == jnp.arange(lengths.shape[0])[None, :], starts[None, :], 0),
        axis=1,
    )
    return (segment, positions - first_row)


def shortconv(extended, kernel_in, segment):
    kernel_taps = kernel_in.shape[0]
    out_rows = extended.shape[0] - kernel_taps + 1
    result = kernel_in[0] * extended[kernel_taps - 1 :]
    for t in range(1, kernel_taps):
        earlier = extended[kernel_taps - 1 - t : kernel_taps - 1 - t + out_rows]
        same_seq = (
            segment[kernel_taps - 1 - t : kernel_taps - 1 - t + out_rows]
            == segment[kernel_taps - 1 :]
        ).astype(F32)[:, None]
        result = result + kernel_in[t] * earlier * same_seq
    return result


def from_behind(block, distance):
    devices = range(lax.axis_size(CTX_AXES))
    route = [(i - distance, i) for i in devices if i - distance in devices]
    return lax.ppermute(block, CTX_AXES, route)


def swap_ctx(block, mask):
    return lax.ppermute(block, CTX_AXES, [(i, i ^ mask) for i in range(lax.axis_size(CTX_AXES))])


def swap_core(block):
    return lax.ppermute(block, "core", [(0, 1), (1, 0)])


def shift_tp(block, distance):
    members = lax.axis_size("tp")
    return lax.ppermute(block, "tp", [(i, (i + distance) % members) for i in range(members)])


def tp_gather(shard):
    return [shard] + [shift_tp(shard, k) for k in range(1, lax.axis_size("tp"))]


def tp_chunks(partial):
    rows = partial.shape[0] // lax.axis_size("tp")
    return [
        partial[k * rows : (k + 1) * rows].astype(F32 if k == 0 else BF16)
        for k in range(lax.axis_size("tp"))
    ]


def tp_reduce(chunks):
    total = chunks[0]
    for k in range(1, len(chunks)):
        total = total + shift_tp(chunks[k], -k).astype(F32)
    return total


def arrange(order, rows):
    return times(order, rows).astype(BF16)


def times(left, right):
    return lax.dot_general(left, right, (((1,), (0,)), ((), ())), preferred_element_type=F32)


def times_t(left, right):
    return lax.dot_general(left, right, (((1,), (1,)), ((), ())), preferred_element_type=F32)


def times_rows(left, right):
    return lax.dot_general(left, right, (((0,), (0,)), ((), ())), preferred_element_type=F32)


def assemble(chunk_refs, target):
    rows = chunk_refs[0].shape[0]
    for k, ref in enumerate(chunk_refs):
        target[k * rows : (k + 1) * rows, :] = ref[...]


def spread(total, chunk_refs):
    rows = chunk_refs[0].shape[0]
    for k, ref in enumerate(chunk_refs):
        ref[...] = total[k * rows : (k + 1) * rows, :].astype(ref.dtype)


def whole(shape):
    return pl.BlockSpec(shape, lambda *_: (0,) * len(shape))


def weight_specs(depth, steps):
    return [
        pl.BlockSpec((depth, 2 * TILE), lambda j: (0, j)),
        pl.BlockSpec((depth, TILE), lambda j: (0, 2 * steps + j)),
    ]


def chunk_shapes(count, rows, width):
    return [jax.ShapeDtypeStruct((rows, width), F32 if k == 0 else BF16) for k in range(count)]


def ffn_forward_kernel(count, *refs):
    x_refs, (gu_ref, dn_ref), outs = refs[:count], refs[count : count + 2], refs[count + 2 : -2]
    x_all, total = refs[-2:]
    step = pl.program_id(0)

    @pl.when(step == 0)
    def _():
        assemble(x_refs, x_all)
        total[...] = jnp.zeros_like(total)

    both = times(x_all[...], gu_ref[...])
    gate, up = both[:, :TILE], both[:, TILE:]
    active = (gate * jax.nn.sigmoid(gate) * up).astype(BF16)
    total[...] += times_t(active, dn_ref[...])

    @pl.when(step == pl.num_programs(0) - 1)
    def _():
        spread(total[...], outs)


def ffn_forward(chunks, pack, steps):
    count, (rows, width) = len(chunks), chunks[0].shape
    tokens = count * rows
    return pl.pallas_call(
        functools.partial(ffn_forward_kernel, count),
        grid=(steps,),
        in_specs=[whole((rows, width))] * count + weight_specs(width, steps),
        out_specs=[whole((rows, width))] * count,
        out_shape=chunk_shapes(count, rows, width),
        scratch_shapes=[pltpu.VMEM((tokens, width), BF16), pltpu.VMEM((tokens, width), F32)],
        compiler_params=pltpu.CompilerParams(vmem_limit_bytes=VMEM_LIMIT),
        cost_estimate=pl.CostEstimate(
            flops=2 * tokens * width * 3 * TILE * steps,
            bytes_accessed=2 * width * 3 * TILE * steps,
            transcendentals=tokens * TILE * steps,
        ),
        name="ffn_forward",
    )(*chunks, pack, pack)


def ffn_backward_kernel(count, forward, core_ref, *refs):
    x_refs, b_refs = refs[:count], refs[count : 2 * count]
    gu_ref, dn_ref = refs[2 * count : 2 * count + 2]
    place = 2 * count + 2
    back_outs = refs[place : place + count]
    place += count
    if forward:
        outs = refs[place : place + count]
        place += count
    keep_ref, side_ref = refs[place : place + 2]
    scratch = refs[place + 2 :]
    x_all, b_all, d_total = scratch[:3]
    step = pl.program_id(0)
    width = x_all.shape[1]

    @pl.when(step == 0)
    def _():
        assemble(x_refs, x_all)
        assemble(b_refs, b_all)
        if forward:
            side_ref[:, :width] = x_all[...]
            side_ref[:, width : 2 * width] = b_all[...]
        d_total[...] = jnp.zeros_like(d_total)
        if forward:
            scratch[3][...] = jnp.zeros_like(scratch[3])

    both = times(x_all[...], gu_ref[...])
    gate, up = both[:, :TILE], both[:, TILE:]
    d_active = times(b_all[...], dn_ref[...])
    sigmoid = jax.nn.sigmoid(gate)
    silu = gate * sigmoid
    active = (silu * up).astype(BF16)
    if forward:
        scratch[3][...] += times_t(active, dn_ref[...])
    d_gate = (d_active * up * (sigmoid * (1.0 + gate * (1.0 - sigmoid)))).astype(BF16)
    d_up = (d_active * silu).astype(BF16)
    d_total[...] += times_t(jnp.concatenate([d_gate, d_up], axis=1), gu_ref[...])
    first = core_ref[0] == 0
    half = TILE // 2
    low, high = active[:, :half], active[:, half:]
    offset = 2 * width if forward else 0
    wide = pl.multiple_of(step * TILE, TILE)
    narrow = pl.multiple_of(pl.num_programs(0) * TILE + step * half, half)
    side_wide = pl.multiple_of(offset + wide, TILE)
    side_narrow = pl.multiple_of(offset + narrow, half)

    @pl.when(first)
    def _():
        keep_ref[:, pl.ds(wide, TILE)] = d_gate
        keep_ref[:, pl.ds(narrow, half)] = low
        side_ref[:, pl.ds(side_wide, TILE)] = d_up
        side_ref[:, pl.ds(side_narrow, half)] = high

    @pl.when(jnp.logical_not(first))
    def _():
        keep_ref[:, pl.ds(wide, TILE)] = d_up
        keep_ref[:, pl.ds(narrow, half)] = high
        side_ref[:, pl.ds(side_wide, TILE)] = d_gate
        side_ref[:, pl.ds(side_narrow, half)] = low

    @pl.when(step == pl.num_programs(0) - 1)
    def _():
        spread(d_total[...], back_outs)
        if forward:
            spread(scratch[3][...], outs)


def ffn_backward(core, chunks, back_chunks, pack, steps, forward):
    count, (rows, width) = len(chunks), chunks[0].shape
    tokens = count * rows
    block = TILE + TILE // 2
    ways = 2 if forward else 1
    side_width = (2 * width if forward else 0) + steps * block
    results = pl.pallas_call(
        functools.partial(ffn_backward_kernel, count, forward),
        grid=(steps,),
        in_specs=[pl.BlockSpec(memory_space=pltpu.SMEM)]
        + [whole((rows, width))] * (2 * count)
        + weight_specs(width, steps),
        out_specs=[whole((rows, width))] * (ways * count)
        + [whole((tokens, steps * block)), whole((tokens, side_width))],
        out_shape=chunk_shapes(count, rows, width) * ways
        + [
            jax.ShapeDtypeStruct((tokens, steps * block), BF16),
            jax.ShapeDtypeStruct((tokens, side_width), BF16),
        ],
        scratch_shapes=[pltpu.VMEM((tokens, width), BF16)] * 2
        + [pltpu.VMEM((tokens, width), F32)] * ways,
        compiler_params=pltpu.CompilerParams(vmem_limit_bytes=VMEM_LIMIT),
        cost_estimate=pl.CostEstimate(
            flops=2 * tokens * width * (4 + ways) * TILE * steps,
            bytes_accessed=2 * width * 3 * TILE * steps + 4 * tokens * side_width,
            transcendentals=tokens * TILE * steps,
        ),
        name="ffn_both" if forward else "ffn_backward",
    )(core, *chunks, *back_chunks, pack, pack)
    return results[:count], results[count : ways * count], results[-2], results[-1]


def gradient_kernel(edge, cut, *refs):
    one_own, one_other, two_own, two_other, own_ref, other_ref = refs[:6]
    out_ref = refs[-1]
    step = pl.program_id(0)

    def product(own_left, other_left, columns):
        total = times_rows(own_left[...], own_ref[:, columns])
        total += times_rows(other_left[...], other_ref[:, columns])
        out_ref[:, columns] = total.astype(BF16)

    @pl.when(step < edge)
    def _():
        product(one_own, one_other, slice(None))

    @pl.when(step > edge if cut else step >= edge)
    def _():
        product(two_own, two_other, slice(None))

    if cut:

        @pl.when(step == edge)
        def _():
            product(one_own, one_other, slice(0, cut))
            product(two_own, two_other, slice(cut, None))


def gradient(lefts, own, other, other_start, block, steps, columns, width, out_width, out_start, target):
    tokens = own.shape[0]
    edge, cut = divmod(columns, block)

    def left_spec(index):
        return pl.BlockSpec((tokens, width), lambda j: (0, index))

    in_specs = [left_spec(index) for unused, index in lefts] + [
        pl.BlockSpec((tokens, block), lambda j: (0, j)),
        pl.BlockSpec((tokens, block), lambda j: (0, other_start + j)),
    ]
    operands = [array for array, unused in lefts] + [own, other]
    aliases = {}
    if target is not None:
        in_specs.append(pl.BlockSpec(memory_space=pl.ANY))
        operands.append(target)
        aliases = {len(operands) - 1: 0}
    return pl.pallas_call(
        functools.partial(gradient_kernel, edge, cut),
        grid=(steps,),
        in_specs=in_specs,
        out_specs=pl.BlockSpec((width, block), lambda j: (0, out_start + j)),
        out_shape=jax.ShapeDtypeStruct((width, out_width), BF16),
        input_output_aliases=aliases,
        compiler_params=pltpu.CompilerParams(vmem_limit_bytes=VMEM_LIMIT),
        cost_estimate=pl.CostEstimate(
            flops=4 * tokens * width * block * steps,
            bytes_accessed=2 * width * block * steps,
            transcendentals=0,
        ),
        name="weight_gradient",
    )(*operands)


def share_rows(summed):
    core = lax.axis_index("core")
    rows = summed.shape[0] // 2
    mine = lax.dynamic_slice_in_dim(summed, core * rows, rows, 0)
    other = swap_core(lax.dynamic_slice_in_dim(summed, (1 - core) * rows, rows, 0))
    first = core == 0
    return jnp.where(first, mine, other).astype(F32), jnp.where(first, other, mine).astype(F32)


def sum_chips(partial):
    return lax.psum_scatter(partial, CHIP_AXES, scatter_dimension=0, tiled=True)


def gather_pack(pack):
    chips = lax.axis_size(CHIP_AXES)
    core = lax.axis_index("core")
    plane = lax.all_to_all(
        jnp.broadcast_to(pack, (chips,) + pack.shape),
        CHIP_AXES,
        split_axis=0,
        concat_axis=0,
        tiled=True,
    )
    other = swap_core(plane)
    both = jnp.zeros((chips, CORES) + pack.shape, BF16)
    both = lax.dynamic_update_slice(both, plane[:, None], (0, core, 0, 0))
    both = lax.dynamic_update_slice(both, other[:, None], (0, 1 - core, 0, 0))
    return both.reshape(-1, pack.shape[1])


def ffn_gradients(low, high, steps, hidden):
    depth = low.shape[0]
    padded = steps * TILE
    gateup = jnp.stack([low[:, :hidden], high[:, :hidden]], axis=1)
    down = jnp.concatenate(
        [part[:, padded:].reshape(depth, steps, TILE // 2) for part in (low, high)], axis=2
    )
    return gateup, down.reshape(depth, padded)[:, :hidden].T


def halves(proj, out):
    first = lax.axis_index("core") == 0
    half = (proj.shape[1] + out.shape[1]) // 2
    late = jnp.concatenate([proj[:, half:], out], axis=1)
    early = proj[:, :half]
    return jnp.where(first, early, late), jnp.where(first, late, early)


def body(
    hidden_in,
    cotangent,
    seq_lengths,
    deal_order,
    mixer_gain,
    mixer_project,
    mixer_kernel,
    mixer_output,
    first_gain,
    first_gateup,
    first_down,
    attend_gain,
    attend_project,
    query_gain,
    key_gain,
    attend_output,
    second_gain,
    second_gateup,
    second_down,
):
    shards = lax.axis_size(TOKEN_AXES)
    contexts = lax.axis_size(CTX_AXES)
    members = lax.axis_size("tp")
    row_count, width = hidden_in.shape
    piece_rows = row_count // shards
    part_rows = piece_rows // members
    chunk = row_count // members
    device = lax.axis_index(TOKEN_AXES)
    own = lax.axis_index("tp")
    core = lax.axis_index("core")
    core_ref = core.reshape(1).astype(jnp.int32)
    depth = mixer_gain.shape[0]
    channels = mixer_output.shape[0]
    hidden = first_down.shape[0]
    heads_width = attend_output.shape[0]
    steps = -(-hidden // TILE)
    padded = steps * TILE
    ffn_width = 3 * padded
    block = TILE + TILE // 2

    def pack_ffn(gateup, down):
        wide = jnp.pad(gateup, ((0, 0), (0, 0), (0, padded - hidden)))
        wide = wide.reshape(depth, 2, steps, TILE).transpose(0, 2, 1, 3).reshape(depth, -1)
        return [wide, jnp.pad(down.T, ((0, 0), (0, padded - hidden)))]

    mixer_pack = jnp.concatenate([mixer_project.reshape(depth, -1), mixer_output.T], axis=1)
    first_pack = jnp.concatenate(
        pack_ffn(first_gateup, first_down) + [attend_project, attend_output.T], axis=1
    )
    second_pack = jnp.concatenate(pack_ffn(second_gateup, second_down), axis=1)
    first_all = lax.all_gather(first_pack, TOKEN_AXES, axis=0, tiled=True)
    second_all = lax.all_gather(second_pack, TOKEN_AXES, axis=0, tiled=True)
    project_b = first_all[:, ffn_width : ffn_width + attend_project.shape[1]]
    output_b_t = first_all[:, ffn_width + attend_project.shape[1] :]

    piece_table = deal_order.reshape(shards, shards, piece_rows)[:, :, 0]
    anchor = piece_table // row_count
    anchor_piece = piece_table % row_count // piece_rows
    send_piece = jnp.sum(jnp.where(anchor == device, anchor_piece, 0), axis=1)
    my_anchor = lax.dynamic_index_in_dim(anchor, device, 0, keepdims=False)
    gains_row = jnp.concatenate(
        [mixer_gain, first_gain, attend_gain, second_gain, jnp.zeros((width - 4 * depth,), BF16)]
    )

    def my_part(rows):
        parts = rows.reshape(shards, members, part_rows, width)
        return lax.dynamic_index_in_dim(parts, own, 1, keepdims=False)[send_piece]

    outgoing = jnp.concatenate(
        [
            my_part(hidden_in),
            my_part(cotangent),
            jnp.broadcast_to(gains_row, (shards, 1, width)),
        ],
        axis=1,
    )
    arrived = lax.all_to_all(outgoing, TOKEN_AXES, split_axis=0, concat_axis=0, tiled=True)
    arrived, mixer_pack = lax.optimization_barrier((arrived, mixer_pack))
    mixer_all = gather_pack(mixer_pack)
    project_a = mixer_all[:, : 3 * channels]
    output_a_t = mixer_all[:, 3 * channels :]
    gains = (
        arrived[:, 2 * part_rows, : 4 * depth]
        .reshape(shards, 4, depth)
        .transpose(1, 0, 2)
        .reshape(4, width)
        .astype(F32)
    )
    gain_a, gain_f, gain_b, gain_s = gains[0], gains[1], gains[2], gains[3]
    parts = arrived[:, : 2 * part_rows][my_anchor]
    own_tokens = parts[:, :part_rows].reshape(chunk, width)
    own_back = parts[:, part_rows:].reshape(chunk, width)
    stream0 = own_tokens.astype(F32)
    upstream = own_back.astype(F32)
    both = tp_gather(jnp.concatenate([own_tokens, own_back]))
    back_s_chunks = [slot[chunk:] for slot in both]

    gathered = jnp.arange(row_count)
    member_of = (own - gathered // chunk) % members
    offsets = (
        gathered % chunk // part_rows * piece_rows + member_of * part_rows + gathered % part_rows
    )
    to_gathered = (offsets[:, None] == gathered[None, :]).astype(BF16)
    to_dealt = (offsets[None, :] == gathered[:, None]).astype(BF16)
    tokens = times(to_dealt, jnp.concatenate([slot[:chunk] for slot in both]))

    kernel_taps = mixer_kernel.shape[0]
    halo = kernel_taps - 1
    local_rows = device * row_count + jnp.arange(row_count)
    halo_segment, unused = locate(
        seq_lengths, local_rows[0] - halo + jnp.arange(row_count + halo)
    )
    segment, places = locate(seq_lengths, device * row_count + offsets)
    ctx = lax.axis_index(CTX_AXES)
    group_rows = jnp.concatenate(
        [
            (lax.axis_index(GROUP_AXES) * contexts + (ctx ^ mask)) * row_count + offsets
            for mask in range(contexts)
        ]
    )
    key_segment, key_places = locate(seq_lengths, group_rows)
    allowed = (segment[:, None] == key_segment[None, :]) & (key_places[None, :] <= places[:, None])
    half_dim = HD // 2
    frequency = ROPE_BASE ** (-(jnp.arange(half_dim).astype(F32) * 2.0 / HD))
    angles = places.astype(F32)[:, None] * frequency[None, :]
    cosine = jnp.cos(angles)
    sine = jnp.sin(angles)

    kernel_local = lax.dynamic_slice_in_dim(mixer_kernel, own * channels, channels, 1).astype(F32)
    mixer_in = norm_rows(tokens, gain_a).astype(BF16)
    mixer_in_other = swap_core(mixer_in)
    halo_pad = 16
    halo_in = from_behind(mixer_in[row_count - halo_pad :], 1)
    proj_a = times(jnp.concatenate([halo_in, mixer_in]), project_a)
    proj_b_part = proj_a[:, :channels]
    proj_c_part = proj_a[halo_pad:, channels : 2 * channels]
    proj_x_part = proj_a[:, 2 * channels :]
    extended = (proj_b_part * proj_x_part)[halo_pad - halo :].astype(BF16).astype(F32)
    conv_out = shortconv(extended, kernel_local, halo_segment)
    gated_rows = (proj_c_part * conv_out).astype(BF16)
    gated_parts = arrange(to_gathered, gated_rows)
    stream1 = stream0 + tp_reduce(tp_chunks(times_t(gated_parts, output_a_t)))

    normed_f = tp_gather(norm_rows(stream1, gain_f).astype(BF16))
    stream2 = stream1 + tp_reduce(ffn_forward(normed_f, first_all, steps))

    groups = H // KVH
    score_scale = HD ** (-0.5)
    qgain_f = query_gain.astype(F32)
    kgain_f = key_gain.astype(F32)

    def qk_maps(query_in, key_in, gain_q, gain_k):
        return (
            rotate(norm_rows(query_in, gain_q), cosine, sine),
            rotate(norm_rows(key_in, gain_k), cosine, sine),
        )

    attend_in = jnp.concatenate(tp_gather(norm_rows(stream2, gain_b).astype(BF16)))
    proj_b = times(attend_in, project_b).reshape(row_count, -1, groups + 2, HD)
    kv_heads = proj_b.shape[1]
    query_raw = proj_b[:, :, :groups]
    key_raw = proj_b[:, :, groups]
    query_f, key_f = qk_maps(query_raw, key_raw, qgain_f, kgain_f)
    query_b = query_f.astype(BF16)
    key_value = jnp.concatenate(
        [
            key_f.astype(BF16).reshape(row_count, -1),
            proj_b[:, :, groups + 1].astype(BF16).reshape(row_count, -1),
        ],
        axis=1,
    )
    key_value_z = swap_ctx(key_value, 2)
    key_value_core = swap_core(jnp.concatenate([key_value, key_value_z]))
    key_value_all = jnp.concatenate(
        [key_value, key_value_core[:row_count], key_value_z, key_value_core[row_count:]]
    )
    key_all = key_value_all[:, : kv_heads * HD].reshape(-1, kv_heads, HD)
    value_all = key_value_all[:, kv_heads * HD :].reshape(-1, kv_heads, HD)
    scores = (
        jnp.einsum("tkgd,nkd->kgtn", query_b, key_all, preferred_element_type=F32) * score_scale
    )
    masked = jnp.where(allowed, scores, NEGATIVE)
    row_top = jnp.max(masked, axis=-1, keepdims=True)
    exponent = jnp.exp(masked - row_top)
    row_total = jnp.sum(exponent, axis=-1, keepdims=True)
    softmax_rows = exponent / row_total
    log_total = row_top + jnp.log(row_total)
    attended = (
        jnp.einsum(
            "kgtn,nkd->tkgd", softmax_rows.astype(BF16), value_all, preferred_element_type=F32
        )
        .astype(BF16)
        .reshape(row_count, -1)
    )
    stream3 = stream2 + tp_reduce(tp_chunks(times_t(attended, output_b_t)))

    normed_s = tp_gather(norm_rows(stream3, gain_s).astype(BF16))
    d_chunks, out_chunks, keep, side = ffn_backward(
        core_ref, normed_s, back_s_chunks, second_all, steps, True
    )
    unused, pullback = jax.vjp(norm_rows, stream3, gain_s)
    d_stream, gain_s_grad = pullback(tp_reduce(d_chunks))
    d_stream3 = upstream + d_stream
    out_others = [shift_tp(out_chunks[k], -k) for k in range(1, members)]
    side_other = swap_core(side)
    ffn_lefts = [(side, 0), (side_other, 0), (side, 1), (side_other, 1)]
    ffn_cols = steps * block
    side_start = 2 * width // block
    partial = gradient(
        ffn_lefts, keep, side_other, side_start, block, steps, padded, width, ffn_cols, 0, None
    )

    back_b = tp_gather(d_stream3.astype(BF16))
    back_b, partial = lax.optimization_barrier((back_b, partial))
    second_grads = share_rows(sum_chips(partial))
    back_b = jnp.concatenate(back_b)
    back_b_other = swap_core(back_b)
    attend_in_other = swap_core(attend_in)
    d_attended_b = times(back_b, output_b_t).astype(BF16).reshape(row_count, -1, groups, HD)
    scores_again = (
        jnp.einsum("tkgd,nkd->kgtn", query_b, key_all, preferred_element_type=F32) * score_scale
    )
    probs_again = jnp.where(allowed, jnp.exp(scores_again - log_total), 0.0)
    d_probs = jnp.einsum("tkgd,nkd->kgtn", d_attended_b, value_all, preferred_element_type=F32)
    d_values = jnp.einsum(
        "kgtn,tkgd->nkd", probs_again.astype(BF16), d_attended_b, preferred_element_type=F32
    )
    inner_sum = jnp.sum(probs_again * d_probs, axis=-1, keepdims=True)
    d_scores = (probs_again * (d_probs - inner_sum)).astype(BF16)
    d_query = (
        jnp.einsum("kgtn,nkd->tkgd", d_scores, key_all, preferred_element_type=F32) * score_scale
    )
    d_keys = (
        jnp.einsum("kgtn,tkgd->nkd", d_scores, query_b, preferred_element_type=F32) * score_scale
    )
    d_key_value = jnp.concatenate(
        [d_keys.reshape(-1, kv_heads * HD), d_values.reshape(-1, kv_heads * HD)], axis=1
    )
    d_slots = d_key_value.reshape(contexts, row_count, -1)
    d_others = jnp.concatenate([d_slots[1], d_slots[3]]).astype(BF16)
    d_others = swap_core(d_others).astype(F32)
    d_far = (d_slots[2] + d_others[row_count:]).astype(BF16)
    d_local = d_slots[0] + d_others[:row_count] + swap_ctx(d_far, 2).astype(F32)
    d_key_local = d_local[:, : kv_heads * HD].reshape(row_count, kv_heads, HD)
    d_value_local = d_local[:, kv_heads * HD :].reshape(row_count, kv_heads, HD)
    unused, pullback = jax.vjp(qk_maps, query_raw, key_raw, qgain_f, kgain_f)
    d_query_raw, d_key_raw, qgain_grad, kgain_grad = pullback((d_query, d_key_local))
    d_proj_b = (
        jnp.concatenate([d_query_raw, d_key_raw[:, :, None], d_value_local[:, :, None]], axis=2)
        .astype(BF16)
        .reshape(row_count, -1)
    )
    d_attend_in = tp_reduce(tp_chunks(times_t(d_proj_b, project_b)))
    unused, pullback = jax.vjp(norm_rows, stream2, gain_b)
    d_norm_b, gain_b_grad = pullback(d_attend_in)
    d_stream2 = d_stream3 + d_norm_b
    keep, send = halves(d_proj_b, attended)
    first_core = core == 0
    attend_cols = keep.shape[1]
    small_tile = 2 * (heads_width + attend_project.shape[1]) // 16
    third = gradient(
        [
            (attend_in, 0),
            (attend_in_other, 0),
            (jnp.where(first_core, attend_in, back_b), 0),
            (jnp.where(first_core, attend_in_other, back_b_other), 0),
        ],
        keep,
        swap_core(send),
        0,
        small_tile,
        attend_cols // small_tile,
        attend_project.shape[1] - attend_cols,
        width,
        ffn_cols + attend_cols,
        ffn_cols // small_tile,
        None,
    )

    back_f = tp_gather(d_stream2.astype(BF16))
    back_f, third = lax.optimization_barrier((back_f, third))
    left_x, left_b = jnp.concatenate(normed_f), jnp.concatenate(back_f)
    ffn_lefts = [(left_x, 0), (swap_core(left_x), 0), (left_b, 0), (swap_core(left_b), 0)]
    d_chunks, unused, keep, side = ffn_backward(
        core_ref, normed_f, back_f, first_all, steps, False
    )
    d_chunks, out_others = lax.optimization_barrier((d_chunks, out_others))
    stream4 = stream3 + out_chunks[0]
    for part in out_others:
        stream4 = stream4 + part.astype(F32)
    partial = gradient(
        ffn_lefts,
        keep,
        swap_core(side),
        0,
        block,
        steps,
        padded,
        width,
        ffn_cols + attend_cols,
        0,
        third,
    )

    unused, pullback = jax.vjp(norm_rows, stream1, gain_f)
    d_stream, gain_f_grad = pullback(tp_reduce(d_chunks))
    d_stream1 = d_stream2 + d_stream

    back_a = tp_gather(d_stream1.astype(BF16))
    back_a, partial = lax.optimization_barrier((back_a, partial))
    first_sums = sum_chips(partial)
    back_a = arrange(to_dealt, jnp.concatenate(back_a))
    back_a_other = swap_core(back_a)
    d_gated = times(back_a, output_a_t)
    d_cgate = d_gated * conv_out
    d_conv = d_gated * proj_c_part
    unused, pullback = jax.vjp(
        lambda ext_rows, kernel_in: shortconv(ext_rows, kernel_in, halo_segment),
        extended,
        kernel_local,
    )
    d_extended, kernel_grad = pullback(d_conv)
    returned = from_behind(d_extended[:halo], -1)
    d_product = d_extended[halo:] + jnp.concatenate(
        [jnp.zeros((row_count - halo, channels), F32), returned]
    )
    d_proj_a = jnp.concatenate(
        [
            d_product * proj_x_part[halo_pad:],
            d_cgate,
            d_product * proj_b_part[halo_pad:],
        ],
        axis=1,
    ).astype(BF16)
    d_chunks = tp_chunks(times_t(arrange(to_gathered, d_proj_a), project_a))
    keep, send = halves(d_proj_a, gated_rows)
    mixer_cols = keep.shape[1]
    partial = gradient(
        [
            (mixer_in, 0),
            (mixer_in_other, 0),
            (jnp.where(first_core, mixer_in, back_a), 0),
            (jnp.where(first_core, mixer_in_other, back_a_other), 0),
        ],
        keep,
        swap_core(send),
        0,
        mixer_cols,
        1,
        3 * channels - mixer_cols,
        width,
        mixer_cols,
        0,
        None,
    )
    kernel_cols = kernel_taps * channels
    gain_start = kernel_cols + 2 * HD
    shared = jnp.concatenate([kernel_grad.reshape(-1), qgain_grad, kgain_grad])
    early_gains = [
        grad.reshape(shards, depth) for grad in (gain_f_grad, gain_b_grad, gain_s_grad)
    ]
    early_row = jnp.concatenate(
        [
            jnp.broadcast_to(shared, (shards, gain_start)),
            jnp.pad(
                jnp.concatenate(early_gains, axis=1),
                ((0, 0), (0, width - gain_start - 3 * depth)),
            ),
        ],
        axis=1,
    )
    d_mixer_in, early_row = lax.optimization_barrier((tp_reduce(d_chunks), early_row))
    unused, pullback = jax.vjp(norm_rows, stream0, gain_a)
    d_norm_a, gain_a_grad = pullback(d_mixer_in)
    d_stream0 = d_stream1 + d_norm_a

    slot_for_anchor = jnp.sum(
        jnp.where(
            my_anchor[None, :] == jnp.arange(shards)[:, None], jnp.arange(shards)[None, :], 0
        ),
        axis=1,
    )
    late_start = gain_start + 3 * depth
    late_row = jnp.pad(
        gain_a_grad.reshape(shards, depth), ((0, 0), (late_start, width - late_start - depth))
    )
    leaving = jnp.concatenate(
        [d_stream0.astype(BF16), stream4.astype(BF16), (early_row + late_row).astype(BF16)]
    )
    line = jnp.arange(shards * piece_rows)
    target, item = line // piece_rows, line % piece_rows
    source = jnp.where(
        item < 2 * part_rows,
        item // part_rows * chunk
        + jnp.repeat(slot_for_anchor, piece_rows) * part_rows
        + item % part_rows,
        jnp.where(item == 2 * part_rows, 2 * chunk + target, -1),
    )
    to_leaving = (source[:, None] == jnp.arange(leaving.shape[0])[None, :]).astype(BF16)
    leaving = arrange(to_leaving, leaving)
    home = lax.all_to_all(
        leaving.reshape(shards, piece_rows, width),
        TOKEN_AXES,
        split_axis=0,
        concat_axis=0,
        tiled=True,
    )
    second_grads = ffn_gradients(*second_grads, steps, hidden)
    home, partial, second_grads = lax.optimization_barrier((home, partial, second_grads))
    place = jnp.arange(2 * chunk + 8)
    small_line = (place == 2 * chunk) | (place == 2 * chunk + 1)
    wanted = (
        place % chunk // part_rows * piece_rows
        + place // chunk * part_rows
        + place % part_rows
    )
    to_payload = jnp.where(
        (place < 2 * chunk)[:, None],
        wanted[:, None] == line[None, :],
        small_line[:, None] & (item == 2 * part_rows)[None, :],
    ).astype(BF16)
    payload = times(to_payload, home.reshape(shards * piece_rows, width))
    rounded = payload.astype(BF16).astype(F32)
    payload = jnp.where((place == 2 * chunk + 1)[:, None], payload - rounded, payload)
    last = tp_gather(payload.astype(BF16))
    mixer_home = lax.all_to_all(
        partial.reshape(shards, depth, mixer_cols),
        TOKEN_AXES,
        split_axis=0,
        concat_axis=0,
        tiled=True,
    )
    last, first_sums = lax.optimization_barrier((last, first_sums))
    low, high = share_rows(first_sums)
    first_grads = ffn_gradients(low[:, :ffn_cols], high[:, :ffn_cols], steps, hidden)
    attend_grads = jnp.concatenate([low[:, ffn_cols:], high[:, ffn_cols:]], axis=1)
    first_grads, attend_grads, mixer_home = lax.optimization_barrier(
        (first_grads, attend_grads, mixer_home)
    )
    mixer_home = mixer_home.reshape(shards // CORES, CORES, depth, mixer_cols)
    mixer_grads = jnp.sum(mixer_home.astype(F32), axis=0)
    mixer_grads = jnp.concatenate([mixer_grads[0], mixer_grads[1]], axis=1)
    home_rows = (
        jnp.repeat(jnp.tile(send_piece, members), part_rows) * piece_rows
        + member_of * part_rows
        + gathered % part_rows
    )
    to_arrival = (home_rows[None, :] == gathered[:, None]).astype(BF16)
    input_gradient = arrange(to_arrival, jnp.concatenate([slot[:chunk] for slot in last]))
    layer_out = arrange(to_arrival, jnp.concatenate([slot[chunk : 2 * chunk] for slot in last]))
    smalls = [
        slot[2 * chunk].astype(F32) + slot[2 * chunk + 1].astype(F32) for slot in last
    ]
    totals = sum(smalls)
    kernel_rows = jnp.stack([small[:kernel_cols].reshape(kernel_taps, channels) for small in smalls])
    kernel_total = jnp.concatenate(
        [
            lax.dynamic_index_in_dim(kernel_rows, (own - member) % members, 0, keepdims=False)
            for member in range(members)
        ],
        axis=1,
    )
    qgain_total = totals[kernel_cols : kernel_cols + HD]
    kgain_total = totals[kernel_cols + HD : kernel_cols + 2 * HD]
    gain_totals = totals[gain_start : gain_start + 4 * depth].reshape(4, depth)

    gateup_s_grad, down_s_grad = second_grads
    gateup_f_grad, down_f_grad = first_grads
    proj_cols = attend_project.shape[1]
    return (
        layer_out,
        input_gradient,
        gain_totals[3],
        mixer_grads[:, : 3 * channels].reshape(depth, 3, channels),
        kernel_total,
        mixer_grads[:, 3 * channels :].T,
        gain_totals[0],
        gateup_f_grad,
        down_f_grad,
        gain_totals[1],
        attend_grads[:, :proj_cols],
        qgain_total,
        kgain_total,
        attend_grads[:, proj_cols:].T,
        gain_totals[2],
        gateup_s_grad,
        down_s_grad,
    )


def solution(mesh):
    names = TOKEN_AXES + ("tp",)
    rings = mesh.shape["fsdp"] // 2, 2, mesh.shape["ctx"] // 2, 2, mesh.shape["tp"]
    tokens = P(TOKEN_AXES, None)
    rows = P(TOKEN_AXES)
    three = P(TOKEN_AXES, None, "tp")
    two = P(TOKEN_AXES, "tp")
    turned = P("tp", TOKEN_AXES)
    return jax.shard_map(
        body,
        mesh=Mesh(mesh.devices.reshape(rings), names),
        in_specs=(
            tokens, tokens, P(), P(),
            rows, three, P(), turned,
            rows, three, turned,
            rows, two, P(), P(), turned,
            rows, three, turned,
        ),
        out_specs=(
            tokens, tokens,
            rows, three, P(), turned,
            rows, three, turned,
            rows, two, P(), P(), turned,
            rows, three, turned,
        ),
        check_vma=False,
    )
```

```python
import functools

import jax
import jax.numpy as jnp
from jax import lax
from jax.experimental import pallas as pl
from jax.experimental.pallas import tpu as pltpu
from jax.sharding import Mesh, PartitionSpec as P

H = 24
KVH = 8
HD = 64

EPSILON = 1e-05
ROPE_BASE = 1000000.0
NEGATIVE = -1e30

CHIP_AXES = ("x", "z_hi", "z_lo")
TOKEN_AXES = CHIP_AXES + ("core",)
GROUP_AXES = ("x", "z_hi")
CTX_AXES = ("z_lo", "core")
Z_AXES = ("z_hi", "z_lo")
CORES = 2
TILE = 256
VMEM_LIMIT = 48 * 1024 * 1024
F32 = jnp.float32
BF16 = jnp.bfloat16


def norm_rows(values, scales):
    return values * lax.rsqrt(jnp.mean(values * values, axis=-1, keepdims=True) + EPSILON) * scales


def rotate(values, cosine, sine):
    half_dim = values.shape[-1] // 2
    shape_out = (values.shape[0],) + (1,) * (values.ndim - 2) + (half_dim,)
    cosine = cosine.reshape(shape_out)
    sine = sine.reshape(shape_out)
    first_half = values[..., :half_dim]
    second_half = values[..., half_dim:]
    return jnp.concatenate(
        [
            first_half * cosine - second_half * sine,
            second_half * cosine + first_half * sine,
        ],
        axis=-1,
    )


def locate(lengths, positions):
    seq_ends = jnp.cumsum(lengths)
    segment = jnp.sum((positions[:, None] >= seq_ends[None, :]).astype(jnp.int32), axis=1)
    starts = seq_ends - lengths
    first_row = jnp.sum(
        jnp.where(segment[:, None] == jnp.arange(lengths.shape[0])[None, :], starts[None, :], 0),
        axis=1,
    )
    return (segment, positions - first_row)


def shortconv(extended, kernel_in, segment):
    kernel_taps = kernel_in.shape[0]
    out_rows = extended.shape[0] - kernel_taps + 1
    result = kernel_in[0] * extended[kernel_taps - 1 :]
    for t in range(1, kernel_taps):
        earlier = extended[kernel_taps - 1 - t : kernel_taps - 1 - t + out_rows]
        same_seq = (
            segment[kernel_taps - 1 - t : kernel_taps - 1 - t + out_rows]
            == segment[kernel_taps - 1 :]
        ).astype(F32)[:, None]
        result = result + kernel_in[t] * earlier * same_seq
    return result


def from_behind(block, distance):
    devices = range(lax.axis_size(CTX_AXES))
    route = [(i - distance, i) for i in devices if i - distance in devices]
    return lax.ppermute(block, CTX_AXES, route)


def swap_ctx(block, mask):
    return lax.ppermute(block, CTX_AXES, [(i, i ^ mask) for i in range(lax.axis_size(CTX_AXES))])


def swap_core(block):
    return lax.ppermute(block, "core", [(0, 1), (1, 0)])


def shift_tp(block, distance):
    members = lax.axis_size("tp")
    return lax.ppermute(block, "tp", [(i, (i + distance) % members) for i in range(members)])


def tp_gather(shard):
    return [shard] + [shift_tp(shard, k) for k in range(1, lax.axis_size("tp"))]


def tp_chunks(partial):
    rows = partial.shape[0] // lax.axis_size("tp")
    return [
        partial[k * rows : (k + 1) * rows].astype(F32 if k == 0 else BF16)
        for k in range(lax.axis_size("tp"))
    ]


def tp_reduce(chunks):
    total = chunks[0]
    for k in range(1, len(chunks)):
        total = total + shift_tp(chunks[k], -k).astype(F32)
    return total


def arrange(order, rows):
    return times(order, rows).astype(BF16)


def times(left, right):
    return lax.dot_general(left, right, (((1,), (0,)), ((), ())), preferred_element_type=F32)


def times_t(left, right):
    return lax.dot_general(left, right, (((1,), (1,)), ((), ())), preferred_element_type=F32)


def times_rows(left, right):
    return lax.dot_general(left, right, (((0,), (0,)), ((), ())), preferred_element_type=F32)


def assemble(chunk_refs, target):
    rows = chunk_refs[0].shape[0]
    for k, ref in enumerate(chunk_refs):
        target[k * rows : (k + 1) * rows, :] = ref[...]


def spread(total, chunk_refs):
    rows = chunk_refs[0].shape[0]
    for k, ref in enumerate(chunk_refs):
        ref[...] = total[k * rows : (k + 1) * rows, :].astype(ref.dtype)


def whole(shape):
    return pl.BlockSpec(shape, lambda *_: (0,) * len(shape))


def weight_specs(depth, steps):
    return [
        pl.BlockSpec((depth, 2 * TILE), lambda j: (0, j)),
        pl.BlockSpec((depth, TILE), lambda j: (0, 2 * steps + j)),
    ]


def chunk_shapes(count, rows, width):
    return [jax.ShapeDtypeStruct((rows, width), F32 if k == 0 else BF16) for k in range(count)]


def ffn_forward_kernel(count, *refs):
    x_refs, (gu_ref, dn_ref), outs = refs[:count], refs[count : count + 2], refs[count + 2 : -2]
    x_all, total = refs[-2:]
    step = pl.program_id(0)

    @pl.when(step == 0)
    def _():
        assemble(x_refs, x_all)
        total[...] = jnp.zeros_like(total)

    both = times(x_all[...], gu_ref[...])
    gate, up = both[:, :TILE], both[:, TILE:]
    active = (gate * jax.nn.sigmoid(gate) * up).astype(BF16)
    total[...] += times_t(active, dn_ref[...])

    @pl.when(step == pl.num_programs(0) - 1)
    def _():
        spread(total[...], outs)


def ffn_forward(chunks, pack, steps):
    count, (rows, width) = len(chunks), chunks[0].shape
    tokens = count * rows
    return pl.pallas_call(
        functools.partial(ffn_forward_kernel, count),
        grid=(steps,),
        in_specs=[whole((rows, width))] * count + weight_specs(width, steps),
        out_specs=[whole((rows, width))] * count,
        out_shape=chunk_shapes(count, rows, width),
        scratch_shapes=[pltpu.VMEM((tokens, width), BF16), pltpu.VMEM((tokens, width), F32)],
        compiler_params=pltpu.CompilerParams(vmem_limit_bytes=VMEM_LIMIT),
        cost_estimate=pl.CostEstimate(
            flops=2 * tokens * width * 3 * TILE * steps,
            bytes_accessed=2 * width * 3 * TILE * steps,
            transcendentals=tokens * TILE * steps,
        ),
        name="ffn_forward",
    )(*chunks, pack, pack)


def ffn_backward_kernel(count, forward, core_ref, *refs):
    x_refs, b_refs = refs[:count], refs[count : 2 * count]
    gu_ref, dn_ref = refs[2 * count : 2 * count + 2]
    place = 2 * count + 2
    back_outs = refs[place : place + count]
    place += count
    if forward:
        outs = refs[place : place + count]
        place += count
    keep_ref, side_ref = refs[place : place + 2]
    scratch = refs[place + 2 :]
    x_all, b_all, d_total = scratch[:3]
    step = pl.program_id(0)
    width = x_all.shape[1]

    @pl.when(step == 0)
    def _():
        assemble(x_refs, x_all)
        assemble(b_refs, b_all)
        if forward:
            side_ref[:, :width] = x_all[...]
            side_ref[:, width : 2 * width] = b_all[...]
        d_total[...] = jnp.zeros_like(d_total)
        if forward:
            scratch[3][...] = jnp.zeros_like(scratch[3])

    both = times(x_all[...], gu_ref[...])
    gate, up = both[:, :TILE], both[:, TILE:]
    d_active = times(b_all[...], dn_ref[...])
    sigmoid = jax.nn.sigmoid(gate)
    silu = gate * sigmoid
    active = (silu * up).astype(BF16)
    if forward:
        scratch[3][...] += times_t(active, dn_ref[...])
    d_gate = (d_active * up * (sigmoid * (1.0 + gate * (1.0 - sigmoid)))).astype(BF16)
    d_up = (d_active * silu).astype(BF16)
    d_total[...] += times_t(jnp.concatenate([d_gate, d_up], axis=1), gu_ref[...])
    first = core_ref[0] == 0
    half = TILE // 2
    low, high = active[:, :half], active[:, half:]
    offset = 2 * width if forward else 0
    wide = pl.multiple_of(step * TILE, TILE)
    narrow = pl.multiple_of(pl.num_programs(0) * TILE + step * half, half)
    side_wide = pl.multiple_of(offset + wide, TILE)
    side_narrow = pl.multiple_of(offset + narrow, half)

    @pl.when(first)
    def _():
        keep_ref[:, pl.ds(wide, TILE)] = d_gate
        keep_ref[:, pl.ds(narrow, half)] = low
        side_ref[:, pl.ds(side_wide, TILE)] = d_up
        side_ref[:, pl.ds(side_narrow, half)] = high

    @pl.when(jnp.logical_not(first))
    def _():
        keep_ref[:, pl.ds(wide, TILE)] = d_up
        keep_ref[:, pl.ds(narrow, half)] = high
        side_ref[:, pl.ds(side_wide, TILE)] = d_gate
        side_ref[:, pl.ds(side_narrow, half)] = low

    @pl.when(step == pl.num_programs(0) - 1)
    def _():
        spread(d_total[...], back_outs)
        if forward:
            spread(scratch[3][...], outs)


def ffn_backward(core, chunks, back_chunks, pack, steps, forward):
    count, (rows, width) = len(chunks), chunks[0].shape
    tokens = count * rows
    block = TILE + TILE // 2
    ways = 2 if forward else 1
    side_width = (2 * width if forward else 0) + steps * block
    results = pl.pallas_call(
        functools.partial(ffn_backward_kernel, count, forward),
        grid=(steps,),
        in_specs=[pl.BlockSpec(memory_space=pltpu.SMEM)]
        + [whole((rows, width))] * (2 * count)
        + weight_specs(width, steps),
        out_specs=[whole((rows, width))] * (ways * count)
        + [whole((tokens, steps * block)), whole((tokens, side_width))],
        out_shape=chunk_shapes(count, rows, width) * ways
        + [
            jax.ShapeDtypeStruct((tokens, steps * block), BF16),
            jax.ShapeDtypeStruct((tokens, side_width), BF16),
        ],
        scratch_shapes=[pltpu.VMEM((tokens, width), BF16)] * 2
        + [pltpu.VMEM((tokens, width), F32)] * ways,
        compiler_params=pltpu.CompilerParams(vmem_limit_bytes=VMEM_LIMIT),
        cost_estimate=pl.CostEstimate(
            flops=2 * tokens * width * (4 + ways) * TILE * steps,
            bytes_accessed=2 * width * 3 * TILE * steps + 4 * tokens * side_width,
            transcendentals=tokens * TILE * steps,
        ),
        name="ffn_both" if forward else "ffn_backward",
    )(core, *chunks, *back_chunks, pack, pack)
    return results[:count], results[count : ways * count], results[-2], results[-1]


def gradient_kernel(edge, cut, *refs):
    one_own, one_other, two_own, two_other, own_ref, other_ref = refs[:6]
    out_ref = refs[-1]
    step = pl.program_id(0)

    def product(own_left, other_left, columns):
        total = times_rows(own_left[...], own_ref[:, columns])
        total += times_rows(other_left[...], other_ref[:, columns])
        out_ref[:, columns] = total.astype(BF16)

    @pl.when(step < edge)
    def _():
        product(one_own, one_other, slice(None))

    @pl.when(step > edge if cut else step >= edge)
    def _():
        product(two_own, two_other, slice(None))

    if cut:

        @pl.when(step == edge)
        def _():
            product(one_own, one_other, slice(0, cut))
            product(two_own, two_other, slice(cut, None))


def gradient(lefts, own, other, other_start, block, steps, columns, width, out_width, out_start, target):
    tokens = own.shape[0]
    edge, cut = divmod(columns, block)

    def left_spec(index):
        return pl.BlockSpec((tokens, width), lambda j: (0, index))

    in_specs = [left_spec(index) for unused, index in lefts] + [
        pl.BlockSpec((tokens, block), lambda j: (0, j)),
        pl.BlockSpec((tokens, block), lambda j: (0, other_start + j)),
    ]
    operands = [array for array, unused in lefts] + [own, other]
    aliases = {}
    if target is not None:
        in_specs.append(pl.BlockSpec(memory_space=pl.ANY))
        operands.append(target)
        aliases = {len(operands) - 1: 0}
    return pl.pallas_call(
        functools.partial(gradient_kernel, edge, cut),
        grid=(steps,),
        in_specs=in_specs,
        out_specs=pl.BlockSpec((width, block), lambda j: (0, out_start + j)),
        out_shape=jax.ShapeDtypeStruct((width, out_width), BF16),
        input_output_aliases=aliases,
        compiler_params=pltpu.CompilerParams(vmem_limit_bytes=VMEM_LIMIT),
        cost_estimate=pl.CostEstimate(
            flops=4 * tokens * width * block * steps,
            bytes_accessed=2 * width * block * steps,
            transcendentals=0,
        ),
        name="weight_gradient",
    )(*operands)


def attend_backward_kernel(scale, groups, *refs):
    q_ref, do_ref, k_ref, v_ref, log_ref, place_ref, key_ref, dq_ref, dk_ref, dv_ref = refs
    head = pl.program_id(0)
    query, d_out, key = q_ref[0], do_ref[0], k_ref[0]
    scores = times_t(key, query) * scale
    same = key_ref[:, 0:1] == place_ref[0:1, :]
    allowed = same & (key_ref[:, 1:2] <= place_ref[1:2, :])
    probs = jnp.where(allowed, jnp.exp(scores - log_ref[0]), 0.0)
    d_probs = times_t(v_ref[0], d_out)
    inner = jnp.sum(probs * d_probs, axis=0, keepdims=True)
    d_scores = (probs * (d_probs - inner)).astype(BF16)
    d_value = times(probs.astype(BF16), d_out)
    d_key = times(d_scores, query) * scale
    dq_ref[0] = (times_rows(key, d_scores) * scale).T

    @pl.when(head % groups == 0)
    def _():
        dk_ref[0] = d_key
        dv_ref[0] = d_value

    @pl.when(head % groups != 0)
    def _():
        dk_ref[0] += d_key
        dv_ref[0] += d_value


def attend_backward(query, d_out, key, value, log_total, place, key_place, scale):
    heads, rows, size = query.shape
    kv_heads, keys = key.shape[:2]
    groups = heads // kv_heads

    def by_head(shape):
        return pl.BlockSpec((1,) + shape, lambda h: (h, 0, 0))

    def by_group(shape):
        return pl.BlockSpec((1,) + shape, lambda h: (h // groups, 0, 0))

    return pl.pallas_call(
        functools.partial(attend_backward_kernel, scale, groups),
        grid=(heads,),
        in_specs=[
            by_head((rows, size)),
            by_head((rows, size)),
            by_group((keys, size)),
            by_group((keys, size)),
            by_head((1, rows)),
            whole(place.shape),
            whole(key_place.shape),
        ],
        out_specs=[by_head((rows, size)), by_group((keys, size)), by_group((keys, size))],
        out_shape=[
            jax.ShapeDtypeStruct((heads, rows, size), F32),
            jax.ShapeDtypeStruct((kv_heads, keys, size), F32),
            jax.ShapeDtypeStruct((kv_heads, keys, size), F32),
        ],
        compiler_params=pltpu.CompilerParams(vmem_limit_bytes=VMEM_LIMIT),
        cost_estimate=pl.CostEstimate(
            flops=10 * heads * rows * keys * size,
            bytes_accessed=4 * heads * rows * size * 2 + 12 * kv_heads * keys * size,
            transcendentals=heads * rows * keys,
        ),
        name="attend_backward",
    )(query, d_out, key, value, log_total, place, key_place)


def share_rows(summed):
    core = lax.axis_index("core")
    rows = summed.shape[0] // 2
    mine = lax.dynamic_slice_in_dim(summed, core * rows, rows, 0)
    other = swap_core(lax.dynamic_slice_in_dim(summed, (1 - core) * rows, rows, 0))
    first = core == 0
    return jnp.where(first, mine, other).astype(F32), jnp.where(first, other, mine).astype(F32)


def sum_chips(partial):
    return lax.psum_scatter(partial, CHIP_AXES, scatter_dimension=0, tiled=True)


def gather_pack(pack):
    chips = lax.axis_size(CHIP_AXES)
    core = lax.axis_index("core")
    plane = lax.all_to_all(
        jnp.broadcast_to(pack, (chips,) + pack.shape),
        CHIP_AXES,
        split_axis=0,
        concat_axis=0,
        tiled=True,
    )
    other = swap_core(plane)
    both = jnp.zeros((chips, CORES) + pack.shape, BF16)
    both = lax.dynamic_update_slice(both, plane[:, None], (0, core, 0, 0))
    both = lax.dynamic_update_slice(both, other[:, None], (0, 1 - core, 0, 0))
    return both.reshape(-1, pack.shape[1])


def ffn_gradients(low, high, steps, hidden):
    depth = low.shape[0]
    padded = steps * TILE
    gateup = jnp.stack([low[:, :hidden], high[:, :hidden]], axis=1)
    down = jnp.concatenate(
        [part[:, padded:].reshape(depth, steps, TILE // 2) for part in (low, high)], axis=2
    )
    return gateup, down.reshape(depth, padded)[:, :hidden].T


def halves(proj, out):
    first = lax.axis_index("core") == 0
    half = (proj.shape[1] + out.shape[1]) // 2
    late = jnp.concatenate([proj[:, half:], out], axis=1)
    early = proj[:, :half]
    return jnp.where(first, early, late), jnp.where(first, late, early)


def body(
    hidden_in,
    cotangent,
    seq_lengths,
    deal_order,
    mixer_gain,
    mixer_project,
    mixer_kernel,
    mixer_output,
    first_gain,
    first_gateup,
    first_down,
    attend_gain,
    attend_project,
    query_gain,
    key_gain,
    attend_output,
    second_gain,
    second_gateup,
    second_down,
):
    shards = lax.axis_size(TOKEN_AXES)
    contexts = lax.axis_size(CTX_AXES)
    members = lax.axis_size("tp")
    row_count, width = hidden_in.shape
    piece_rows = row_count // shards
    part_rows = piece_rows // members
    chunk = row_count // members
    device = lax.axis_index(TOKEN_AXES)
    own = lax.axis_index("tp")
    core = lax.axis_index("core")
    core_ref = core.reshape(1).astype(jnp.int32)
    depth = mixer_gain.shape[0]
    channels = mixer_output.shape[0]
    hidden = first_down.shape[0]
    heads_width = attend_output.shape[0]
    steps = -(-hidden // TILE)
    padded = steps * TILE
    ffn_width = 3 * padded
    block = TILE + TILE // 2

    def pack_ffn(gateup, down):
        wide = jnp.pad(gateup, ((0, 0), (0, 0), (0, padded - hidden)))
        wide = wide.reshape(depth, 2, steps, TILE).transpose(0, 2, 1, 3).reshape(depth, -1)
        return [wide, jnp.pad(down.T, ((0, 0), (0, padded - hidden)))]

    mixer_pack = jnp.concatenate([mixer_project.reshape(depth, -1), mixer_output.T], axis=1)
    first_pack = jnp.concatenate(
        pack_ffn(first_gateup, first_down) + [attend_project, attend_output.T], axis=1
    )
    second_pack = jnp.concatenate(pack_ffn(second_gateup, second_down), axis=1)
    first_all = lax.all_gather(first_pack, TOKEN_AXES, axis=0, tiled=True)
    second_all = lax.all_gather(second_pack, TOKEN_AXES, axis=0, tiled=True)
    project_b = first_all[:, ffn_width : ffn_width + attend_project.shape[1]]
    output_b_t = first_all[:, ffn_width + attend_project.shape[1] :]

    piece_table = deal_order.reshape(shards, shards, piece_rows)[:, :, 0]
    anchor = piece_table // row_count
    anchor_piece = piece_table % row_count // piece_rows
    send_piece = jnp.sum(jnp.where(anchor == device, anchor_piece, 0), axis=1)
    my_anchor = lax.dynamic_index_in_dim(anchor, device, 0, keepdims=False)
    gains_row = jnp.concatenate(
        [mixer_gain, first_gain, attend_gain, second_gain, jnp.zeros((width - 4 * depth,), BF16)]
    )

    def my_part(rows):
        parts = rows.reshape(shards, members, part_rows, width)
        return lax.dynamic_index_in_dim(parts, own, 1, keepdims=False)[send_piece]

    outgoing = jnp.concatenate(
        [
            my_part(hidden_in),
            my_part(cotangent),
            jnp.broadcast_to(gains_row, (shards, 1, width)),
        ],
        axis=1,
    )
    arrived = lax.all_to_all(outgoing, TOKEN_AXES, split_axis=0, concat_axis=0, tiled=True)
    arrived, mixer_pack = lax.optimization_barrier((arrived, mixer_pack))
    mixer_all = gather_pack(mixer_pack)
    project_a = mixer_all[:, : 3 * channels]
    output_a_t = mixer_all[:, 3 * channels :]
    gains = (
        arrived[:, 2 * part_rows, : 4 * depth]
        .reshape(shards, 4, depth)
        .transpose(1, 0, 2)
        .reshape(4, width)
        .astype(F32)
    )
    gain_a, gain_f, gain_b, gain_s = gains[0], gains[1], gains[2], gains[3]
    parts = arrived[:, : 2 * part_rows][my_anchor]
    own_tokens = parts[:, :part_rows].reshape(chunk, width)
    own_back = parts[:, part_rows:].reshape(chunk, width)
    stream0 = own_tokens.astype(F32)
    upstream = own_back.astype(F32)
    both = tp_gather(jnp.concatenate([own_tokens, own_back]))
    back_s_chunks = [slot[chunk:] for slot in both]

    gathered = jnp.arange(row_count)
    member_of = (own - gathered // chunk) % members
    offsets = (
        gathered % chunk // part_rows * piece_rows + member_of * part_rows + gathered % part_rows
    )
    to_gathered = (offsets[:, None] == gathered[None, :]).astype(BF16)
    to_dealt = (offsets[None, :] == gathered[:, None]).astype(BF16)
    tokens = times(to_dealt, jnp.concatenate([slot[:chunk] for slot in both]))

    kernel_taps = mixer_kernel.shape[0]
    halo = kernel_taps - 1
    local_rows = device * row_count + jnp.arange(row_count)
    halo_segment, unused = locate(
        seq_lengths, local_rows[0] - halo + jnp.arange(row_count + halo)
    )
    segment, places = locate(seq_lengths, device * row_count + offsets)
    ctx = lax.axis_index(CTX_AXES)
    group_rows = jnp.concatenate(
        [
            (lax.axis_index(GROUP_AXES) * contexts + (ctx ^ mask)) * row_count + offsets
            for mask in range(contexts)
        ]
    )
    key_segment, key_places = locate(seq_lengths, group_rows)
    allowed = (segment[:, None] == key_segment[None, :]) & (key_places[None, :] <= places[:, None])
    half_dim = HD // 2
    frequency = ROPE_BASE ** (-(jnp.arange(half_dim).astype(F32) * 2.0 / HD))
    angles = places.astype(F32)[:, None] * frequency[None, :]
    cosine = jnp.cos(angles)
    sine = jnp.sin(angles)

    kernel_local = lax.dynamic_slice_in_dim(mixer_kernel, own * channels, channels, 1).astype(F32)
    mixer_in = norm_rows(tokens, gain_a).astype(BF16)
    mixer_in_other = swap_core(mixer_in)
    halo_pad = 16
    halo_in = from_behind(mixer_in[row_count - halo_pad :], 1)
    proj_a = times(jnp.concatenate([halo_in, mixer_in]), project_a)
    proj_b_part = proj_a[:, :channels]
    proj_c_part = proj_a[halo_pad:, channels : 2 * channels]
    proj_x_part = proj_a[:, 2 * channels :]
    extended = (proj_b_part * proj_x_part)[halo_pad - halo :].astype(BF16).astype(F32)
    conv_out = shortconv(extended, kernel_local, halo_segment)
    gated_rows = (proj_c_part * conv_out).astype(BF16)
    gated_parts = arrange(to_gathered, gated_rows)
    stream1 = stream0 + tp_reduce(tp_chunks(times_t(gated_parts, output_a_t)))

    normed_f = tp_gather(norm_rows(stream1, gain_f).astype(BF16))
    stream2 = stream1 + tp_reduce(ffn_forward(normed_f, first_all, steps))

    groups = H // KVH
    score_scale = HD ** (-0.5)
    qgain_f = query_gain.astype(F32)
    kgain_f = key_gain.astype(F32)

    def qk_maps(query_in, key_in, gain_q, gain_k):
        return (
            rotate(norm_rows(query_in, gain_q), cosine, sine),
            rotate(norm_rows(key_in, gain_k), cosine, sine),
        )

    attend_in = jnp.concatenate(tp_gather(norm_rows(stream2, gain_b).astype(BF16)))
    proj_b = times(attend_in, project_b).reshape(row_count, -1, groups + 2, HD)
    kv_heads = proj_b.shape[1]
    query_raw = proj_b[:, :, :groups]
    key_raw = proj_b[:, :, groups]
    query_f, key_f = qk_maps(query_raw, key_raw, qgain_f, kgain_f)
    query_b = query_f.astype(BF16)
    key_value = jnp.concatenate(
        [
            key_f.astype(BF16).reshape(row_count, -1),
            proj_b[:, :, groups + 1].astype(BF16).reshape(row_count, -1),
        ],
        axis=1,
    )
    key_value_z = swap_ctx(key_value, 2)
    key_value_core = swap_core(jnp.concatenate([key_value, key_value_z]))
    key_value_all = jnp.concatenate(
        [key_value, key_value_core[:row_count], key_value_z, key_value_core[row_count:]]
    )
    key_all = key_value_all[:, : kv_heads * HD].reshape(-1, kv_heads, HD)
    value_all = key_value_all[:, kv_heads * HD :].reshape(-1, kv_heads, HD)
    scores = (
        jnp.einsum("tkgd,nkd->kgtn", query_b, key_all, preferred_element_type=F32) * score_scale
    )
    masked = jnp.where(allowed, scores, NEGATIVE)
    row_top = jnp.max(masked, axis=-1, keepdims=True)
    exponent = jnp.exp(masked - row_top)
    row_total = jnp.sum(exponent, axis=-1, keepdims=True)
    softmax_rows = exponent / row_total
    log_total = row_top + jnp.log(row_total)
    attended = (
        jnp.einsum(
            "kgtn,nkd->tkgd", softmax_rows.astype(BF16), value_all, preferred_element_type=F32
        )
        .astype(BF16)
        .reshape(row_count, -1)
    )
    stream3 = stream2 + tp_reduce(tp_chunks(times_t(attended, output_b_t)))

    normed_s = tp_gather(norm_rows(stream3, gain_s).astype(BF16))
    d_chunks, out_chunks, keep, side = ffn_backward(
        core_ref, normed_s, back_s_chunks, second_all, steps, True
    )
    unused, pullback = jax.vjp(norm_rows, stream3, gain_s)
    d_stream, gain_s_grad = pullback(tp_reduce(d_chunks))
    d_stream3 = upstream + d_stream
    out_others = [shift_tp(out_chunks[k], -k) for k in range(1, members)]
    side_other = swap_core(side)
    ffn_lefts = [(side, 0), (side_other, 0), (side, 1), (side_other, 1)]
    ffn_cols = steps * block
    side_start = 2 * width // block
    partial = gradient(
        ffn_lefts, keep, side_other, side_start, block, steps, padded, width, ffn_cols, 0, None
    )

    back_b = tp_gather(d_stream3.astype(BF16))
    back_b, partial = lax.optimization_barrier((back_b, partial))
    second_grads = share_rows(sum_chips(partial))
    back_b = jnp.concatenate(back_b)
    back_b_other = swap_core(back_b)
    attend_in_other = swap_core(attend_in)
    d_attended_b = times(back_b, output_b_t).astype(BF16).reshape(row_count, -1, HD)
    d_query, d_keys, d_values = attend_backward(
        query_b.reshape(row_count, -1, HD).transpose(1, 0, 2),
        d_attended_b.transpose(1, 0, 2),
        key_all.transpose(1, 0, 2),
        value_all.transpose(1, 0, 2),
        log_total.reshape(-1, 1, row_count),
        jnp.stack([segment, places]),
        jnp.stack([key_segment, key_places], axis=1),
        score_scale,
    )
    d_query = d_query.transpose(1, 0, 2).reshape(row_count, kv_heads, groups, HD)
    d_key_value = jnp.concatenate([d_keys, d_values]).transpose(1, 0, 2)
    d_key_value = d_key_value.reshape(-1, 2 * kv_heads * HD)
    d_slots = d_key_value.reshape(contexts, row_count, -1)
    d_others = jnp.concatenate([d_slots[1], d_slots[3]]).astype(BF16)
    d_others = swap_core(d_others).astype(F32)
    d_far = (d_slots[2] + d_others[row_count:]).astype(BF16)
    d_local = d_slots[0] + d_others[:row_count] + swap_ctx(d_far, 2).astype(F32)
    d_key_local = d_local[:, : kv_heads * HD].reshape(row_count, kv_heads, HD)
    d_value_local = d_local[:, kv_heads * HD :].reshape(row_count, kv_heads, HD)
    unused, pullback = jax.vjp(qk_maps, query_raw, key_raw, qgain_f, kgain_f)
    d_query_raw, d_key_raw, qgain_grad, kgain_grad = pullback((d_query, d_key_local))
    d_proj_b = (
        jnp.concatenate([d_query_raw, d_key_raw[:, :, None], d_value_local[:, :, None]], axis=2)
        .astype(BF16)
        .reshape(row_count, -1)
    )
    d_attend_in = tp_reduce(tp_chunks(times_t(d_proj_b, project_b)))
    unused, pullback = jax.vjp(norm_rows, stream2, gain_b)
    d_norm_b, gain_b_grad = pullback(d_attend_in)
    d_stream2 = d_stream3 + d_norm_b
    keep, send = halves(d_proj_b, attended)
    first_core = core == 0
    attend_cols = keep.shape[1]
    small_tile = 2 * (heads_width + attend_project.shape[1]) // 16
    third = gradient(
        [
            (attend_in, 0),
            (attend_in_other, 0),
            (jnp.where(first_core, attend_in, back_b), 0),
            (jnp.where(first_core, attend_in_other, back_b_other), 0),
        ],
        keep,
        swap_core(send),
        0,
        small_tile,
        attend_cols // small_tile,
        attend_project.shape[1] - attend_cols,
        width,
        ffn_cols + attend_cols,
        ffn_cols // small_tile,
        None,
    )

    back_f = tp_gather(d_stream2.astype(BF16))
    back_f, third = lax.optimization_barrier((back_f, third))
    left_x, left_b = jnp.concatenate(normed_f), jnp.concatenate(back_f)
    left_others = [swap_core(left_x), swap_core(left_b)]
    d_chunks, unused, keep, side = ffn_backward(
        core_ref, normed_f, back_f, first_all, steps, False
    )
    d_chunks, out_others, left_others, side_other = lax.optimization_barrier(
        (d_chunks, out_others, left_others, swap_core(side))
    )
    ffn_lefts = [(left_x, 0), (left_others[0], 0), (left_b, 0), (left_others[1], 0)]
    stream4 = stream3 + out_chunks[0]
    for part in out_others:
        stream4 = stream4 + part.astype(F32)
    partial = gradient(
        ffn_lefts,
        keep,
        side_other,
        0,
        block,
        steps,
        padded,
        width,
        ffn_cols + attend_cols,
        0,
        third,
    )

    d_normed, partial = lax.optimization_barrier((tp_reduce(d_chunks), partial))
    unused, pullback = jax.vjp(norm_rows, stream1, gain_f)
    d_stream, gain_f_grad = pullback(d_normed)
    d_stream1 = d_stream2 + d_stream

    back_a = tp_gather(d_stream1.astype(BF16))
    first_sums = sum_chips(partial)
    back_a = arrange(to_dealt, jnp.concatenate(back_a))
    back_a_other = swap_core(back_a)
    d_gated = times(back_a, output_a_t)
    d_cgate = d_gated * conv_out
    d_conv = d_gated * proj_c_part
    unused, pullback = jax.vjp(
        lambda ext_rows, kernel_in: shortconv(ext_rows, kernel_in, halo_segment),
        extended,
        kernel_local,
    )
    d_extended, kernel_grad = pullback(d_conv)
    returned = from_behind(d_extended[:halo], -1)
    d_product = d_extended[halo:] + jnp.concatenate(
        [jnp.zeros((row_count - halo, channels), F32), returned]
    )
    d_proj_a = jnp.concatenate(
        [
            d_product * proj_x_part[halo_pad:],
            d_cgate,
            d_product * proj_b_part[halo_pad:],
        ],
        axis=1,
    ).astype(BF16)
    d_chunks = tp_chunks(times_t(arrange(to_gathered, d_proj_a), project_a))
    keep, send = halves(d_proj_a, gated_rows)
    mixer_cols = keep.shape[1]
    partial = gradient(
        [
            (mixer_in, 0),
            (mixer_in_other, 0),
            (jnp.where(first_core, mixer_in, back_a), 0),
            (jnp.where(first_core, mixer_in_other, back_a_other), 0),
        ],
        keep,
        swap_core(send),
        0,
        mixer_cols,
        1,
        3 * channels - mixer_cols,
        width,
        mixer_cols,
        0,
        None,
    )
    kernel_cols = kernel_taps * channels
    gain_start = kernel_cols + 2 * HD
    shared = jnp.concatenate([kernel_grad.reshape(-1), qgain_grad, kgain_grad])
    early_gains = [
        grad.reshape(shards, depth) for grad in (gain_f_grad, gain_b_grad, gain_s_grad)
    ]
    early_row = jnp.concatenate(
        [
            jnp.broadcast_to(shared, (shards, gain_start)),
            jnp.pad(
                jnp.concatenate(early_gains, axis=1),
                ((0, 0), (0, width - gain_start - 3 * depth)),
            ),
        ],
        axis=1,
    )
    d_mixer_in, early_row = lax.optimization_barrier((tp_reduce(d_chunks), early_row))
    unused, pullback = jax.vjp(norm_rows, stream0, gain_a)
    d_norm_a, gain_a_grad = pullback(d_mixer_in)
    d_stream0 = d_stream1 + d_norm_a

    slot_for_anchor = jnp.sum(
        jnp.where(
            my_anchor[None, :] == jnp.arange(shards)[:, None], jnp.arange(shards)[None, :], 0
        ),
        axis=1,
    )
    late_start = gain_start + 3 * depth
    late_row = jnp.pad(
        gain_a_grad.reshape(shards, depth), ((0, 0), (late_start, width - late_start - depth))
    )
    leaving = jnp.concatenate(
        [d_stream0.astype(BF16), stream4.astype(BF16), (early_row + late_row).astype(BF16)]
    )
    line = jnp.arange(shards * piece_rows)
    target, item = line // piece_rows, line % piece_rows
    source = jnp.where(
        item < 2 * part_rows,
        item // part_rows * chunk
        + jnp.repeat(slot_for_anchor, piece_rows) * part_rows
        + item % part_rows,
        jnp.where(item == 2 * part_rows, 2 * chunk + target, -1),
    )
    to_leaving = (source[:, None] == jnp.arange(leaving.shape[0])[None, :]).astype(BF16)
    leaving = arrange(to_leaving, leaving)
    home = lax.all_to_all(
        leaving.reshape(shards, piece_rows, width),
        TOKEN_AXES,
        split_axis=0,
        concat_axis=0,
        tiled=True,
    )
    second_grads = ffn_gradients(*second_grads, steps, hidden)
    home, partial, second_grads = lax.optimization_barrier((home, partial, second_grads))
    place = jnp.arange(2 * chunk + 8)
    small_line = (place == 2 * chunk) | (place == 2 * chunk + 1)
    wanted = (
        place % chunk // part_rows * piece_rows
        + place // chunk * part_rows
        + place % part_rows
    )
    to_payload = jnp.where(
        (place < 2 * chunk)[:, None],
        wanted[:, None] == line[None, :],
        small_line[:, None] & (item == 2 * part_rows)[None, :],
    ).astype(BF16)
    payload = times(to_payload, home.reshape(shards * piece_rows, width))
    rounded = payload.astype(BF16).astype(F32)
    payload = jnp.where((place == 2 * chunk + 1)[:, None], payload - rounded, payload)
    last = tp_gather(payload.astype(BF16))
    mixer_home = lax.all_to_all(
        partial.reshape(shards, depth, mixer_cols),
        TOKEN_AXES,
        split_axis=0,
        concat_axis=0,
        tiled=True,
    )
    mixer_home = mixer_home.reshape(shards // CORES, CORES, depth, mixer_cols)
    mixer_grads = jnp.sum(mixer_home.astype(F32), axis=0)
    mixer_grads = jnp.concatenate([mixer_grads[0], mixer_grads[1]], axis=1)
    home_rows = (
        jnp.repeat(jnp.tile(send_piece, members), part_rows) * piece_rows
        + member_of * part_rows
        + gathered % part_rows
    )
    to_arrival = (home_rows[None, :] == gathered[:, None]).astype(BF16)
    input_gradient = arrange(to_arrival, jnp.concatenate([slot[:chunk] for slot in last]))
    layer_out = arrange(to_arrival, jnp.concatenate([slot[chunk : 2 * chunk] for slot in last]))
    first_sums, layer_out, input_gradient, mixer_grads = lax.optimization_barrier(
        (first_sums, layer_out, input_gradient, mixer_grads)
    )
    low, high = share_rows(first_sums)
    first_grads = ffn_gradients(low[:, :ffn_cols], high[:, :ffn_cols], steps, hidden)
    attend_grads = jnp.concatenate([low[:, ffn_cols:], high[:, ffn_cols:]], axis=1)
    smalls = [
        slot[2 * chunk].astype(F32) + slot[2 * chunk + 1].astype(F32) for slot in last
    ]
    totals = sum(smalls)
    kernel_rows = jnp.stack([small[:kernel_cols].reshape(kernel_taps, channels) for small in smalls])
    kernel_total = jnp.concatenate(
        [
            lax.dynamic_index_in_dim(kernel_rows, (own - member) % members, 0, keepdims=False)
            for member in range(members)
        ],
        axis=1,
    )
    qgain_total = totals[kernel_cols : kernel_cols + HD]
    kgain_total = totals[kernel_cols + HD : kernel_cols + 2 * HD]
    gain_totals = totals[gain_start : gain_start + 4 * depth].reshape(4, depth)

    gateup_s_grad, down_s_grad = second_grads
    gateup_f_grad, down_f_grad = first_grads
    proj_cols = attend_project.shape[1]
    return (
        layer_out,
        input_gradient,
        gain_totals[3],
        mixer_grads[:, : 3 * channels].reshape(depth, 3, channels),
        kernel_total,
        mixer_grads[:, 3 * channels :].T,
        gain_totals[0],
        gateup_f_grad,
        down_f_grad,
        gain_totals[1],
        attend_grads[:, :proj_cols],
        qgain_total,
        kgain_total,
        attend_grads[:, proj_cols:].T,
        gain_totals[2],
        gateup_s_grad,
        down_s_grad,
    )


def solution(mesh):
    names = TOKEN_AXES + ("tp",)
    rings = mesh.shape["fsdp"] // 2, 2, mesh.shape["ctx"] // 2, 2, mesh.shape["tp"]
    tokens = P(TOKEN_AXES, None)
    rows = P(TOKEN_AXES)
    three = P(TOKEN_AXES, None, "tp")
    two = P(TOKEN_AXES, "tp")
    turned = P("tp", TOKEN_AXES)
    return jax.shard_map(
        body,
        mesh=Mesh(mesh.devices.reshape(rings), names),
        in_specs=(
            tokens, tokens, P(), P(),
            rows, three, P(), turned,
            rows, three, turned,
            rows, two, P(), P(), turned,
            rows, three, turned,
        ),
        out_specs=(
            tokens, tokens,
            rows, three, P(), turned,
            rows, three, turned,
            rows, two, P(), P(), turned,
            rows, three, turned,
        ),
        check_vma=False,
    )
```

```python
import functools

import jax
import jax.numpy as jnp
from jax import lax
from jax.experimental import pallas as pl
from jax.experimental.pallas import tpu as pltpu
from jax.sharding import Mesh, PartitionSpec as P

H = 24
KVH = 8
HD = 64

EPSILON = 1e-05
ROPE_BASE = 1000000.0
NEGATIVE = -1e30

CHIP_AXES = ("x", "z_hi", "z_lo")
TOKEN_AXES = CHIP_AXES + ("core",)
GROUP_AXES = ("x", "z_hi")
CTX_AXES = ("z_lo", "core")
Z_AXES = ("z_hi", "z_lo")
CORES = 2
TILE = 256
MIB = 1024 * 1024
F32 = jnp.float32
BF16 = jnp.bfloat16


def norm_rows(values, scales):
    return values * lax.rsqrt(jnp.mean(values * values, axis=-1, keepdims=True) + EPSILON) * scales


def rotate(values, cosine, sine):
    half_dim = values.shape[-1] // 2
    shape_out = (values.shape[0],) + (1,) * (values.ndim - 2) + (half_dim,)
    cosine = cosine.reshape(shape_out)
    sine = sine.reshape(shape_out)
    first_half = values[..., :half_dim]
    second_half = values[..., half_dim:]
    return jnp.concatenate(
        [
            first_half * cosine - second_half * sine,
            second_half * cosine + first_half * sine,
        ],
        axis=-1,
    )


def locate(lengths, positions):
    seq_ends = jnp.cumsum(lengths)
    segment = jnp.sum((positions[:, None] >= seq_ends[None, :]).astype(jnp.int32), axis=1)
    starts = seq_ends - lengths
    first_row = jnp.sum(
        jnp.where(segment[:, None] == jnp.arange(lengths.shape[0])[None, :], starts[None, :], 0),
        axis=1,
    )
    return (segment, positions - first_row)


def shortconv(extended, kernel_in, segment):
    kernel_taps = kernel_in.shape[0]
    out_rows = extended.shape[0] - kernel_taps + 1
    result = kernel_in[0] * extended[kernel_taps - 1 :]
    for t in range(1, kernel_taps):
        earlier = extended[kernel_taps - 1 - t : kernel_taps - 1 - t + out_rows]
        same_seq = (
            segment[kernel_taps - 1 - t : kernel_taps - 1 - t + out_rows]
            == segment[kernel_taps - 1 :]
        ).astype(F32)[:, None]
        result = result + kernel_in[t] * earlier * same_seq
    return result


def from_behind(block, distance):
    devices = range(lax.axis_size(CTX_AXES))
    route = [(i - distance, i) for i in devices if i - distance in devices]
    return lax.ppermute(block, CTX_AXES, route)


def swap_ctx(block, mask):
    return lax.ppermute(block, CTX_AXES, [(i, i ^ mask) for i in range(lax.axis_size(CTX_AXES))])


def swap_core(block):
    return lax.ppermute(block, "core", [(0, 1), (1, 0)])


def shift_tp(block, distance):
    members = lax.axis_size("tp")
    return lax.ppermute(block, "tp", [(i, (i + distance) % members) for i in range(members)])


def tp_gather(shard):
    return [shard] + [shift_tp(shard, k) for k in range(1, lax.axis_size("tp"))]


def tp_chunks(partial):
    rows = partial.shape[0] // lax.axis_size("tp")
    return [
        partial[k * rows : (k + 1) * rows].astype(F32 if k == 0 else BF16)
        for k in range(lax.axis_size("tp"))
    ]


def tp_reduce(chunks):
    total = chunks[0]
    for k in range(1, len(chunks)):
        total = total + shift_tp(chunks[k], -k).astype(F32)
    return total


def arrange(order, rows):
    return times(order, rows).astype(BF16)


def times(left, right):
    return lax.dot_general(left, right, (((1,), (0,)), ((), ())), preferred_element_type=F32)


def times_t(left, right):
    return lax.dot_general(left, right, (((1,), (1,)), ((), ())), preferred_element_type=F32)


def times_rows(left, right):
    return lax.dot_general(left, right, (((0,), (0,)), ((), ())), preferred_element_type=F32)


def assemble(chunk_refs, target):
    rows = chunk_refs[0].shape[0]
    for k, ref in enumerate(chunk_refs):
        target[k * rows : (k + 1) * rows, :] = ref[...]


def spread(total, chunk_refs):
    rows = chunk_refs[0].shape[0]
    for k, ref in enumerate(chunk_refs):
        ref[...] = total[k * rows : (k + 1) * rows, :].astype(ref.dtype)


def whole(shape):
    return pl.BlockSpec(shape, lambda *_: (0,) * len(shape))


def weight_specs(depth, steps):
    return [
        pl.BlockSpec((depth, 2 * TILE), lambda j: (0, j)),
        pl.BlockSpec((depth, TILE), lambda j: (0, 2 * steps + j)),
    ]


def chunk_shapes(count, rows, width):
    return [jax.ShapeDtypeStruct((rows, width), F32 if k == 0 else BF16) for k in range(count)]


def ffn_forward_kernel(count, *refs):
    x_refs, (gu_ref, dn_ref), outs = refs[:count], refs[count : count + 2], refs[count + 2 : -2]
    x_all, total = refs[-2:]
    step = pl.program_id(0)

    @pl.when(step == 0)
    def _():
        assemble(x_refs, x_all)
        total[...] = jnp.zeros_like(total)

    both = times(x_all[...], gu_ref[...])
    gate, up = both[:, :TILE], both[:, TILE:]
    active = (gate * jax.nn.sigmoid(gate) * up).astype(BF16)
    total[...] += times_t(active, dn_ref[...])

    @pl.when(step == pl.num_programs(0) - 1)
    def _():
        spread(total[...], outs)


def ffn_forward(chunks, pack, steps):
    count, (rows, width) = len(chunks), chunks[0].shape
    tokens = count * rows
    return pl.pallas_call(
        functools.partial(ffn_forward_kernel, count),
        grid=(steps,),
        in_specs=[whole((rows, width))] * count + weight_specs(width, steps),
        out_specs=[whole((rows, width))] * count,
        out_shape=chunk_shapes(count, rows, width),
        scratch_shapes=[pltpu.VMEM((tokens, width), BF16), pltpu.VMEM((tokens, width), F32)],
        compiler_params=pltpu.CompilerParams(vmem_limit_bytes=20 * MIB),
        cost_estimate=pl.CostEstimate(
            flops=2 * tokens * width * 3 * TILE * steps,
            bytes_accessed=2 * width * 3 * TILE * steps,
            transcendentals=tokens * TILE * steps,
        ),
        name="ffn_forward",
    )(*chunks, pack, pack)


def ffn_backward_kernel(count, forward, core_ref, *refs):
    x_refs, b_refs = refs[:count], refs[count : 2 * count]
    gu_ref, dn_ref = refs[2 * count : 2 * count + 2]
    place = 2 * count + 2
    back_outs = refs[place : place + count]
    place += count
    if forward:
        outs = refs[place : place + count]
        place += count
    keep_ref, side_ref = refs[place : place + 2]
    scratch = refs[place + 2 :]
    x_all, b_all, d_total = scratch[:3]
    step = pl.program_id(0)
    width = x_all.shape[1]

    @pl.when(step == 0)
    def _():
        assemble(x_refs, x_all)
        assemble(b_refs, b_all)
        if forward:
            side_ref[:, :width] = x_all[...]
            side_ref[:, width : 2 * width] = b_all[...]
        d_total[...] = jnp.zeros_like(d_total)
        if forward:
            scratch[3][...] = jnp.zeros_like(scratch[3])

    both = times(x_all[...], gu_ref[...])
    gate, up = both[:, :TILE], both[:, TILE:]
    d_active = times(b_all[...], dn_ref[...])
    sigmoid = jax.nn.sigmoid(gate)
    silu = gate * sigmoid
    active = (silu * up).astype(BF16)
    if forward:
        scratch[3][...] += times_t(active, dn_ref[...])
    d_gate = (d_active * up * (sigmoid * (1.0 + gate * (1.0 - sigmoid)))).astype(BF16)
    d_up = (d_active * silu).astype(BF16)
    d_total[...] += times_t(jnp.concatenate([d_gate, d_up], axis=1), gu_ref[...])
    first = core_ref[0] == 0
    half = TILE // 2
    low, high = active[:, :half], active[:, half:]
    offset = 2 * width if forward else 0
    wide = pl.multiple_of(step * TILE, TILE)
    narrow = pl.multiple_of(pl.num_programs(0) * TILE + step * half, half)
    side_wide = pl.multiple_of(offset + wide, TILE)
    side_narrow = pl.multiple_of(offset + narrow, half)

    @pl.when(first)
    def _():
        keep_ref[:, pl.ds(wide, TILE)] = d_gate
        keep_ref[:, pl.ds(narrow, half)] = low
        side_ref[:, pl.ds(side_wide, TILE)] = d_up
        side_ref[:, pl.ds(side_narrow, half)] = high

    @pl.when(jnp.logical_not(first))
    def _():
        keep_ref[:, pl.ds(wide, TILE)] = d_up
        keep_ref[:, pl.ds(narrow, half)] = high
        side_ref[:, pl.ds(side_wide, TILE)] = d_gate
        side_ref[:, pl.ds(side_narrow, half)] = low

    @pl.when(step == pl.num_programs(0) - 1)
    def _():
        spread(d_total[...], back_outs)
        if forward:
            spread(scratch[3][...], outs)


def ffn_backward(core, chunks, back_chunks, pack, steps, forward):
    count, (rows, width) = len(chunks), chunks[0].shape
    tokens = count * rows
    block = TILE + TILE // 2
    ways = 2 if forward else 1
    side_width = (2 * width if forward else 0) + steps * block
    results = pl.pallas_call(
        functools.partial(ffn_backward_kernel, count, forward),
        grid=(steps,),
        in_specs=[pl.BlockSpec(memory_space=pltpu.SMEM)]
        + [whole((rows, width))] * (2 * count)
        + weight_specs(width, steps),
        out_specs=[whole((rows, width))] * (ways * count)
        + [whole((tokens, steps * block)), whole((tokens, side_width))],
        out_shape=chunk_shapes(count, rows, width) * ways
        + [
            jax.ShapeDtypeStruct((tokens, steps * block), BF16),
            jax.ShapeDtypeStruct((tokens, side_width), BF16),
        ],
        scratch_shapes=[pltpu.VMEM((tokens, width), BF16)] * 2
        + [pltpu.VMEM((tokens, width), F32)] * ways,
        compiler_params=pltpu.CompilerParams(vmem_limit_bytes=(36 if forward else 28) * MIB),
        cost_estimate=pl.CostEstimate(
            flops=2 * tokens * width * (4 + ways) * TILE * steps,
            bytes_accessed=2 * width * 3 * TILE * steps + 4 * tokens * side_width,
            transcendentals=tokens * TILE * steps,
        ),
        name="ffn_both" if forward else "ffn_backward",
    )(core, *chunks, *back_chunks, pack, pack)
    return results[:count], results[count : ways * count], results[-2], results[-1]


def gradient_kernel(edge, cut, *refs):
    one_own, one_other, two_own, two_other, own_ref, other_ref = refs[:6]
    out_ref = refs[-1]
    step = pl.program_id(0)

    def product(own_left, other_left, columns):
        total = times_rows(own_left[...], own_ref[:, columns])
        total += times_rows(other_left[...], other_ref[:, columns])
        out_ref[:, columns] = total.astype(BF16)

    @pl.when(step < edge)
    def _():
        product(one_own, one_other, slice(None))

    @pl.when(step > edge if cut else step >= edge)
    def _():
        product(two_own, two_other, slice(None))

    if cut:

        @pl.when(step == edge)
        def _():
            product(one_own, one_other, slice(0, cut))
            product(two_own, two_other, slice(cut, None))


def gradient(lefts, own, other, other_start, block, steps, columns, width, out_width, out_start, target):
    tokens = own.shape[0]
    edge, cut = divmod(columns, block)

    def left_spec(index):
        return pl.BlockSpec((tokens, width), lambda j: (0, index))

    in_specs = [left_spec(index) for unused, index in lefts] + [
        pl.BlockSpec((tokens, block), lambda j: (0, j)),
        pl.BlockSpec((tokens, block), lambda j: (0, other_start + j)),
    ]
    operands = [array for array, unused in lefts] + [own, other]
    aliases = {}
    if target is not None:
        in_specs.append(pl.BlockSpec(memory_space=pl.ANY))
        operands.append(target)
        aliases = {len(operands) - 1: 0}
    return pl.pallas_call(
        functools.partial(gradient_kernel, edge, cut),
        grid=(steps,),
        in_specs=in_specs,
        out_specs=pl.BlockSpec((width, block), lambda j: (0, out_start + j)),
        out_shape=jax.ShapeDtypeStruct((width, out_width), BF16),
        input_output_aliases=aliases,
        compiler_params=pltpu.CompilerParams(vmem_limit_bytes=28 * MIB),
        cost_estimate=pl.CostEstimate(
            flops=4 * tokens * width * block * steps,
            bytes_accessed=2 * width * block * steps,
            transcendentals=0,
        ),
        name="weight_gradient",
    )(*operands)


def attend_backward_kernel(
    scale, kv_heads, size, q_ref, do_ref, kv_ref, raw_ref, cos_ref, sin_ref, gain_ref, place_ref, key_ref,
    dq_ref, dkv_ref, dgain_ref,
):
    groups = q_ref.shape[1] // (kv_heads * size)
    half = size // 2
    cosine, sine, gain = cos_ref[...], sin_ref[...], gain_ref[...]
    allowed = key_ref[:, 0:1] == place_ref[0:1, :]
    allowed = allowed & (key_ref[:, 1:2] <= place_ref[1:2, :])
    d_gain = jnp.zeros_like(gain)
    for group in range(kv_heads):
        columns = slice(group * size, (group + 1) * size)
        value_columns = slice((kv_heads + group) * size, (kv_heads + group + 1) * size)
        key, value = kv_ref[:, columns], kv_ref[:, value_columns]
        d_key = d_value = None
        for member in range(groups):
            head = group * groups + member
            head_columns = slice(head * size, (head + 1) * size)
            query, d_out = q_ref[:, head_columns], do_ref[:, head_columns]
            scores = jnp.where(allowed, times_t(key, query) * scale, NEGATIVE)
            probs = jnp.exp(scores - jnp.max(scores, axis=0, keepdims=True))
            probs = probs / jnp.sum(probs, axis=0, keepdims=True)
            d_probs = times_t(value, d_out)
            inner = jnp.sum(probs * d_probs, axis=0, keepdims=True)
            d_scores = (probs * (d_probs - inner)).astype(BF16)
            part_value = times(probs.astype(BF16), d_out)
            part_key = times(d_scores, query) * scale
            d_value = part_value if d_value is None else d_value + part_value
            d_key = part_key if d_key is None else d_key + part_key
            d_query = (times_rows(key, d_scores) * scale).T
            first, second = d_query[:, :half], d_query[:, half:]
            d_query = jnp.concatenate(
                [first * cosine + second * sine, second * cosine - first * sine], axis=1
            )
            start = (group * (groups + 2) + member) * size
            raw = raw_ref[:, start : start + size]
            spread_of = lax.rsqrt(jnp.mean(raw * raw, axis=1, keepdims=True) + EPSILON)
            d_gain += jnp.sum(d_query * raw * spread_of, axis=0, keepdims=True)
            scaled = d_query * gain
            d_raw = spread_of * scaled - raw * (
                spread_of * spread_of * spread_of * jnp.mean(scaled * raw, axis=1, keepdims=True)
            )
            dq_ref[:, head_columns] = d_raw.astype(BF16)
        dkv_ref[:, columns] = d_key
        dkv_ref[:, value_columns] = d_value
    dgain_ref[...] = d_gain


def attend_backward(query, d_out, key_value, raw, cosine, sine, gain, place, key_place, kv_heads, scale):
    rows, width = query.shape
    keys = key_value.shape[0]
    size = key_value.shape[1] // (2 * kv_heads)
    operands = (query, d_out, key_value, raw, cosine, sine, gain, place, key_place)
    return pl.pallas_call(
        functools.partial(attend_backward_kernel, scale, kv_heads, size),
        out_shape=[
            jax.ShapeDtypeStruct((rows, width), BF16),
            jax.ShapeDtypeStruct(key_value.shape, F32),
            jax.ShapeDtypeStruct((1, size), F32),
        ],
        compiler_params=pltpu.CompilerParams(vmem_limit_bytes=36 * MIB),
        cost_estimate=pl.CostEstimate(
            flops=10 * rows * keys * width,
            bytes_accessed=4 * rows * width * 2 + 12 * keys * kv_heads * size,
            transcendentals=rows * keys * width // size,
        ),
        name="attend_backward",
    )(*operands)


def share_rows(summed):
    core = lax.axis_index("core")
    rows = summed.shape[0] // 2
    mine = lax.dynamic_slice_in_dim(summed, core * rows, rows, 0)
    other = swap_core(lax.dynamic_slice_in_dim(summed, (1 - core) * rows, rows, 0))
    first = core == 0
    return jnp.where(first, mine, other).astype(F32), jnp.where(first, other, mine).astype(F32)


def sum_chips(partial):
    return lax.psum_scatter(partial, CHIP_AXES, scatter_dimension=0, tiled=True)


def gather_pack(pack):
    chips = lax.axis_size(CHIP_AXES)
    core = lax.axis_index("core")
    plane = lax.all_to_all(
        jnp.broadcast_to(pack, (chips,) + pack.shape),
        CHIP_AXES,
        split_axis=0,
        concat_axis=0,
        tiled=True,
    )
    other = swap_core(plane)
    both = jnp.zeros((chips, CORES) + pack.shape, BF16)
    both = lax.dynamic_update_slice(both, plane[:, None], (0, core, 0, 0))
    both = lax.dynamic_update_slice(both, other[:, None], (0, 1 - core, 0, 0))
    return both.reshape(-1, pack.shape[1])


def ffn_gradients(low, high, steps, hidden):
    depth = low.shape[0]
    padded = steps * TILE
    gateup = jnp.stack([low[:, :hidden], high[:, :hidden]], axis=1)
    down = jnp.concatenate(
        [part[:, padded:].reshape(depth, steps, TILE // 2) for part in (low, high)], axis=2
    )
    return gateup, down.reshape(depth, padded)[:, :hidden].T


def halves(proj, out):
    first = lax.axis_index("core") == 0
    half = (proj.shape[1] + out.shape[1]) // 2
    late = jnp.concatenate([proj[:, half:], out], axis=1)
    early = proj[:, :half]
    return jnp.where(first, early, late), jnp.where(first, late, early)


def body(
    hidden_in,
    cotangent,
    seq_lengths,
    deal_order,
    mixer_gain,
    mixer_project,
    mixer_kernel,
    mixer_output,
    first_gain,
    first_gateup,
    first_down,
    attend_gain,
    attend_project,
    query_gain,
    key_gain,
    attend_output,
    second_gain,
    second_gateup,
    second_down,
):
    shards = lax.axis_size(TOKEN_AXES)
    contexts = lax.axis_size(CTX_AXES)
    members = lax.axis_size("tp")
    row_count, width = hidden_in.shape
    piece_rows = row_count // shards
    part_rows = piece_rows // members
    chunk = row_count // members
    device = lax.axis_index(TOKEN_AXES)
    own = lax.axis_index("tp")
    core = lax.axis_index("core")
    core_ref = core.reshape(1).astype(jnp.int32)
    depth = mixer_gain.shape[0]
    channels = mixer_output.shape[0]
    hidden = first_down.shape[0]
    heads_width = attend_output.shape[0]
    steps = -(-hidden // TILE)
    padded = steps * TILE
    ffn_width = 3 * padded
    block = TILE + TILE // 2

    def pack_ffn(gateup, down):
        wide = jnp.pad(gateup, ((0, 0), (0, 0), (0, padded - hidden)))
        wide = wide.reshape(depth, 2, steps, TILE).transpose(0, 2, 1, 3).reshape(depth, -1)
        return [wide, jnp.pad(down.T, ((0, 0), (0, padded - hidden)))]

    mixer_pack = jnp.concatenate([mixer_project.reshape(depth, -1), mixer_output.T], axis=1)
    first_pack = jnp.concatenate(
        pack_ffn(first_gateup, first_down) + [attend_project, attend_output.T], axis=1
    )
    second_pack = jnp.concatenate(pack_ffn(second_gateup, second_down), axis=1)
    piece_table = deal_order.reshape(shards, shards, piece_rows)[:, :, 0]
    anchor = piece_table // row_count
    anchor_piece = piece_table % row_count // piece_rows
    send_piece = jnp.sum(jnp.where(anchor == device, anchor_piece, 0), axis=1)
    my_anchor = lax.dynamic_index_in_dim(anchor, device, 0, keepdims=False)
    gains_row = jnp.concatenate(
        [mixer_gain, first_gain, attend_gain, second_gain, jnp.zeros((width - 4 * depth,), BF16)]
    )

    def my_part(rows):
        parts = rows.reshape(shards, members, part_rows, width)
        return lax.dynamic_index_in_dim(parts, own, 1, keepdims=False)[send_piece]

    outgoing = jnp.concatenate(
        [
            my_part(hidden_in),
            my_part(cotangent),
            jnp.broadcast_to(gains_row, (shards, 1, width)),
        ],
        axis=1,
    )
    arrived = lax.all_to_all(outgoing, TOKEN_AXES, split_axis=0, concat_axis=0, tiled=True)
    arrived, mixer_pack, first_pack = lax.optimization_barrier((arrived, mixer_pack, first_pack))
    first_all = lax.all_gather(first_pack, TOKEN_AXES, axis=0, tiled=True)
    second_all = lax.all_gather(second_pack, TOKEN_AXES, axis=0, tiled=True)
    project_b = first_all[:, ffn_width : ffn_width + attend_project.shape[1]]
    output_b_t = first_all[:, ffn_width + attend_project.shape[1] :]
    mixer_all = gather_pack(mixer_pack)
    project_a = mixer_all[:, : 3 * channels]
    output_a_t = mixer_all[:, 3 * channels :]
    gains = (
        arrived[:, 2 * part_rows, : 4 * depth]
        .reshape(shards, 4, depth)
        .transpose(1, 0, 2)
        .reshape(4, width)
        .astype(F32)
    )
    gain_a, gain_f, gain_b, gain_s = gains[0], gains[1], gains[2], gains[3]
    parts = arrived[:, : 2 * part_rows][my_anchor]
    own_tokens = parts[:, :part_rows].reshape(chunk, width)
    own_back = parts[:, part_rows:].reshape(chunk, width)
    stream0 = own_tokens.astype(F32)
    upstream = own_back.astype(F32)
    both = tp_gather(jnp.concatenate([own_tokens, own_back]))
    back_s_chunks = [slot[chunk:] for slot in both]

    gathered = jnp.arange(row_count)
    member_of = (own - gathered // chunk) % members
    offsets = (
        gathered % chunk // part_rows * piece_rows + member_of * part_rows + gathered % part_rows
    )
    to_gathered = (offsets[:, None] == gathered[None, :]).astype(BF16)
    to_dealt = (offsets[None, :] == gathered[:, None]).astype(BF16)
    tokens = times(to_dealt, jnp.concatenate([slot[:chunk] for slot in both]))

    kernel_taps = mixer_kernel.shape[0]
    halo = kernel_taps - 1
    local_rows = device * row_count + jnp.arange(row_count)
    halo_segment, unused = locate(
        seq_lengths, local_rows[0] - halo + jnp.arange(row_count + halo)
    )
    segment, places = locate(seq_lengths, device * row_count + offsets)
    ctx = lax.axis_index(CTX_AXES)
    group_rows = jnp.concatenate(
        [
            (lax.axis_index(GROUP_AXES) * contexts + (ctx ^ mask)) * row_count + offsets
            for mask in range(contexts)
        ]
    )
    key_segment, key_places = locate(seq_lengths, group_rows)
    allowed = (segment[:, None] == key_segment[None, :]) & (key_places[None, :] <= places[:, None])
    half_dim = HD // 2
    frequency = ROPE_BASE ** (-(jnp.arange(half_dim).astype(F32) * 2.0 / HD))
    angles = places.astype(F32)[:, None] * frequency[None, :]
    cosine = jnp.cos(angles)
    sine = jnp.sin(angles)

    kernel_local = lax.dynamic_slice_in_dim(mixer_kernel, own * channels, channels, 1).astype(F32)
    mixer_in = norm_rows(tokens, gain_a).astype(BF16)
    mixer_in_other = swap_core(mixer_in)
    halo_pad = 16
    halo_in = from_behind(mixer_in[row_count - halo_pad :], 1)
    proj_a = times(jnp.concatenate([halo_in, mixer_in]), project_a)
    proj_b_part = proj_a[:, :channels]
    proj_c_part = proj_a[halo_pad:, channels : 2 * channels]
    proj_x_part = proj_a[:, 2 * channels :]
    extended = (proj_b_part * proj_x_part)[halo_pad - halo :].astype(BF16).astype(F32)
    conv_out = shortconv(extended, kernel_local, halo_segment)
    gated_rows = (proj_c_part * conv_out).astype(BF16)
    gated_parts = arrange(to_gathered, gated_rows)
    stream1 = stream0 + tp_reduce(tp_chunks(times_t(gated_parts, output_a_t)))

    normed_f = tp_gather(norm_rows(stream1, gain_f).astype(BF16))
    stream2 = stream1 + tp_reduce(ffn_forward(normed_f, first_all, steps))

    groups = H // KVH
    score_scale = HD ** (-0.5)
    qgain_f = query_gain.astype(F32)
    kgain_f = key_gain.astype(F32)

    def qk_maps(query_in, key_in, gain_q, gain_k):
        return (
            rotate(norm_rows(query_in, gain_q), cosine, sine),
            rotate(norm_rows(key_in, gain_k), cosine, sine),
        )

    attend_in = jnp.concatenate(tp_gather(norm_rows(stream2, gain_b).astype(BF16)))
    proj_b = times(attend_in, project_b).reshape(row_count, -1, groups + 2, HD)
    kv_heads = proj_b.shape[1]
    query_raw = proj_b[:, :, :groups]
    key_raw = proj_b[:, :, groups]
    query_f, key_f = qk_maps(query_raw, key_raw, qgain_f, kgain_f)
    query_b = query_f.astype(BF16)
    key_value = jnp.concatenate(
        [
            key_f.astype(BF16).reshape(row_count, -1),
            proj_b[:, :, groups + 1].astype(BF16).reshape(row_count, -1),
        ],
        axis=1,
    )
    key_value_z = swap_ctx(key_value, 2)
    key_value_core = swap_core(jnp.concatenate([key_value, key_value_z]))
    key_value_all = jnp.concatenate(
        [key_value, key_value_core[:row_count], key_value_z, key_value_core[row_count:]]
    )
    key_all = key_value_all[:, : kv_heads * HD].reshape(-1, kv_heads, HD)
    value_all = key_value_all[:, kv_heads * HD :].reshape(-1, kv_heads, HD)
    scores = (
        jnp.einsum("tkgd,nkd->kgtn", query_b, key_all, preferred_element_type=F32) * score_scale
    )
    masked = jnp.where(allowed, scores, NEGATIVE)
    row_top = jnp.max(masked, axis=-1, keepdims=True)
    exponent = jnp.exp(masked - row_top)
    row_total = jnp.sum(exponent, axis=-1, keepdims=True)
    softmax_rows = exponent / row_total
    attended = (
        jnp.einsum(
            "kgtn,nkd->tkgd", softmax_rows.astype(BF16), value_all, preferred_element_type=F32
        )
        .astype(BF16)
        .reshape(row_count, -1)
    )
    stream3 = stream2 + tp_reduce(tp_chunks(times_t(attended, output_b_t)))

    normed_s = tp_gather(norm_rows(stream3, gain_s).astype(BF16))
    d_chunks, out_chunks, keep, side = ffn_backward(
        core_ref, normed_s, back_s_chunks, second_all, steps, True
    )
    unused, pullback = jax.vjp(norm_rows, stream3, gain_s)
    d_stream, gain_s_grad = pullback(tp_reduce(d_chunks))
    d_stream3 = upstream + d_stream
    out_others = [shift_tp(out_chunks[k], -k) for k in range(1, members)]
    side_other = swap_core(side)
    ffn_lefts = [(side, 0), (side_other, 0), (side, 1), (side_other, 1)]
    ffn_cols = steps * block
    side_start = 2 * width // block
    partial = gradient(
        ffn_lefts, keep, side_other, side_start, block, steps, padded, width, ffn_cols, 0, None
    )

    back_b = tp_gather(d_stream3.astype(BF16))
    back_b, partial = lax.optimization_barrier((back_b, partial))
    second_grads = share_rows(sum_chips(partial))
    back_b = jnp.concatenate(back_b)
    back_b_other = swap_core(back_b)
    attend_in_other = swap_core(attend_in)
    d_attended_b = times(back_b, output_b_t).astype(BF16)
    d_query_raw, d_key_value, qgain_grad = attend_backward(
        query_b.reshape(row_count, -1),
        d_attended_b,
        key_value_all,
        proj_b.reshape(row_count, -1),
        cosine,
        sine,
        qgain_f[None],
        jnp.stack([segment, places]),
        jnp.stack([key_segment, key_places], axis=1),
        kv_heads,
        score_scale,
    )
    qgain_grad = qgain_grad[0]
    d_slots = d_key_value.reshape(contexts, row_count, -1)
    d_others = jnp.concatenate([d_slots[1], d_slots[3]]).astype(BF16)
    d_others = swap_core(d_others).astype(F32)
    d_far = (d_slots[2] + d_others[row_count:]).astype(BF16)
    d_local = d_slots[0] + d_others[:row_count] + swap_ctx(d_far, 2).astype(F32)
    d_key_local = d_local[:, : kv_heads * HD].reshape(row_count, kv_heads, HD)
    d_value_local = d_local[:, kv_heads * HD :].reshape(row_count, kv_heads, HD)
    unused, pullback = jax.vjp(
        lambda key_in, gain_k: rotate(norm_rows(key_in, gain_k), cosine, sine), key_raw, kgain_f
    )
    d_key_raw, kgain_grad = pullback(d_key_local)
    d_proj_b = jnp.concatenate(
        [
            d_query_raw.reshape(row_count, kv_heads, groups, HD),
            d_key_raw[:, :, None].astype(BF16),
            d_value_local[:, :, None].astype(BF16),
        ],
        axis=2,
    ).reshape(row_count, -1)
    d_attend_in = tp_reduce(tp_chunks(times_t(d_proj_b, project_b)))
    unused, pullback = jax.vjp(norm_rows, stream2, gain_b)
    d_norm_b, gain_b_grad = pullback(d_attend_in)
    d_stream2 = d_stream3 + d_norm_b
    keep, send = halves(d_proj_b, attended)
    first_core = core == 0
    attend_cols = keep.shape[1]
    small_tile = 2 * (heads_width + attend_project.shape[1]) // 16
    third = gradient(
        [
            (attend_in, 0),
            (attend_in_other, 0),
            (jnp.where(first_core, attend_in, back_b), 0),
            (jnp.where(first_core, attend_in_other, back_b_other), 0),
        ],
        keep,
        swap_core(send),
        0,
        small_tile,
        attend_cols // small_tile,
        attend_project.shape[1] - attend_cols,
        width,
        ffn_cols + attend_cols,
        ffn_cols // small_tile,
        None,
    )

    back_f = tp_gather(d_stream2.astype(BF16))
    back_f, third = lax.optimization_barrier((back_f, third))
    left_x, left_b = jnp.concatenate(normed_f), jnp.concatenate(back_f)
    ffn_lefts = [(left_x, 0), (swap_core(left_x), 0), (left_b, 0), (swap_core(left_b), 0)]
    d_chunks, unused, keep, side = ffn_backward(
        core_ref, normed_f, back_f, first_all, steps, False
    )
    d_chunks, out_others = lax.optimization_barrier((d_chunks, out_others))
    stream4 = stream3 + out_chunks[0]
    for part in out_others:
        stream4 = stream4 + part.astype(F32)
    partial = gradient(
        ffn_lefts,
        keep,
        swap_core(side),
        0,
        block,
        steps,
        padded,
        width,
        ffn_cols + attend_cols,
        0,
        third,
    )

    unused, pullback = jax.vjp(norm_rows, stream1, gain_f)
    d_stream, gain_f_grad = pullback(tp_reduce(d_chunks))
    d_stream1 = d_stream2 + d_stream

    back_a = tp_gather(d_stream1.astype(BF16))
    back_a, partial = lax.optimization_barrier((back_a, partial))
    first_sums = sum_chips(partial)
    back_a = arrange(to_dealt, jnp.concatenate(back_a))
    back_a_other = swap_core(back_a)
    d_gated = times(back_a, output_a_t)
    d_cgate = d_gated * conv_out
    d_conv = d_gated * proj_c_part
    unused, pullback = jax.vjp(
        lambda ext_rows, kernel_in: shortconv(ext_rows, kernel_in, halo_segment),
        extended,
        kernel_local,
    )
    d_extended, kernel_grad = pullback(d_conv)
    returned = from_behind(d_extended[:halo], -1)
    d_product = d_extended[halo:] + jnp.concatenate(
        [jnp.zeros((row_count - halo, channels), F32), returned]
    )
    d_proj_a = jnp.concatenate(
        [
            d_product * proj_x_part[halo_pad:],
            d_cgate,
            d_product * proj_b_part[halo_pad:],
        ],
        axis=1,
    ).astype(BF16)
    d_chunks = tp_chunks(times_t(arrange(to_gathered, d_proj_a), project_a))
    keep, send = halves(d_proj_a, gated_rows)
    mixer_cols = keep.shape[1]
    partial = gradient(
        [
            (mixer_in, 0),
            (mixer_in_other, 0),
            (jnp.where(first_core, mixer_in, back_a), 0),
            (jnp.where(first_core, mixer_in_other, back_a_other), 0),
        ],
        keep,
        swap_core(send),
        0,
        mixer_cols,
        1,
        3 * channels - mixer_cols,
        width,
        mixer_cols,
        0,
        None,
    )
    kernel_cols = kernel_taps * channels
    gain_start = kernel_cols + 2 * HD
    shared = jnp.concatenate([kernel_grad.reshape(-1), qgain_grad, kgain_grad])
    early_gains = [
        grad.reshape(shards, depth) for grad in (gain_f_grad, gain_b_grad, gain_s_grad)
    ]
    early_row = jnp.concatenate(
        [
            jnp.broadcast_to(shared, (shards, gain_start)),
            jnp.pad(
                jnp.concatenate(early_gains, axis=1),
                ((0, 0), (0, width - gain_start - 3 * depth)),
            ),
        ],
        axis=1,
    )
    d_mixer_in, early_row = lax.optimization_barrier((tp_reduce(d_chunks), early_row))
    unused, pullback = jax.vjp(norm_rows, stream0, gain_a)
    d_norm_a, gain_a_grad = pullback(d_mixer_in)
    d_stream0 = d_stream1 + d_norm_a

    slot_for_anchor = jnp.sum(
        jnp.where(
            my_anchor[None, :] == jnp.arange(shards)[:, None], jnp.arange(shards)[None, :], 0
        ),
        axis=1,
    )
    late_start = gain_start + 3 * depth
    late_row = jnp.pad(
        gain_a_grad.reshape(shards, depth), ((0, 0), (late_start, width - late_start - depth))
    )
    leaving = jnp.concatenate(
        [d_stream0.astype(BF16), stream4.astype(BF16), (early_row + late_row).astype(BF16)]
    )
    line = jnp.arange(shards * piece_rows)
    target, item = line // piece_rows, line % piece_rows
    source = jnp.where(
        item < 2 * part_rows,
        item // part_rows * chunk
        + jnp.repeat(slot_for_anchor, piece_rows) * part_rows
        + item % part_rows,
        jnp.where(item == 2 * part_rows, 2 * chunk + target, -1),
    )
    to_leaving = (source[:, None] == jnp.arange(leaving.shape[0])[None, :]).astype(BF16)
    leaving = arrange(to_leaving, leaving)
    home = lax.all_to_all(
        leaving.reshape(shards, piece_rows, width),
        TOKEN_AXES,
        split_axis=0,
        concat_axis=0,
        tiled=True,
    )
    second_grads = ffn_gradients(*second_grads, steps, hidden)
    home, partial, second_grads = lax.optimization_barrier((home, partial, second_grads))
    place = jnp.arange(2 * chunk + 8)
    small_line = (place == 2 * chunk) | (place == 2 * chunk + 1)
    wanted = (
        place % chunk // part_rows * piece_rows
        + place // chunk * part_rows
        + place % part_rows
    )
    to_payload = jnp.where(
        (place < 2 * chunk)[:, None],
        wanted[:, None] == line[None, :],
        small_line[:, None] & (item == 2 * part_rows)[None, :],
    ).astype(BF16)
    payload = times(to_payload, home.reshape(shards * piece_rows, width))
    rounded = payload.astype(BF16).astype(F32)
    payload = jnp.where((place == 2 * chunk + 1)[:, None], payload - rounded, payload)
    last = tp_gather(payload.astype(BF16))
    mixer_home = lax.all_to_all(
        partial.reshape(shards, depth, mixer_cols),
        TOKEN_AXES,
        split_axis=0,
        concat_axis=0,
        tiled=True,
    )
    home_rows = (
        jnp.repeat(jnp.tile(send_piece, members), part_rows) * piece_rows
        + member_of * part_rows
        + gathered % part_rows
    )
    to_arrival = (home_rows[None, :] == gathered[:, None]).astype(BF16)
    input_gradient = arrange(to_arrival, jnp.concatenate([slot[:chunk] for slot in last]))
    layer_out = arrange(to_arrival, jnp.concatenate([slot[chunk : 2 * chunk] for slot in last]))
    first_sums, layer_out, input_gradient = lax.optimization_barrier(
        (first_sums, layer_out, input_gradient)
    )
    low, high = share_rows(first_sums)
    first_grads = ffn_gradients(low[:, :ffn_cols], high[:, :ffn_cols], steps, hidden)
    attend_grads = jnp.concatenate([low[:, ffn_cols:], high[:, ffn_cols:]], axis=1)
    first_grads, attend_grads, mixer_home = lax.optimization_barrier(
        (first_grads, attend_grads, mixer_home)
    )
    mixer_home = mixer_home.reshape(shards // CORES, CORES, depth, mixer_cols)
    mixer_grads = jnp.sum(mixer_home.astype(F32), axis=0)
    mixer_grads = jnp.concatenate([mixer_grads[0], mixer_grads[1]], axis=1)
    smalls = [
        slot[2 * chunk].astype(F32) + slot[2 * chunk + 1].astype(F32) for slot in last
    ]
    totals = sum(smalls)
    kernel_rows = jnp.stack([small[:kernel_cols].reshape(kernel_taps, channels) for small in smalls])
    kernel_total = jnp.concatenate(
        [
            lax.dynamic_index_in_dim(kernel_rows, (own - member) % members, 0, keepdims=False)
            for member in range(members)
        ],
        axis=1,
    )
    qgain_total = totals[kernel_cols : kernel_cols + HD]
    kgain_total = totals[kernel_cols + HD : kernel_cols + 2 * HD]
    gain_totals = totals[gain_start : gain_start + 4 * depth].reshape(4, depth)

    gateup_s_grad, down_s_grad = second_grads
    gateup_f_grad, down_f_grad = first_grads
    proj_cols = attend_project.shape[1]
    return (
        layer_out,
        input_gradient,
        gain_totals[3],
        mixer_grads[:, : 3 * channels].reshape(depth, 3, channels),
        kernel_total,
        mixer_grads[:, 3 * channels :].T,
        gain_totals[0],
        gateup_f_grad,
        down_f_grad,
        gain_totals[1],
        attend_grads[:, :proj_cols],
        qgain_total,
        kgain_total,
        attend_grads[:, proj_cols:].T,
        gain_totals[2],
        gateup_s_grad,
        down_s_grad,
    )


def solution(mesh):
    names = TOKEN_AXES + ("tp",)
    rings = mesh.shape["fsdp"] // 2, 2, mesh.shape["ctx"] // 2, 2, mesh.shape["tp"]
    tokens = P(TOKEN_AXES, None)
    rows = P(TOKEN_AXES)
    three = P(TOKEN_AXES, None, "tp")
    two = P(TOKEN_AXES, "tp")
    turned = P("tp", TOKEN_AXES)
    return jax.shard_map(
        body,
        mesh=Mesh(mesh.devices.reshape(rings), names),
        in_specs=(
            tokens, tokens, P(), P(),
            rows, three, P(), turned,
            rows, three, turned,
            rows, two, P(), P(), turned,
            rows, three, turned,
        ),
        out_specs=(
            tokens, tokens,
            rows, three, P(), turned,
            rows, three, turned,
            rows, two, P(), P(), turned,
            rows, three, turned,
        ),
        check_vma=False,
    )
```

```python
import functools

import jax
import jax.numpy as jnp
from jax import lax
from jax.experimental import pallas as pl
from jax.experimental.pallas import tpu as pltpu
from jax.sharding import Mesh, PartitionSpec as P

H = 24
KVH = 8
HD = 64

EPSILON = 1e-05
ROPE_BASE = 1000000.0
NEGATIVE = -1e30

CHIP_AXES = ("x", "z_hi", "z_lo")
TOKEN_AXES = CHIP_AXES + ("core",)
GROUP_AXES = ("x", "z_hi")
CTX_AXES = ("z_lo", "core")
Z_AXES = ("z_hi", "z_lo")
CORES = 2
TILE = 256
VMEM_LIMIT = 48 * 1024 * 1024
F32 = jnp.float32
BF16 = jnp.bfloat16


def norm_rows(values, scales):
    return values * lax.rsqrt(jnp.mean(values * values, axis=-1, keepdims=True) + EPSILON) * scales


def rotate(values, cosine, sine):
    half_dim = values.shape[-1] // 2
    shape_out = (values.shape[0],) + (1,) * (values.ndim - 2) + (half_dim,)
    cosine = cosine.reshape(shape_out)
    sine = sine.reshape(shape_out)
    first_half = values[..., :half_dim]
    second_half = values[..., half_dim:]
    return jnp.concatenate(
        [
            first_half * cosine - second_half * sine,
            second_half * cosine + first_half * sine,
        ],
        axis=-1,
    )


def locate(lengths, positions):
    seq_ends = jnp.cumsum(lengths)
    segment = jnp.sum((positions[:, None] >= seq_ends[None, :]).astype(jnp.int32), axis=1)
    starts = seq_ends - lengths
    first_row = jnp.sum(
        jnp.where(segment[:, None] == jnp.arange(lengths.shape[0])[None, :], starts[None, :], 0),
        axis=1,
    )
    return (segment, positions - first_row)


def shortconv(extended, kernel_in, segment):
    kernel_taps = kernel_in.shape[0]
    out_rows = extended.shape[0] - kernel_taps + 1
    result = kernel_in[0] * extended[kernel_taps - 1 :]
    for t in range(1, kernel_taps):
        earlier = extended[kernel_taps - 1 - t : kernel_taps - 1 - t + out_rows]
        same_seq = (
            segment[kernel_taps - 1 - t : kernel_taps - 1 - t + out_rows]
            == segment[kernel_taps - 1 :]
        ).astype(F32)[:, None]
        result = result + kernel_in[t] * earlier * same_seq
    return result


def from_behind(block, distance):
    devices = range(lax.axis_size(CTX_AXES))
    route = [(i - distance, i) for i in devices if i - distance in devices]
    return lax.ppermute(block, CTX_AXES, route)


def swap_ctx(block, mask):
    return lax.ppermute(block, CTX_AXES, [(i, i ^ mask) for i in range(lax.axis_size(CTX_AXES))])


def swap_core(block):
    return lax.ppermute(block, "core", [(0, 1), (1, 0)])


def shift_tp(block, distance):
    members = lax.axis_size("tp")
    return lax.ppermute(block, "tp", [(i, (i + distance) % members) for i in range(members)])


def tp_gather(shard):
    return [shard] + [shift_tp(shard, k) for k in range(1, lax.axis_size("tp"))]


def tp_chunks(partial):
    rows = partial.shape[0] // lax.axis_size("tp")
    return [
        partial[k * rows : (k + 1) * rows].astype(F32 if k == 0 else BF16)
        for k in range(lax.axis_size("tp"))
    ]


def tp_reduce(chunks):
    total = chunks[0]
    for k in range(1, len(chunks)):
        total = total + shift_tp(chunks[k], -k).astype(F32)
    return total


def arrange(order, rows):
    return times(order, rows).astype(BF16)


def times(left, right):
    return lax.dot_general(left, right, (((1,), (0,)), ((), ())), preferred_element_type=F32)


def times_t(left, right):
    return lax.dot_general(left, right, (((1,), (1,)), ((), ())), preferred_element_type=F32)


def times_rows(left, right):
    return lax.dot_general(left, right, (((0,), (0,)), ((), ())), preferred_element_type=F32)


def assemble(chunk_refs, target):
    rows = chunk_refs[0].shape[0]
    for k, ref in enumerate(chunk_refs):
        target[k * rows : (k + 1) * rows, :] = ref[...]


def spread(total, chunk_refs):
    rows = chunk_refs[0].shape[0]
    for k, ref in enumerate(chunk_refs):
        ref[...] = total[k * rows : (k + 1) * rows, :].astype(ref.dtype)


def whole(shape):
    return pl.BlockSpec(shape, lambda *_: (0,) * len(shape))


def weight_specs(depth, steps):
    return [
        pl.BlockSpec((depth, 2 * TILE), lambda j: (0, j)),
        pl.BlockSpec((depth, TILE), lambda j: (0, 2 * steps + j)),
    ]


def chunk_shapes(count, rows, width):
    return [jax.ShapeDtypeStruct((rows, width), F32 if k == 0 else BF16) for k in range(count)]


def ffn_forward_kernel(count, *refs):
    x_refs, (gu_ref, dn_ref), outs = refs[:count], refs[count : count + 2], refs[count + 2 : -2]
    x_all, total = refs[-2:]
    step = pl.program_id(0)

    @pl.when(step == 0)
    def _():
        assemble(x_refs, x_all)
        total[...] = jnp.zeros_like(total)

    both = times(x_all[...], gu_ref[...])
    gate, up = both[:, :TILE], both[:, TILE:]
    active = (gate * jax.nn.sigmoid(gate) * up).astype(BF16)
    total[...] += times_t(active, dn_ref[...])

    @pl.when(step == pl.num_programs(0) - 1)
    def _():
        spread(total[...], outs)


def ffn_forward(chunks, pack, steps):
    count, (rows, width) = len(chunks), chunks[0].shape
    tokens = count * rows
    return pl.pallas_call(
        functools.partial(ffn_forward_kernel, count),
        grid=(steps,),
        in_specs=[whole((rows, width))] * count + weight_specs(width, steps),
        out_specs=[whole((rows, width))] * count,
        out_shape=chunk_shapes(count, rows, width),
        scratch_shapes=[pltpu.VMEM((tokens, width), BF16), pltpu.VMEM((tokens, width), F32)],
        compiler_params=pltpu.CompilerParams(vmem_limit_bytes=VMEM_LIMIT),
        cost_estimate=pl.CostEstimate(
            flops=2 * tokens * width * 3 * TILE * steps,
            bytes_accessed=2 * width * 3 * TILE * steps,
            transcendentals=tokens * TILE * steps,
        ),
        name="ffn_forward",
    )(*chunks, pack, pack)


def ffn_backward_kernel(count, forward, core_ref, *refs):
    x_refs, b_refs = refs[:count], refs[count : 2 * count]
    gu_ref, dn_ref = refs[2 * count : 2 * count + 2]
    place = 2 * count + 2
    back_outs = refs[place : place + count]
    place += count
    if forward:
        outs = refs[place : place + count]
        place += count
    keep_ref, side_ref = refs[place : place + 2]
    scratch = refs[place + 2 :]
    x_all, b_all, d_total = scratch[:3]
    step = pl.program_id(0)
    width = x_all.shape[1]

    @pl.when(step == 0)
    def _():
        assemble(x_refs, x_all)
        assemble(b_refs, b_all)
        if forward:
            side_ref[:, :width] = x_all[...]
            side_ref[:, width : 2 * width] = b_all[...]
        d_total[...] = jnp.zeros_like(d_total)
        if forward:
            scratch[3][...] = jnp.zeros_like(scratch[3])

    both = times(x_all[...], gu_ref[...])
    gate, up = both[:, :TILE], both[:, TILE:]
    d_active = times(b_all[...], dn_ref[...])
    sigmoid = jax.nn.sigmoid(gate)
    silu = gate * sigmoid
    active = (silu * up).astype(BF16)
    if forward:
        scratch[3][...] += times_t(active, dn_ref[...])
    d_gate = (d_active * up * (sigmoid * (1.0 + gate * (1.0 - sigmoid)))).astype(BF16)
    d_up = (d_active * silu).astype(BF16)
    d_total[...] += times_t(jnp.concatenate([d_gate, d_up], axis=1), gu_ref[...])
    first = core_ref[0] == 0
    half = TILE // 2
    low, high = active[:, :half], active[:, half:]
    offset = 2 * width if forward else 0
    wide = pl.multiple_of(step * TILE, TILE)
    narrow = pl.multiple_of(pl.num_programs(0) * TILE + step * half, half)
    side_wide = pl.multiple_of(offset + wide, TILE)
    side_narrow = pl.multiple_of(offset + narrow, half)

    @pl.when(first)
    def _():
        keep_ref[:, pl.ds(wide, TILE)] = d_gate
        keep_ref[:, pl.ds(narrow, half)] = low
        side_ref[:, pl.ds(side_wide, TILE)] = d_up
        side_ref[:, pl.ds(side_narrow, half)] = high

    @pl.when(jnp.logical_not(first))
    def _():
        keep_ref[:, pl.ds(wide, TILE)] = d_up
        keep_ref[:, pl.ds(narrow, half)] = high
        side_ref[:, pl.ds(side_wide, TILE)] = d_gate
        side_ref[:, pl.ds(side_narrow, half)] = low

    @pl.when(step == pl.num_programs(0) - 1)
    def _():
        spread(d_total[...], back_outs)
        if forward:
            spread(scratch[3][...], outs)


def ffn_backward(core, chunks, back_chunks, pack, steps, forward):
    count, (rows, width) = len(chunks), chunks[0].shape
    tokens = count * rows
    block = TILE + TILE // 2
    ways = 2 if forward else 1
    side_width = (2 * width if forward else 0) + steps * block
    results = pl.pallas_call(
        functools.partial(ffn_backward_kernel, count, forward),
        grid=(steps,),
        in_specs=[pl.BlockSpec(memory_space=pltpu.SMEM)]
        + [whole((rows, width))] * (2 * count)
        + weight_specs(width, steps),
        out_specs=[whole((rows, width))] * (ways * count)
        + [whole((tokens, steps * block)), whole((tokens, side_width))],
        out_shape=chunk_shapes(count, rows, width) * ways
        + [
            jax.ShapeDtypeStruct((tokens, steps * block), BF16),
            jax.ShapeDtypeStruct((tokens, side_width), BF16),
        ],
        scratch_shapes=[pltpu.VMEM((tokens, width), BF16)] * 2
        + [pltpu.VMEM((tokens, width), F32)] * ways,
        compiler_params=pltpu.CompilerParams(vmem_limit_bytes=VMEM_LIMIT),
        cost_estimate=pl.CostEstimate(
            flops=2 * tokens * width * (4 + ways) * TILE * steps,
            bytes_accessed=2 * width * 3 * TILE * steps + 4 * tokens * side_width,
            transcendentals=tokens * TILE * steps,
        ),
        name="ffn_both" if forward else "ffn_backward",
    )(core, *chunks, *back_chunks, pack, pack)
    return results[:count], results[count : ways * count], results[-2], results[-1]


def gradient_kernel(edge, cut, *refs):
    one_own, one_other, two_own, two_other, own_ref, other_ref = refs[:6]
    out_ref = refs[-1]
    step = pl.program_id(0)

    def product(own_left, other_left, columns):
        total = times_rows(own_left[...], own_ref[:, columns])
        total += times_rows(other_left[...], other_ref[:, columns])
        out_ref[:, columns] = total.astype(BF16)

    @pl.when(step < edge)
    def _():
        product(one_own, one_other, slice(None))

    @pl.when(step > edge if cut else step >= edge)
    def _():
        product(two_own, two_other, slice(None))

    if cut:

        @pl.when(step == edge)
        def _():
            product(one_own, one_other, slice(0, cut))
            product(two_own, two_other, slice(cut, None))


def gradient(lefts, own, other, other_start, block, steps, columns, width, out_width, out_start, target):
    tokens = own.shape[0]
    edge, cut = divmod(columns, block)

    def left_spec(index):
        return pl.BlockSpec((tokens, width), lambda j: (0, index))

    in_specs = [left_spec(index) for unused, index in lefts] + [
        pl.BlockSpec((tokens, block), lambda j: (0, j)),
        pl.BlockSpec((tokens, block), lambda j: (0, other_start + j)),
    ]
    operands = [array for array, unused in lefts] + [own, other]
    aliases = {}
    if target is not None:
        in_specs.append(pl.BlockSpec(memory_space=pl.ANY))
        operands.append(target)
        aliases = {len(operands) - 1: 0}
    return pl.pallas_call(
        functools.partial(gradient_kernel, edge, cut),
        grid=(steps,),
        in_specs=in_specs,
        out_specs=pl.BlockSpec((width, block), lambda j: (0, out_start + j)),
        out_shape=jax.ShapeDtypeStruct((width, out_width), BF16),
        input_output_aliases=aliases,
        compiler_params=pltpu.CompilerParams(vmem_limit_bytes=VMEM_LIMIT),
        cost_estimate=pl.CostEstimate(
            flops=4 * tokens * width * block * steps,
            bytes_accessed=2 * width * block * steps,
            transcendentals=0,
        ),
        name="weight_gradient",
    )(*operands)


def sum_chips(partial):
    return lax.psum_scatter(partial, CHIP_AXES, scatter_dimension=0, tiled=True)


def gather_pack(pack):
    chips = lax.axis_size(CHIP_AXES)
    core = lax.axis_index("core")
    plane = lax.all_to_all(
        jnp.broadcast_to(pack, (chips,) + pack.shape),
        CHIP_AXES,
        split_axis=0,
        concat_axis=0,
        tiled=True,
    )
    other = swap_core(plane)
    both = jnp.zeros((chips, CORES) + pack.shape, BF16)
    both = lax.dynamic_update_slice(both, plane[:, None], (0, core, 0, 0))
    both = lax.dynamic_update_slice(both, other[:, None], (0, 1 - core, 0, 0))
    return both.reshape(-1, pack.shape[1])


def finish_kernel(steps, core_ref, sum_ref, other_ref, gateup_ref, down_ref, *rest):
    core = core_ref[0]
    rows, hidden = down_ref.shape
    padded = steps * TILE
    half = TILE // 2
    first = core == 0
    mine = sum_ref[pl.ds(pl.multiple_of(core * rows, rows), rows), :].astype(F32)
    other = other_ref[...].astype(F32)
    low = jnp.where(first, mine, other)
    high = jnp.where(first, other, mine)
    gateup_ref[:, 0, :] = low[:, :hidden]
    gateup_ref[:, 1, :] = high[:, :hidden]
    for step in range(steps):
        source = padded + step * half
        for part, columns in enumerate((low, high)):
            place = step * TILE + part * half
            size = min(half, hidden - place)
            if size > 0:
                down_ref[:, place : place + size] = columns[:, source : source + size]
    for ref in rest:
        start = padded + steps * half
        size = low.shape[1] - start
        ref[:, :size] = low[:, start:]
        ref[:, size:] = high[:, start:]


def finish(summed, steps, hidden):
    core = lax.axis_index("core")
    rows, columns = summed.shape[0] // 2, summed.shape[1]
    other = swap_core(lax.dynamic_slice_in_dim(summed, (1 - core) * rows, rows, 0))
    extra = 2 * (columns - steps * (TILE + TILE // 2))
    return pl.pallas_call(
        functools.partial(finish_kernel, steps),
        in_specs=[
            pl.BlockSpec(memory_space=pltpu.SMEM),
            pl.BlockSpec(memory_space=pltpu.VMEM),
            pl.BlockSpec(memory_space=pltpu.VMEM),
        ],
        out_shape=[
            jax.ShapeDtypeStruct((rows, 2, hidden), F32),
            jax.ShapeDtypeStruct((rows, hidden), F32),
        ]
        + [jax.ShapeDtypeStruct((rows, extra), F32)] * (extra > 0),
        compiler_params=pltpu.CompilerParams(vmem_limit_bytes=VMEM_LIMIT),
        cost_estimate=pl.CostEstimate(
            flops=4 * rows * columns, bytes_accessed=16 * rows * columns, transcendentals=0
        ),
        name="finish_gradients",
    )(core.reshape(1).astype(jnp.int32), summed, other)


def halves(proj, out):
    first = lax.axis_index("core") == 0
    half = (proj.shape[1] + out.shape[1]) // 2
    late = jnp.concatenate([proj[:, half:], out], axis=1)
    early = proj[:, :half]
    return jnp.where(first, early, late), jnp.where(first, late, early)


def body(
    hidden_in,
    cotangent,
    seq_lengths,
    deal_order,
    mixer_gain,
    mixer_project,
    mixer_kernel,
    mixer_output,
    first_gain,
    first_gateup,
    first_down,
    attend_gain,
    attend_project,
    query_gain,
    key_gain,
    attend_output,
    second_gain,
    second_gateup,
    second_down,
):
    shards = lax.axis_size(TOKEN_AXES)
    contexts = lax.axis_size(CTX_AXES)
    members = lax.axis_size("tp")
    row_count, width = hidden_in.shape
    piece_rows = row_count // shards
    part_rows = piece_rows // members
    chunk = row_count // members
    device = lax.axis_index(TOKEN_AXES)
    own = lax.axis_index("tp")
    core = lax.axis_index("core")
    core_ref = core.reshape(1).astype(jnp.int32)
    depth = mixer_gain.shape[0]
    channels = mixer_output.shape[0]
    hidden = first_down.shape[0]
    heads_width = attend_output.shape[0]
    steps = -(-hidden // TILE)
    padded = steps * TILE
    ffn_width = 3 * padded
    block = TILE + TILE // 2

    def pack_ffn(gateup, down):
        wide = jnp.pad(gateup, ((0, 0), (0, 0), (0, padded - hidden)))
        wide = wide.reshape(depth, 2, steps, TILE).transpose(0, 2, 1, 3).reshape(depth, -1)
        return [wide, jnp.pad(down.T, ((0, 0), (0, padded - hidden)))]

    mixer_pack = jnp.concatenate([mixer_project.reshape(depth, -1), mixer_output.T], axis=1)
    first_pack = jnp.concatenate(
        pack_ffn(first_gateup, first_down) + [attend_project, attend_output.T], axis=1
    )
    second_pack = jnp.concatenate(pack_ffn(second_gateup, second_down), axis=1)
    piece_table = deal_order.reshape(shards, shards, piece_rows)[:, :, 0]
    anchor = piece_table // row_count
    anchor_piece = piece_table % row_count // piece_rows
    send_piece = jnp.sum(jnp.where(anchor == device, anchor_piece, 0), axis=1)
    my_anchor = lax.dynamic_index_in_dim(anchor, device, 0, keepdims=False)
    gains_row = jnp.concatenate(
        [mixer_gain, first_gain, attend_gain, second_gain, jnp.zeros((width - 4 * depth,), BF16)]
    )

    def my_part(rows):
        parts = rows.reshape(shards, members, part_rows, width)
        return lax.dynamic_index_in_dim(parts, own, 1, keepdims=False)[send_piece]

    outgoing = jnp.concatenate(
        [
            my_part(hidden_in),
            my_part(cotangent),
            jnp.broadcast_to(gains_row, (shards, 1, width)),
        ],
        axis=1,
    )
    arrived = lax.all_to_all(outgoing, TOKEN_AXES, split_axis=0, concat_axis=0, tiled=True)
    arrived, mixer_pack, first_pack = lax.optimization_barrier((arrived, mixer_pack, first_pack))
    first_all = lax.all_gather(first_pack, TOKEN_AXES, axis=0, tiled=True)
    second_all = lax.all_gather(second_pack, TOKEN_AXES, axis=0, tiled=True)
    project_b = first_all[:, ffn_width : ffn_width + attend_project.shape[1]]
    output_b_t = first_all[:, ffn_width + attend_project.shape[1] :]
    mixer_all = gather_pack(mixer_pack)
    project_a = mixer_all[:, : 3 * channels]
    output_a_t = mixer_all[:, 3 * channels :]
    gains = (
        arrived[:, 2 * part_rows, : 4 * depth]
        .reshape(shards, 4, depth)
        .transpose(1, 0, 2)
        .reshape(4, width)
        .astype(F32)
    )
    gain_a, gain_f, gain_b, gain_s = gains[0], gains[1], gains[2], gains[3]
    parts = arrived[:, : 2 * part_rows][my_anchor]
    own_tokens = parts[:, :part_rows].reshape(chunk, width)
    own_back = parts[:, part_rows:].reshape(chunk, width)
    stream0 = own_tokens.astype(F32)
    upstream = own_back.astype(F32)
    both = tp_gather(jnp.concatenate([own_tokens, own_back]))
    back_s_chunks = [slot[chunk:] for slot in both]

    gathered = jnp.arange(row_count)
    member_of = (own - gathered // chunk) % members
    offsets = (
        gathered % chunk // part_rows * piece_rows + member_of * part_rows + gathered % part_rows
    )
    to_gathered = (offsets[:, None] == gathered[None, :]).astype(BF16)
    to_dealt = (offsets[None, :] == gathered[:, None]).astype(BF16)
    tokens = times(to_dealt, jnp.concatenate([slot[:chunk] for slot in both]))

    kernel_taps = mixer_kernel.shape[0]
    halo = kernel_taps - 1
    local_rows = device * row_count + jnp.arange(row_count)
    halo_segment, unused = locate(
        seq_lengths, local_rows[0] - halo + jnp.arange(row_count + halo)
    )
    segment, places = locate(seq_lengths, device * row_count + offsets)
    ctx = lax.axis_index(CTX_AXES)
    group_rows = jnp.concatenate(
        [
            (lax.axis_index(GROUP_AXES) * contexts + (ctx ^ mask)) * row_count + offsets
            for mask in range(contexts)
        ]
    )
    key_segment, key_places = locate(seq_lengths, group_rows)
    allowed = (segment[:, None] == key_segment[None, :]) & (key_places[None, :] <= places[:, None])
    half_dim = HD // 2
    frequency = ROPE_BASE ** (-(jnp.arange(half_dim).astype(F32) * 2.0 / HD))
    angles = places.astype(F32)[:, None] * frequency[None, :]
    cosine = jnp.cos(angles)
    sine = jnp.sin(angles)

    kernel_local = lax.dynamic_slice_in_dim(mixer_kernel, own * channels, channels, 1).astype(F32)
    mixer_in = norm_rows(tokens, gain_a).astype(BF16)
    mixer_in_other = swap_core(mixer_in)
    halo_pad = 16
    halo_in = from_behind(mixer_in[row_count - halo_pad :], 1)
    proj_a = times(jnp.concatenate([halo_in, mixer_in]), project_a)
    proj_b_part = proj_a[:, :channels]
    proj_c_part = proj_a[halo_pad:, channels : 2 * channels]
    proj_x_part = proj_a[:, 2 * channels :]
    extended = (proj_b_part * proj_x_part)[halo_pad - halo :].astype(BF16).astype(F32)
    conv_out = shortconv(extended, kernel_local, halo_segment)
    gated_rows = (proj_c_part * conv_out).astype(BF16)
    gated_parts = arrange(to_gathered, gated_rows)
    stream1 = stream0 + tp_reduce(tp_chunks(times_t(gated_parts, output_a_t)))

    normed_f = tp_gather(norm_rows(stream1, gain_f).astype(BF16))
    stream2 = stream1 + tp_reduce(ffn_forward(normed_f, first_all, steps))

    groups = H // KVH
    score_scale = HD ** (-0.5)
    qgain_f = query_gain.astype(F32)
    kgain_f = key_gain.astype(F32)

    def qk_maps(query_in, key_in, gain_q, gain_k):
        return (
            rotate(norm_rows(query_in, gain_q), cosine, sine),
            rotate(norm_rows(key_in, gain_k), cosine, sine),
        )

    attend_in = jnp.concatenate(tp_gather(norm_rows(stream2, gain_b).astype(BF16)))
    proj_b = times(attend_in, project_b).reshape(row_count, -1, groups + 2, HD)
    kv_heads = proj_b.shape[1]
    query_raw = proj_b[:, :, :groups]
    key_raw = proj_b[:, :, groups]
    query_f, key_f = qk_maps(query_raw, key_raw, qgain_f, kgain_f)
    query_b = query_f.astype(BF16)
    key_value = jnp.concatenate(
        [
            key_f.astype(BF16).reshape(row_count, -1),
            proj_b[:, :, groups + 1].astype(BF16).reshape(row_count, -1),
        ],
        axis=1,
    )
    key_value_z = swap_ctx(key_value, 2)
    key_value_core = swap_core(jnp.concatenate([key_value, key_value_z]))
    key_value_all = jnp.concatenate(
        [key_value, key_value_core[:row_count], key_value_z, key_value_core[row_count:]]
    )
    key_all = key_value_all[:, : kv_heads * HD].reshape(-1, kv_heads, HD)
    value_all = key_value_all[:, kv_heads * HD :].reshape(-1, kv_heads, HD)
    scores = (
        jnp.einsum("tkgd,nkd->kgtn", query_b, key_all, preferred_element_type=F32) * score_scale
    )
    masked = jnp.where(allowed, scores, NEGATIVE)
    row_top = jnp.max(masked, axis=-1, keepdims=True)
    exponent = jnp.exp(masked - row_top)
    row_total = jnp.sum(exponent, axis=-1, keepdims=True)
    softmax_rows = exponent / row_total
    log_total = row_top + jnp.log(row_total)
    attended = (
        jnp.einsum(
            "kgtn,nkd->tkgd", softmax_rows.astype(BF16), value_all, preferred_element_type=F32
        )
        .astype(BF16)
        .reshape(row_count, -1)
    )
    stream3 = stream2 + tp_reduce(tp_chunks(times_t(attended, output_b_t)))

    normed_s = tp_gather(norm_rows(stream3, gain_s).astype(BF16))
    d_chunks, out_chunks, keep, side = ffn_backward(
        core_ref, normed_s, back_s_chunks, second_all, steps, True
    )
    unused, pullback = jax.vjp(norm_rows, stream3, gain_s)
    d_stream, gain_s_grad = pullback(tp_reduce(d_chunks))
    d_stream3 = upstream + d_stream
    out_others = [shift_tp(out_chunks[k], -k) for k in range(1, members)]
    side_other = swap_core(side)
    ffn_lefts = [(side, 0), (side_other, 0), (side, 1), (side_other, 1)]
    ffn_cols = steps * block
    side_start = 2 * width // block
    partial = gradient(
        ffn_lefts, keep, side_other, side_start, block, steps, padded, width, ffn_cols, 0, None
    )

    back_b = tp_gather(d_stream3.astype(BF16))
    back_b, partial = lax.optimization_barrier((back_b, partial))
    second_sums = sum_chips(partial)
    back_b = jnp.concatenate(back_b)
    back_b_other = swap_core(back_b)
    attend_in_other = swap_core(attend_in)
    d_attended_b = times(back_b, output_b_t).astype(BF16).reshape(row_count, -1, groups, HD)
    scores_again = (
        jnp.einsum("tkgd,nkd->kgtn", query_b, key_all, preferred_element_type=F32) * score_scale
    )
    probs_again = jnp.where(allowed, jnp.exp(scores_again - log_total), 0.0)
    d_probs = jnp.einsum("tkgd,nkd->kgtn", d_attended_b, value_all, preferred_element_type=F32)
    d_values = jnp.einsum(
        "kgtn,tkgd->nkd", probs_again.astype(BF16), d_attended_b, preferred_element_type=F32
    )
    inner_sum = jnp.sum(probs_again * d_probs, axis=-1, keepdims=True)
    d_scores = (probs_again * (d_probs - inner_sum)).astype(BF16)
    d_query = (
        jnp.einsum("kgtn,nkd->tkgd", d_scores, key_all, preferred_element_type=F32) * score_scale
    )
    d_keys = (
        jnp.einsum("kgtn,tkgd->nkd", d_scores, query_b, preferred_element_type=F32) * score_scale
    )
    d_key_value = jnp.concatenate(
        [d_keys.reshape(-1, kv_heads * HD), d_values.reshape(-1, kv_heads * HD)], axis=1
    )
    d_slots = d_key_value.reshape(contexts, row_count, -1)
    d_others = jnp.concatenate([d_slots[1], d_slots[3]]).astype(BF16)
    d_others = swap_core(d_others).astype(F32)
    d_far = (d_slots[2] + d_others[row_count:]).astype(BF16)
    d_local = d_slots[0] + d_others[:row_count] + swap_ctx(d_far, 2).astype(F32)
    d_key_local = d_local[:, : kv_heads * HD].reshape(row_count, kv_heads, HD)
    d_value_local = d_local[:, kv_heads * HD :].reshape(row_count, kv_heads, HD)
    unused, pullback = jax.vjp(qk_maps, query_raw, key_raw, qgain_f, kgain_f)
    d_query_raw, d_key_raw, qgain_grad, kgain_grad = pullback((d_query, d_key_local))
    d_proj_b = (
        jnp.concatenate([d_query_raw, d_key_raw[:, :, None], d_value_local[:, :, None]], axis=2)
        .astype(BF16)
        .reshape(row_count, -1)
    )
    d_attend_in = tp_reduce(tp_chunks(times_t(d_proj_b, project_b)))
    unused, pullback = jax.vjp(norm_rows, stream2, gain_b)
    d_norm_b, gain_b_grad = pullback(d_attend_in)
    d_stream2 = d_stream3 + d_norm_b
    keep, send = halves(d_proj_b, attended)
    first_core = core == 0
    attend_cols = keep.shape[1]
    small_tile = 2 * (heads_width + attend_project.shape[1]) // 16
    third = gradient(
        [
            (attend_in, 0),
            (attend_in_other, 0),
            (jnp.where(first_core, attend_in, back_b), 0),
            (jnp.where(first_core, attend_in_other, back_b_other), 0),
        ],
        keep,
        swap_core(send),
        0,
        small_tile,
        attend_cols // small_tile,
        attend_project.shape[1] - attend_cols,
        width,
        ffn_cols + attend_cols,
        ffn_cols // small_tile,
        None,
    )

    back_f = tp_gather(d_stream2.astype(BF16))
    back_f, third = lax.optimization_barrier((back_f, third))
    left_x, left_b = jnp.concatenate(normed_f), jnp.concatenate(back_f)
    left_others = [swap_core(left_x), swap_core(left_b)]
    d_chunks, unused, keep, side = ffn_backward(
        core_ref, normed_f, back_f, first_all, steps, False
    )
    d_chunks, left_others = lax.optimization_barrier((d_chunks, left_others))
    d_chunks, side_other = lax.optimization_barrier((d_chunks, swap_core(side)))
    ffn_lefts = [(left_x, 0), (left_others[0], 0), (left_b, 0), (left_others[1], 0)]
    partial = gradient(
        ffn_lefts,
        keep,
        side_other,
        0,
        block,
        steps,
        padded,
        width,
        ffn_cols + attend_cols,
        0,
        third,
    )

    d_normed, partial = lax.optimization_barrier((tp_reduce(d_chunks), partial))
    unused, pullback = jax.vjp(norm_rows, stream1, gain_f)
    d_stream, gain_f_grad = pullback(d_normed)
    d_stream1 = d_stream2 + d_stream

    back_a = tp_gather(d_stream1.astype(BF16))
    first_sums = sum_chips(partial)
    back_a = arrange(to_dealt, jnp.concatenate(back_a))
    back_a_other = swap_core(back_a)
    d_gated = times(back_a, output_a_t)
    d_cgate = d_gated * conv_out
    d_conv = d_gated * proj_c_part
    unused, pullback = jax.vjp(
        lambda ext_rows, kernel_in: shortconv(ext_rows, kernel_in, halo_segment),
        extended,
        kernel_local,
    )
    d_extended, kernel_grad = pullback(d_conv)
    returned = from_behind(d_extended[:halo], -1)
    d_product = d_extended[halo:] + jnp.concatenate(
        [jnp.zeros((row_count - halo, channels), F32), returned]
    )
    d_proj_a = jnp.concatenate(
        [
            d_product * proj_x_part[halo_pad:],
            d_cgate,
            d_product * proj_b_part[halo_pad:],
        ],
        axis=1,
    ).astype(BF16)
    d_proj_a, out_others = lax.optimization_barrier((d_proj_a, out_others))
    stream4 = stream3 + out_chunks[0]
    for part in out_others:
        stream4 = stream4 + part.astype(F32)
    d_chunks = tp_chunks(times_t(arrange(to_gathered, d_proj_a), project_a))
    keep, send = halves(d_proj_a, gated_rows)
    mixer_cols = keep.shape[1]
    partial = gradient(
        [
            (mixer_in, 0),
            (mixer_in_other, 0),
            (jnp.where(first_core, mixer_in, back_a), 0),
            (jnp.where(first_core, mixer_in_other, back_a_other), 0),
        ],
        keep,
        swap_core(send),
        0,
        mixer_cols,
        1,
        3 * channels - mixer_cols,
        width,
        mixer_cols,
        0,
        None,
    )
    kernel_cols = kernel_taps * channels
    gain_start = kernel_cols + 2 * HD
    shared = jnp.concatenate([kernel_grad.reshape(-1), qgain_grad, kgain_grad])
    early_gains = [
        grad.reshape(shards, depth) for grad in (gain_f_grad, gain_b_grad, gain_s_grad)
    ]
    early_row = jnp.concatenate(
        [
            jnp.broadcast_to(shared, (shards, gain_start)),
            jnp.pad(
                jnp.concatenate(early_gains, axis=1),
                ((0, 0), (0, width - gain_start - 3 * depth)),
            ),
        ],
        axis=1,
    )
    d_mixer_in, early_row = lax.optimization_barrier((tp_reduce(d_chunks), early_row))
    unused, pullback = jax.vjp(norm_rows, stream0, gain_a)
    d_norm_a, gain_a_grad = pullback(d_mixer_in)
    d_stream0 = d_stream1 + d_norm_a

    slot_for_anchor = jnp.sum(
        jnp.where(
            my_anchor[None, :] == jnp.arange(shards)[:, None], jnp.arange(shards)[None, :], 0
        ),
        axis=1,
    )
    late_start = gain_start + 3 * depth
    late_row = jnp.pad(
        gain_a_grad.reshape(shards, depth), ((0, 0), (late_start, width - late_start - depth))
    )
    leaving = jnp.concatenate(
        [d_stream0.astype(BF16), stream4.astype(BF16), (early_row + late_row).astype(BF16)]
    )
    line = jnp.arange(shards * piece_rows)
    target, item = line // piece_rows, line % piece_rows
    source = jnp.where(
        item < 2 * part_rows,
        item // part_rows * chunk
        + jnp.repeat(slot_for_anchor, piece_rows) * part_rows
        + item % part_rows,
        jnp.where(item == 2 * part_rows, 2 * chunk + target, -1),
    )
    to_leaving = (source[:, None] == jnp.arange(leaving.shape[0])[None, :]).astype(BF16)
    leaving = arrange(to_leaving, leaving)
    home = lax.all_to_all(
        leaving.reshape(shards, piece_rows, width),
        TOKEN_AXES,
        split_axis=0,
        concat_axis=0,
        tiled=True,
    )
    second_grads = finish(second_sums, steps, hidden)
    home, partial, second_grads = lax.optimization_barrier((home, partial, second_grads))
    place = jnp.arange(2 * chunk + 8)
    small_line = (place == 2 * chunk) | (place == 2 * chunk + 1)
    wanted = (
        place % chunk // part_rows * piece_rows
        + place // chunk * part_rows
        + place % part_rows
    )
    to_payload = jnp.where(
        (place < 2 * chunk)[:, None],
        wanted[:, None] == line[None, :],
        small_line[:, None] & (item == 2 * part_rows)[None, :],
    ).astype(BF16)
    payload = times(to_payload, home.reshape(shards * piece_rows, width))
    rounded = payload.astype(BF16).astype(F32)
    payload = jnp.where((place == 2 * chunk + 1)[:, None], payload - rounded, payload)
    last = tp_gather(payload.astype(BF16))
    mixer_home = lax.all_to_all(
        partial.reshape(shards, depth, mixer_cols),
        TOKEN_AXES,
        split_axis=0,
        concat_axis=0,
        tiled=True,
    )
    home_rows = (
        jnp.repeat(jnp.tile(send_piece, members), part_rows) * piece_rows
        + member_of * part_rows
        + gathered % part_rows
    )
    to_arrival = (home_rows[None, :] == gathered[:, None]).astype(BF16)
    input_gradient = arrange(to_arrival, jnp.concatenate([slot[:chunk] for slot in last]))
    layer_out = arrange(to_arrival, jnp.concatenate([slot[chunk : 2 * chunk] for slot in last]))
    first_sums, layer_out, input_gradient = lax.optimization_barrier(
        (first_sums, layer_out, input_gradient)
    )
    *first_grads, attend_grads = finish(first_sums, steps, hidden)
    first_grads, attend_grads, mixer_home = lax.optimization_barrier(
        (first_grads, attend_grads, mixer_home)
    )
    mixer_home = mixer_home.reshape(shards // CORES, CORES, depth, mixer_cols)
    mixer_grads = jnp.sum(mixer_home.astype(F32), axis=0)
    mixer_grads = jnp.concatenate([mixer_grads[0], mixer_grads[1]], axis=1)
    smalls = [
        slot[2 * chunk].astype(F32) + slot[2 * chunk + 1].astype(F32) for slot in last
    ]
    totals = sum(smalls)
    kernel_rows = jnp.stack([small[:kernel_cols].reshape(kernel_taps, channels) for small in smalls])
    kernel_total = jnp.concatenate(
        [
            lax.dynamic_index_in_dim(kernel_rows, (own - member) % members, 0, keepdims=False)
            for member in range(members)
        ],
        axis=1,
    )
    qgain_total = totals[kernel_cols : kernel_cols + HD]
    kgain_total = totals[kernel_cols + HD : kernel_cols + 2 * HD]
    gain_totals = totals[gain_start : gain_start + 4 * depth].reshape(4, depth)

    gateup_s_grad, down_s_grad = second_grads
    gateup_f_grad, down_f_grad = first_grads
    proj_cols = attend_project.shape[1]
    return (
        layer_out,
        input_gradient,
        gain_totals[3],
        mixer_grads[:, : 3 * channels].reshape(depth, 3, channels),
        kernel_total,
        mixer_grads[:, 3 * channels :].T,
        gain_totals[0],
        gateup_f_grad,
        down_f_grad.T,
        gain_totals[1],
        attend_grads[:, :proj_cols],
        qgain_total,
        kgain_total,
        attend_grads[:, proj_cols:].T,
        gain_totals[2],
        gateup_s_grad,
        down_s_grad.T,
    )


def solution(mesh):
    names = TOKEN_AXES + ("tp",)
    rings = mesh.shape["fsdp"] // 2, 2, mesh.shape["ctx"] // 2, 2, mesh.shape["tp"]
    tokens = P(TOKEN_AXES, None)
    rows = P(TOKEN_AXES)
    three = P(TOKEN_AXES, None, "tp")
    two = P(TOKEN_AXES, "tp")
    turned = P("tp", TOKEN_AXES)
    return jax.shard_map(
        body,
        mesh=Mesh(mesh.devices.reshape(rings), names),
        in_specs=(
            tokens, tokens, P(), P(),
            rows, three, P(), turned,
            rows, three, turned,
            rows, two, P(), P(), turned,
            rows, three, turned,
        ),
        out_specs=(
            tokens, tokens,
            rows, three, P(), turned,
            rows, three, turned,
            rows, two, P(), P(), turned,
            rows, three, turned,
        ),
        check_vma=False,
    )
```

```python
import functools

import jax
import jax.numpy as jnp
from jax import lax
from jax.experimental import pallas as pl
from jax.experimental.pallas import tpu as pltpu
from jax.sharding import Mesh, PartitionSpec as P

H = 24
KVH = 8
HD = 64

EPSILON = 1e-05
ROPE_BASE = 1000000.0
NEGATIVE = -1e30

CHIP_AXES = ("x", "z_hi", "z_lo")
TOKEN_AXES = CHIP_AXES + ("core",)
GROUP_AXES = ("x", "z_hi")
CTX_AXES = ("z_lo", "core")
Z_AXES = ("z_hi", "z_lo")
CORES = 2
TILE = 256
VMEM_LIMIT = 48 * 1024 * 1024
MIDDLE_LIMIT = 24 * 1024 * 1024
SMALL_LIMIT = 12 * 1024 * 1024
F32 = jnp.float32
BF16 = jnp.bfloat16


def norm_rows(values, scales):
    return values * lax.rsqrt(jnp.mean(values * values, axis=-1, keepdims=True) + EPSILON) * scales


def locate(lengths, positions):
    seq_ends = jnp.cumsum(lengths)
    segment = jnp.sum((positions[:, None] >= seq_ends[None, :]).astype(jnp.int32), axis=1)
    starts = seq_ends - lengths
    first_row = jnp.sum(
        jnp.where(segment[:, None] == jnp.arange(lengths.shape[0])[None, :], starts[None, :], 0),
        axis=1,
    )
    return (segment, positions - first_row)


def shortconv(extended, kernel_in, segment):
    kernel_taps = kernel_in.shape[0]
    out_rows = extended.shape[0] - kernel_taps + 1
    result = kernel_in[0] * extended[kernel_taps - 1 :]
    for t in range(1, kernel_taps):
        earlier = extended[kernel_taps - 1 - t : kernel_taps - 1 - t + out_rows]
        same_seq = (
            segment[kernel_taps - 1 - t : kernel_taps - 1 - t + out_rows]
            == segment[kernel_taps - 1 :]
        ).astype(F32)[:, None]
        result = result + kernel_in[t] * earlier * same_seq
    return result


def from_behind(block, distance):
    devices = range(lax.axis_size(CTX_AXES))
    route = [(i - distance, i) for i in devices if i - distance in devices]
    return lax.ppermute(block, CTX_AXES, route)


def swap_ctx(block, mask):
    return lax.ppermute(block, CTX_AXES, [(i, i ^ mask) for i in range(lax.axis_size(CTX_AXES))])


def swap_core(block):
    return lax.ppermute(block, "core", [(0, 1), (1, 0)])


def shift_tp(block, distance):
    members = lax.axis_size("tp")
    return lax.ppermute(block, "tp", [(i, (i + distance) % members) for i in range(members)])


def tp_gather(shard):
    return [shard] + [shift_tp(shard, k) for k in range(1, lax.axis_size("tp"))]


def tp_chunks(partial):
    rows = partial.shape[0] // lax.axis_size("tp")
    return [
        partial[k * rows : (k + 1) * rows].astype(F32 if k == 0 else BF16)
        for k in range(lax.axis_size("tp"))
    ]


def tp_scatter(chunks):
    return [chunks[0]] + [shift_tp(chunks[k], -k) for k in range(1, len(chunks))]


def add_parts(parts):
    total = parts[0]
    for part in parts[1:]:
        total = total + part.astype(F32)
    return total


def arrange(order, rows):
    return times(order, rows).astype(BF16)


def times(left, right):
    return lax.dot_general(left, right, (((1,), (0,)), ((), ())), preferred_element_type=F32)


def times_t(left, right):
    return lax.dot_general(left, right, (((1,), (1,)), ((), ())), preferred_element_type=F32)


def times_rows(left, right):
    return lax.dot_general(left, right, (((0,), (0,)), ((), ())), preferred_element_type=F32)


def assemble(chunk_refs, target):
    rows = chunk_refs[0].shape[0]
    for k, ref in enumerate(chunk_refs):
        target[k * rows : (k + 1) * rows, :] = ref[...]


def spread(total, chunk_refs):
    rows = chunk_refs[0].shape[0]
    for k, ref in enumerate(chunk_refs):
        ref[...] = total[k * rows : (k + 1) * rows, :].astype(ref.dtype)


def whole(shape):
    return pl.BlockSpec(shape, lambda *_: (0,) * len(shape))


def one_step(kernel, operands, out_shape, limit, name, flops):
    size = sum(v.size * v.dtype.itemsize for v in list(operands) + list(out_shape))
    return pl.pallas_call(
        kernel,
        grid=(1,),
        in_specs=[whole(v.shape) for v in operands],
        out_specs=[whole(v.shape) for v in out_shape],
        out_shape=out_shape,
        compiler_params=pltpu.CompilerParams(vmem_limit_bytes=limit),
        cost_estimate=pl.CostEstimate(flops=flops, bytes_accessed=size, transcendentals=0),
        name=name,
    )(*operands)


def sum_refs(refs):
    total = refs[0][...]
    for ref in refs[1:]:
        total = total + ref[...].astype(F32)
    return total


def add_norm_kernel(*refs):
    stream_ref, gain_ref, out_ref, normed_ref = refs[-4:]
    stream = stream_ref[...] + sum_refs(refs[:-4])
    out_ref[...] = stream
    normed_ref[...] = norm_rows(stream, gain_ref[...]).astype(BF16)


def add_norm(parts, stream, gain):
    return one_step(
        add_norm_kernel,
        [*parts, stream, gain[None]],
        [jax.ShapeDtypeStruct(stream.shape, F32), jax.ShapeDtypeStruct(stream.shape, BF16)],
        SMALL_LIMIT,
        "add_norm",
        10 * stream.size,
    )


def norm_backward_kernel(*refs):
    stream_ref, gain_ref, upward_ref, out_ref, rounded_ref, gain_grad_ref = refs[-6:]
    stream = stream_ref[...]
    d_normed = sum_refs(refs[:-6])
    spread_of = lax.rsqrt(jnp.mean(stream * stream, axis=1, keepdims=True) + EPSILON)
    gain_grad_ref[...] = jnp.sum(d_normed * stream * spread_of, axis=0, keepdims=True)
    scaled = d_normed * gain_ref[...]
    inner = jnp.mean(scaled * stream, axis=1, keepdims=True)
    result = upward_ref[...] + spread_of * scaled - stream * (
        spread_of * spread_of * spread_of * inner
    )
    out_ref[...] = result
    rounded_ref[...] = result.astype(BF16)


def norm_backward(parts, stream, gain, upward):
    out, rounded, gain_grad = one_step(
        norm_backward_kernel,
        [*parts, stream, gain[None], upward],
        [
            jax.ShapeDtypeStruct(stream.shape, F32),
            jax.ShapeDtypeStruct(stream.shape, BF16),
            jax.ShapeDtypeStruct((1, stream.shape[1]), F32),
        ],
        SMALL_LIMIT,
        "norm_backward",
        20 * stream.size,
    )
    return out, rounded, gain_grad[0]


def weight_specs(depth, steps):
    return [
        pl.BlockSpec((depth, 2 * TILE), lambda j: (0, j)),
        pl.BlockSpec((depth, TILE), lambda j: (0, 2 * steps + j)),
    ]


def chunk_shapes(count, rows, width):
    return [jax.ShapeDtypeStruct((rows, width), F32 if k == 0 else BF16) for k in range(count)]


def ffn_forward_kernel(count, *refs):
    x_refs, (gu_ref, dn_ref), outs = refs[:count], refs[count : count + 2], refs[count + 2 : -2]
    x_all, total = refs[-2:]
    step = pl.program_id(0)

    @pl.when(step == 0)
    def _():
        assemble(x_refs, x_all)
        total[...] = jnp.zeros_like(total)

    both = times(x_all[...], gu_ref[...])
    gate, up = both[:, :TILE], both[:, TILE:]
    active = (gate * jax.nn.sigmoid(gate) * up).astype(BF16)
    total[...] += times_t(active, dn_ref[...])

    @pl.when(step == pl.num_programs(0) - 1)
    def _():
        spread(total[...], outs)


def ffn_forward(chunks, pack, steps):
    count, (rows, width) = len(chunks), chunks[0].shape
    tokens = count * rows
    return pl.pallas_call(
        functools.partial(ffn_forward_kernel, count),
        grid=(steps,),
        in_specs=[whole((rows, width))] * count + weight_specs(width, steps),
        out_specs=[whole((rows, width))] * count,
        out_shape=chunk_shapes(count, rows, width),
        scratch_shapes=[pltpu.VMEM((tokens, width), BF16), pltpu.VMEM((tokens, width), F32)],
        compiler_params=pltpu.CompilerParams(vmem_limit_bytes=VMEM_LIMIT),
        cost_estimate=pl.CostEstimate(
            flops=2 * tokens * width * 3 * TILE * steps,
            bytes_accessed=2 * width * 3 * TILE * steps,
            transcendentals=tokens * TILE * steps,
        ),
        name="ffn_forward",
    )(*chunks, pack, pack)


def ffn_backward_kernel(count, forward, core_ref, *refs):
    x_refs, b_refs = refs[:count], refs[count : 2 * count]
    gu_ref, dn_ref = refs[2 * count : 2 * count + 2]
    place = 2 * count + 2
    back_outs = refs[place : place + count]
    place += count
    if forward:
        outs = refs[place : place + count]
        place += count
    keep_ref, side_ref = refs[place : place + 2]
    scratch = refs[place + 2 :]
    x_all, b_all, d_total = scratch[:3]
    step = pl.program_id(0)
    width = x_all.shape[1]

    @pl.when(step == 0)
    def _():
        assemble(x_refs, x_all)
        assemble(b_refs, b_all)
        if forward:
            side_ref[:, :width] = x_all[...]
            side_ref[:, width : 2 * width] = b_all[...]
        d_total[...] = jnp.zeros_like(d_total)
        if forward:
            scratch[3][...] = jnp.zeros_like(scratch[3])

    both = times(x_all[...], gu_ref[...])
    gate, up = both[:, :TILE], both[:, TILE:]
    d_active = times(b_all[...], dn_ref[...])
    sigmoid = jax.nn.sigmoid(gate)
    silu = gate * sigmoid
    active = (silu * up).astype(BF16)
    if forward:
        scratch[3][...] += times_t(active, dn_ref[...])
    d_gate = (d_active * up * (sigmoid * (1.0 + gate * (1.0 - sigmoid)))).astype(BF16)
    d_up = (d_active * silu).astype(BF16)
    d_total[...] += times_t(jnp.concatenate([d_gate, d_up], axis=1), gu_ref[...])
    first = core_ref[0] == 0
    half = TILE // 2
    low, high = active[:, :half], active[:, half:]
    offset = 2 * width if forward else 0
    wide = pl.multiple_of(step * TILE, TILE)
    narrow = pl.multiple_of(pl.num_programs(0) * TILE + step * half, half)
    side_wide = pl.multiple_of(offset + wide, TILE)
    side_narrow = pl.multiple_of(offset + narrow, half)

    @pl.when(first)
    def _():
        keep_ref[:, pl.ds(wide, TILE)] = d_gate
        keep_ref[:, pl.ds(narrow, half)] = low
        side_ref[:, pl.ds(side_wide, TILE)] = d_up
        side_ref[:, pl.ds(side_narrow, half)] = high

    @pl.when(jnp.logical_not(first))
    def _():
        keep_ref[:, pl.ds(wide, TILE)] = d_up
        keep_ref[:, pl.ds(narrow, half)] = high
        side_ref[:, pl.ds(side_wide, TILE)] = d_gate
        side_ref[:, pl.ds(side_narrow, half)] = low

    @pl.when(step == pl.num_programs(0) - 1)
    def _():
        spread(d_total[...], back_outs)
        if forward:
            spread(scratch[3][...], outs)


def ffn_backward(core, chunks, back_chunks, pack, steps, forward):
    count, (rows, width) = len(chunks), chunks[0].shape
    tokens = count * rows
    block = TILE + TILE // 2
    ways = 2 if forward else 1
    side_width = (2 * width if forward else 0) + steps * block
    results = pl.pallas_call(
        functools.partial(ffn_backward_kernel, count, forward),
        grid=(steps,),
        in_specs=[pl.BlockSpec(memory_space=pltpu.SMEM)]
        + [whole((rows, width))] * (2 * count)
        + weight_specs(width, steps),
        out_specs=[whole((rows, width))] * (ways * count)
        + [whole((tokens, steps * block)), whole((tokens, side_width))],
        out_shape=chunk_shapes(count, rows, width) * ways
        + [
            jax.ShapeDtypeStruct((tokens, steps * block), BF16),
            jax.ShapeDtypeStruct((tokens, side_width), BF16),
        ],
        scratch_shapes=[pltpu.VMEM((tokens, width), BF16)] * 2
        + [pltpu.VMEM((tokens, width), F32)] * ways,
        compiler_params=pltpu.CompilerParams(vmem_limit_bytes=VMEM_LIMIT),
        cost_estimate=pl.CostEstimate(
            flops=2 * tokens * width * (4 + ways) * TILE * steps,
            bytes_accessed=2 * width * 3 * TILE * steps + 4 * tokens * side_width,
            transcendentals=tokens * TILE * steps,
        ),
        name="ffn_both" if forward else "ffn_backward",
    )(core, *chunks, *back_chunks, pack, pack)
    return results[:count], results[count : ways * count], results[-2], results[-1]


def gradient_kernel(edge, cut, *refs):
    one_own, one_other, two_own, two_other, own_ref, other_ref = refs[:6]
    out_ref = refs[-1]
    step = pl.program_id(0)

    def product(own_left, other_left, columns):
        total = times_rows(own_left[...], own_ref[:, columns])
        total += times_rows(other_left[...], other_ref[:, columns])
        out_ref[:, columns] = total.astype(BF16)

    @pl.when(step < edge)
    def _():
        product(one_own, one_other, slice(None))

    @pl.when(step > edge if cut else step >= edge)
    def _():
        product(two_own, two_other, slice(None))

    if cut:

        @pl.when(step == edge)
        def _():
            product(one_own, one_other, slice(0, cut))
            product(two_own, two_other, slice(cut, None))


def gradient(lefts, own, other, other_start, block, steps, columns, width, out_width, out_start, target):
    tokens = own.shape[0]
    edge, cut = divmod(columns, block)

    def left_spec(index):
        return pl.BlockSpec((tokens, width), lambda j: (0, index))

    in_specs = [left_spec(index) for unused, index in lefts] + [
        pl.BlockSpec((tokens, block), lambda j: (0, j)),
        pl.BlockSpec((tokens, block), lambda j: (0, other_start + j)),
    ]
    operands = [array for array, unused in lefts] + [own, other]
    aliases = {}
    if target is not None:
        in_specs.append(pl.BlockSpec(memory_space=pl.ANY))
        operands.append(target)
        aliases = {len(operands) - 1: 0}
    return pl.pallas_call(
        functools.partial(gradient_kernel, edge, cut),
        grid=(steps,),
        in_specs=in_specs,
        out_specs=pl.BlockSpec((width, block), lambda j: (0, out_start + j)),
        out_shape=jax.ShapeDtypeStruct((width, out_width), BF16),
        input_output_aliases=aliases,
        compiler_params=pltpu.CompilerParams(vmem_limit_bytes=VMEM_LIMIT),
        cost_estimate=pl.CostEstimate(
            flops=4 * tokens * width * block * steps,
            bytes_accessed=2 * width * block * steps,
            transcendentals=0,
        ),
        name="weight_gradient",
    )(*operands)


def turn(rows, cosine, sine):
    half = rows.shape[1] // 2
    first, second = rows[:, :half], rows[:, half:]
    return jnp.concatenate(
        [first * cosine - second * sine, second * cosine + first * sine], axis=1
    )


def head_backward(d_rows, raw, cosine, sine, gain):
    d_normed = turn(d_rows, cosine, -sine)
    spread_of = lax.rsqrt(jnp.mean(raw * raw, axis=1, keepdims=True) + EPSILON)
    d_gain = jnp.sum(d_normed * raw * spread_of, axis=0, keepdims=True)
    scaled = d_normed * gain
    inner = jnp.mean(scaled * raw, axis=1, keepdims=True)
    d_raw = spread_of * scaled - raw * (spread_of * spread_of * spread_of * inner)
    return d_raw.astype(BF16), d_gain


def heads_kernel(groups, raw_ref, cos_ref, sin_ref, query_gain_ref, key_gain_ref, q_ref, kv_ref):
    size = query_gain_ref.shape[1]
    kv_heads = raw_ref.shape[1] // ((groups + 2) * size)
    cosine, sine = cos_ref[...], sin_ref[...]
    for group in range(kv_heads):
        start = group * (groups + 2) * size
        for member in range(groups):
            raw = raw_ref[:, start + member * size : start + (member + 1) * size]
            head = group * groups + member
            rows = turn(norm_rows(raw, query_gain_ref[...]), cosine, sine)
            q_ref[:, head * size : (head + 1) * size] = rows.astype(BF16)
        start += groups * size
        rows = turn(norm_rows(raw_ref[:, start : start + size], key_gain_ref[...]), cosine, sine)
        kv_ref[:, group * size : (group + 1) * size] = rows.astype(BF16)
        value_start = (kv_heads + group) * size
        kv_ref[:, value_start : value_start + size] = raw_ref[
            :, start + size : start + 2 * size
        ].astype(BF16)


def head_probs(key, query, scale, barred):
    scores = times_t(key, query) * scale + barred
    probs = jnp.exp(scores - jnp.max(scores, axis=0, keepdims=True))
    return probs / jnp.sum(probs, axis=0, keepdims=True)


def attend_kernel(scale, size, q_ref, kv_ref, barred_ref, out_ref):
    kv_heads = kv_ref.shape[1] // (2 * size)
    groups = q_ref.shape[1] // (kv_heads * size)
    barred = barred_ref[...].astype(F32)
    for head in range(kv_heads * groups):
        group = head // groups
        columns = slice(head * size, (head + 1) * size)
        key = kv_ref[:, group * size : (group + 1) * size]
        value = kv_ref[:, (kv_heads + group) * size : (kv_heads + group + 1) * size]
        probs = head_probs(key, q_ref[:, columns], scale, barred).astype(BF16)
        out_ref[:, columns] = times_rows(value, probs).T.astype(BF16)


def attend_backward_kernel(
    scale, q_ref, do_ref, kv_ref, barred_ref, raw_ref, cos_ref, sin_ref, gain_ref,
    dq_ref, near_ref, cross_ref, gain_grad_ref,
):
    size = gain_ref.shape[1]
    kv_heads = kv_ref.shape[1] // (2 * size)
    groups = q_ref.shape[1] // (kv_heads * size)
    rows = kv_ref.shape[0] // 4
    cosine, sine, gain = cos_ref[...], sin_ref[...], gain_ref[...]
    barred = barred_ref[...].astype(F32)
    gain_grad = jnp.zeros_like(gain)
    for group in range(kv_heads):
        columns = slice(group * size, (group + 1) * size)
        value_columns = slice((kv_heads + group) * size, (kv_heads + group + 1) * size)
        key, value = kv_ref[:, columns], kv_ref[:, value_columns]
        d_key = d_value = None
        for member in range(groups):
            head = group * groups + member
            head_columns = slice(head * size, (head + 1) * size)
            query, d_out = q_ref[:, head_columns], do_ref[:, head_columns]
            probs = head_probs(key, query, scale, barred)
            d_probs = times_t(value, d_out)
            inner = jnp.sum(probs * d_probs, axis=0, keepdims=True)
            d_scores = (probs * (d_probs - inner)).astype(BF16)
            part_value = times(probs.astype(BF16), d_out)
            part_key = times(d_scores, query) * scale
            d_value = part_value if d_value is None else d_value + part_value
            d_key = part_key if d_key is None else d_key + part_key
            d_query = (times_rows(key, d_scores) * scale).T
            start = (group * (groups + 2) + member) * size
            d_raw, d_gain = head_backward(
                d_query, raw_ref[:, start : start + size], cosine, sine, gain
            )
            dq_ref[:, head_columns] = d_raw
            gain_grad += d_gain
        for part, place in ((d_key, columns), (d_value, value_columns)):
            near_ref[:rows, place] = part[:rows]
            near_ref[rows:, place] = part[2 * rows : 3 * rows]
            cross_ref[:rows, place] = part[rows : 2 * rows].astype(BF16)
            cross_ref[rows:, place] = part[3 * rows :].astype(BF16)
    gain_grad_ref[...] = gain_grad


def assemble_kernel(groups, dq_ref, near_ref, cross_ref, far_ref, raw_ref, cos_ref, sin_ref, gain_ref, out_ref, gain_grad_ref):
    size = gain_ref.shape[1]
    kv_heads = raw_ref.shape[1] // ((groups + 2) * size)
    rows = raw_ref.shape[0]
    both = near_ref[:rows, :] + cross_ref[:rows, :].astype(F32) + far_ref[...].astype(F32)
    gain_grad = jnp.zeros_like(gain_ref[...])
    for group in range(kv_heads):
        start = group * (groups + 2) * size
        out_ref[:, start : start + groups * size] = dq_ref[
            :, group * groups * size : (group + 1) * groups * size
        ]
        start += groups * size
        d_raw, d_gain = head_backward(
            both[:, group * size : (group + 1) * size],
            raw_ref[:, start : start + size],
            cos_ref[...],
            sin_ref[...],
            gain_ref[...],
        )
        gain_grad += d_gain
        out_ref[:, start : start + size] = d_raw
        value_start = (kv_heads + group) * size
        out_ref[:, start + size : start + 2 * size] = both[
            :, value_start : value_start + size
        ].astype(BF16)
    gain_grad_ref[...] = gain_grad


def sum_chips(partial):
    return lax.psum_scatter(partial, CHIP_AXES, scatter_dimension=0, tiled=True)


def gather_pack(pack):
    chips = lax.axis_size(CHIP_AXES)
    core = lax.axis_index("core")
    plane = lax.all_to_all(
        jnp.broadcast_to(pack, (chips,) + pack.shape),
        CHIP_AXES,
        split_axis=0,
        concat_axis=0,
        tiled=True,
    )
    other = swap_core(plane)
    both = jnp.zeros((chips, CORES) + pack.shape, BF16)
    both = lax.dynamic_update_slice(both, plane[:, None], (0, core, 0, 0))
    both = lax.dynamic_update_slice(both, other[:, None], (0, 1 - core, 0, 0))
    return both.reshape(-1, pack.shape[1])


def finish_kernel(steps, core_ref, sum_ref, other_ref, gateup_ref, down_ref, *rest):
    core = core_ref[0]
    rows, hidden = down_ref.shape
    padded = steps * TILE
    half = TILE // 2
    first = core == 0
    mine = sum_ref[pl.ds(pl.multiple_of(core * rows, rows), rows), :].astype(F32)
    other = other_ref[...].astype(F32)
    low = jnp.where(first, mine, other)
    high = jnp.where(first, other, mine)
    gateup_ref[:, 0, :] = low[:, :hidden]
    gateup_ref[:, 1, :] = high[:, :hidden]
    for step in range(steps):
        source = padded + step * half
        for part, columns in enumerate((low, high)):
            place = step * TILE + part * half
            size = min(half, hidden - place)
            if size > 0:
                down_ref[:, place : place + size] = columns[:, source : source + size]
    for ref in rest:
        start = padded + steps * half
        size = low.shape[1] - start
        ref[:, :size] = low[:, start:]
        ref[:, size:] = high[:, start:]


def finish(summed, steps, hidden):
    core = lax.axis_index("core")
    rows, columns = summed.shape[0] // 2, summed.shape[1]
    other = swap_core(lax.dynamic_slice_in_dim(summed, (1 - core) * rows, rows, 0))
    extra = 2 * (columns - steps * (TILE + TILE // 2))
    return pl.pallas_call(
        functools.partial(finish_kernel, steps),
        grid=(1,),
        in_specs=[
            pl.BlockSpec(memory_space=pltpu.SMEM),
            whole(summed.shape),
            whole(other.shape),
        ],
        out_specs=[whole((rows, 2, hidden)), whole((rows, hidden))]
        + [whole((rows, extra))] * (extra > 0),
        out_shape=[
            jax.ShapeDtypeStruct((rows, 2, hidden), F32),
            jax.ShapeDtypeStruct((rows, hidden), F32),
        ]
        + [jax.ShapeDtypeStruct((rows, extra), F32)] * (extra > 0),
        compiler_params=pltpu.CompilerParams(vmem_limit_bytes=VMEM_LIMIT),
        cost_estimate=pl.CostEstimate(
            flops=4 * rows * columns, bytes_accessed=16 * rows * columns, transcendentals=0
        ),
        name="finish_gradients",
    )(core.reshape(1).astype(jnp.int32), summed, other)


def halves(proj, out):
    first = lax.axis_index("core") == 0
    half = (proj.shape[1] + out.shape[1]) // 2
    late = jnp.concatenate([proj[:, half:], out], axis=1)
    early = proj[:, :half]
    return jnp.where(first, early, late), jnp.where(first, late, early)


def body(
    hidden_in,
    cotangent,
    seq_lengths,
    deal_order,
    mixer_gain,
    mixer_project,
    mixer_kernel,
    mixer_output,
    first_gain,
    first_gateup,
    first_down,
    attend_gain,
    attend_project,
    query_gain,
    key_gain,
    attend_output,
    second_gain,
    second_gateup,
    second_down,
):
    shards = lax.axis_size(TOKEN_AXES)
    contexts = lax.axis_size(CTX_AXES)
    members = lax.axis_size("tp")
    row_count, width = hidden_in.shape
    piece_rows = row_count // shards
    part_rows = piece_rows // members
    chunk = row_count // members
    device = lax.axis_index(TOKEN_AXES)
    own = lax.axis_index("tp")
    core = lax.axis_index("core")
    core_ref = core.reshape(1).astype(jnp.int32)
    depth = mixer_gain.shape[0]
    channels = mixer_output.shape[0]
    hidden = first_down.shape[0]
    heads_width = attend_output.shape[0]
    steps = -(-hidden // TILE)
    padded = steps * TILE
    ffn_width = 3 * padded
    block = TILE + TILE // 2

    def pack_ffn(gateup, down):
        wide = jnp.pad(gateup, ((0, 0), (0, 0), (0, padded - hidden)))
        wide = wide.reshape(depth, 2, steps, TILE).transpose(0, 2, 1, 3).reshape(depth, -1)
        return [wide, jnp.pad(down.T, ((0, 0), (0, padded - hidden)))]

    mixer_pack = jnp.concatenate([mixer_project.reshape(depth, -1), mixer_output.T], axis=1)
    first_pack = jnp.concatenate(
        pack_ffn(first_gateup, first_down) + [attend_project, attend_output.T], axis=1
    )
    second_pack = jnp.concatenate(pack_ffn(second_gateup, second_down), axis=1)
    piece_table = deal_order.reshape(shards, shards, piece_rows)[:, :, 0]
    anchor = piece_table // row_count
    anchor_piece = piece_table % row_count // piece_rows
    send_piece = jnp.sum(jnp.where(anchor == device, anchor_piece, 0), axis=1)
    my_anchor = lax.dynamic_index_in_dim(anchor, device, 0, keepdims=False)
    gains_row = jnp.concatenate(
        [mixer_gain, first_gain, attend_gain, second_gain, jnp.zeros((width - 4 * depth,), BF16)]
    )

    def my_part(rows):
        parts = rows.reshape(shards, members, part_rows, width)
        return lax.dynamic_index_in_dim(parts, own, 1, keepdims=False)[send_piece]

    outgoing = jnp.concatenate(
        [
            my_part(hidden_in),
            my_part(cotangent),
            jnp.broadcast_to(gains_row, (shards, 1, width)),
        ],
        axis=1,
    )
    arrived = lax.all_to_all(outgoing, TOKEN_AXES, split_axis=0, concat_axis=0, tiled=True)
    arrived, mixer_pack, first_pack = lax.optimization_barrier((arrived, mixer_pack, first_pack))
    first_all = lax.all_gather(first_pack, TOKEN_AXES, axis=0, tiled=True)
    second_all = lax.all_gather(second_pack, TOKEN_AXES, axis=0, tiled=True)
    project_b = first_all[:, ffn_width : ffn_width + attend_project.shape[1]]
    output_b_t = first_all[:, ffn_width + attend_project.shape[1] :]
    mixer_all = gather_pack(mixer_pack)
    project_a = mixer_all[:, : 3 * channels]
    output_a_t = mixer_all[:, 3 * channels :]
    gains = (
        arrived[:, 2 * part_rows, : 4 * depth]
        .reshape(shards, 4, depth)
        .transpose(1, 0, 2)
        .reshape(4, width)
        .astype(F32)
    )
    gain_a, gain_f, gain_b, gain_s = gains[0], gains[1], gains[2], gains[3]
    parts = arrived[:, : 2 * part_rows][my_anchor]
    own_tokens = parts[:, :part_rows].reshape(chunk, width)
    own_back = parts[:, part_rows:].reshape(chunk, width)
    stream0 = own_tokens.astype(F32)
    upstream = own_back.astype(F32)
    both = tp_gather(jnp.concatenate([own_tokens, own_back]))
    back_s_chunks = [slot[chunk:] for slot in both]

    gathered = jnp.arange(row_count)
    member_of = (own - gathered // chunk) % members
    offsets = (
        gathered % chunk // part_rows * piece_rows + member_of * part_rows + gathered % part_rows
    )
    to_gathered = (offsets[:, None] == gathered[None, :]).astype(BF16)
    to_dealt = (offsets[None, :] == gathered[:, None]).astype(BF16)
    tokens = times(to_dealt, jnp.concatenate([slot[:chunk] for slot in both]))

    kernel_taps = mixer_kernel.shape[0]
    halo = kernel_taps - 1
    local_rows = device * row_count + jnp.arange(row_count)
    halo_segment, unused = locate(
        seq_lengths, local_rows[0] - halo + jnp.arange(row_count + halo)
    )
    segment, places = locate(seq_lengths, device * row_count + offsets)
    ctx = lax.axis_index(CTX_AXES)
    group_rows = jnp.concatenate(
        [
            (lax.axis_index(GROUP_AXES) * contexts + (ctx ^ mask)) * row_count + offsets
            for mask in range(contexts)
        ]
    )
    key_segment, key_places = locate(seq_lengths, group_rows)
    allowed = (segment[None, :] == key_segment[:, None]) & (key_places[:, None] <= places[None, :])
    barred = jnp.where(allowed, 0.0, NEGATIVE).astype(BF16)
    half_dim = HD // 2
    frequency = ROPE_BASE ** (-(jnp.arange(half_dim).astype(F32) * 2.0 / HD))
    angles = places.astype(F32)[:, None] * frequency[None, :]
    cosine = jnp.cos(angles)
    sine = jnp.sin(angles)

    kernel_local = lax.dynamic_slice_in_dim(mixer_kernel, own * channels, channels, 1).astype(F32)
    mixer_in = norm_rows(tokens, gain_a).astype(BF16)
    mixer_in_other = swap_core(mixer_in)
    halo_pad = 16
    halo_in = from_behind(mixer_in[row_count - halo_pad :], 1)
    proj_a = times(jnp.concatenate([halo_in, mixer_in]), project_a)
    proj_b_part = proj_a[:, :channels]
    proj_c_part = proj_a[halo_pad:, channels : 2 * channels]
    proj_x_part = proj_a[:, 2 * channels :]
    extended = (proj_b_part * proj_x_part)[halo_pad - halo :].astype(BF16).astype(F32)
    conv_out = shortconv(extended, kernel_local, halo_segment)
    gated_rows = (proj_c_part * conv_out).astype(BF16)
    gated_parts = arrange(to_gathered, gated_rows)
    stream1, normed = add_norm(
        tp_scatter(tp_chunks(times_t(gated_parts, output_a_t))), stream0, gain_f
    )

    normed_f = tp_gather(normed)
    stream2, normed = add_norm(
        tp_scatter(ffn_forward(normed_f, first_all, steps)), stream1, gain_b
    )

    groups = H // KVH
    score_scale = HD ** (-0.5)
    qgain_f = query_gain.astype(F32)[None]
    kgain_f = key_gain.astype(F32)[None]
    attend_in = jnp.concatenate(tp_gather(normed))
    proj_b = times(attend_in, project_b)
    kv_width = 2 * HD * (proj_b.shape[1] // (HD * (groups + 2)))
    query_b, key_value = one_step(
        functools.partial(heads_kernel, groups),
        [proj_b, cosine, sine, qgain_f, kgain_f],
        [
            jax.ShapeDtypeStruct((row_count, heads_width), BF16),
            jax.ShapeDtypeStruct((row_count, kv_width), BF16),
        ],
        SMALL_LIMIT,
        "heads",
        20 * proj_b.size,
    )
    key_value_z = swap_ctx(key_value, 2)
    key_value_core = swap_core(jnp.concatenate([key_value, key_value_z]))
    key_value_all = jnp.concatenate(
        [key_value, key_value_core[:row_count], key_value_z, key_value_core[row_count:]]
    )
    attend_flops = 2 * key_value_all.shape[0] * query_b.size
    (attended,) = one_step(
        functools.partial(attend_kernel, score_scale, HD),
        [query_b, key_value_all, barred],
        [jax.ShapeDtypeStruct(query_b.shape, BF16)],
        MIDDLE_LIMIT,
        "attend",
        2 * attend_flops,
    )
    stream3, normed = add_norm(
        tp_scatter(tp_chunks(times_t(attended, output_b_t))), stream2, gain_s
    )

    normed_s = tp_gather(normed)
    d_chunks, out_chunks, keep, side = ffn_backward(
        core_ref, normed_s, back_s_chunks, second_all, steps, True
    )
    d_stream3, back_b, gain_s_grad = norm_backward(
        tp_scatter(d_chunks), stream3, gain_s, upstream
    )
    out_others = [shift_tp(out_chunks[k], -k) for k in range(1, members)]
    side_other = swap_core(side)
    ffn_lefts = [(side, 0), (side_other, 0), (side, 1), (side_other, 1)]
    ffn_cols = steps * block
    side_start = 2 * width // block
    partial = gradient(
        ffn_lefts, keep, side_other, side_start, block, steps, padded, width, ffn_cols, 0, None
    )

    back_b = tp_gather(back_b)
    back_b, partial = lax.optimization_barrier((back_b, partial))
    second_sums = sum_chips(partial)
    back_b = jnp.concatenate(back_b)
    back_b_other = swap_core(back_b)
    attend_in_other = swap_core(attend_in)
    d_attended_b = times(back_b, output_b_t).astype(BF16)
    pair_rows = 2 * row_count
    d_query, near, cross, qgain_grad = one_step(
        functools.partial(attend_backward_kernel, score_scale),
        [query_b, d_attended_b, key_value_all, barred, proj_b, cosine, sine, qgain_f],
        [
            jax.ShapeDtypeStruct(query_b.shape, BF16),
            jax.ShapeDtypeStruct((pair_rows, kv_width), F32),
            jax.ShapeDtypeStruct((pair_rows, kv_width), BF16),
            jax.ShapeDtypeStruct((1, HD), F32),
        ],
        MIDDLE_LIMIT,
        "attend_backward",
        5 * attend_flops,
    )
    cross = swap_core(cross)
    far = (near[row_count:] + cross[row_count:].astype(F32)).astype(BF16)
    d_proj_b, kgain_grad = one_step(
        functools.partial(assemble_kernel, groups),
        [d_query, near, cross, swap_ctx(far, 2), proj_b, cosine, sine, kgain_f],
        [jax.ShapeDtypeStruct(proj_b.shape, BF16), jax.ShapeDtypeStruct((1, HD), F32)],
        SMALL_LIMIT,
        "assemble",
        20 * proj_b.size,
    )
    d_stream2, back_f, gain_b_grad = norm_backward(
        tp_scatter(tp_chunks(times_t(d_proj_b, project_b))), stream2, gain_b, d_stream3
    )
    keep, send = halves(d_proj_b, attended)
    first_core = core == 0
    attend_cols = keep.shape[1]
    small_tile = 2 * (heads_width + attend_project.shape[1]) // 16
    third = gradient(
        [
            (attend_in, 0),
            (attend_in_other, 0),
            (jnp.where(first_core, attend_in, back_b), 0),
            (jnp.where(first_core, attend_in_other, back_b_other), 0),
        ],
        keep,
        swap_core(send),
        0,
        small_tile,
        attend_cols // small_tile,
        attend_project.shape[1] - attend_cols,
        width,
        ffn_cols + attend_cols,
        ffn_cols // small_tile,
        None,
    )

    back_f = tp_gather(back_f)
    back_f, third = lax.optimization_barrier((back_f, third))
    left_x, left_b = jnp.concatenate(normed_f), jnp.concatenate(back_f)
    left_others = [swap_core(left_x), swap_core(left_b)]
    d_chunks, unused, keep, side = ffn_backward(
        core_ref, normed_f, back_f, first_all, steps, False
    )
    d_chunks, left_others = lax.optimization_barrier((d_chunks, left_others))
    d_chunks, side_other = lax.optimization_barrier((d_chunks, swap_core(side)))
    ffn_lefts = [(left_x, 0), (left_others[0], 0), (left_b, 0), (left_others[1], 0)]
    partial = gradient(
        ffn_lefts,
        keep,
        side_other,
        0,
        block,
        steps,
        padded,
        width,
        ffn_cols + attend_cols,
        0,
        third,
    )

    d_parts, partial = lax.optimization_barrier((tp_scatter(d_chunks), partial))
    d_stream1, back_a, gain_f_grad = norm_backward(d_parts, stream1, gain_f, d_stream2)

    back_a = tp_gather(back_a)
    first_sums = sum_chips(partial)
    back_a = arrange(to_dealt, jnp.concatenate(back_a))
    back_a_other = swap_core(back_a)
    d_gated = times(back_a, output_a_t)
    d_cgate = d_gated * conv_out
    d_conv = d_gated * proj_c_part
    unused, pullback = jax.vjp(
        lambda ext_rows, kernel_in: shortconv(ext_rows, kernel_in, halo_segment),
        extended,
        kernel_local,
    )
    d_extended, kernel_grad = pullback(d_conv)
    returned = from_behind(d_extended[:halo], -1)
    d_product = d_extended[halo:] + jnp.concatenate(
        [jnp.zeros((row_count - halo, channels), F32), returned]
    )
    d_proj_a = jnp.concatenate(
        [
            d_product * proj_x_part[halo_pad:],
            d_cgate,
            d_product * proj_b_part[halo_pad:],
        ],
        axis=1,
    ).astype(BF16)
    d_proj_a, out_others = lax.optimization_barrier((d_proj_a, out_others))
    stream4 = stream3 + add_parts([out_chunks[0], *out_others])
    d_chunks = tp_chunks(times_t(arrange(to_gathered, d_proj_a), project_a))
    keep, send = halves(d_proj_a, gated_rows)
    mixer_cols = keep.shape[1]
    partial = gradient(
        [
            (mixer_in, 0),
            (mixer_in_other, 0),
            (jnp.where(first_core, mixer_in, back_a), 0),
            (jnp.where(first_core, mixer_in_other, back_a_other), 0),
        ],
        keep,
        swap_core(send),
        0,
        mixer_cols,
        1,
        3 * channels - mixer_cols,
        width,
        mixer_cols,
        0,
        None,
    )
    kernel_cols = kernel_taps * channels
    gain_start = kernel_cols + 2 * HD
    shared = jnp.concatenate([kernel_grad.reshape(-1), qgain_grad[0], kgain_grad[0]])
    early_gains = [
        grad.reshape(shards, depth) for grad in (gain_f_grad, gain_b_grad, gain_s_grad)
    ]
    early_row = jnp.concatenate(
        [
            jnp.broadcast_to(shared, (shards, gain_start)),
            jnp.pad(
                jnp.concatenate(early_gains, axis=1),
                ((0, 0), (0, width - gain_start - 3 * depth)),
            ),
        ],
        axis=1,
    )
    d_parts, early_row = lax.optimization_barrier((tp_scatter(d_chunks), early_row))
    unused, d_stream0, gain_a_grad = norm_backward(d_parts, stream0, gain_a, d_stream1)

    slot_for_anchor = jnp.sum(
        jnp.where(
            my_anchor[None, :] == jnp.arange(shards)[:, None], jnp.arange(shards)[None, :], 0
        ),
        axis=1,
    )
    late_start = gain_start + 3 * depth
    late_row = jnp.pad(
        gain_a_grad.reshape(shards, depth), ((0, 0), (late_start, width - late_start - depth))
    )
    leaving = jnp.concatenate(
        [d_stream0, stream4.astype(BF16), (early_row + late_row).astype(BF16)]
    )
    line = jnp.arange(shards * piece_rows)
    target, item = line // piece_rows, line % piece_rows
    source = jnp.where(
        item < 2 * part_rows,
        item // part_rows * chunk
        + jnp.repeat(slot_for_anchor, piece_rows) * part_rows
        + item % part_rows,
        jnp.where(item == 2 * part_rows, 2 * chunk + target, -1),
    )
    to_leaving = (source[:, None] == jnp.arange(leaving.shape[0])[None, :]).astype(BF16)
    leaving = arrange(to_leaving, leaving)
    home = lax.all_to_all(
        leaving.reshape(shards, piece_rows, width),
        TOKEN_AXES,
        split_axis=0,
        concat_axis=0,
        tiled=True,
    )
    second_grads = finish(second_sums, steps, hidden)
    home, partial, second_grads = lax.optimization_barrier((home, partial, second_grads))
    place = jnp.arange(2 * chunk + 8)
    small_line = (place == 2 * chunk) | (place == 2 * chunk + 1)
    wanted = (
        place % chunk // part_rows * piece_rows
        + place // chunk * part_rows
        + place % part_rows
    )
    to_payload = jnp.where(
        (place < 2 * chunk)[:, None],
        wanted[:, None] == line[None, :],
        small_line[:, None] & (item == 2 * part_rows)[None, :],
    ).astype(BF16)
    payload = times(to_payload, home.reshape(shards * piece_rows, width))
    rounded = payload.astype(BF16).astype(F32)
    payload = jnp.where((place == 2 * chunk + 1)[:, None], payload - rounded, payload)
    last = tp_gather(payload.astype(BF16))
    mixer_home = lax.all_to_all(
        partial.reshape(shards, depth, mixer_cols),
        TOKEN_AXES,
        split_axis=0,
        concat_axis=0,
        tiled=True,
    )
    home_rows = (
        jnp.repeat(jnp.tile(send_piece, members), part_rows) * piece_rows
        + member_of * part_rows
        + gathered % part_rows
    )
    to_arrival = (home_rows[None, :] == gathered[:, None]).astype(BF16)
    input_gradient = arrange(to_arrival, jnp.concatenate([slot[:chunk] for slot in last]))
    layer_out = arrange(to_arrival, jnp.concatenate([slot[chunk : 2 * chunk] for slot in last]))
    first_sums, layer_out, input_gradient = lax.optimization_barrier(
        (first_sums, layer_out, input_gradient)
    )
    *first_grads, attend_grads = finish(first_sums, steps, hidden)
    first_grads, attend_grads, mixer_home = lax.optimization_barrier(
        (first_grads, attend_grads, mixer_home)
    )
    mixer_home = mixer_home.reshape(shards // CORES, CORES, depth, mixer_cols)
    mixer_grads = jnp.sum(mixer_home.astype(F32), axis=0)
    mixer_grads = jnp.concatenate([mixer_grads[0], mixer_grads[1]], axis=1)
    smalls = [
        slot[2 * chunk].astype(F32) + slot[2 * chunk + 1].astype(F32) for slot in last
    ]
    totals = sum(smalls)
    kernel_rows = jnp.stack([small[:kernel_cols].reshape(kernel_taps, channels) for small in smalls])
    kernel_total = jnp.concatenate(
        [
            lax.dynamic_index_in_dim(kernel_rows, (own - member) % members, 0, keepdims=False)
            for member in range(members)
        ],
        axis=1,
    )
    qgain_total = totals[kernel_cols : kernel_cols + HD]
    kgain_total = totals[kernel_cols + HD : kernel_cols + 2 * HD]
    gain_totals = totals[gain_start : gain_start + 4 * depth].reshape(4, depth)

    gateup_s_grad, down_s_grad = second_grads
    gateup_f_grad, down_f_grad = first_grads
    proj_cols = attend_project.shape[1]
    return (
        layer_out,
        input_gradient,
        gain_totals[3],
        mixer_grads[:, : 3 * channels].reshape(depth, 3, channels),
        kernel_total,
        mixer_grads[:, 3 * channels :].T,
        gain_totals[0],
        gateup_f_grad,
        down_f_grad.T,
        gain_totals[1],
        attend_grads[:, :proj_cols],
        qgain_total,
        kgain_total,
        attend_grads[:, proj_cols:].T,
        gain_totals[2],
        gateup_s_grad,
        down_s_grad.T,
    )


def solution(mesh):
    names = TOKEN_AXES + ("tp",)
    rings = mesh.shape["fsdp"] // 2, 2, mesh.shape["ctx"] // 2, 2, mesh.shape["tp"]
    tokens = P(TOKEN_AXES, None)
    rows = P(TOKEN_AXES)
    three = P(TOKEN_AXES, None, "tp")
    two = P(TOKEN_AXES, "tp")
    turned = P("tp", TOKEN_AXES)
    return jax.shard_map(
        body,
        mesh=Mesh(mesh.devices.reshape(rings), names),
        in_specs=(
            tokens, tokens, P(), P(),
            rows, three, P(), turned,
            rows, three, turned,
            rows, two, P(), P(), turned,
            rows, three, turned,
        ),
        out_specs=(
            tokens, tokens,
            rows, three, P(), turned,
            rows, three, turned,
            rows, two, P(), P(), turned,
            rows, three, turned,
        ),
        check_vma=False,
    )
```

```python
import functools

import jax
import jax.numpy as jnp
from jax import lax
from jax.experimental import pallas as pl
from jax.experimental.pallas import tpu as pltpu
from jax.sharding import Mesh, PartitionSpec as P

H = 24
KVH = 8
HD = 64

EPSILON = 1e-05
ROPE_BASE = 1000000.0
NEGATIVE = -1e30

CHIP_AXES = ("x", "z_hi", "z_lo")
TOKEN_AXES = CHIP_AXES + ("core",)
GROUP_AXES = ("x", "z_hi")
CTX_AXES = ("z_lo", "core")
Z_AXES = ("z_hi", "z_lo")
CORES = 2
TILE = 256
VMEM_LIMIT = 48 * 1024 * 1024
MIDDLE_LIMIT = 24 * 1024 * 1024
SMALL_LIMIT = 12 * 1024 * 1024
F32 = jnp.float32
BF16 = jnp.bfloat16


def norm_rows(values, scales):
    return values * lax.rsqrt(jnp.mean(values * values, axis=-1, keepdims=True) + EPSILON) * scales


def locate(lengths, positions):
    seq_ends = jnp.cumsum(lengths)
    segment = jnp.sum((positions[:, None] >= seq_ends[None, :]).astype(jnp.int32), axis=1)
    starts = seq_ends - lengths
    first_row = jnp.sum(
        jnp.where(segment[:, None] == jnp.arange(lengths.shape[0])[None, :], starts[None, :], 0),
        axis=1,
    )
    return (segment, positions - first_row)


def shortconv(extended, kernel_in, segment):
    kernel_taps = kernel_in.shape[0]
    out_rows = extended.shape[0] - kernel_taps + 1
    result = kernel_in[0] * extended[kernel_taps - 1 :]
    for t in range(1, kernel_taps):
        earlier = extended[kernel_taps - 1 - t : kernel_taps - 1 - t + out_rows]
        same_seq = (
            segment[kernel_taps - 1 - t : kernel_taps - 1 - t + out_rows]
            == segment[kernel_taps - 1 :]
        ).astype(F32)[:, None]
        result = result + kernel_in[t] * earlier * same_seq
    return result


def from_behind(block, distance):
    devices = range(lax.axis_size(CTX_AXES))
    route = [(i - distance, i) for i in devices if i - distance in devices]
    return lax.ppermute(block, CTX_AXES, route)


def swap_ctx(block, mask):
    return lax.ppermute(block, CTX_AXES, [(i, i ^ mask) for i in range(lax.axis_size(CTX_AXES))])


def swap_core(block):
    return lax.ppermute(block, "core", [(0, 1), (1, 0)])


def shift_tp(block, distance):
    members = lax.axis_size("tp")
    return lax.ppermute(block, "tp", [(i, (i + distance) % members) for i in range(members)])


def tp_gather(shard):
    return [shard] + [shift_tp(shard, k) for k in range(1, lax.axis_size("tp"))]


def tp_chunks(partial):
    rows = partial.shape[0] // lax.axis_size("tp")
    return [
        partial[k * rows : (k + 1) * rows].astype(F32 if k == 0 else BF16)
        for k in range(lax.axis_size("tp"))
    ]


def tp_scatter(chunks):
    return [chunks[0]] + [shift_tp(chunks[k], -k) for k in range(1, len(chunks))]


def add_parts(parts):
    total = parts[0]
    for part in parts[1:]:
        total = total + part.astype(F32)
    return total


def arrange(order, rows):
    return times(order, rows).astype(BF16)


def times(left, right):
    return lax.dot_general(left, right, (((1,), (0,)), ((), ())), preferred_element_type=F32)


def times_t(left, right):
    return lax.dot_general(left, right, (((1,), (1,)), ((), ())), preferred_element_type=F32)


def times_rows(left, right):
    return lax.dot_general(left, right, (((0,), (0,)), ((), ())), preferred_element_type=F32)


def assemble(chunk_refs, target):
    rows = chunk_refs[0].shape[0]
    for k, ref in enumerate(chunk_refs):
        target[k * rows : (k + 1) * rows, :] = ref[...]


def spread(total, chunk_refs):
    rows = chunk_refs[0].shape[0]
    for k, ref in enumerate(chunk_refs):
        ref[...] = total[k * rows : (k + 1) * rows, :].astype(ref.dtype)


def whole(shape):
    return pl.BlockSpec(shape, lambda *_: (0,) * len(shape))


def one_step(kernel, operands, out_shape, limit, name, flops):
    size = sum(v.size * v.dtype.itemsize for v in list(operands) + list(out_shape))
    return pl.pallas_call(
        kernel,
        grid=(1,),
        in_specs=[whole(v.shape) for v in operands],
        out_specs=[whole(v.shape) for v in out_shape],
        out_shape=out_shape,
        compiler_params=pltpu.CompilerParams(vmem_limit_bytes=limit),
        cost_estimate=pl.CostEstimate(flops=flops, bytes_accessed=size, transcendentals=0),
        name=name,
    )(*operands)


def sum_refs(refs):
    total = refs[0][...]
    for ref in refs[1:]:
        total = total + ref[...].astype(F32)
    return total


def add_norm_kernel(*refs):
    stream_ref, gain_ref, out_ref, normed_ref = refs[-4:]
    stream = stream_ref[...] + sum_refs(refs[:-4])
    out_ref[...] = stream
    normed_ref[...] = norm_rows(stream, gain_ref[...]).astype(BF16)


def add_norm(parts, stream, gain):
    return one_step(
        add_norm_kernel,
        [*parts, stream, gain[None]],
        [jax.ShapeDtypeStruct(stream.shape, F32), jax.ShapeDtypeStruct(stream.shape, BF16)],
        SMALL_LIMIT,
        "add_norm",
        10 * stream.size,
    )


def norm_backward_kernel(*refs):
    stream_ref, gain_ref, upward_ref, out_ref, rounded_ref, gain_grad_ref = refs[-6:]
    stream = stream_ref[...]
    d_normed = sum_refs(refs[:-6])
    spread_of = lax.rsqrt(jnp.mean(stream * stream, axis=1, keepdims=True) + EPSILON)
    gain_grad_ref[...] = jnp.sum(d_normed * stream * spread_of, axis=0, keepdims=True)
    scaled = d_normed * gain_ref[...]
    inner = jnp.mean(scaled * stream, axis=1, keepdims=True)
    result = upward_ref[...] + spread_of * scaled - stream * (
        spread_of * spread_of * spread_of * inner
    )
    out_ref[...] = result
    rounded_ref[...] = result.astype(BF16)


def norm_backward(parts, stream, gain, upward):
    out, rounded, gain_grad = one_step(
        norm_backward_kernel,
        [*parts, stream, gain[None], upward],
        [
            jax.ShapeDtypeStruct(stream.shape, F32),
            jax.ShapeDtypeStruct(stream.shape, BF16),
            jax.ShapeDtypeStruct((1, stream.shape[1]), F32),
        ],
        SMALL_LIMIT,
        "norm_backward",
        20 * stream.size,
    )
    return out, rounded, gain_grad[0]


def weight_specs(depth, steps):
    return [
        pl.BlockSpec((depth, 2 * TILE), lambda j: (0, j)),
        pl.BlockSpec((depth, TILE), lambda j: (0, 2 * steps + j)),
    ]


def chunk_shapes(count, rows, width):
    return [jax.ShapeDtypeStruct((rows, width), F32 if k == 0 else BF16) for k in range(count)]


def ffn_forward_kernel(count, *refs):
    x_refs, (gu_ref, dn_ref), outs = refs[:count], refs[count : count + 2], refs[count + 2 : -2]
    x_all, total = refs[-2:]
    step = pl.program_id(0)

    @pl.when(step == 0)
    def _():
        assemble(x_refs, x_all)
        total[...] = jnp.zeros_like(total)

    both = times(x_all[...], gu_ref[...])
    gate, up = both[:, :TILE], both[:, TILE:]
    active = (gate * jax.nn.sigmoid(gate) * up).astype(BF16)
    total[...] += times_t(active, dn_ref[...])

    @pl.when(step == pl.num_programs(0) - 1)
    def _():
        spread(total[...], outs)


def ffn_forward(chunks, pack, steps):
    count, (rows, width) = len(chunks), chunks[0].shape
    tokens = count * rows
    return pl.pallas_call(
        functools.partial(ffn_forward_kernel, count),
        grid=(steps,),
        in_specs=[whole((rows, width))] * count + weight_specs(width, steps),
        out_specs=[whole((rows, width))] * count,
        out_shape=chunk_shapes(count, rows, width),
        scratch_shapes=[pltpu.VMEM((tokens, width), BF16), pltpu.VMEM((tokens, width), F32)],
        compiler_params=pltpu.CompilerParams(vmem_limit_bytes=VMEM_LIMIT),
        cost_estimate=pl.CostEstimate(
            flops=2 * tokens * width * 3 * TILE * steps,
            bytes_accessed=2 * width * 3 * TILE * steps,
            transcendentals=tokens * TILE * steps,
        ),
        name="ffn_forward",
    )(*chunks, pack, pack)


def ffn_backward_kernel(count, back_count, forward, core_ref, *refs):
    x_refs, b_refs = refs[:count], refs[count : count + back_count]
    place = count + back_count
    gu_ref, dn_ref = refs[place : place + 2]
    place += 2
    back_outs = refs[place : place + count]
    place += count
    if forward:
        outs = refs[place : place + count]
        place += count
    keep_ref, side_ref = refs[place : place + 2]
    scratch = refs[place + 2 :]
    x_all, b_all, d_total = scratch[:3]
    step = pl.program_id(0)
    width = x_all.shape[1]

    @pl.when(step == 0)
    def _():
        assemble(x_refs, x_all)
        assemble(b_refs, b_all)
        if forward:
            side_ref[:, :width] = x_all[...]
            side_ref[:, width : 2 * width] = b_all[...]
        d_total[...] = jnp.zeros_like(d_total)
        if forward:
            scratch[3][...] = jnp.zeros_like(scratch[3])

    both = times(x_all[...], gu_ref[...])
    gate, up = both[:, :TILE], both[:, TILE:]
    d_active = times(b_all[...], dn_ref[...])
    sigmoid = jax.nn.sigmoid(gate)
    silu = gate * sigmoid
    active = (silu * up).astype(BF16)
    if forward:
        scratch[3][...] += times_t(active, dn_ref[...])
    d_gate = (d_active * up * (sigmoid * (1.0 + gate * (1.0 - sigmoid)))).astype(BF16)
    d_up = (d_active * silu).astype(BF16)
    d_total[...] += times_t(jnp.concatenate([d_gate, d_up], axis=1), gu_ref[...])
    first = core_ref[0] == 0
    half = TILE // 2
    low, high = active[:, :half], active[:, half:]
    offset = 2 * width if forward else 0
    wide = pl.multiple_of(step * TILE, TILE)
    narrow = pl.multiple_of(pl.num_programs(0) * TILE + step * half, half)
    side_wide = pl.multiple_of(offset + wide, TILE)
    side_narrow = pl.multiple_of(offset + narrow, half)

    @pl.when(first)
    def _():
        keep_ref[:, pl.ds(wide, TILE)] = d_gate
        keep_ref[:, pl.ds(narrow, half)] = low
        side_ref[:, pl.ds(side_wide, TILE)] = d_up
        side_ref[:, pl.ds(side_narrow, half)] = high

    @pl.when(jnp.logical_not(first))
    def _():
        keep_ref[:, pl.ds(wide, TILE)] = d_up
        keep_ref[:, pl.ds(narrow, half)] = high
        side_ref[:, pl.ds(side_wide, TILE)] = d_gate
        side_ref[:, pl.ds(side_narrow, half)] = low

    @pl.when(step == pl.num_programs(0) - 1)
    def _():
        spread(d_total[...], back_outs)
        if forward:
            spread(scratch[3][...], outs)


def ffn_backward(core, chunks, back_chunks, pack, steps, forward):
    count, (rows, width) = len(chunks), chunks[0].shape
    tokens = count * rows
    block = TILE + TILE // 2
    ways = 2 if forward else 1
    side_width = (2 * width if forward else 0) + steps * block
    results = pl.pallas_call(
        functools.partial(ffn_backward_kernel, count, len(back_chunks), forward),
        grid=(steps,),
        in_specs=[pl.BlockSpec(memory_space=pltpu.SMEM)]
        + [whole(v.shape) for v in (*chunks, *back_chunks)]
        + weight_specs(width, steps),
        out_specs=[whole((rows, width))] * (ways * count)
        + [whole((tokens, steps * block)), whole((tokens, side_width))],
        out_shape=chunk_shapes(count, rows, width) * ways
        + [
            jax.ShapeDtypeStruct((tokens, steps * block), BF16),
            jax.ShapeDtypeStruct((tokens, side_width), BF16),
        ],
        scratch_shapes=[pltpu.VMEM((tokens, width), BF16)] * 2
        + [pltpu.VMEM((tokens, width), F32)] * ways,
        compiler_params=pltpu.CompilerParams(vmem_limit_bytes=VMEM_LIMIT),
        cost_estimate=pl.CostEstimate(
            flops=2 * tokens * width * (4 + ways) * TILE * steps,
            bytes_accessed=2 * width * 3 * TILE * steps + 4 * tokens * side_width,
            transcendentals=tokens * TILE * steps,
        ),
        name="ffn_both" if forward else "ffn_backward",
    )(core, *chunks, *back_chunks, pack, pack)
    return results[:count], results[count : ways * count], results[-2], results[-1]


def gradient_kernel(edge, cut, *refs):
    one_own, one_other, two_own, two_other, own_ref, other_ref = refs[:6]
    out_ref = refs[-1]
    step = pl.program_id(0)

    def product(own_left, other_left, columns):
        total = times_rows(own_left[...], own_ref[:, columns])
        total += times_rows(other_left[...], other_ref[:, columns])
        out_ref[:, columns] = total.astype(BF16)

    @pl.when(step < edge)
    def _():
        product(one_own, one_other, slice(None))

    @pl.when(step > edge if cut else step >= edge)
    def _():
        product(two_own, two_other, slice(None))

    if cut:

        @pl.when(step == edge)
        def _():
            product(one_own, one_other, slice(0, cut))
            product(two_own, two_other, slice(cut, None))


def gradient(lefts, own, other, other_start, block, steps, columns, width, out_width, out_start, target):
    tokens = own.shape[0]
    edge, cut = divmod(columns, block)

    def left_spec(index):
        return pl.BlockSpec((tokens, width), lambda j: (0, index))

    in_specs = [left_spec(index) for unused, index in lefts] + [
        pl.BlockSpec((tokens, block), lambda j: (0, j)),
        pl.BlockSpec((tokens, block), lambda j: (0, other_start + j)),
    ]
    operands = [array for array, unused in lefts] + [own, other]
    aliases = {}
    if target is not None:
        in_specs.append(pl.BlockSpec(memory_space=pl.ANY))
        operands.append(target)
        aliases = {len(operands) - 1: 0}
    return pl.pallas_call(
        functools.partial(gradient_kernel, edge, cut),
        grid=(steps,),
        in_specs=in_specs,
        out_specs=pl.BlockSpec((width, block), lambda j: (0, out_start + j)),
        out_shape=jax.ShapeDtypeStruct((width, out_width), BF16),
        input_output_aliases=aliases,
        compiler_params=pltpu.CompilerParams(vmem_limit_bytes=VMEM_LIMIT),
        cost_estimate=pl.CostEstimate(
            flops=4 * tokens * width * block * steps,
            bytes_accessed=2 * width * block * steps,
            transcendentals=0,
        ),
        name="weight_gradient",
    )(*operands)


def turn(rows, cosine, sine):
    half = rows.shape[1] // 2
    first, second = rows[:, :half], rows[:, half:]
    return jnp.concatenate(
        [first * cosine - second * sine, second * cosine + first * sine], axis=1
    )


def head_backward(d_rows, raw, cosine, sine, gain):
    d_normed = turn(d_rows, cosine, -sine)
    spread_of = lax.rsqrt(jnp.mean(raw * raw, axis=1, keepdims=True) + EPSILON)
    d_gain = jnp.sum(d_normed * raw * spread_of, axis=0, keepdims=True)
    scaled = d_normed * gain
    inner = jnp.mean(scaled * raw, axis=1, keepdims=True)
    d_raw = spread_of * scaled - raw * (spread_of * spread_of * spread_of * inner)
    return d_raw.astype(BF16), d_gain


def heads_kernel(groups, raw_ref, cos_ref, sin_ref, query_gain_ref, key_gain_ref, q_ref, kv_ref):
    size = query_gain_ref.shape[1]
    kv_heads = raw_ref.shape[1] // ((groups + 2) * size)
    cosine, sine = cos_ref[...], sin_ref[...]
    for group in range(kv_heads):
        start = group * (groups + 2) * size
        for member in range(groups):
            raw = raw_ref[:, start + member * size : start + (member + 1) * size]
            head = group * groups + member
            rows = turn(norm_rows(raw, query_gain_ref[...]), cosine, sine)
            q_ref[:, head * size : (head + 1) * size] = rows.astype(BF16)
        start += groups * size
        rows = turn(norm_rows(raw_ref[:, start : start + size], key_gain_ref[...]), cosine, sine)
        kv_ref[:, group * size : (group + 1) * size] = rows.astype(BF16)
        value_start = (kv_heads + group) * size
        kv_ref[:, value_start : value_start + size] = raw_ref[
            :, start + size : start + 2 * size
        ].astype(BF16)


def head_probs(key, query, scale, barred):
    scores = times_t(key, query) * scale + barred
    probs = jnp.exp(scores - jnp.max(scores, axis=0, keepdims=True))
    return probs / jnp.sum(probs, axis=0, keepdims=True)


def attend_kernel(scale, size, q_ref, kv_ref, barred_ref, out_ref):
    kv_heads = kv_ref.shape[1] // (2 * size)
    groups = q_ref.shape[1] // (kv_heads * size)
    barred = barred_ref[...].astype(F32)
    for head in range(kv_heads * groups):
        group = head // groups
        columns = slice(head * size, (head + 1) * size)
        key = kv_ref[:, group * size : (group + 1) * size]
        value = kv_ref[:, (kv_heads + group) * size : (kv_heads + group + 1) * size]
        probs = head_probs(key, q_ref[:, columns], scale, barred).astype(BF16)
        out_ref[:, columns] = times_rows(value, probs).T.astype(BF16)


def attend_backward_kernel(
    scale, q_ref, do_ref, kv_ref, barred_ref, raw_ref, cos_ref, sin_ref, gain_ref,
    dq_ref, near_ref, cross_ref, gain_grad_ref,
):
    size = gain_ref.shape[1]
    kv_heads = kv_ref.shape[1] // (2 * size)
    groups = q_ref.shape[1] // (kv_heads * size)
    rows = kv_ref.shape[0] // 4
    cosine, sine, gain = cos_ref[...], sin_ref[...], gain_ref[...]
    barred = barred_ref[...].astype(F32)
    gain_grad = jnp.zeros_like(gain)
    for group in range(kv_heads):
        columns = slice(group * size, (group + 1) * size)
        value_columns = slice((kv_heads + group) * size, (kv_heads + group + 1) * size)
        key, value = kv_ref[:, columns], kv_ref[:, value_columns]
        d_key = d_value = None
        for member in range(groups):
            head = group * groups + member
            head_columns = slice(head * size, (head + 1) * size)
            query, d_out = q_ref[:, head_columns], do_ref[:, head_columns]
            probs = head_probs(key, query, scale, barred)
            d_probs = times_t(value, d_out)
            inner = jnp.sum(probs * d_probs, axis=0, keepdims=True)
            d_scores = (probs * (d_probs - inner)).astype(BF16)
            part_value = times(probs.astype(BF16), d_out)
            part_key = times(d_scores, query) * scale
            d_value = part_value if d_value is None else d_value + part_value
            d_key = part_key if d_key is None else d_key + part_key
            d_query = (times_rows(key, d_scores) * scale).T
            start = (group * (groups + 2) + member) * size
            d_raw, d_gain = head_backward(
                d_query, raw_ref[:, start : start + size], cosine, sine, gain
            )
            dq_ref[:, head_columns] = d_raw
            gain_grad += d_gain
        for part, place in ((d_key, columns), (d_value, value_columns)):
            near_ref[:rows, place] = part[:rows]
            near_ref[rows:, place] = part[2 * rows : 3 * rows]
            cross_ref[:rows, place] = part[rows : 2 * rows].astype(BF16)
            cross_ref[rows:, place] = part[3 * rows :].astype(BF16)
    gain_grad_ref[...] = gain_grad


def assemble_kernel(groups, dq_ref, near_ref, cross_ref, far_ref, raw_ref, cos_ref, sin_ref, gain_ref, out_ref, gain_grad_ref):
    size = gain_ref.shape[1]
    kv_heads = raw_ref.shape[1] // ((groups + 2) * size)
    rows = raw_ref.shape[0]
    both = near_ref[:rows, :] + cross_ref[:rows, :].astype(F32) + far_ref[...].astype(F32)
    gain_grad = jnp.zeros_like(gain_ref[...])
    for group in range(kv_heads):
        start = group * (groups + 2) * size
        out_ref[:, start : start + groups * size] = dq_ref[
            :, group * groups * size : (group + 1) * groups * size
        ]
        start += groups * size
        d_raw, d_gain = head_backward(
            both[:, group * size : (group + 1) * size],
            raw_ref[:, start : start + size],
            cos_ref[...],
            sin_ref[...],
            gain_ref[...],
        )
        gain_grad += d_gain
        out_ref[:, start : start + size] = d_raw
        value_start = (kv_heads + group) * size
        out_ref[:, start + size : start + 2 * size] = both[
            :, value_start : value_start + size
        ].astype(BF16)
    gain_grad_ref[...] = gain_grad


def sum_chips(partial):
    return lax.psum_scatter(partial, CHIP_AXES, scatter_dimension=0, tiled=True)


def gather_pack(pack):
    chips = lax.axis_size(CHIP_AXES)
    core = lax.axis_index("core")
    plane = lax.all_to_all(
        jnp.broadcast_to(pack, (chips,) + pack.shape),
        CHIP_AXES,
        split_axis=0,
        concat_axis=0,
        tiled=True,
    )
    other = swap_core(plane)
    both = jnp.zeros((chips, CORES) + pack.shape, BF16)
    both = lax.dynamic_update_slice(both, plane[:, None], (0, core, 0, 0))
    both = lax.dynamic_update_slice(both, other[:, None], (0, 1 - core, 0, 0))
    return both.reshape(-1, pack.shape[1])


def finish_kernel(steps, core_ref, sum_ref, other_ref, gateup_ref, down_ref, *rest):
    core = core_ref[0]
    rows, hidden = down_ref.shape
    padded = steps * TILE
    half = TILE // 2
    first = core == 0
    mine = sum_ref[pl.ds(pl.multiple_of(core * rows, rows), rows), :].astype(F32)
    other = other_ref[...].astype(F32)
    low = jnp.where(first, mine, other)
    high = jnp.where(first, other, mine)
    gateup_ref[:, 0, :] = low[:, :hidden]
    gateup_ref[:, 1, :] = high[:, :hidden]
    for step in range(steps):
        source = padded + step * half
        for part, columns in enumerate((low, high)):
            place = step * TILE + part * half
            size = min(half, hidden - place)
            if size > 0:
                down_ref[:, place : place + size] = columns[:, source : source + size]
    for ref in rest:
        start = padded + steps * half
        size = low.shape[1] - start
        ref[:, :size] = low[:, start:]
        ref[:, size:] = high[:, start:]


def finish(summed, steps, hidden):
    core = lax.axis_index("core")
    rows, columns = summed.shape[0] // 2, summed.shape[1]
    other = swap_core(lax.dynamic_slice_in_dim(summed, (1 - core) * rows, rows, 0))
    extra = 2 * (columns - steps * (TILE + TILE // 2))
    return pl.pallas_call(
        functools.partial(finish_kernel, steps),
        grid=(1,),
        in_specs=[
            pl.BlockSpec(memory_space=pltpu.SMEM),
            whole(summed.shape),
            whole(other.shape),
        ],
        out_specs=[whole((rows, 2, hidden)), whole((rows, hidden))]
        + [whole((rows, extra))] * (extra > 0),
        out_shape=[
            jax.ShapeDtypeStruct((rows, 2, hidden), F32),
            jax.ShapeDtypeStruct((rows, hidden), F32),
        ]
        + [jax.ShapeDtypeStruct((rows, extra), F32)] * (extra > 0),
        compiler_params=pltpu.CompilerParams(vmem_limit_bytes=VMEM_LIMIT),
        cost_estimate=pl.CostEstimate(
            flops=4 * rows * columns, bytes_accessed=16 * rows * columns, transcendentals=0
        ),
        name="finish_gradients",
    )(core.reshape(1).astype(jnp.int32), summed, other)


def halves(proj, out):
    first = lax.axis_index("core") == 0
    half = (proj.shape[1] + out.shape[1]) // 2
    late = jnp.concatenate([proj[:, half:], out], axis=1)
    early = proj[:, :half]
    return jnp.where(first, early, late), jnp.where(first, late, early)


def body(
    hidden_in,
    cotangent,
    seq_lengths,
    deal_order,
    mixer_gain,
    mixer_project,
    mixer_kernel,
    mixer_output,
    first_gain,
    first_gateup,
    first_down,
    attend_gain,
    attend_project,
    query_gain,
    key_gain,
    attend_output,
    second_gain,
    second_gateup,
    second_down,
):
    shards = lax.axis_size(TOKEN_AXES)
    contexts = lax.axis_size(CTX_AXES)
    members = lax.axis_size("tp")
    row_count, width = hidden_in.shape
    piece_rows = row_count // shards
    part_rows = piece_rows // members
    chunk = row_count // members
    device = lax.axis_index(TOKEN_AXES)
    own = lax.axis_index("tp")
    core = lax.axis_index("core")
    core_ref = core.reshape(1).astype(jnp.int32)
    depth = mixer_gain.shape[0]
    channels = mixer_output.shape[0]
    hidden = first_down.shape[0]
    heads_width = attend_output.shape[0]
    steps = -(-hidden // TILE)
    padded = steps * TILE
    ffn_width = 3 * padded
    block = TILE + TILE // 2

    def pack_ffn(gateup, down):
        wide = jnp.pad(gateup, ((0, 0), (0, 0), (0, padded - hidden)))
        wide = wide.reshape(depth, 2, steps, TILE).transpose(0, 2, 1, 3).reshape(depth, -1)
        return [wide, jnp.pad(down.T, ((0, 0), (0, padded - hidden)))]

    mixer_pack = jnp.concatenate([mixer_project.reshape(depth, -1), mixer_output.T], axis=1)
    first_pack = jnp.concatenate(
        pack_ffn(first_gateup, first_down) + [attend_project, attend_output.T], axis=1
    )
    second_pack = jnp.concatenate(pack_ffn(second_gateup, second_down), axis=1)
    piece_table = deal_order.reshape(shards, shards, piece_rows)[:, :, 0]
    anchor = piece_table // row_count
    anchor_piece = piece_table % row_count // piece_rows
    send_piece = jnp.sum(jnp.where(anchor == device, anchor_piece, 0), axis=1)
    my_anchor = lax.dynamic_index_in_dim(anchor, device, 0, keepdims=False)
    gains_row = jnp.concatenate(
        [mixer_gain, first_gain, attend_gain, second_gain, jnp.zeros((width - 4 * depth,), BF16)]
    )

    def my_part(rows):
        parts = rows.reshape(shards, members, part_rows, width)
        return lax.dynamic_index_in_dim(parts, own, 1, keepdims=False)[send_piece]

    outgoing = jnp.concatenate(
        [
            my_part(hidden_in),
            my_part(cotangent),
            jnp.broadcast_to(gains_row, (shards, 1, width)),
        ],
        axis=1,
    )
    arrived = lax.all_to_all(outgoing, TOKEN_AXES, split_axis=0, concat_axis=0, tiled=True)
    arrived, mixer_pack, first_pack = lax.optimization_barrier((arrived, mixer_pack, first_pack))
    first_all = lax.all_gather(first_pack, TOKEN_AXES, axis=0, tiled=True)
    second_all = lax.all_gather(second_pack, TOKEN_AXES, axis=0, tiled=True)
    project_b = first_all[:, ffn_width : ffn_width + attend_project.shape[1]]
    output_b_t = first_all[:, ffn_width + attend_project.shape[1] :]
    mixer_all = gather_pack(mixer_pack)
    project_a = mixer_all[:, : 3 * channels]
    output_a_t = mixer_all[:, 3 * channels :]
    gains = (
        arrived[:, 2 * part_rows, : 4 * depth]
        .reshape(shards, 4, depth)
        .transpose(1, 0, 2)
        .reshape(4, width)
        .astype(F32)
    )
    gain_a, gain_f, gain_b, gain_s = gains[0], gains[1], gains[2], gains[3]
    parts = arrived[:, : 2 * part_rows][my_anchor]
    own_tokens = parts[:, :part_rows].reshape(chunk, width)
    own_back = parts[:, part_rows:].reshape(chunk, width)
    stream0 = own_tokens.astype(F32)
    upstream = own_back.astype(F32)
    both = tp_gather(jnp.concatenate([own_tokens, own_back]))
    back_s = jnp.concatenate([slot[chunk:] for slot in both])

    gathered = jnp.arange(row_count)
    member_of = (own - gathered // chunk) % members
    offsets = (
        gathered % chunk // part_rows * piece_rows + member_of * part_rows + gathered % part_rows
    )
    to_gathered = (offsets[:, None] == gathered[None, :]).astype(BF16)
    to_dealt = (offsets[None, :] == gathered[:, None]).astype(BF16)
    tokens = times(to_dealt, jnp.concatenate([slot[:chunk] for slot in both]))

    kernel_taps = mixer_kernel.shape[0]
    halo = kernel_taps - 1
    local_rows = device * row_count + jnp.arange(row_count)
    halo_segment, unused = locate(
        seq_lengths, local_rows[0] - halo + jnp.arange(row_count + halo)
    )
    segment, places = locate(seq_lengths, device * row_count + offsets)
    ctx = lax.axis_index(CTX_AXES)
    group_rows = jnp.concatenate(
        [
            (lax.axis_index(GROUP_AXES) * contexts + (ctx ^ mask)) * row_count + offsets
            for mask in range(contexts)
        ]
    )
    key_segment, key_places = locate(seq_lengths, group_rows)
    allowed = (segment[None, :] == key_segment[:, None]) & (key_places[:, None] <= places[None, :])
    barred = jnp.where(allowed, 0.0, NEGATIVE).astype(BF16)
    half_dim = HD // 2
    frequency = ROPE_BASE ** (-(jnp.arange(half_dim).astype(F32) * 2.0 / HD))
    angles = places.astype(F32)[:, None] * frequency[None, :]
    cosine = jnp.cos(angles)
    sine = jnp.sin(angles)

    kernel_local = lax.dynamic_slice_in_dim(mixer_kernel, own * channels, channels, 1).astype(F32)
    mixer_in = norm_rows(tokens, gain_a).astype(BF16)
    mixer_in_other = swap_core(mixer_in)
    halo_pad = 16
    halo_in = from_behind(mixer_in[row_count - halo_pad :], 1)
    proj_a = times(jnp.concatenate([halo_in, mixer_in]), project_a)
    proj_b_part = proj_a[:, :channels]
    proj_c_part = proj_a[halo_pad:, channels : 2 * channels]
    proj_x_part = proj_a[:, 2 * channels :]
    extended = (proj_b_part * proj_x_part)[halo_pad - halo :].astype(BF16).astype(F32)
    conv_out = shortconv(extended, kernel_local, halo_segment)
    gated_rows = (proj_c_part * conv_out).astype(BF16)
    gated_parts = arrange(to_gathered, gated_rows)
    stream1, normed = add_norm(
        tp_scatter(tp_chunks(times_t(gated_parts, output_a_t))), stream0, gain_f
    )

    normed_f = tp_gather(normed)
    stream2, normed = add_norm(
        tp_scatter(ffn_forward(normed_f, first_all, steps)), stream1, gain_b
    )

    groups = H // KVH
    score_scale = HD ** (-0.5)
    qgain_f = query_gain.astype(F32)[None]
    kgain_f = key_gain.astype(F32)[None]
    attend_in = jnp.concatenate(tp_gather(normed))
    proj_b = times(attend_in, project_b)
    kv_width = 2 * HD * (proj_b.shape[1] // (HD * (groups + 2)))
    query_b, key_value = one_step(
        functools.partial(heads_kernel, groups),
        [proj_b, cosine, sine, qgain_f, kgain_f],
        [
            jax.ShapeDtypeStruct((row_count, heads_width), BF16),
            jax.ShapeDtypeStruct((row_count, kv_width), BF16),
        ],
        SMALL_LIMIT,
        "heads",
        20 * proj_b.size,
    )
    key_value_z = swap_ctx(key_value, 2)
    key_value_core = swap_core(jnp.concatenate([key_value, key_value_z]))
    key_value_all = jnp.concatenate(
        [key_value, key_value_core[:row_count], key_value_z, key_value_core[row_count:]]
    )
    attend_flops = 2 * key_value_all.shape[0] * query_b.size
    (attended,) = one_step(
        functools.partial(attend_kernel, score_scale, HD),
        [query_b, key_value_all, barred],
        [jax.ShapeDtypeStruct(query_b.shape, BF16)],
        MIDDLE_LIMIT,
        "attend",
        2 * attend_flops,
    )
    stream3, normed = add_norm(
        tp_scatter(tp_chunks(times_t(attended, output_b_t))), stream2, gain_s
    )

    normed_s = tp_gather(normed)
    d_chunks, out_chunks, keep, side = ffn_backward(
        core_ref, normed_s, [back_s], second_all, steps, True
    )
    d_stream3, back_b, gain_s_grad = norm_backward(
        tp_scatter(d_chunks), stream3, gain_s, upstream
    )
    out_others = [shift_tp(out_chunks[k], -k) for k in range(1, members)]
    side_other = swap_core(side)
    ffn_lefts = [(side, 0), (side_other, 0), (side, 1), (side_other, 1)]
    ffn_cols = steps * block
    side_start = 2 * width // block
    partial = gradient(
        ffn_lefts, keep, side_other, side_start, block, steps, padded, width, ffn_cols, 0, None
    )

    back_b = tp_gather(back_b)
    back_b, partial = lax.optimization_barrier((back_b, partial))
    second_sums = sum_chips(partial)
    back_b = jnp.concatenate(back_b)
    back_b_other = swap_core(back_b)
    attend_in_other = swap_core(attend_in)
    d_attended_b = times(back_b, output_b_t).astype(BF16)
    pair_rows = 2 * row_count
    d_query, near, cross, qgain_grad = one_step(
        functools.partial(attend_backward_kernel, score_scale),
        [query_b, d_attended_b, key_value_all, barred, proj_b, cosine, sine, qgain_f],
        [
            jax.ShapeDtypeStruct(query_b.shape, BF16),
            jax.ShapeDtypeStruct((pair_rows, kv_width), F32),
            jax.ShapeDtypeStruct((pair_rows, kv_width), BF16),
            jax.ShapeDtypeStruct((1, HD), F32),
        ],
        MIDDLE_LIMIT,
        "attend_backward",
        5 * attend_flops,
    )
    cross = swap_core(cross)
    far = (near[row_count:] + cross[row_count:].astype(F32)).astype(BF16)
    d_proj_b, kgain_grad = one_step(
        functools.partial(assemble_kernel, groups),
        [d_query, near, cross, swap_ctx(far, 2), proj_b, cosine, sine, kgain_f],
        [jax.ShapeDtypeStruct(proj_b.shape, BF16), jax.ShapeDtypeStruct((1, HD), F32)],
        SMALL_LIMIT,
        "assemble",
        20 * proj_b.size,
    )
    d_stream2, back_f, gain_b_grad = norm_backward(
        tp_scatter(tp_chunks(times_t(d_proj_b, project_b))), stream2, gain_b, d_stream3
    )
    keep, send = halves(d_proj_b, attended)
    first_core = core == 0
    attend_cols = keep.shape[1]
    small_tile = 2 * (heads_width + attend_project.shape[1]) // 16
    third = gradient(
        [
            (attend_in, 0),
            (attend_in_other, 0),
            (jnp.where(first_core, attend_in, back_b), 0),
            (jnp.where(first_core, attend_in_other, back_b_other), 0),
        ],
        keep,
        swap_core(send),
        0,
        small_tile,
        attend_cols // small_tile,
        attend_project.shape[1] - attend_cols,
        width,
        ffn_cols + attend_cols,
        ffn_cols // small_tile,
        None,
    )

    back_f = tp_gather(back_f)
    back_f, third = lax.optimization_barrier((back_f, third))
    left_x, left_b = jnp.concatenate(normed_f), jnp.concatenate(back_f)
    left_others = [swap_core(left_x), swap_core(left_b)]
    d_chunks, unused, keep, side = ffn_backward(
        core_ref, normed_f, back_f, first_all, steps, False
    )
    d_chunks, left_others = lax.optimization_barrier((d_chunks, left_others))
    d_chunks, side_other = lax.optimization_barrier((d_chunks, swap_core(side)))
    ffn_lefts = [(left_x, 0), (left_others[0], 0), (left_b, 0), (left_others[1], 0)]
    partial = gradient(
        ffn_lefts,
        keep,
        side_other,
        0,
        block,
        steps,
        padded,
        width,
        ffn_cols + attend_cols,
        0,
        third,
    )

    d_parts, partial = lax.optimization_barrier((tp_scatter(d_chunks), partial))
    d_stream1, back_a, gain_f_grad = norm_backward(d_parts, stream1, gain_f, d_stream2)

    back_a = tp_gather(back_a)
    first_sums = sum_chips(partial)
    back_a = arrange(to_dealt, jnp.concatenate(back_a))
    back_a_other = swap_core(back_a)
    d_gated = times(back_a, output_a_t)
    d_cgate = d_gated * conv_out
    d_conv = d_gated * proj_c_part
    unused, pullback = jax.vjp(
        lambda ext_rows, kernel_in: shortconv(ext_rows, kernel_in, halo_segment),
        extended,
        kernel_local,
    )
    d_extended, kernel_grad = pullback(d_conv)
    returned = from_behind(d_extended[:halo], -1)
    d_product = d_extended[halo:] + jnp.concatenate(
        [jnp.zeros((row_count - halo, channels), F32), returned]
    )
    d_proj_a = jnp.concatenate(
        [
            d_product * proj_x_part[halo_pad:],
            d_cgate,
            d_product * proj_b_part[halo_pad:],
        ],
        axis=1,
    ).astype(BF16)
    d_proj_a, out_others = lax.optimization_barrier((d_proj_a, out_others))
    stream4 = stream3 + add_parts([out_chunks[0], *out_others])
    d_chunks = tp_chunks(times_t(arrange(to_gathered, d_proj_a), project_a))
    keep, send = halves(d_proj_a, gated_rows)
    mixer_cols = keep.shape[1]
    partial = gradient(
        [
            (mixer_in, 0),
            (mixer_in_other, 0),
            (jnp.where(first_core, mixer_in, back_a), 0),
            (jnp.where(first_core, mixer_in_other, back_a_other), 0),
        ],
        keep,
        swap_core(send),
        0,
        mixer_cols,
        1,
        3 * channels - mixer_cols,
        width,
        mixer_cols,
        0,
        None,
    )
    kernel_cols = kernel_taps * channels
    gain_start = kernel_cols + 2 * HD
    shared = jnp.concatenate([kernel_grad.reshape(-1), qgain_grad[0], kgain_grad[0]])
    early_gains = [
        grad.reshape(shards, depth) for grad in (gain_f_grad, gain_b_grad, gain_s_grad)
    ]
    early_row = jnp.concatenate(
        [
            jnp.broadcast_to(shared, (shards, gain_start)),
            jnp.pad(
                jnp.concatenate(early_gains, axis=1),
                ((0, 0), (0, width - gain_start - 3 * depth)),
            ),
        ],
        axis=1,
    )
    d_parts, early_row = lax.optimization_barrier((tp_scatter(d_chunks), early_row))
    unused, d_stream0, gain_a_grad = norm_backward(d_parts, stream0, gain_a, d_stream1)

    slot_for_anchor = jnp.sum(
        jnp.where(
            my_anchor[None, :] == jnp.arange(shards)[:, None], jnp.arange(shards)[None, :], 0
        ),
        axis=1,
    )
    late_start = gain_start + 3 * depth
    late_row = jnp.pad(
        gain_a_grad.reshape(shards, depth), ((0, 0), (late_start, width - late_start - depth))
    )
    leaving = jnp.concatenate(
        [d_stream0, stream4.astype(BF16), (early_row + late_row).astype(BF16)]
    )
    line = jnp.arange(shards * piece_rows)
    target, item = line // piece_rows, line % piece_rows
    source = jnp.where(
        item < 2 * part_rows,
        item // part_rows * chunk
        + jnp.repeat(slot_for_anchor, piece_rows) * part_rows
        + item % part_rows,
        jnp.where(item == 2 * part_rows, 2 * chunk + target, -1),
    )
    to_leaving = (source[:, None] == jnp.arange(leaving.shape[0])[None, :]).astype(BF16)
    leaving = arrange(to_leaving, leaving)
    home = lax.all_to_all(
        leaving.reshape(shards, piece_rows, width),
        TOKEN_AXES,
        split_axis=0,
        concat_axis=0,
        tiled=True,
    )
    mixer_home = lax.all_to_all(
        partial.reshape(shards, depth, mixer_cols),
        TOKEN_AXES,
        split_axis=0,
        concat_axis=0,
        tiled=True,
    )
    second_grads = finish(second_sums, steps, hidden)
    home, mixer_home, second_grads = lax.optimization_barrier((home, mixer_home, second_grads))
    place = jnp.arange(2 * chunk + 8)
    small_line = (place == 2 * chunk) | (place == 2 * chunk + 1)
    wanted = (
        place % chunk // part_rows * piece_rows
        + place // chunk * part_rows
        + place % part_rows
    )
    to_payload = jnp.where(
        (place < 2 * chunk)[:, None],
        wanted[:, None] == line[None, :],
        small_line[:, None] & (item == 2 * part_rows)[None, :],
    ).astype(BF16)
    payload = times(to_payload, home.reshape(shards * piece_rows, width))
    rounded = payload.astype(BF16).astype(F32)
    payload = jnp.where((place == 2 * chunk + 1)[:, None], payload - rounded, payload)
    last = tp_gather(payload.astype(BF16))
    home_rows = (
        jnp.repeat(jnp.tile(send_piece, members), part_rows) * piece_rows
        + member_of * part_rows
        + gathered % part_rows
    )
    to_arrival = (home_rows[None, :] == gathered[:, None]).astype(BF16)
    input_gradient = arrange(to_arrival, jnp.concatenate([slot[:chunk] for slot in last]))
    layer_out = arrange(to_arrival, jnp.concatenate([slot[chunk : 2 * chunk] for slot in last]))
    first_sums, layer_out, input_gradient = lax.optimization_barrier(
        (first_sums, layer_out, input_gradient)
    )
    *first_grads, attend_grads = finish(first_sums, steps, hidden)
    first_grads, attend_grads, mixer_home = lax.optimization_barrier(
        (first_grads, attend_grads, mixer_home)
    )
    mixer_home = mixer_home.reshape(shards // CORES, CORES, depth, mixer_cols)
    mixer_grads = jnp.sum(mixer_home.astype(F32), axis=0)
    mixer_grads = jnp.concatenate([mixer_grads[0], mixer_grads[1]], axis=1)
    smalls = [
        slot[2 * chunk].astype(F32) + slot[2 * chunk + 1].astype(F32) for slot in last
    ]
    totals = sum(smalls)
    kernel_rows = jnp.stack([small[:kernel_cols].reshape(kernel_taps, channels) for small in smalls])
    kernel_total = jnp.concatenate(
        [
            lax.dynamic_index_in_dim(kernel_rows, (own - member) % members, 0, keepdims=False)
            for member in range(members)
        ],
        axis=1,
    )
    qgain_total = totals[kernel_cols : kernel_cols + HD]
    kgain_total = totals[kernel_cols + HD : kernel_cols + 2 * HD]
    gain_totals = totals[gain_start : gain_start + 4 * depth].reshape(4, depth)

    gateup_s_grad, down_s_grad = second_grads
    gateup_f_grad, down_f_grad = first_grads
    proj_cols = attend_project.shape[1]
    return (
        layer_out,
        input_gradient,
        gain_totals[3],
        mixer_grads[:, : 3 * channels].reshape(depth, 3, channels),
        kernel_total,
        mixer_grads[:, 3 * channels :].T,
        gain_totals[0],
        gateup_f_grad,
        down_f_grad.T,
        gain_totals[1],
        attend_grads[:, :proj_cols],
        qgain_total,
        kgain_total,
        attend_grads[:, proj_cols:].T,
        gain_totals[2],
        gateup_s_grad,
        down_s_grad.T,
    )


def solution(mesh):
    names = TOKEN_AXES + ("tp",)
    rings = mesh.shape["fsdp"] // 2, 2, mesh.shape["ctx"] // 2, 2, mesh.shape["tp"]
    tokens = P(TOKEN_AXES, None)
    rows = P(TOKEN_AXES)
    three = P(TOKEN_AXES, None, "tp")
    two = P(TOKEN_AXES, "tp")
    turned = P("tp", TOKEN_AXES)
    return jax.shard_map(
        body,
        mesh=Mesh(mesh.devices.reshape(rings), names),
        in_specs=(
            tokens, tokens, P(), P(),
            rows, three, P(), turned,
            rows, three, turned,
            rows, two, P(), P(), turned,
            rows, three, turned,
        ),
        out_specs=(
            tokens, tokens,
            rows, three, P(), turned,
            rows, three, turned,
            rows, two, P(), P(), turned,
            rows, three, turned,
        ),
        check_vma=False,
    )
```

```python
import functools

import jax
import jax.numpy as jnp
from jax import lax
from jax.experimental import pallas as pl
from jax.experimental.pallas import tpu as pltpu
from jax.sharding import Mesh, PartitionSpec as P

H = 24
KVH = 8
HD = 64

EPSILON = 1e-05
ROPE_BASE = 1000000.0
NEGATIVE = -1e30

CHIP_AXES = ("x", "z_hi", "z_lo")
TOKEN_AXES = CHIP_AXES + ("core",)
GROUP_AXES = ("x", "z_hi")
CTX_AXES = ("z_lo", "core")
Z_AXES = ("z_hi", "z_lo")
CORES = 2
TILE = 256
VMEM_LIMIT = 48 * 1024 * 1024
MIDDLE_LIMIT = 24 * 1024 * 1024
SMALL_LIMIT = 12 * 1024 * 1024
F32 = jnp.float32
BF16 = jnp.bfloat16


def norm_rows(values, scales):
    return values * lax.rsqrt(jnp.mean(values * values, axis=-1, keepdims=True) + EPSILON) * scales


def locate(lengths, positions):
    seq_ends = jnp.cumsum(lengths)
    segment = jnp.sum((positions[:, None] >= seq_ends[None, :]).astype(jnp.int32), axis=1)
    starts = seq_ends - lengths
    first_row = jnp.sum(
        jnp.where(segment[:, None] == jnp.arange(lengths.shape[0])[None, :], starts[None, :], 0),
        axis=1,
    )
    return (segment, positions - first_row)


def shortconv(extended, kernel_in, segment):
    kernel_taps = kernel_in.shape[0]
    out_rows = extended.shape[0] - kernel_taps + 1
    result = kernel_in[0] * extended[kernel_taps - 1 :]
    for t in range(1, kernel_taps):
        earlier = extended[kernel_taps - 1 - t : kernel_taps - 1 - t + out_rows]
        same_seq = (
            segment[kernel_taps - 1 - t : kernel_taps - 1 - t + out_rows]
            == segment[kernel_taps - 1 :]
        ).astype(F32)[:, None]
        result = result + kernel_in[t] * earlier * same_seq
    return result


def from_behind(block, distance):
    devices = range(lax.axis_size(CTX_AXES))
    route = [(i - distance, i) for i in devices if i - distance in devices]
    return lax.ppermute(block, CTX_AXES, route)


def swap_ctx(block, mask):
    return lax.ppermute(block, CTX_AXES, [(i, i ^ mask) for i in range(lax.axis_size(CTX_AXES))])


def swap_core(block):
    return lax.ppermute(block, "core", [(0, 1), (1, 0)])


def shift_ring(block, axis, distance):
    ring = lax.axis_size(axis)
    return lax.ppermute(block, axis, [(i, (i + distance) % ring) for i in range(ring)])


def shift_tp(block, distance):
    members = lax.axis_size("tp")
    return lax.ppermute(block, "tp", [(i, (i + distance) % members) for i in range(members)])


def tp_gather(shard):
    return [shard] + [shift_tp(shard, k) for k in range(1, lax.axis_size("tp"))]


def tp_chunks(partial):
    rows = partial.shape[0] // lax.axis_size("tp")
    return [
        partial[k * rows : (k + 1) * rows].astype(F32 if k == 0 else BF16)
        for k in range(lax.axis_size("tp"))
    ]


def tp_scatter(chunks):
    return [chunks[0]] + [shift_tp(chunks[k], -k) for k in range(1, len(chunks))]


def add_parts(parts):
    total = parts[0]
    for part in parts[1:]:
        total = total + part.astype(F32)
    return total


def arrange(order, rows):
    return times(order, rows).astype(BF16)


def times(left, right):
    return lax.dot_general(left, right, (((1,), (0,)), ((), ())), preferred_element_type=F32)


def times_t(left, right):
    return lax.dot_general(left, right, (((1,), (1,)), ((), ())), preferred_element_type=F32)


def times_rows(left, right):
    return lax.dot_general(left, right, (((0,), (0,)), ((), ())), preferred_element_type=F32)


def assemble(chunk_refs, target):
    rows = chunk_refs[0].shape[0]
    for k, ref in enumerate(chunk_refs):
        target[k * rows : (k + 1) * rows, :] = ref[...]


def spread(total, chunk_refs):
    rows = chunk_refs[0].shape[0]
    for k, ref in enumerate(chunk_refs):
        ref[...] = total[k * rows : (k + 1) * rows, :].astype(ref.dtype)


def whole(shape):
    return pl.BlockSpec(shape, lambda *_: (0,) * len(shape))


def one_step(kernel, operands, out_shape, limit, name, flops):
    size = sum(v.size * v.dtype.itemsize for v in list(operands) + list(out_shape))
    return pl.pallas_call(
        kernel,
        grid=(1,),
        in_specs=[whole(v.shape) for v in operands],
        out_specs=[whole(v.shape) for v in out_shape],
        out_shape=out_shape,
        compiler_params=pltpu.CompilerParams(vmem_limit_bytes=limit),
        cost_estimate=pl.CostEstimate(flops=flops, bytes_accessed=size, transcendentals=0),
        name=name,
    )(*operands)


def sum_refs(refs):
    total = refs[0][...]
    for ref in refs[1:]:
        total = total + ref[...].astype(F32)
    return total


def add_norm_kernel(*refs):
    stream_ref, gain_ref, out_ref, normed_ref = refs[-4:]
    stream = stream_ref[...] + sum_refs(refs[:-4])
    out_ref[...] = stream
    normed_ref[...] = norm_rows(stream, gain_ref[...]).astype(BF16)


def add_norm(parts, stream, gain):
    return one_step(
        add_norm_kernel,
        [*parts, stream, gain[None]],
        [jax.ShapeDtypeStruct(stream.shape, F32), jax.ShapeDtypeStruct(stream.shape, BF16)],
        SMALL_LIMIT,
        "add_norm",
        10 * stream.size,
    )


def norm_backward_kernel(*refs):
    stream_ref, gain_ref, upward_ref, out_ref, rounded_ref, gain_grad_ref = refs[-6:]
    stream = stream_ref[...]
    d_normed = sum_refs(refs[:-6])
    spread_of = lax.rsqrt(jnp.mean(stream * stream, axis=1, keepdims=True) + EPSILON)
    gain_grad_ref[...] = jnp.sum(d_normed * stream * spread_of, axis=0, keepdims=True)
    scaled = d_normed * gain_ref[...]
    inner = jnp.mean(scaled * stream, axis=1, keepdims=True)
    result = upward_ref[...] + spread_of * scaled - stream * (
        spread_of * spread_of * spread_of * inner
    )
    out_ref[...] = result
    rounded_ref[...] = result.astype(BF16)


def norm_backward(parts, stream, gain, upward):
    out, rounded, gain_grad = one_step(
        norm_backward_kernel,
        [*parts, stream, gain[None], upward],
        [
            jax.ShapeDtypeStruct(stream.shape, F32),
            jax.ShapeDtypeStruct(stream.shape, BF16),
            jax.ShapeDtypeStruct((1, stream.shape[1]), F32),
        ],
        SMALL_LIMIT,
        "norm_backward",
        20 * stream.size,
    )
    return out, rounded, gain_grad[0]


def weight_specs(depth, steps):
    return [
        pl.BlockSpec((depth, 2 * TILE), lambda j: (0, j)),
        pl.BlockSpec((depth, TILE), lambda j: (0, 2 * steps + j)),
    ]


def chunk_shapes(count, rows, width):
    return [jax.ShapeDtypeStruct((rows, width), F32 if k == 0 else BF16) for k in range(count)]


def ffn_forward_kernel(count, *refs):
    x_refs, (gu_ref, dn_ref), outs = refs[:count], refs[count : count + 2], refs[count + 2 : -2]
    x_all, total = refs[-2:]
    step = pl.program_id(0)

    @pl.when(step == 0)
    def _():
        assemble(x_refs, x_all)
        total[...] = jnp.zeros_like(total)

    both = times(x_all[...], gu_ref[...])
    gate, up = both[:, :TILE], both[:, TILE:]
    active = (gate * jax.nn.sigmoid(gate) * up).astype(BF16)
    total[...] += times_t(active, dn_ref[...])

    @pl.when(step == pl.num_programs(0) - 1)
    def _():
        spread(total[...], outs)


def ffn_forward(chunks, pack, steps):
    count, (rows, width) = len(chunks), chunks[0].shape
    tokens = count * rows
    return pl.pallas_call(
        functools.partial(ffn_forward_kernel, count),
        grid=(steps,),
        in_specs=[whole((rows, width))] * count + weight_specs(width, steps),
        out_specs=[whole((rows, width))] * count,
        out_shape=chunk_shapes(count, rows, width),
        scratch_shapes=[pltpu.VMEM((tokens, width), BF16), pltpu.VMEM((tokens, width), F32)],
        compiler_params=pltpu.CompilerParams(vmem_limit_bytes=VMEM_LIMIT),
        cost_estimate=pl.CostEstimate(
            flops=2 * tokens * width * 3 * TILE * steps,
            bytes_accessed=2 * width * 3 * TILE * steps,
            transcendentals=tokens * TILE * steps,
        ),
        name="ffn_forward",
    )(*chunks, pack, pack)


def ffn_backward_kernel(count, back_count, forward, core_ref, *refs):
    x_refs, b_refs = refs[:count], refs[count : count + back_count]
    place = count + back_count
    gu_ref, dn_ref = refs[place : place + 2]
    place += 2
    back_outs = refs[place : place + count]
    place += count
    if forward:
        outs = refs[place : place + count]
        place += count
    keep_ref, side_ref = refs[place : place + 2]
    scratch = refs[place + 2 :]
    x_all, b_all, d_total = scratch[:3]
    step = pl.program_id(0)
    width = x_all.shape[1]

    @pl.when(step == 0)
    def _():
        assemble(x_refs, x_all)
        assemble(b_refs, b_all)
        if forward:
            side_ref[:, :width] = x_all[...]
            side_ref[:, width : 2 * width] = b_all[...]
        d_total[...] = jnp.zeros_like(d_total)
        if forward:
            scratch[3][...] = jnp.zeros_like(scratch[3])

    both = times(x_all[...], gu_ref[...])
    gate, up = both[:, :TILE], both[:, TILE:]
    d_active = times(b_all[...], dn_ref[...])
    sigmoid = jax.nn.sigmoid(gate)
    silu = gate * sigmoid
    active = (silu * up).astype(BF16)
    if forward:
        scratch[3][...] += times_t(active, dn_ref[...])
    d_gate = (d_active * up * (sigmoid * (1.0 + gate * (1.0 - sigmoid)))).astype(BF16)
    d_up = (d_active * silu).astype(BF16)
    d_total[...] += times_t(jnp.concatenate([d_gate, d_up], axis=1), gu_ref[...])
    first = core_ref[0] == 0
    half = TILE // 2
    low, high = active[:, :half], active[:, half:]
    offset = 2 * width if forward else 0
    wide = pl.multiple_of(step * TILE, TILE)
    narrow = pl.multiple_of(pl.num_programs(0) * TILE + step * half, half)
    side_wide = pl.multiple_of(offset + wide, TILE)
    side_narrow = pl.multiple_of(offset + narrow, half)

    @pl.when(first)
    def _():
        keep_ref[:, pl.ds(wide, TILE)] = d_gate
        keep_ref[:, pl.ds(narrow, half)] = low
        side_ref[:, pl.ds(side_wide, TILE)] = d_up
        side_ref[:, pl.ds(side_narrow, half)] = high

    @pl.when(jnp.logical_not(first))
    def _():
        keep_ref[:, pl.ds(wide, TILE)] = d_up
        keep_ref[:, pl.ds(narrow, half)] = high
        side_ref[:, pl.ds(side_wide, TILE)] = d_gate
        side_ref[:, pl.ds(side_narrow, half)] = low

    @pl.when(step == pl.num_programs(0) - 1)
    def _():
        spread(d_total[...], back_outs)
        if forward:
            spread(scratch[3][...], outs)


def ffn_backward(core, chunks, back_chunks, pack, steps, forward):
    count, (rows, width) = len(chunks), chunks[0].shape
    tokens = count * rows
    block = TILE + TILE // 2
    ways = 2 if forward else 1
    side_width = (2 * width if forward else 0) + steps * block
    results = pl.pallas_call(
        functools.partial(ffn_backward_kernel, count, len(back_chunks), forward),
        grid=(steps,),
        in_specs=[pl.BlockSpec(memory_space=pltpu.SMEM)]
        + [whole(v.shape) for v in (*chunks, *back_chunks)]
        + weight_specs(width, steps),
        out_specs=[whole((rows, width))] * (ways * count)
        + [whole((tokens, steps * block)), whole((tokens, side_width))],
        out_shape=chunk_shapes(count, rows, width) * ways
        + [
            jax.ShapeDtypeStruct((tokens, steps * block), BF16),
            jax.ShapeDtypeStruct((tokens, side_width), BF16),
        ],
        scratch_shapes=[pltpu.VMEM((tokens, width), BF16)] * 2
        + [pltpu.VMEM((tokens, width), F32)] * ways,
        compiler_params=pltpu.CompilerParams(vmem_limit_bytes=VMEM_LIMIT),
        cost_estimate=pl.CostEstimate(
            flops=2 * tokens * width * (4 + ways) * TILE * steps,
            bytes_accessed=2 * width * 3 * TILE * steps + 4 * tokens * side_width,
            transcendentals=tokens * TILE * steps,
        ),
        name="ffn_both" if forward else "ffn_backward",
    )(core, *chunks, *back_chunks, pack, pack)
    return results[:count], results[count : ways * count], results[-2], results[-1]


def gradient_kernel(edge, cut, *refs):
    one_own, one_other, two_own, two_other, own_ref, other_ref = refs[:6]
    out_ref = refs[-1]
    step = pl.program_id(0)

    def product(own_left, other_left, columns):
        total = times_rows(own_left[...], own_ref[:, columns])
        total += times_rows(other_left[...], other_ref[:, columns])
        out_ref[:, columns] = total.astype(BF16)

    @pl.when(step < edge)
    def _():
        product(one_own, one_other, slice(None))

    @pl.when(step > edge if cut else step >= edge)
    def _():
        product(two_own, two_other, slice(None))

    if cut:

        @pl.when(step == edge)
        def _():
            product(one_own, one_other, slice(0, cut))
            product(two_own, two_other, slice(cut, None))


def gradient(lefts, own, other, other_start, block, steps, columns, width, out_width, out_start, target):
    tokens = own.shape[0]
    edge, cut = divmod(columns, block)

    def left_spec(index):
        return pl.BlockSpec((tokens, width), lambda j: (0, index))

    in_specs = [left_spec(index) for unused, index in lefts] + [
        pl.BlockSpec((tokens, block), lambda j: (0, j)),
        pl.BlockSpec((tokens, block), lambda j: (0, other_start + j)),
    ]
    operands = [array for array, unused in lefts] + [own, other]
    aliases = {}
    if target is not None:
        in_specs.append(pl.BlockSpec(memory_space=pl.ANY))
        operands.append(target)
        aliases = {len(operands) - 1: 0}
    return pl.pallas_call(
        functools.partial(gradient_kernel, edge, cut),
        grid=(steps,),
        in_specs=in_specs,
        out_specs=pl.BlockSpec((width, block), lambda j: (0, out_start + j)),
        out_shape=jax.ShapeDtypeStruct((width, out_width), BF16),
        input_output_aliases=aliases,
        compiler_params=pltpu.CompilerParams(vmem_limit_bytes=VMEM_LIMIT),
        cost_estimate=pl.CostEstimate(
            flops=4 * tokens * width * block * steps,
            bytes_accessed=2 * width * block * steps,
            transcendentals=0,
        ),
        name="weight_gradient",
    )(*operands)


def turn(rows, cosine, sine):
    half = rows.shape[1] // 2
    first, second = rows[:, :half], rows[:, half:]
    return jnp.concatenate(
        [first * cosine - second * sine, second * cosine + first * sine], axis=1
    )


def head_backward(d_rows, raw, cosine, sine, gain):
    d_normed = turn(d_rows, cosine, -sine)
    spread_of = lax.rsqrt(jnp.mean(raw * raw, axis=1, keepdims=True) + EPSILON)
    d_gain = jnp.sum(d_normed * raw * spread_of, axis=0, keepdims=True)
    scaled = d_normed * gain
    inner = jnp.mean(scaled * raw, axis=1, keepdims=True)
    d_raw = spread_of * scaled - raw * (spread_of * spread_of * spread_of * inner)
    return d_raw.astype(BF16), d_gain


def heads_kernel(groups, raw_ref, cos_ref, sin_ref, query_gain_ref, key_gain_ref, q_ref, kv_ref):
    size = query_gain_ref.shape[1]
    kv_heads = raw_ref.shape[1] // ((groups + 2) * size)
    cosine, sine = cos_ref[...], sin_ref[...]
    for group in range(kv_heads):
        start = group * (groups + 2) * size
        for member in range(groups):
            raw = raw_ref[:, start + member * size : start + (member + 1) * size]
            head = group * groups + member
            rows = turn(norm_rows(raw, query_gain_ref[...]), cosine, sine)
            q_ref[:, head * size : (head + 1) * size] = rows.astype(BF16)
        start += groups * size
        rows = turn(norm_rows(raw_ref[:, start : start + size], key_gain_ref[...]), cosine, sine)
        kv_ref[:, group * size : (group + 1) * size] = rows.astype(BF16)
        value_start = (kv_heads + group) * size
        kv_ref[:, value_start : value_start + size] = raw_ref[
            :, start + size : start + 2 * size
        ].astype(BF16)


def head_probs(key, query, scale, barred):
    scores = times_t(key, query) * scale + barred
    probs = jnp.exp(scores - jnp.max(scores, axis=0, keepdims=True))
    return probs / jnp.sum(probs, axis=0, keepdims=True)


def attend_kernel(scale, size, q_ref, kv_ref, barred_ref, out_ref):
    kv_heads = kv_ref.shape[1] // (2 * size)
    groups = q_ref.shape[1] // (kv_heads * size)
    barred = barred_ref[...].astype(F32)
    for head in range(kv_heads * groups):
        group = head // groups
        columns = slice(head * size, (head + 1) * size)
        key = kv_ref[:, group * size : (group + 1) * size]
        value = kv_ref[:, (kv_heads + group) * size : (kv_heads + group + 1) * size]
        probs = head_probs(key, q_ref[:, columns], scale, barred).astype(BF16)
        out_ref[:, columns] = times_rows(value, probs).T.astype(BF16)


def attend_backward_kernel(
    scale, q_ref, do_ref, kv_ref, barred_ref, raw_ref, cos_ref, sin_ref, gain_ref,
    dq_ref, near_ref, cross_ref, gain_grad_ref,
):
    size = gain_ref.shape[1]
    kv_heads = kv_ref.shape[1] // (2 * size)
    groups = q_ref.shape[1] // (kv_heads * size)
    rows = kv_ref.shape[0] // 4
    cosine, sine, gain = cos_ref[...], sin_ref[...], gain_ref[...]
    barred = barred_ref[...].astype(F32)
    gain_grad = jnp.zeros_like(gain)
    for group in range(kv_heads):
        columns = slice(group * size, (group + 1) * size)
        value_columns = slice((kv_heads + group) * size, (kv_heads + group + 1) * size)
        key, value = kv_ref[:, columns], kv_ref[:, value_columns]
        d_key = d_value = None
        for member in range(groups):
            head = group * groups + member
            head_columns = slice(head * size, (head + 1) * size)
            query, d_out = q_ref[:, head_columns], do_ref[:, head_columns]
            probs = head_probs(key, query, scale, barred)
            d_probs = times_t(value, d_out)
            inner = jnp.sum(probs * d_probs, axis=0, keepdims=True)
            d_scores = (probs * (d_probs - inner)).astype(BF16)
            part_value = times(probs.astype(BF16), d_out)
            part_key = times(d_scores, query) * scale
            d_value = part_value if d_value is None else d_value + part_value
            d_key = part_key if d_key is None else d_key + part_key
            d_query = (times_rows(key, d_scores) * scale).T
            start = (group * (groups + 2) + member) * size
            d_raw, d_gain = head_backward(
                d_query, raw_ref[:, start : start + size], cosine, sine, gain
            )
            dq_ref[:, head_columns] = d_raw
            gain_grad += d_gain
        for part, place in ((d_key, columns), (d_value, value_columns)):
            near_ref[:rows, place] = part[:rows]
            near_ref[rows:, place] = part[2 * rows : 3 * rows]
            cross_ref[:rows, place] = part[rows : 2 * rows].astype(BF16)
            cross_ref[rows:, place] = part[3 * rows :].astype(BF16)
    gain_grad_ref[...] = gain_grad


def assemble_kernel(groups, dq_ref, near_ref, cross_ref, far_ref, raw_ref, cos_ref, sin_ref, gain_ref, out_ref, gain_grad_ref):
    size = gain_ref.shape[1]
    kv_heads = raw_ref.shape[1] // ((groups + 2) * size)
    rows = raw_ref.shape[0]
    both = near_ref[:rows, :] + cross_ref[:rows, :].astype(F32) + far_ref[...].astype(F32)
    gain_grad = jnp.zeros_like(gain_ref[...])
    for group in range(kv_heads):
        start = group * (groups + 2) * size
        out_ref[:, start : start + groups * size] = dq_ref[
            :, group * groups * size : (group + 1) * groups * size
        ]
        start += groups * size
        d_raw, d_gain = head_backward(
            both[:, group * size : (group + 1) * size],
            raw_ref[:, start : start + size],
            cos_ref[...],
            sin_ref[...],
            gain_ref[...],
        )
        gain_grad += d_gain
        out_ref[:, start : start + size] = d_raw
        value_start = (kv_heads + group) * size
        out_ref[:, start + size : start + 2 * size] = both[
            :, value_start : value_start + size
        ].astype(BF16)
    gain_grad_ref[...] = gain_grad


def sum_chips(partial):
    return lax.psum_scatter(partial, CHIP_AXES, scatter_dimension=0, tiled=True)


def fill(shape, parts):
    result = jnp.zeros(shape, BF16)
    for part, place in parts:
        result = lax.dynamic_update_slice(result, part, place)
    return result


def gather_first(pack):
    rows, columns = pack.shape
    half = columns // 2
    ring = lax.axis_size("x")
    x, z = lax.axis_index("x"), lax.axis_index(Z_AXES)
    low, high = pack[:, :half], pack[:, half:]
    low_parts = [(shift_ring(low, "x", k)[None] if k else low[None], k) for k in range(ring)]
    high_parts = [(shift_ring(high, Z_AXES, k)[None] if k else high[None], k) for k in range(ring)]
    low = fill((ring, rows, half), [(v, ((x - k) % ring, 0, 0)) for v, k in low_parts])
    high = fill((ring, rows, half), [(v, ((z - k) % ring, 0, 0)) for v, k in high_parts])
    return low, high


def gather_second(low, high):
    ring, rows, half = low.shape
    columns = 2 * half
    x, z = lax.axis_index("x"), lax.axis_index(Z_AXES)
    parts = []
    for k in range(ring):
        part = shift_ring(low, Z_AXES, k) if k else low
        parts.append((part[:, None], (0, (z - k) % ring, 0, 0)))
        part = shift_ring(high, "x", k) if k else high
        parts.append((part[None], ((x - k) % ring, 0, 0, half)))
    return fill((ring, ring, rows, columns), parts)


def gather_third(plane):
    ring, ring, rows, columns = plane.shape
    core = lax.axis_index("core")
    other = swap_core(plane)
    both = fill(
        (ring, ring, CORES, rows, columns),
        [
            (plane[:, :, None], (0, 0, core, 0, 0)),
            (other[:, :, None], (0, 0, 1 - core, 0, 0)),
        ],
    )
    return both.reshape(-1, columns)


def finish_kernel(steps, core_ref, sum_ref, other_ref, gateup_ref, down_ref, *rest):
    core = core_ref[0]
    rows, hidden = down_ref.shape
    padded = steps * TILE
    half = TILE // 2
    first = core == 0
    mine = sum_ref[pl.ds(pl.multiple_of(core * rows, rows), rows), :].astype(F32)
    other = other_ref[...].astype(F32)
    low = jnp.where(first, mine, other)
    high = jnp.where(first, other, mine)
    gateup_ref[:, 0, :] = low[:, :hidden]
    gateup_ref[:, 1, :] = high[:, :hidden]
    for step in range(steps):
        source = padded + step * half
        for part, columns in enumerate((low, high)):
            place = step * TILE + part * half
            size = min(half, hidden - place)
            if size > 0:
                down_ref[:, place : place + size] = columns[:, source : source + size]
    for ref in rest:
        start = padded + steps * half
        size = low.shape[1] - start
        ref[:, :size] = low[:, start:]
        ref[:, size:] = high[:, start:]


def finish(summed, steps, hidden):
    core = lax.axis_index("core")
    rows, columns = summed.shape[0] // 2, summed.shape[1]
    other = swap_core(lax.dynamic_slice_in_dim(summed, (1 - core) * rows, rows, 0))
    extra = 2 * (columns - steps * (TILE + TILE // 2))
    return pl.pallas_call(
        functools.partial(finish_kernel, steps),
        grid=(1,),
        in_specs=[
            pl.BlockSpec(memory_space=pltpu.SMEM),
            whole(summed.shape),
            whole(other.shape),
        ],
        out_specs=[whole((rows, 2, hidden)), whole((rows, hidden))]
        + [whole((rows, extra))] * (extra > 0),
        out_shape=[
            jax.ShapeDtypeStruct((rows, 2, hidden), F32),
            jax.ShapeDtypeStruct((rows, hidden), F32),
        ]
        + [jax.ShapeDtypeStruct((rows, extra), F32)] * (extra > 0),
        compiler_params=pltpu.CompilerParams(vmem_limit_bytes=VMEM_LIMIT),
        cost_estimate=pl.CostEstimate(
            flops=4 * rows * columns, bytes_accessed=16 * rows * columns, transcendentals=0
        ),
        name="finish_gradients",
    )(core.reshape(1).astype(jnp.int32), summed, other)


def halves(proj, out):
    first = lax.axis_index("core") == 0
    half = (proj.shape[1] + out.shape[1]) // 2
    late = jnp.concatenate([proj[:, half:], out], axis=1)
    early = proj[:, :half]
    return jnp.where(first, early, late), jnp.where(first, late, early)


def body(
    hidden_in,
    cotangent,
    seq_lengths,
    deal_order,
    mixer_gain,
    mixer_project,
    mixer_kernel,
    mixer_output,
    first_gain,
    first_gateup,
    first_down,
    attend_gain,
    attend_project,
    query_gain,
    key_gain,
    attend_output,
    second_gain,
    second_gateup,
    second_down,
):
    shards = lax.axis_size(TOKEN_AXES)
    contexts = lax.axis_size(CTX_AXES)
    members = lax.axis_size("tp")
    row_count, width = hidden_in.shape
    piece_rows = row_count // shards
    part_rows = piece_rows // members
    chunk = row_count // members
    device = lax.axis_index(TOKEN_AXES)
    own = lax.axis_index("tp")
    core = lax.axis_index("core")
    core_ref = core.reshape(1).astype(jnp.int32)
    depth = mixer_gain.shape[0]
    channels = mixer_output.shape[0]
    hidden = first_down.shape[0]
    heads_width = attend_output.shape[0]
    steps = -(-hidden // TILE)
    padded = steps * TILE
    ffn_width = 3 * padded
    block = TILE + TILE // 2

    def pack_ffn(gateup, down):
        wide = jnp.pad(gateup, ((0, 0), (0, 0), (0, padded - hidden)))
        wide = wide.reshape(depth, 2, steps, TILE).transpose(0, 2, 1, 3).reshape(depth, -1)
        return [wide, jnp.pad(down.T, ((0, 0), (0, padded - hidden)))]

    mixer_pack = jnp.concatenate([mixer_project.reshape(depth, -1), mixer_output.T], axis=1)
    first_pack = jnp.concatenate(
        pack_ffn(first_gateup, first_down) + [attend_project, attend_output.T], axis=1
    )
    second_pack = jnp.concatenate(pack_ffn(second_gateup, second_down), axis=1)
    piece_table = deal_order.reshape(shards, shards, piece_rows)[:, :, 0]
    anchor = piece_table // row_count
    anchor_piece = piece_table % row_count // piece_rows
    send_piece = jnp.sum(jnp.where(anchor == device, anchor_piece, 0), axis=1)
    my_anchor = lax.dynamic_index_in_dim(anchor, device, 0, keepdims=False)
    gains_row = jnp.concatenate(
        [mixer_gain, first_gain, attend_gain, second_gain, jnp.zeros((width - 4 * depth,), BF16)]
    )

    def my_part(rows):
        parts = rows.reshape(shards, members, part_rows, width)
        return lax.dynamic_index_in_dim(parts, own, 1, keepdims=False)[send_piece]

    outgoing = jnp.concatenate(
        [
            my_part(hidden_in),
            my_part(cotangent),
            jnp.broadcast_to(gains_row, (shards, 1, width)),
        ],
        axis=1,
    )
    arrived = lax.all_to_all(outgoing, TOKEN_AXES, split_axis=0, concat_axis=0, tiled=True)
    mixer_low, mixer_high = gather_first(mixer_pack)
    mixer_low, mixer_high, first_pack = lax.optimization_barrier(
        (mixer_low, mixer_high, first_pack)
    )
    first_all = lax.all_gather(first_pack, TOKEN_AXES, axis=0, tiled=True)
    second_all = lax.all_gather(second_pack, TOKEN_AXES, axis=0, tiled=True)
    project_b = first_all[:, ffn_width : ffn_width + attend_project.shape[1]]
    output_b_t = first_all[:, ffn_width + attend_project.shape[1] :]
    gains = (
        arrived[:, 2 * part_rows, : 4 * depth]
        .reshape(shards, 4, depth)
        .transpose(1, 0, 2)
        .reshape(4, width)
        .astype(F32)
    )
    gain_a, gain_f, gain_b, gain_s = gains[0], gains[1], gains[2], gains[3]
    parts = arrived[:, : 2 * part_rows][my_anchor]
    own_tokens = parts[:, :part_rows].reshape(chunk, width)
    own_back = parts[:, part_rows:].reshape(chunk, width)
    stream0 = own_tokens.astype(F32)
    upstream = own_back.astype(F32)
    both = tp_gather(jnp.concatenate([own_tokens, own_back]))
    both, mixer_plane = lax.optimization_barrier((both, gather_second(mixer_low, mixer_high)))
    mixer_all = gather_third(mixer_plane)
    project_a = mixer_all[:, : 3 * channels]
    output_a_t = mixer_all[:, 3 * channels :]
    back_s = jnp.concatenate([slot[chunk:] for slot in both])

    gathered = jnp.arange(row_count)
    member_of = (own - gathered // chunk) % members
    offsets = (
        gathered % chunk // part_rows * piece_rows + member_of * part_rows + gathered % part_rows
    )
    to_gathered = (offsets[:, None] == gathered[None, :]).astype(BF16)
    to_dealt = (offsets[None, :] == gathered[:, None]).astype(BF16)
    tokens = times(to_dealt, jnp.concatenate([slot[:chunk] for slot in both]))

    kernel_taps = mixer_kernel.shape[0]
    halo = kernel_taps - 1
    local_rows = device * row_count + jnp.arange(row_count)
    halo_segment, unused = locate(
        seq_lengths, local_rows[0] - halo + jnp.arange(row_count + halo)
    )
    segment, places = locate(seq_lengths, device * row_count + offsets)
    ctx = lax.axis_index(CTX_AXES)
    group_rows = jnp.concatenate(
        [
            (lax.axis_index(GROUP_AXES) * contexts + (ctx ^ mask)) * row_count + offsets
            for mask in range(contexts)
        ]
    )
    key_segment, key_places = locate(seq_lengths, group_rows)
    allowed = (segment[None, :] == key_segment[:, None]) & (key_places[:, None] <= places[None, :])
    barred = jnp.where(allowed, 0.0, NEGATIVE).astype(BF16)
    half_dim = HD // 2
    frequency = ROPE_BASE ** (-(jnp.arange(half_dim).astype(F32) * 2.0 / HD))
    angles = places.astype(F32)[:, None] * frequency[None, :]
    cosine = jnp.cos(angles)
    sine = jnp.sin(angles)

    kernel_local = lax.dynamic_slice_in_dim(mixer_kernel, own * channels, channels, 1).astype(F32)
    mixer_in = norm_rows(tokens, gain_a).astype(BF16)
    mixer_in_other = swap_core(mixer_in)
    halo_pad = 16
    halo_in = from_behind(mixer_in[row_count - halo_pad :], 1)
    proj_a = times(jnp.concatenate([halo_in, mixer_in]), project_a)
    proj_b_part = proj_a[:, :channels]
    proj_c_part = proj_a[halo_pad:, channels : 2 * channels]
    proj_x_part = proj_a[:, 2 * channels :]
    extended = (proj_b_part * proj_x_part)[halo_pad - halo :].astype(BF16).astype(F32)
    conv_out = shortconv(extended, kernel_local, halo_segment)
    gated_rows = (proj_c_part * conv_out).astype(BF16)
    gated_parts = arrange(to_gathered, gated_rows)
    stream1, normed = add_norm(
        tp_scatter(tp_chunks(times_t(gated_parts, output_a_t))), stream0, gain_f
    )

    normed_f = tp_gather(normed)
    stream2, normed = add_norm(
        tp_scatter(ffn_forward(normed_f, first_all, steps)), stream1, gain_b
    )

    groups = H // KVH
    score_scale = HD ** (-0.5)
    qgain_f = query_gain.astype(F32)[None]
    kgain_f = key_gain.astype(F32)[None]
    attend_in = jnp.concatenate(tp_gather(normed))
    proj_b = times(attend_in, project_b)
    kv_width = 2 * HD * (proj_b.shape[1] // (HD * (groups + 2)))
    query_b, key_value = one_step(
        functools.partial(heads_kernel, groups),
        [proj_b, cosine, sine, qgain_f, kgain_f],
        [
            jax.ShapeDtypeStruct((row_count, heads_width), BF16),
            jax.ShapeDtypeStruct((row_count, kv_width), BF16),
        ],
        SMALL_LIMIT,
        "heads",
        20 * proj_b.size,
    )
    key_value_z = swap_ctx(key_value, 2)
    key_value_core = swap_core(jnp.concatenate([key_value, key_value_z]))
    key_value_all = jnp.concatenate(
        [key_value, key_value_core[:row_count], key_value_z, key_value_core[row_count:]]
    )
    attend_flops = 2 * key_value_all.shape[0] * query_b.size
    (attended,) = one_step(
        functools.partial(attend_kernel, score_scale, HD),
        [query_b, key_value_all, barred],
        [jax.ShapeDtypeStruct(query_b.shape, BF16)],
        MIDDLE_LIMIT,
        "attend",
        2 * attend_flops,
    )
    stream3, normed = add_norm(
        tp_scatter(tp_chunks(times_t(attended, output_b_t))), stream2, gain_s
    )

    normed_s = tp_gather(normed)
    d_chunks, out_chunks, keep, side = ffn_backward(
        core_ref, normed_s, [back_s], second_all, steps, True
    )
    d_stream3, back_b, gain_s_grad = norm_backward(
        tp_scatter(d_chunks), stream3, gain_s, upstream
    )
    out_others = [shift_tp(out_chunks[k], -k) for k in range(1, members)]
    side_other = swap_core(side)
    ffn_lefts = [(side, 0), (side_other, 0), (side, 1), (side_other, 1)]
    ffn_cols = steps * block
    side_start = 2 * width // block
    partial = gradient(
        ffn_lefts, keep, side_other, side_start, block, steps, padded, width, ffn_cols, 0, None
    )

    back_b = tp_gather(back_b)
    back_b, partial = lax.optimization_barrier((back_b, partial))
    second_sums = sum_chips(partial)
    back_b = jnp.concatenate(back_b)
    back_b_other = swap_core(back_b)
    attend_in_other = swap_core(attend_in)
    d_attended_b = times(back_b, output_b_t).astype(BF16)
    pair_rows = 2 * row_count
    d_query, near, cross, qgain_grad = one_step(
        functools.partial(attend_backward_kernel, score_scale),
        [query_b, d_attended_b, key_value_all, barred, proj_b, cosine, sine, qgain_f],
        [
            jax.ShapeDtypeStruct(query_b.shape, BF16),
            jax.ShapeDtypeStruct((pair_rows, kv_width), F32),
            jax.ShapeDtypeStruct((pair_rows, kv_width), BF16),
            jax.ShapeDtypeStruct((1, HD), F32),
        ],
        MIDDLE_LIMIT,
        "attend_backward",
        5 * attend_flops,
    )
    cross = swap_core(cross)
    far = (near[row_count:] + cross[row_count:].astype(F32)).astype(BF16)
    d_proj_b, kgain_grad = one_step(
        functools.partial(assemble_kernel, groups),
        [d_query, near, cross, swap_ctx(far, 2), proj_b, cosine, sine, kgain_f],
        [jax.ShapeDtypeStruct(proj_b.shape, BF16), jax.ShapeDtypeStruct((1, HD), F32)],
        SMALL_LIMIT,
        "assemble",
        20 * proj_b.size,
    )
    d_stream2, back_f, gain_b_grad = norm_backward(
        tp_scatter(tp_chunks(times_t(d_proj_b, project_b))), stream2, gain_b, d_stream3
    )
    keep, send = halves(d_proj_b, attended)
    first_core = core == 0
    attend_cols = keep.shape[1]
    small_tile = 2 * (heads_width + attend_project.shape[1]) // 16
    third = gradient(
        [
            (attend_in, 0),
            (attend_in_other, 0),
            (jnp.where(first_core, attend_in, back_b), 0),
            (jnp.where(first_core, attend_in_other, back_b_other), 0),
        ],
        keep,
        swap_core(send),
        0,
        small_tile,
        attend_cols // small_tile,
        attend_project.shape[1] - attend_cols,
        width,
        ffn_cols + attend_cols,
        ffn_cols // small_tile,
        None,
    )

    back_f = tp_gather(back_f)
    back_f, third = lax.optimization_barrier((back_f, third))
    left_x, left_b = jnp.concatenate(normed_f), jnp.concatenate(back_f)
    left_others = [swap_core(left_x), swap_core(left_b)]
    d_chunks, unused, keep, side = ffn_backward(
        core_ref, normed_f, back_f, first_all, steps, False
    )
    d_chunks, left_others = lax.optimization_barrier((d_chunks, left_others))
    d_chunks, side_other = lax.optimization_barrier((d_chunks, swap_core(side)))
    ffn_lefts = [(left_x, 0), (left_others[0], 0), (left_b, 0), (left_others[1], 0)]
    partial = gradient(
        ffn_lefts,
        keep,
        side_other,
        0,
        block,
        steps,
        padded,
        width,
        ffn_cols + attend_cols,
        0,
        third,
    )

    d_parts, partial = lax.optimization_barrier((tp_scatter(d_chunks), partial))
    d_stream1, back_a, gain_f_grad = norm_backward(d_parts, stream1, gain_f, d_stream2)

    back_a = tp_gather(back_a)
    first_sums = sum_chips(partial)
    back_a = arrange(to_dealt, jnp.concatenate(back_a))
    back_a_other = swap_core(back_a)
    d_gated = times(back_a, output_a_t)
    d_cgate = d_gated * conv_out
    d_conv = d_gated * proj_c_part
    unused, pullback = jax.vjp(
        lambda ext_rows, kernel_in: shortconv(ext_rows, kernel_in, halo_segment),
        extended,
        kernel_local,
    )
    d_extended, kernel_grad = pullback(d_conv)
    returned = from_behind(d_extended[:halo], -1)
    d_product = d_extended[halo:] + jnp.concatenate(
        [jnp.zeros((row_count - halo, channels), F32), returned]
    )
    d_proj_a = jnp.concatenate(
        [
            d_product * proj_x_part[halo_pad:],
            d_cgate,
            d_product * proj_b_part[halo_pad:],
        ],
        axis=1,
    ).astype(BF16)
    d_proj_a, out_others = lax.optimization_barrier((d_proj_a, out_others))
    stream4 = stream3 + add_parts([out_chunks[0], *out_others])
    d_chunks = tp_chunks(times_t(arrange(to_gathered, d_proj_a), project_a))
    keep, send = halves(d_proj_a, gated_rows)
    mixer_cols = keep.shape[1]
    partial = gradient(
        [
            (mixer_in, 0),
            (mixer_in_other, 0),
            (jnp.where(first_core, mixer_in, back_a), 0),
            (jnp.where(first_core, mixer_in_other, back_a_other), 0),
        ],
        keep,
        swap_core(send),
        0,
        mixer_cols,
        1,
        3 * channels - mixer_cols,
        width,
        mixer_cols,
        0,
        None,
    )
    kernel_cols = kernel_taps * channels
    gain_start = kernel_cols + 2 * HD
    shared = jnp.concatenate([kernel_grad.reshape(-1), qgain_grad[0], kgain_grad[0]])
    early_gains = [
        grad.reshape(shards, depth) for grad in (gain_f_grad, gain_b_grad, gain_s_grad)
    ]
    early_row = jnp.concatenate(
        [
            jnp.broadcast_to(shared, (shards, gain_start)),
            jnp.pad(
                jnp.concatenate(early_gains, axis=1),
                ((0, 0), (0, width - gain_start - 3 * depth)),
            ),
        ],
        axis=1,
    )
    d_parts, early_row = lax.optimization_barrier((tp_scatter(d_chunks), early_row))
    unused, d_stream0, gain_a_grad = norm_backward(d_parts, stream0, gain_a, d_stream1)

    slot_for_anchor = jnp.sum(
        jnp.where(
            my_anchor[None, :] == jnp.arange(shards)[:, None], jnp.arange(shards)[None, :], 0
        ),
        axis=1,
    )
    late_start = gain_start + 3 * depth
    late_row = jnp.pad(
        gain_a_grad.reshape(shards, depth), ((0, 0), (late_start, width - late_start - depth))
    )
    leaving = jnp.concatenate(
        [d_stream0, stream4.astype(BF16), (early_row + late_row).astype(BF16)]
    )
    line = jnp.arange(shards * piece_rows)
    target, item = line // piece_rows, line % piece_rows
    source = jnp.where(
        item < 2 * part_rows,
        item // part_rows * chunk
        + jnp.repeat(slot_for_anchor, piece_rows) * part_rows
        + item % part_rows,
        jnp.where(item == 2 * part_rows, 2 * chunk + target, -1),
    )
    to_leaving = (source[:, None] == jnp.arange(leaving.shape[0])[None, :]).astype(BF16)
    leaving = arrange(to_leaving, leaving)
    home = lax.all_to_all(
        leaving.reshape(shards, piece_rows, width),
        TOKEN_AXES,
        split_axis=0,
        concat_axis=0,
        tiled=True,
    )
    second_grads = finish(second_sums, steps, hidden)
    home, partial, second_grads = lax.optimization_barrier((home, partial, second_grads))
    place = jnp.arange(2 * chunk + 8)
    small_line = (place == 2 * chunk) | (place == 2 * chunk + 1)
    wanted = (
        place % chunk // part_rows * piece_rows
        + place // chunk * part_rows
        + place % part_rows
    )
    to_payload = jnp.where(
        (place < 2 * chunk)[:, None],
        wanted[:, None] == line[None, :],
        small_line[:, None] & (item == 2 * part_rows)[None, :],
    ).astype(BF16)
    payload = times(to_payload, home.reshape(shards * piece_rows, width))
    rounded = payload.astype(BF16).astype(F32)
    payload = jnp.where((place == 2 * chunk + 1)[:, None], payload - rounded, payload)
    last = tp_gather(payload.astype(BF16))
    mixer_home = lax.all_to_all(
        partial.reshape(shards, depth, mixer_cols),
        TOKEN_AXES,
        split_axis=0,
        concat_axis=0,
        tiled=True,
    )
    home_rows = (
        jnp.repeat(jnp.tile(send_piece, members), part_rows) * piece_rows
        + member_of * part_rows
        + gathered % part_rows
    )
    to_arrival = (home_rows[None, :] == gathered[:, None]).astype(BF16)
    input_gradient = arrange(to_arrival, jnp.concatenate([slot[:chunk] for slot in last]))
    layer_out = arrange(to_arrival, jnp.concatenate([slot[chunk : 2 * chunk] for slot in last]))
    first_sums, layer_out, input_gradient = lax.optimization_barrier(
        (first_sums, layer_out, input_gradient)
    )
    *first_grads, attend_grads = finish(first_sums, steps, hidden)
    first_grads, attend_grads, mixer_home = lax.optimization_barrier(
        (first_grads, attend_grads, mixer_home)
    )
    mixer_home = mixer_home.reshape(shards // CORES, CORES, depth, mixer_cols)
    mixer_grads = jnp.sum(mixer_home.astype(F32), axis=0)
    mixer_grads = jnp.concatenate([mixer_grads[0], mixer_grads[1]], axis=1)
    smalls = [
        slot[2 * chunk].astype(F32) + slot[2 * chunk + 1].astype(F32) for slot in last
    ]
    totals = sum(smalls)
    kernel_rows = jnp.stack([small[:kernel_cols].reshape(kernel_taps, channels) for small in smalls])
    kernel_total = jnp.concatenate(
        [
            lax.dynamic_index_in_dim(kernel_rows, (own - member) % members, 0, keepdims=False)
            for member in range(members)
        ],
        axis=1,
    )
    qgain_total = totals[kernel_cols : kernel_cols + HD]
    kgain_total = totals[kernel_cols + HD : kernel_cols + 2 * HD]
    gain_totals = totals[gain_start : gain_start + 4 * depth].reshape(4, depth)

    gateup_s_grad, down_s_grad = second_grads
    gateup_f_grad, down_f_grad = first_grads
    proj_cols = attend_project.shape[1]
    return (
        layer_out,
        input_gradient,
        gain_totals[3],
        mixer_grads[:, : 3 * channels].reshape(depth, 3, channels),
        kernel_total,
        mixer_grads[:, 3 * channels :].T,
        gain_totals[0],
        gateup_f_grad,
        down_f_grad.T,
        gain_totals[1],
        attend_grads[:, :proj_cols],
        qgain_total,
        kgain_total,
        attend_grads[:, proj_cols:].T,
        gain_totals[2],
        gateup_s_grad,
        down_s_grad.T,
    )


def solution(mesh):
    names = TOKEN_AXES + ("tp",)
    rings = mesh.shape["fsdp"] // 2, 2, mesh.shape["ctx"] // 2, 2, mesh.shape["tp"]
    tokens = P(TOKEN_AXES, None)
    rows = P(TOKEN_AXES)
    three = P(TOKEN_AXES, None, "tp")
    two = P(TOKEN_AXES, "tp")
    turned = P("tp", TOKEN_AXES)
    return jax.shard_map(
        body,
        mesh=Mesh(mesh.devices.reshape(rings), names),
        in_specs=(
            tokens, tokens, P(), P(),
            rows, three, P(), turned,
            rows, three, turned,
            rows, two, P(), P(), turned,
            rows, three, turned,
        ),
        out_specs=(
            tokens, tokens,
            rows, three, P(), turned,
            rows, three, turned,
            rows, two, P(), P(), turned,
            rows, three, turned,
        ),
        check_vma=False,
    )
```

```python
import functools

import jax
import jax.numpy as jnp
from jax import lax
from jax.experimental import pallas as pl
from jax.experimental.pallas import tpu as pltpu
from jax.sharding import Mesh, PartitionSpec as P

H = 24
KVH = 8
HD = 64

EPSILON = 1e-05
ROPE_BASE = 1000000.0
NEGATIVE = -1e30

CHIP_AXES = ("x", "z_hi", "z_lo")
TOKEN_AXES = CHIP_AXES + ("core",)
GROUP_AXES = ("x", "z_hi")
CTX_AXES = ("z_lo", "core")
Z_AXES = ("z_hi", "z_lo")
CORES = 2
TILE = 256
VMEM_LIMIT = 48 * 1024 * 1024
MIDDLE_LIMIT = 24 * 1024 * 1024
SMALL_LIMIT = 12 * 1024 * 1024
F32 = jnp.float32
BF16 = jnp.bfloat16


def norm_rows(values, scales):
    return values * lax.rsqrt(jnp.mean(values * values, axis=-1, keepdims=True) + EPSILON) * scales


def locate(lengths, positions):
    seq_ends = jnp.cumsum(lengths)
    segment = jnp.sum((positions[:, None] >= seq_ends[None, :]).astype(jnp.int32), axis=1)
    starts = seq_ends - lengths
    first_row = jnp.sum(
        jnp.where(segment[:, None] == jnp.arange(lengths.shape[0])[None, :], starts[None, :], 0),
        axis=1,
    )
    return (segment, positions - first_row)


def shortconv(extended, kernel_in, segment):
    kernel_taps = kernel_in.shape[0]
    out_rows = extended.shape[0] - kernel_taps + 1
    result = kernel_in[0] * extended[kernel_taps - 1 :]
    for t in range(1, kernel_taps):
        earlier = extended[kernel_taps - 1 - t : kernel_taps - 1 - t + out_rows]
        same_seq = (
            segment[kernel_taps - 1 - t : kernel_taps - 1 - t + out_rows]
            == segment[kernel_taps - 1 :]
        ).astype(F32)[:, None]
        result = result + kernel_in[t] * earlier * same_seq
    return result


def from_behind(block, distance):
    devices = range(lax.axis_size(CTX_AXES))
    route = [(i - distance, i) for i in devices if i - distance in devices]
    return lax.ppermute(block, CTX_AXES, route)


def swap_ctx(block, mask):
    return lax.ppermute(block, CTX_AXES, [(i, i ^ mask) for i in range(lax.axis_size(CTX_AXES))])


def swap_core(block):
    return lax.ppermute(block, "core", [(0, 1), (1, 0)])


def shift_tp(block, distance):
    members = lax.axis_size("tp")
    return lax.ppermute(block, "tp", [(i, (i + distance) % members) for i in range(members)])


def tp_gather(shard):
    return [shard] + [shift_tp(shard, k) for k in range(1, lax.axis_size("tp"))]


def tp_chunks(partial):
    rows = partial.shape[0] // lax.axis_size("tp")
    return [
        partial[k * rows : (k + 1) * rows].astype(F32 if k == 0 else BF16)
        for k in range(lax.axis_size("tp"))
    ]


def tp_scatter(chunks):
    return [chunks[0]] + [shift_tp(chunks[k], -k) for k in range(1, len(chunks))]


def add_parts(parts):
    total = parts[0]
    for part in parts[1:]:
        total = total + part.astype(F32)
    return total


def arrange(order, rows):
    return times(order, rows).astype(BF16)


def times(left, right):
    return lax.dot_general(left, right, (((1,), (0,)), ((), ())), preferred_element_type=F32)


def times_t(left, right):
    return lax.dot_general(left, right, (((1,), (1,)), ((), ())), preferred_element_type=F32)


def times_rows(left, right):
    return lax.dot_general(left, right, (((0,), (0,)), ((), ())), preferred_element_type=F32)


def assemble(chunk_refs, target):
    rows = chunk_refs[0].shape[0]
    for k, ref in enumerate(chunk_refs):
        target[k * rows : (k + 1) * rows, :] = ref[...]


def spread(total, chunk_refs):
    rows = chunk_refs[0].shape[0]
    for k, ref in enumerate(chunk_refs):
        ref[...] = total[k * rows : (k + 1) * rows, :].astype(ref.dtype)


def whole(shape):
    return pl.BlockSpec(shape, lambda *_: (0,) * len(shape))


def one_step(kernel, operands, out_shape, limit, name, flops):
    size = sum(v.size * v.dtype.itemsize for v in list(operands) + list(out_shape))
    return pl.pallas_call(
        kernel,
        grid=(1,),
        in_specs=[whole(v.shape) for v in operands],
        out_specs=[whole(v.shape) for v in out_shape],
        out_shape=out_shape,
        compiler_params=pltpu.CompilerParams(vmem_limit_bytes=limit),
        cost_estimate=pl.CostEstimate(flops=flops, bytes_accessed=size, transcendentals=0),
        name=name,
    )(*operands)


def sum_refs(refs):
    total = refs[0][...]
    for ref in refs[1:]:
        total = total + ref[...].astype(F32)
    return total


def add_norm_kernel(*refs):
    stream_ref, gain_ref, out_ref, normed_ref = refs[-4:]
    stream = stream_ref[...] + sum_refs(refs[:-4])
    out_ref[...] = stream
    normed_ref[...] = norm_rows(stream, gain_ref[...]).astype(BF16)


def add_norm(parts, stream, gain):
    return one_step(
        add_norm_kernel,
        [*parts, stream, gain[None]],
        [jax.ShapeDtypeStruct(stream.shape, F32), jax.ShapeDtypeStruct(stream.shape, BF16)],
        SMALL_LIMIT,
        "add_norm",
        10 * stream.size,
    )


def norm_backward_kernel(*refs):
    stream_ref, gain_ref, upward_ref, out_ref, rounded_ref, gain_grad_ref = refs[-6:]
    stream = stream_ref[...]
    d_normed = sum_refs(refs[:-6])
    spread_of = lax.rsqrt(jnp.mean(stream * stream, axis=1, keepdims=True) + EPSILON)
    gain_grad_ref[...] = jnp.sum(d_normed * stream * spread_of, axis=0, keepdims=True)
    scaled = d_normed * gain_ref[...]
    inner = jnp.mean(scaled * stream, axis=1, keepdims=True)
    result = upward_ref[...] + spread_of * scaled - stream * (
        spread_of * spread_of * spread_of * inner
    )
    out_ref[...] = result
    rounded_ref[...] = result.astype(BF16)


def norm_backward(parts, stream, gain, upward):
    out, rounded, gain_grad = one_step(
        norm_backward_kernel,
        [*parts, stream, gain[None], upward],
        [
            jax.ShapeDtypeStruct(stream.shape, F32),
            jax.ShapeDtypeStruct(stream.shape, BF16),
            jax.ShapeDtypeStruct((1, stream.shape[1]), F32),
        ],
        SMALL_LIMIT,
        "norm_backward",
        20 * stream.size,
    )
    return out, rounded, gain_grad[0]


def weight_specs(depth, steps):
    return [
        pl.BlockSpec((depth, 2 * TILE), lambda j: (0, j)),
        pl.BlockSpec((depth, TILE), lambda j: (0, 2 * steps + j)),
    ]


def chunk_shapes(count, rows, width):
    return [jax.ShapeDtypeStruct((rows, width), F32 if k == 0 else BF16) for k in range(count)]


def ffn_forward_kernel(count, *refs):
    x_refs, (gu_ref, dn_ref), outs = refs[:count], refs[count : count + 2], refs[count + 2 : -2]
    x_all, total = refs[-2:]
    step = pl.program_id(0)

    @pl.when(step == 0)
    def _():
        assemble(x_refs, x_all)
        total[...] = jnp.zeros_like(total)

    both = times(x_all[...], gu_ref[...])
    gate, up = both[:, :TILE], both[:, TILE:]
    active = (gate * jax.nn.sigmoid(gate) * up).astype(BF16)
    total[...] += times_t(active, dn_ref[...])

    @pl.when(step == pl.num_programs(0) - 1)
    def _():
        spread(total[...], outs)


def ffn_forward(chunks, pack, steps):
    count, (rows, width) = len(chunks), chunks[0].shape
    tokens = count * rows
    return pl.pallas_call(
        functools.partial(ffn_forward_kernel, count),
        grid=(steps,),
        in_specs=[whole((rows, width))] * count + weight_specs(width, steps),
        out_specs=[whole((rows, width))] * count,
        out_shape=chunk_shapes(count, rows, width),
        scratch_shapes=[pltpu.VMEM((tokens, width), BF16), pltpu.VMEM((tokens, width), F32)],
        compiler_params=pltpu.CompilerParams(vmem_limit_bytes=VMEM_LIMIT),
        cost_estimate=pl.CostEstimate(
            flops=2 * tokens * width * 3 * TILE * steps,
            bytes_accessed=2 * width * 3 * TILE * steps,
            transcendentals=tokens * TILE * steps,
        ),
        name="ffn_forward",
    )(*chunks, pack, pack)


def ffn_backward_kernel(count, back_count, forward, core_ref, *refs):
    x_refs, b_refs = refs[:count], refs[count : count + back_count]
    place = count + back_count
    gu_ref, dn_ref = refs[place : place + 2]
    place += 2
    back_outs = refs[place : place + count]
    place += count
    if forward:
        outs = refs[place : place + count]
        place += count
    keep_ref, side_ref = refs[place : place + 2]
    scratch = refs[place + 2 :]
    x_all, b_all, d_total = scratch[:3]
    step = pl.program_id(0)
    width = x_all.shape[1]

    @pl.when(step == 0)
    def _():
        assemble(x_refs, x_all)
        assemble(b_refs, b_all)
        if forward:
            side_ref[:, :width] = x_all[...]
            side_ref[:, width : 2 * width] = b_all[...]
        d_total[...] = jnp.zeros_like(d_total)
        if forward:
            scratch[3][...] = jnp.zeros_like(scratch[3])

    both = times(x_all[...], gu_ref[...])
    gate, up = both[:, :TILE], both[:, TILE:]
    d_active = times(b_all[...], dn_ref[...])
    sigmoid = jax.nn.sigmoid(gate)
    silu = gate * sigmoid
    active = (silu * up).astype(BF16)
    if forward:
        scratch[3][...] += times_t(active, dn_ref[...])
    d_gate = (d_active * up * (sigmoid * (1.0 + gate * (1.0 - sigmoid)))).astype(BF16)
    d_up = (d_active * silu).astype(BF16)
    d_total[...] += times_t(jnp.concatenate([d_gate, d_up], axis=1), gu_ref[...])
    first = core_ref[0] == 0
    half = TILE // 2
    low, high = active[:, :half], active[:, half:]
    offset = 2 * width if forward else 0
    wide = pl.multiple_of(step * TILE, TILE)
    narrow = pl.multiple_of(pl.num_programs(0) * TILE + step * half, half)
    side_wide = pl.multiple_of(offset + wide, TILE)
    side_narrow = pl.multiple_of(offset + narrow, half)

    @pl.when(first)
    def _():
        keep_ref[:, pl.ds(wide, TILE)] = d_gate
        keep_ref[:, pl.ds(narrow, half)] = low
        side_ref[:, pl.ds(side_wide, TILE)] = d_up
        side_ref[:, pl.ds(side_narrow, half)] = high

    @pl.when(jnp.logical_not(first))
    def _():
        keep_ref[:, pl.ds(wide, TILE)] = d_up
        keep_ref[:, pl.ds(narrow, half)] = high
        side_ref[:, pl.ds(side_wide, TILE)] = d_gate
        side_ref[:, pl.ds(side_narrow, half)] = low

    @pl.when(step == pl.num_programs(0) - 1)
    def _():
        spread(d_total[...], back_outs)
        if forward:
            spread(scratch[3][...], outs)


def ffn_backward(core, chunks, back_chunks, pack, steps, forward):
    count, (rows, width) = len(chunks), chunks[0].shape
    tokens = count * rows
    block = TILE + TILE // 2
    ways = 2 if forward else 1
    side_width = (2 * width if forward else 0) + steps * block
    results = pl.pallas_call(
        functools.partial(ffn_backward_kernel, count, len(back_chunks), forward),
        grid=(steps,),
        in_specs=[pl.BlockSpec(memory_space=pltpu.SMEM)]
        + [whole(v.shape) for v in (*chunks, *back_chunks)]
        + weight_specs(width, steps),
        out_specs=[whole((rows, width))] * (ways * count)
        + [whole((tokens, steps * block)), whole((tokens, side_width))],
        out_shape=chunk_shapes(count, rows, width) * ways
        + [
            jax.ShapeDtypeStruct((tokens, steps * block), BF16),
            jax.ShapeDtypeStruct((tokens, side_width), BF16),
        ],
        scratch_shapes=[pltpu.VMEM((tokens, width), BF16)] * 2
        + [pltpu.VMEM((tokens, width), F32)] * ways,
        compiler_params=pltpu.CompilerParams(vmem_limit_bytes=VMEM_LIMIT),
        cost_estimate=pl.CostEstimate(
            flops=2 * tokens * width * (4 + ways) * TILE * steps,
            bytes_accessed=2 * width * 3 * TILE * steps + 4 * tokens * side_width,
            transcendentals=tokens * TILE * steps,
        ),
        name="ffn_both" if forward else "ffn_backward",
    )(core, *chunks, *back_chunks, pack, pack)
    return results[:count], results[count : ways * count], results[-2], results[-1]


def gradient_kernel(edge, cut, *refs):
    one_own, one_other, two_own, two_other, own_ref, other_ref = refs[:6]
    out_ref = refs[-1]
    step = pl.program_id(0)

    def product(own_left, other_left, columns):
        total = times_rows(own_left[...], own_ref[:, columns])
        total += times_rows(other_left[...], other_ref[:, columns])
        out_ref[:, columns] = total.astype(BF16)

    @pl.when(step < edge)
    def _():
        product(one_own, one_other, slice(None))

    @pl.when(step > edge if cut else step >= edge)
    def _():
        product(two_own, two_other, slice(None))

    if cut:

        @pl.when(step == edge)
        def _():
            product(one_own, one_other, slice(0, cut))
            product(two_own, two_other, slice(cut, None))


def gradient(lefts, own, other, other_start, block, steps, columns, width, out_width, out_start, target):
    tokens = own.shape[0]
    edge, cut = divmod(columns, block)

    def left_spec(index):
        return pl.BlockSpec((tokens, width), lambda j: (0, index))

    in_specs = [left_spec(index) for unused, index in lefts] + [
        pl.BlockSpec((tokens, block), lambda j: (0, j)),
        pl.BlockSpec((tokens, block), lambda j: (0, other_start + j)),
    ]
    operands = [array for array, unused in lefts] + [own, other]
    aliases = {}
    if target is not None:
        in_specs.append(pl.BlockSpec(memory_space=pl.ANY))
        operands.append(target)
        aliases = {len(operands) - 1: 0}
    return pl.pallas_call(
        functools.partial(gradient_kernel, edge, cut),
        grid=(steps,),
        in_specs=in_specs,
        out_specs=pl.BlockSpec((width, block), lambda j: (0, out_start + j)),
        out_shape=jax.ShapeDtypeStruct((width, out_width), BF16),
        input_output_aliases=aliases,
        compiler_params=pltpu.CompilerParams(vmem_limit_bytes=VMEM_LIMIT),
        cost_estimate=pl.CostEstimate(
            flops=4 * tokens * width * block * steps,
            bytes_accessed=2 * width * block * steps,
            transcendentals=0,
        ),
        name="weight_gradient",
    )(*operands)


def turn(rows, cosine, sine):
    half = rows.shape[1] // 2
    first, second = rows[:, :half], rows[:, half:]
    return jnp.concatenate(
        [first * cosine - second * sine, second * cosine + first * sine], axis=1
    )


def head_backward(d_rows, raw, cosine, sine, gain):
    d_normed = turn(d_rows, cosine, -sine)
    spread_of = lax.rsqrt(jnp.mean(raw * raw, axis=1, keepdims=True) + EPSILON)
    d_gain = jnp.sum(d_normed * raw * spread_of, axis=0, keepdims=True)
    scaled = d_normed * gain
    inner = jnp.mean(scaled * raw, axis=1, keepdims=True)
    d_raw = spread_of * scaled - raw * (spread_of * spread_of * spread_of * inner)
    return d_raw.astype(BF16), d_gain


def heads_kernel(groups, raw_ref, cos_ref, sin_ref, query_gain_ref, key_gain_ref, q_ref, kv_ref):
    size = query_gain_ref.shape[1]
    kv_heads = raw_ref.shape[1] // ((groups + 2) * size)
    cosine, sine = cos_ref[...], sin_ref[...]
    for group in range(kv_heads):
        start = group * (groups + 2) * size
        for member in range(groups):
            raw = raw_ref[:, start + member * size : start + (member + 1) * size]
            head = group * groups + member
            rows = turn(norm_rows(raw, query_gain_ref[...]), cosine, sine)
            q_ref[:, head * size : (head + 1) * size] = rows.astype(BF16)
        start += groups * size
        rows = turn(norm_rows(raw_ref[:, start : start + size], key_gain_ref[...]), cosine, sine)
        kv_ref[:, group * size : (group + 1) * size] = rows.astype(BF16)
        value_start = (kv_heads + group) * size
        kv_ref[:, value_start : value_start + size] = raw_ref[
            :, start + size : start + 2 * size
        ].astype(BF16)


def head_probs(key, query, scale, barred):
    scores = times_t(key, query) * scale + barred
    probs = jnp.exp(scores - jnp.max(scores, axis=0, keepdims=True))
    return probs / jnp.sum(probs, axis=0, keepdims=True)


def attend_kernel(scale, size, q_ref, kv_ref, barred_ref, out_ref):
    kv_heads = kv_ref.shape[1] // (2 * size)
    groups = q_ref.shape[1] // (kv_heads * size)
    barred = barred_ref[...].astype(F32)
    for head in range(kv_heads * groups):
        group = head // groups
        columns = slice(head * size, (head + 1) * size)
        key = kv_ref[:, group * size : (group + 1) * size]
        value = kv_ref[:, (kv_heads + group) * size : (kv_heads + group + 1) * size]
        probs = head_probs(key, q_ref[:, columns], scale, barred).astype(BF16)
        out_ref[:, columns] = times_rows(value, probs).T.astype(BF16)


def attend_backward_kernel(
    scale, q_ref, do_ref, kv_ref, barred_ref, raw_ref, cos_ref, sin_ref, gain_ref,
    dq_ref, near_ref, cross_ref, gain_grad_ref,
):
    size = gain_ref.shape[1]
    kv_heads = kv_ref.shape[1] // (2 * size)
    groups = q_ref.shape[1] // (kv_heads * size)
    rows = kv_ref.shape[0] // 4
    cosine, sine, gain = cos_ref[...], sin_ref[...], gain_ref[...]
    barred = barred_ref[...].astype(F32)
    gain_grad = jnp.zeros_like(gain)
    for group in range(kv_heads):
        columns = slice(group * size, (group + 1) * size)
        value_columns = slice((kv_heads + group) * size, (kv_heads + group + 1) * size)
        key, value = kv_ref[:, columns], kv_ref[:, value_columns]
        d_key = d_value = None
        for member in range(groups):
            head = group * groups + member
            head_columns = slice(head * size, (head + 1) * size)
            query, d_out = q_ref[:, head_columns], do_ref[:, head_columns]
            probs = head_probs(key, query, scale, barred)
            d_probs = times_t(value, d_out)
            inner = jnp.sum(probs * d_probs, axis=0, keepdims=True)
            d_scores = (probs * (d_probs - inner)).astype(BF16)
            part_value = times(probs.astype(BF16), d_out)
            part_key = times(d_scores, query) * scale
            d_value = part_value if d_value is None else d_value + part_value
            d_key = part_key if d_key is None else d_key + part_key
            d_query = (times_rows(key, d_scores) * scale).T
            start = (group * (groups + 2) + member) * size
            d_raw, d_gain = head_backward(
                d_query, raw_ref[:, start : start + size], cosine, sine, gain
            )
            dq_ref[:, head_columns] = d_raw
            gain_grad += d_gain
        for part, place in ((d_key, columns), (d_value, value_columns)):
            near_ref[:rows, place] = part[:rows]
            near_ref[rows:, place] = part[2 * rows : 3 * rows]
            cross_ref[:rows, place] = part[rows : 2 * rows].astype(BF16)
            cross_ref[rows:, place] = part[3 * rows :].astype(BF16)
    gain_grad_ref[...] = gain_grad


def assemble_kernel(groups, dq_ref, near_ref, cross_ref, far_ref, raw_ref, cos_ref, sin_ref, gain_ref, out_ref, gain_grad_ref):
    size = gain_ref.shape[1]
    kv_heads = raw_ref.shape[1] // ((groups + 2) * size)
    rows = raw_ref.shape[0]
    both = near_ref[:rows, :] + cross_ref[:rows, :].astype(F32) + far_ref[...].astype(F32)
    gain_grad = jnp.zeros_like(gain_ref[...])
    for group in range(kv_heads):
        start = group * (groups + 2) * size
        out_ref[:, start : start + groups * size] = dq_ref[
            :, group * groups * size : (group + 1) * groups * size
        ]
        start += groups * size
        d_raw, d_gain = head_backward(
            both[:, group * size : (group + 1) * size],
            raw_ref[:, start : start + size],
            cos_ref[...],
            sin_ref[...],
            gain_ref[...],
        )
        gain_grad += d_gain
        out_ref[:, start : start + size] = d_raw
        value_start = (kv_heads + group) * size
        out_ref[:, start + size : start + 2 * size] = both[
            :, value_start : value_start + size
        ].astype(BF16)
    gain_grad_ref[...] = gain_grad


def sum_chips(partial):
    return lax.psum_scatter(partial, CHIP_AXES, scatter_dimension=0, tiled=True)


def spread_pack(pack):
    return jnp.broadcast_to(pack, (lax.axis_size(CHIP_AXES),) + pack.shape)


def gather_pack(spread):
    chips, rows, columns = spread.shape
    core = lax.axis_index("core")
    plane = lax.all_to_all(spread, CHIP_AXES, split_axis=0, concat_axis=0, tiled=True)
    other = swap_core(plane)
    both = jnp.zeros((chips, CORES, rows, columns), BF16)
    both = lax.dynamic_update_slice(both, plane[:, None], (0, core, 0, 0))
    both = lax.dynamic_update_slice(both, other[:, None], (0, 1 - core, 0, 0))
    return both.reshape(-1, columns)


def finish_kernel(steps, core_ref, sum_ref, other_ref, gateup_ref, down_ref, *rest):
    core = core_ref[0]
    rows, hidden = down_ref.shape
    padded = steps * TILE
    half = TILE // 2
    first = core == 0
    mine = sum_ref[pl.ds(pl.multiple_of(core * rows, rows), rows), :].astype(F32)
    other = other_ref[...].astype(F32)
    low = jnp.where(first, mine, other)
    high = jnp.where(first, other, mine)
    gateup_ref[:, 0, :] = low[:, :hidden]
    gateup_ref[:, 1, :] = high[:, :hidden]
    for step in range(steps):
        source = padded + step * half
        for part, columns in enumerate((low, high)):
            place = step * TILE + part * half
            size = min(half, hidden - place)
            if size > 0:
                down_ref[:, place : place + size] = columns[:, source : source + size]
    for ref in rest:
        start = padded + steps * half
        size = low.shape[1] - start
        ref[:, :size] = low[:, start:]
        ref[:, size:] = high[:, start:]


def finish(summed, steps, hidden):
    core = lax.axis_index("core")
    rows, columns = summed.shape[0] // 2, summed.shape[1]
    other = swap_core(lax.dynamic_slice_in_dim(summed, (1 - core) * rows, rows, 0))
    extra = 2 * (columns - steps * (TILE + TILE // 2))
    return pl.pallas_call(
        functools.partial(finish_kernel, steps),
        grid=(1,),
        in_specs=[
            pl.BlockSpec(memory_space=pltpu.SMEM),
            whole(summed.shape),
            whole(other.shape),
        ],
        out_specs=[whole((rows, 2, hidden)), whole((rows, hidden))]
        + [whole((rows, extra))] * (extra > 0),
        out_shape=[
            jax.ShapeDtypeStruct((rows, 2, hidden), F32),
            jax.ShapeDtypeStruct((rows, hidden), F32),
        ]
        + [jax.ShapeDtypeStruct((rows, extra), F32)] * (extra > 0),
        compiler_params=pltpu.CompilerParams(vmem_limit_bytes=VMEM_LIMIT),
        cost_estimate=pl.CostEstimate(
            flops=4 * rows * columns, bytes_accessed=16 * rows * columns, transcendentals=0
        ),
        name="finish_gradients",
    )(core.reshape(1).astype(jnp.int32), summed, other)


def halves(proj, out):
    first = lax.axis_index("core") == 0
    half = (proj.shape[1] + out.shape[1]) // 2
    late = jnp.concatenate([proj[:, half:], out], axis=1)
    early = proj[:, :half]
    return jnp.where(first, early, late), jnp.where(first, late, early)


def body(
    hidden_in,
    cotangent,
    seq_lengths,
    deal_order,
    mixer_gain,
    mixer_project,
    mixer_kernel,
    mixer_output,
    first_gain,
    first_gateup,
    first_down,
    attend_gain,
    attend_project,
    query_gain,
    key_gain,
    attend_output,
    second_gain,
    second_gateup,
    second_down,
):
    shards = lax.axis_size(TOKEN_AXES)
    contexts = lax.axis_size(CTX_AXES)
    members = lax.axis_size("tp")
    row_count, width = hidden_in.shape
    piece_rows = row_count // shards
    part_rows = piece_rows // members
    chunk = row_count // members
    device = lax.axis_index(TOKEN_AXES)
    own = lax.axis_index("tp")
    core = lax.axis_index("core")
    core_ref = core.reshape(1).astype(jnp.int32)
    depth = mixer_gain.shape[0]
    channels = mixer_output.shape[0]
    hidden = first_down.shape[0]
    heads_width = attend_output.shape[0]
    steps = -(-hidden // TILE)
    padded = steps * TILE
    ffn_width = 3 * padded
    block = TILE + TILE // 2

    piece_table = deal_order.reshape(shards, shards, piece_rows)[:, :, 0]
    anchor = piece_table // row_count
    anchor_piece = piece_table % row_count // piece_rows
    send_piece = jnp.sum(jnp.where(anchor == device, anchor_piece, 0), axis=1)
    my_anchor = lax.dynamic_index_in_dim(anchor, device, 0, keepdims=False)
    gains_row = jnp.concatenate(
        [mixer_gain, first_gain, attend_gain, second_gain, jnp.zeros((width - 4 * depth,), BF16)]
    )

    def my_part(rows):
        parts = rows.reshape(shards, members, part_rows, width)
        return lax.dynamic_index_in_dim(parts, own, 1, keepdims=False)[send_piece]

    outgoing = jnp.concatenate(
        [
            my_part(hidden_in),
            my_part(cotangent),
            jnp.broadcast_to(gains_row, (shards, 1, width)),
        ],
        axis=1,
    )
    outgoing, weights = lax.optimization_barrier(
        (
            outgoing,
            (
                mixer_project,
                mixer_output,
                first_gateup,
                first_down,
                attend_project,
                attend_output,
                second_gateup,
                second_down,
            ),
        )
    )
    mixer_project, mixer_output, first_gateup, first_down = weights[:4]
    attend_project, attend_output, second_gateup, second_down = weights[4:]
    arrived = lax.all_to_all(outgoing, TOKEN_AXES, split_axis=0, concat_axis=0, tiled=True)

    def pack_ffn(gateup, down):
        wide = jnp.pad(gateup, ((0, 0), (0, 0), (0, padded - hidden)))
        wide = wide.reshape(depth, 2, steps, TILE).transpose(0, 2, 1, 3).reshape(depth, -1)
        return [wide, jnp.pad(down.T, ((0, 0), (0, padded - hidden)))]

    mixer_pack = jnp.concatenate([mixer_project.reshape(depth, -1), mixer_output.T], axis=1)
    first_pack = jnp.concatenate(
        pack_ffn(first_gateup, first_down) + [attend_project, attend_output.T], axis=1
    )
    second_pack = jnp.concatenate(pack_ffn(second_gateup, second_down), axis=1)
    mixer_pack = spread_pack(mixer_pack)
    arrived, mixer_pack = lax.optimization_barrier((arrived, mixer_pack))
    first_all = lax.all_gather(first_pack, TOKEN_AXES, axis=0, tiled=True)
    second_all = lax.all_gather(second_pack, TOKEN_AXES, axis=0, tiled=True)
    project_b = first_all[:, ffn_width : ffn_width + attend_project.shape[1]]
    output_b_t = first_all[:, ffn_width + attend_project.shape[1] :]
    mixer_all = gather_pack(mixer_pack)
    project_a = mixer_all[:, : 3 * channels]
    output_a_t = mixer_all[:, 3 * channels :]
    gains = (
        arrived[:, 2 * part_rows, : 4 * depth]
        .reshape(shards, 4, depth)
        .transpose(1, 0, 2)
        .reshape(4, width)
        .astype(F32)
    )
    gain_a, gain_f, gain_b, gain_s = gains[0], gains[1], gains[2], gains[3]
    parts = arrived[:, : 2 * part_rows][my_anchor]
    own_tokens = parts[:, :part_rows].reshape(chunk, width)
    own_back = parts[:, part_rows:].reshape(chunk, width)
    stream0 = own_tokens.astype(F32)
    upstream = own_back.astype(F32)
    both = tp_gather(jnp.concatenate([own_tokens, own_back]))
    back_s = jnp.concatenate([slot[chunk:] for slot in both])

    gathered = jnp.arange(row_count)
    member_of = (own - gathered // chunk) % members
    offsets = (
        gathered % chunk // part_rows * piece_rows + member_of * part_rows + gathered % part_rows
    )
    to_gathered = (offsets[:, None] == gathered[None, :]).astype(BF16)
    to_dealt = (offsets[None, :] == gathered[:, None]).astype(BF16)
    tokens = times(to_dealt, jnp.concatenate([slot[:chunk] for slot in both]))

    kernel_taps = mixer_kernel.shape[0]
    halo = kernel_taps - 1
    local_rows = device * row_count + jnp.arange(row_count)
    halo_segment, unused = locate(
        seq_lengths, local_rows[0] - halo + jnp.arange(row_count + halo)
    )
    segment, places = locate(seq_lengths, device * row_count + offsets)
    ctx = lax.axis_index(CTX_AXES)
    group_rows = jnp.concatenate(
        [
            (lax.axis_index(GROUP_AXES) * contexts + (ctx ^ mask)) * row_count + offsets
            for mask in range(contexts)
        ]
    )
    key_segment, key_places = locate(seq_lengths, group_rows)
    allowed = (segment[None, :] == key_segment[:, None]) & (key_places[:, None] <= places[None, :])
    barred = jnp.where(allowed, 0.0, NEGATIVE).astype(BF16)
    half_dim = HD // 2
    frequency = ROPE_BASE ** (-(jnp.arange(half_dim).astype(F32) * 2.0 / HD))
    angles = places.astype(F32)[:, None] * frequency[None, :]
    cosine = jnp.cos(angles)
    sine = jnp.sin(angles)

    kernel_local = lax.dynamic_slice_in_dim(mixer_kernel, own * channels, channels, 1).astype(F32)
    mixer_in = norm_rows(tokens, gain_a).astype(BF16)
    mixer_in_other = swap_core(mixer_in)
    halo_pad = 16
    halo_in = from_behind(mixer_in[row_count - halo_pad :], 1)
    proj_a = times(jnp.concatenate([halo_in, mixer_in]), project_a)
    proj_b_part = proj_a[:, :channels]
    proj_c_part = proj_a[halo_pad:, channels : 2 * channels]
    proj_x_part = proj_a[:, 2 * channels :]
    extended = (proj_b_part * proj_x_part)[halo_pad - halo :].astype(BF16).astype(F32)
    conv_out = shortconv(extended, kernel_local, halo_segment)
    gated_rows = (proj_c_part * conv_out).astype(BF16)
    gated_parts = arrange(to_gathered, gated_rows)
    stream1, normed = add_norm(
        tp_scatter(tp_chunks(times_t(gated_parts, output_a_t))), stream0, gain_f
    )

    normed_f = tp_gather(normed)
    stream2, normed = add_norm(
        tp_scatter(ffn_forward(normed_f, first_all, steps)), stream1, gain_b
    )

    groups = H // KVH
    score_scale = HD ** (-0.5)
    qgain_f = query_gain.astype(F32)[None]
    kgain_f = key_gain.astype(F32)[None]
    attend_in = jnp.concatenate(tp_gather(normed))
    proj_b = times(attend_in, project_b)
    kv_width = 2 * HD * (proj_b.shape[1] // (HD * (groups + 2)))
    query_b, key_value = one_step(
        functools.partial(heads_kernel, groups),
        [proj_b, cosine, sine, qgain_f, kgain_f],
        [
            jax.ShapeDtypeStruct((row_count, heads_width), BF16),
            jax.ShapeDtypeStruct((row_count, kv_width), BF16),
        ],
        SMALL_LIMIT,
        "heads",
        20 * proj_b.size,
    )
    key_value_z = swap_ctx(key_value, 2)
    key_value_core = swap_core(jnp.concatenate([key_value, key_value_z]))
    key_value_all = jnp.concatenate(
        [key_value, key_value_core[:row_count], key_value_z, key_value_core[row_count:]]
    )
    attend_flops = 2 * key_value_all.shape[0] * query_b.size
    (attended,) = one_step(
        functools.partial(attend_kernel, score_scale, HD),
        [query_b, key_value_all, barred],
        [jax.ShapeDtypeStruct(query_b.shape, BF16)],
        MIDDLE_LIMIT,
        "attend",
        2 * attend_flops,
    )
    stream3, normed = add_norm(
        tp_scatter(tp_chunks(times_t(attended, output_b_t))), stream2, gain_s
    )

    normed_s = tp_gather(normed)
    d_chunks, out_chunks, keep, side = ffn_backward(
        core_ref, normed_s, [back_s], second_all, steps, True
    )
    d_stream3, back_b, gain_s_grad = norm_backward(
        tp_scatter(d_chunks), stream3, gain_s, upstream
    )
    out_others = [shift_tp(out_chunks[k], -k) for k in range(1, members)]
    side_other = swap_core(side)
    ffn_lefts = [(side, 0), (side_other, 0), (side, 1), (side_other, 1)]
    ffn_cols = steps * block
    side_start = 2 * width // block
    partial = gradient(
        ffn_lefts, keep, side_other, side_start, block, steps, padded, width, ffn_cols, 0, None
    )

    back_b = tp_gather(back_b)
    back_b, partial = lax.optimization_barrier((back_b, partial))
    second_sums = sum_chips(partial)
    back_b = jnp.concatenate(back_b)
    back_b_other = swap_core(back_b)
    attend_in_other = swap_core(attend_in)
    d_attended_b = times(back_b, output_b_t).astype(BF16)
    pair_rows = 2 * row_count
    d_query, near, cross, qgain_grad = one_step(
        functools.partial(attend_backward_kernel, score_scale),
        [query_b, d_attended_b, key_value_all, barred, proj_b, cosine, sine, qgain_f],
        [
            jax.ShapeDtypeStruct(query_b.shape, BF16),
            jax.ShapeDtypeStruct((pair_rows, kv_width), F32),
            jax.ShapeDtypeStruct((pair_rows, kv_width), BF16),
            jax.ShapeDtypeStruct((1, HD), F32),
        ],
        MIDDLE_LIMIT,
        "attend_backward",
        5 * attend_flops,
    )
    cross = swap_core(cross)
    far = (near[row_count:] + cross[row_count:].astype(F32)).astype(BF16)
    d_proj_b, kgain_grad = one_step(
        functools.partial(assemble_kernel, groups),
        [d_query, near, cross, swap_ctx(far, 2), proj_b, cosine, sine, kgain_f],
        [jax.ShapeDtypeStruct(proj_b.shape, BF16), jax.ShapeDtypeStruct((1, HD), F32)],
        SMALL_LIMIT,
        "assemble",
        20 * proj_b.size,
    )
    d_stream2, back_f, gain_b_grad = norm_backward(
        tp_scatter(tp_chunks(times_t(d_proj_b, project_b))), stream2, gain_b, d_stream3
    )
    keep, send = halves(d_proj_b, attended)
    first_core = core == 0
    attend_cols = keep.shape[1]
    small_tile = 2 * (heads_width + attend_project.shape[1]) // 16
    third = gradient(
        [
            (attend_in, 0),
            (attend_in_other, 0),
            (jnp.where(first_core, attend_in, back_b), 0),
            (jnp.where(first_core, attend_in_other, back_b_other), 0),
        ],
        keep,
        swap_core(send),
        0,
        small_tile,
        attend_cols // small_tile,
        attend_project.shape[1] - attend_cols,
        width,
        ffn_cols + attend_cols,
        ffn_cols // small_tile,
        None,
    )

    back_f = tp_gather(back_f)
    back_f, third = lax.optimization_barrier((back_f, third))
    left_x, left_b = jnp.concatenate(normed_f), jnp.concatenate(back_f)
    left_others = [swap_core(left_x), swap_core(left_b)]
    d_chunks, unused, keep, side = ffn_backward(
        core_ref, normed_f, back_f, first_all, steps, False
    )
    d_chunks, left_others = lax.optimization_barrier((d_chunks, left_others))
    d_chunks, side_other = lax.optimization_barrier((d_chunks, swap_core(side)))
    ffn_lefts = [(left_x, 0), (left_others[0], 0), (left_b, 0), (left_others[1], 0)]
    partial = gradient(
        ffn_lefts,
        keep,
        side_other,
        0,
        block,
        steps,
        padded,
        width,
        ffn_cols + attend_cols,
        0,
        third,
    )

    d_parts, partial = lax.optimization_barrier((tp_scatter(d_chunks), partial))
    d_stream1, back_a, gain_f_grad = norm_backward(d_parts, stream1, gain_f, d_stream2)

    back_a = tp_gather(back_a)
    first_sums = sum_chips(partial)
    back_a = arrange(to_dealt, jnp.concatenate(back_a))
    back_a_other = swap_core(back_a)
    d_gated = times(back_a, output_a_t)
    d_cgate = d_gated * conv_out
    d_conv = d_gated * proj_c_part
    unused, pullback = jax.vjp(
        lambda ext_rows, kernel_in: shortconv(ext_rows, kernel_in, halo_segment),
        extended,
        kernel_local,
    )
    d_extended, kernel_grad = pullback(d_conv)
    returned = from_behind(d_extended[:halo], -1)
    d_product = d_extended[halo:] + jnp.concatenate(
        [jnp.zeros((row_count - halo, channels), F32), returned]
    )
    d_proj_a = jnp.concatenate(
        [
            d_product * proj_x_part[halo_pad:],
            d_cgate,
            d_product * proj_b_part[halo_pad:],
        ],
        axis=1,
    ).astype(BF16)
    d_proj_a, out_others = lax.optimization_barrier((d_proj_a, out_others))
    stream4 = stream3 + add_parts([out_chunks[0], *out_others])
    d_chunks = tp_chunks(times_t(arrange(to_gathered, d_proj_a), project_a))
    keep, send = halves(d_proj_a, gated_rows)
    mixer_cols = keep.shape[1]
    partial = gradient(
        [
            (mixer_in, 0),
            (mixer_in_other, 0),
            (jnp.where(first_core, mixer_in, back_a), 0),
            (jnp.where(first_core, mixer_in_other, back_a_other), 0),
        ],
        keep,
        swap_core(send),
        0,
        mixer_cols,
        1,
        3 * channels - mixer_cols,
        width,
        mixer_cols,
        0,
        None,
    )
    kernel_cols = kernel_taps * channels
    gain_start = kernel_cols + 2 * HD
    shared = jnp.concatenate([kernel_grad.reshape(-1), qgain_grad[0], kgain_grad[0]])
    early_gains = [
        grad.reshape(shards, depth) for grad in (gain_f_grad, gain_b_grad, gain_s_grad)
    ]
    early_row = jnp.concatenate(
        [
            jnp.broadcast_to(shared, (shards, gain_start)),
            jnp.pad(
                jnp.concatenate(early_gains, axis=1),
                ((0, 0), (0, width - gain_start - 3 * depth)),
            ),
        ],
        axis=1,
    )
    d_parts, early_row = lax.optimization_barrier((tp_scatter(d_chunks), early_row))
    unused, d_stream0, gain_a_grad = norm_backward(d_parts, stream0, gain_a, d_stream1)

    slot_for_anchor = jnp.sum(
        jnp.where(
            my_anchor[None, :] == jnp.arange(shards)[:, None], jnp.arange(shards)[None, :], 0
        ),
        axis=1,
    )
    late_start = gain_start + 3 * depth
    late_row = jnp.pad(
        gain_a_grad.reshape(shards, depth), ((0, 0), (late_start, width - late_start - depth))
    )
    leaving = jnp.concatenate(
        [d_stream0, stream4.astype(BF16), (early_row + late_row).astype(BF16)]
    )
    line = jnp.arange(shards * piece_rows)
    target, item = line // piece_rows, line % piece_rows
    source = jnp.where(
        item < 2 * part_rows,
        item // part_rows * chunk
        + jnp.repeat(slot_for_anchor, piece_rows) * part_rows
        + item % part_rows,
        jnp.where(item == 2 * part_rows, 2 * chunk + target, -1),
    )
    to_leaving = (source[:, None] == jnp.arange(leaving.shape[0])[None, :]).astype(BF16)
    leaving = arrange(to_leaving, leaving)
    home = lax.all_to_all(
        leaving.reshape(shards, piece_rows, width),
        TOKEN_AXES,
        split_axis=0,
        concat_axis=0,
        tiled=True,
    )
    second_grads = finish(second_sums, steps, hidden)
    home, partial, second_grads = lax.optimization_barrier((home, partial, second_grads))
    place = jnp.arange(2 * chunk + 8)
    small_line = (place == 2 * chunk) | (place == 2 * chunk + 1)
    wanted = (
        place % chunk // part_rows * piece_rows
        + place // chunk * part_rows
        + place % part_rows
    )
    to_payload = jnp.where(
        (place < 2 * chunk)[:, None],
        wanted[:, None] == line[None, :],
        small_line[:, None] & (item == 2 * part_rows)[None, :],
    ).astype(BF16)
    payload = times(to_payload, home.reshape(shards * piece_rows, width))
    rounded = payload.astype(BF16).astype(F32)
    payload = jnp.where((place == 2 * chunk + 1)[:, None], payload - rounded, payload)
    last = tp_gather(payload.astype(BF16))
    mixer_home = lax.all_to_all(
        partial.reshape(shards, depth, mixer_cols),
        TOKEN_AXES,
        split_axis=0,
        concat_axis=0,
        tiled=True,
    )
    home_rows = (
        jnp.repeat(jnp.tile(send_piece, members), part_rows) * piece_rows
        + member_of * part_rows
        + gathered % part_rows
    )
    to_arrival = (home_rows[None, :] == gathered[:, None]).astype(BF16)
    input_gradient = arrange(to_arrival, jnp.concatenate([slot[:chunk] for slot in last]))
    layer_out = arrange(to_arrival, jnp.concatenate([slot[chunk : 2 * chunk] for slot in last]))
    first_sums, layer_out, input_gradient = lax.optimization_barrier(
        (first_sums, layer_out, input_gradient)
    )
    *first_grads, attend_grads = finish(first_sums, steps, hidden)
    first_grads, attend_grads, mixer_home = lax.optimization_barrier(
        (first_grads, attend_grads, mixer_home)
    )
    mixer_home = mixer_home.reshape(shards // CORES, CORES, depth, mixer_cols)
    mixer_grads = jnp.sum(mixer_home.astype(F32), axis=0)
    mixer_grads = jnp.concatenate([mixer_grads[0], mixer_grads[1]], axis=1)
    smalls = [
        slot[2 * chunk].astype(F32) + slot[2 * chunk + 1].astype(F32) for slot in last
    ]
    totals = sum(smalls)
    kernel_rows = jnp.stack([small[:kernel_cols].reshape(kernel_taps, channels) for small in smalls])
    kernel_total = jnp.concatenate(
        [
            lax.dynamic_index_in_dim(kernel_rows, (own - member) % members, 0, keepdims=False)
            for member in range(members)
        ],
        axis=1,
    )
    qgain_total = totals[kernel_cols : kernel_cols + HD]
    kgain_total = totals[kernel_cols + HD : kernel_cols + 2 * HD]
    gain_totals = totals[gain_start : gain_start + 4 * depth].reshape(4, depth)

    gateup_s_grad, down_s_grad = second_grads
    gateup_f_grad, down_f_grad = first_grads
    proj_cols = attend_project.shape[1]
    return (
        layer_out,
        input_gradient,
        gain_totals[3],
        mixer_grads[:, : 3 * channels].reshape(depth, 3, channels),
        kernel_total,
        mixer_grads[:, 3 * channels :].T,
        gain_totals[0],
        gateup_f_grad,
        down_f_grad.T,
        gain_totals[1],
        attend_grads[:, :proj_cols],
        qgain_total,
        kgain_total,
        attend_grads[:, proj_cols:].T,
        gain_totals[2],
        gateup_s_grad,
        down_s_grad.T,
    )


def solution(mesh):
    names = TOKEN_AXES + ("tp",)
    rings = mesh.shape["fsdp"] // 2, 2, mesh.shape["ctx"] // 2, 2, mesh.shape["tp"]
    tokens = P(TOKEN_AXES, None)
    rows = P(TOKEN_AXES)
    three = P(TOKEN_AXES, None, "tp")
    two = P(TOKEN_AXES, "tp")
    turned = P("tp", TOKEN_AXES)
    return jax.shard_map(
        body,
        mesh=Mesh(mesh.devices.reshape(rings), names),
        in_specs=(
            tokens, tokens, P(), P(),
            rows, three, P(), turned,
            rows, three, turned,
            rows, two, P(), P(), turned,
            rows, three, turned,
        ),
        out_specs=(
            tokens, tokens,
            rows, three, P(), turned,
            rows, three, turned,
            rows, two, P(), P(), turned,
            rows, three, turned,
        ),
        check_vma=False,
    )
```

```python
import functools

import jax
import jax.numpy as jnp
from jax import lax
from jax.experimental import pallas as pl
from jax.experimental.pallas import tpu as pltpu
from jax.sharding import Mesh, PartitionSpec as P

H = 24
KVH = 8
HD = 64

EPSILON = 1e-05
ROPE_BASE = 1000000.0
NEGATIVE = -1e30

CHIP_AXES = ("x", "z_hi", "z_lo")
TOKEN_AXES = CHIP_AXES + ("core",)
GROUP_AXES = ("x", "z_hi")
CTX_AXES = ("z_lo", "core")
Z_AXES = ("z_hi", "z_lo")
CORES = 2
TILE = 256
VMEM_LIMIT = 48 * 1024 * 1024
MIDDLE_LIMIT = 24 * 1024 * 1024
SMALL_LIMIT = 12 * 1024 * 1024
F32 = jnp.float32
BF16 = jnp.bfloat16


def norm_rows(values, scales):
    return values * lax.rsqrt(jnp.mean(values * values, axis=-1, keepdims=True) + EPSILON) * scales


def locate(lengths, positions):
    seq_ends = jnp.cumsum(lengths)
    segment = jnp.sum((positions[:, None] >= seq_ends[None, :]).astype(jnp.int32), axis=1)
    starts = seq_ends - lengths
    first_row = jnp.sum(
        jnp.where(segment[:, None] == jnp.arange(lengths.shape[0])[None, :], starts[None, :], 0),
        axis=1,
    )
    return (segment, positions - first_row)


def shortconv(extended, kernel_in, segment):
    kernel_taps = kernel_in.shape[0]
    out_rows = extended.shape[0] - kernel_taps + 1
    result = kernel_in[0] * extended[kernel_taps - 1 :]
    for t in range(1, kernel_taps):
        earlier = extended[kernel_taps - 1 - t : kernel_taps - 1 - t + out_rows]
        same_seq = (
            segment[kernel_taps - 1 - t : kernel_taps - 1 - t + out_rows]
            == segment[kernel_taps - 1 :]
        ).astype(F32)[:, None]
        result = result + kernel_in[t] * earlier * same_seq
    return result


def from_behind(block, distance):
    devices = range(lax.axis_size(CTX_AXES))
    route = [(i - distance, i) for i in devices if i - distance in devices]
    return lax.ppermute(block, CTX_AXES, route)


def swap_ctx(block, mask):
    return lax.ppermute(block, CTX_AXES, [(i, i ^ mask) for i in range(lax.axis_size(CTX_AXES))])


def swap_core(block):
    return lax.ppermute(block, "core", [(0, 1), (1, 0)])


def shift_tp(block, distance):
    members = lax.axis_size("tp")
    return lax.ppermute(block, "tp", [(i, (i + distance) % members) for i in range(members)])


def tp_gather(shard):
    return [shard] + [shift_tp(shard, k) for k in range(1, lax.axis_size("tp"))]


def tp_chunks(partial):
    rows = partial.shape[0] // lax.axis_size("tp")
    return [
        partial[k * rows : (k + 1) * rows].astype(F32 if k == 0 else BF16)
        for k in range(lax.axis_size("tp"))
    ]


def tp_scatter(chunks):
    return [chunks[0]] + [shift_tp(chunks[k], -k) for k in range(1, len(chunks))]


def add_parts(parts):
    total = parts[0]
    for part in parts[1:]:
        total = total + part.astype(F32)
    return total


def arrange(order, rows):
    return times(order, rows).astype(BF16)


def times(left, right):
    return lax.dot_general(left, right, (((1,), (0,)), ((), ())), preferred_element_type=F32)


def times_t(left, right):
    return lax.dot_general(left, right, (((1,), (1,)), ((), ())), preferred_element_type=F32)


def times_rows(left, right):
    return lax.dot_general(left, right, (((0,), (0,)), ((), ())), preferred_element_type=F32)


def assemble(chunk_refs, target):
    rows = chunk_refs[0].shape[0]
    for k, ref in enumerate(chunk_refs):
        target[k * rows : (k + 1) * rows, :] = ref[...]


def spread(total, chunk_refs):
    rows = chunk_refs[0].shape[0]
    for k, ref in enumerate(chunk_refs):
        ref[...] = total[k * rows : (k + 1) * rows, :].astype(ref.dtype)


def whole(shape):
    return pl.BlockSpec(shape, lambda *_: (0,) * len(shape))


def one_step(kernel, operands, out_shape, limit, name, flops):
    size = sum(v.size * v.dtype.itemsize for v in list(operands) + list(out_shape))
    return pl.pallas_call(
        kernel,
        grid=(1,),
        in_specs=[whole(v.shape) for v in operands],
        out_specs=[whole(v.shape) for v in out_shape],
        out_shape=out_shape,
        compiler_params=pltpu.CompilerParams(vmem_limit_bytes=limit),
        cost_estimate=pl.CostEstimate(flops=flops, bytes_accessed=size, transcendentals=0),
        name=name,
    )(*operands)


def sum_refs(refs):
    total = refs[0][...]
    for ref in refs[1:]:
        total = total + ref[...].astype(F32)
    return total


def add_norm_kernel(*refs):
    stream_ref, gain_ref, out_ref, normed_ref = refs[-4:]
    stream = stream_ref[...] + sum_refs(refs[:-4])
    out_ref[...] = stream
    normed_ref[...] = norm_rows(stream, gain_ref[...]).astype(BF16)


def add_norm(parts, stream, gain):
    return one_step(
        add_norm_kernel,
        [*parts, stream, gain[None]],
        [jax.ShapeDtypeStruct(stream.shape, F32), jax.ShapeDtypeStruct(stream.shape, BF16)],
        SMALL_LIMIT,
        "add_norm",
        10 * stream.size,
    )


def norm_backward_kernel(*refs):
    stream_ref, gain_ref, upward_ref, out_ref, rounded_ref, gain_grad_ref = refs[-6:]
    stream = stream_ref[...]
    d_normed = sum_refs(refs[:-6])
    spread_of = lax.rsqrt(jnp.mean(stream * stream, axis=1, keepdims=True) + EPSILON)
    gain_grad_ref[...] = jnp.sum(d_normed * stream * spread_of, axis=0, keepdims=True)
    scaled = d_normed * gain_ref[...]
    inner = jnp.mean(scaled * stream, axis=1, keepdims=True)
    result = upward_ref[...] + spread_of * scaled - stream * (
        spread_of * spread_of * spread_of * inner
    )
    out_ref[...] = result
    rounded_ref[...] = result.astype(BF16)


def norm_backward(parts, stream, gain, upward):
    out, rounded, gain_grad = one_step(
        norm_backward_kernel,
        [*parts, stream, gain[None], upward],
        [
            jax.ShapeDtypeStruct(stream.shape, F32),
            jax.ShapeDtypeStruct(stream.shape, BF16),
            jax.ShapeDtypeStruct((1, stream.shape[1]), F32),
        ],
        SMALL_LIMIT,
        "norm_backward",
        20 * stream.size,
    )
    return out, rounded, gain_grad[0]


def weight_specs(depth, steps):
    return [
        pl.BlockSpec((depth, 2 * TILE), lambda j: (0, j)),
        pl.BlockSpec((depth, TILE), lambda j: (0, 2 * steps + j)),
    ]


def chunk_shapes(count, rows, width):
    return [jax.ShapeDtypeStruct((rows, width), F32 if k == 0 else BF16) for k in range(count)]


def ffn_forward_kernel(count, *refs):
    x_refs, (gu_ref, dn_ref), outs = refs[:count], refs[count : count + 2], refs[count + 2 : -2]
    x_all, total = refs[-2:]
    step = pl.program_id(0)

    @pl.when(step == 0)
    def _():
        assemble(x_refs, x_all)
        total[...] = jnp.zeros_like(total)

    both = times(x_all[...], gu_ref[...])
    gate, up = both[:, :TILE], both[:, TILE:]
    active = (gate * jax.nn.sigmoid(gate) * up).astype(BF16)
    total[...] += times_t(active, dn_ref[...])

    @pl.when(step == pl.num_programs(0) - 1)
    def _():
        spread(total[...], outs)


def ffn_forward(chunks, pack, steps):
    count, (rows, width) = len(chunks), chunks[0].shape
    tokens = count * rows
    return pl.pallas_call(
        functools.partial(ffn_forward_kernel, count),
        grid=(steps,),
        in_specs=[whole((rows, width))] * count + weight_specs(width, steps),
        out_specs=[whole((rows, width))] * count,
        out_shape=chunk_shapes(count, rows, width),
        scratch_shapes=[pltpu.VMEM((tokens, width), BF16), pltpu.VMEM((tokens, width), F32)],
        compiler_params=pltpu.CompilerParams(vmem_limit_bytes=VMEM_LIMIT),
        cost_estimate=pl.CostEstimate(
            flops=2 * tokens * width * 3 * TILE * steps,
            bytes_accessed=2 * width * 3 * TILE * steps,
            transcendentals=tokens * TILE * steps,
        ),
        name="ffn_forward",
    )(*chunks, pack, pack)


def ffn_backward_kernel(count, back_count, forward, core_ref, *refs):
    x_refs, b_refs = refs[:count], refs[count : count + back_count]
    place = count + back_count
    gu_ref, dn_ref = refs[place : place + 2]
    place += 2
    back_outs = refs[place : place + count]
    place += count
    if forward:
        outs = refs[place : place + count]
        place += count
    keep_ref, side_ref = refs[place : place + 2]
    scratch = refs[place + 2 :]
    x_all, b_all, d_total = scratch[:3]
    step = pl.program_id(0)
    width = x_all.shape[1]

    @pl.when(step == 0)
    def _():
        assemble(x_refs, x_all)
        assemble(b_refs, b_all)
        if forward:
            side_ref[:, :width] = x_all[...]
            side_ref[:, width : 2 * width] = b_all[...]
        d_total[...] = jnp.zeros_like(d_total)
        if forward:
            scratch[3][...] = jnp.zeros_like(scratch[3])

    both = times(x_all[...], gu_ref[...])
    gate, up = both[:, :TILE], both[:, TILE:]
    d_active = times(b_all[...], dn_ref[...])
    sigmoid = jax.nn.sigmoid(gate)
    silu = gate * sigmoid
    active = (silu * up).astype(BF16)
    if forward:
        scratch[3][...] += times_t(active, dn_ref[...])
    d_gate = (d_active * up * (sigmoid * (1.0 + gate * (1.0 - sigmoid)))).astype(BF16)
    d_up = (d_active * silu).astype(BF16)
    d_total[...] += times_t(jnp.concatenate([d_gate, d_up], axis=1), gu_ref[...])
    first = core_ref[0] == 0
    half = TILE // 2
    low, high = active[:, :half], active[:, half:]
    offset = 2 * width if forward else 0
    wide = pl.multiple_of(step * TILE, TILE)
    narrow = pl.multiple_of(pl.num_programs(0) * TILE + step * half, half)
    side_wide = pl.multiple_of(offset + wide, TILE)
    side_narrow = pl.multiple_of(offset + narrow, half)

    @pl.when(first)
    def _():
        keep_ref[:, pl.ds(wide, TILE)] = d_gate
        keep_ref[:, pl.ds(narrow, half)] = low
        side_ref[:, pl.ds(side_wide, TILE)] = d_up
        side_ref[:, pl.ds(side_narrow, half)] = high

    @pl.when(jnp.logical_not(first))
    def _():
        keep_ref[:, pl.ds(wide, TILE)] = d_up
        keep_ref[:, pl.ds(narrow, half)] = high
        side_ref[:, pl.ds(side_wide, TILE)] = d_gate
        side_ref[:, pl.ds(side_narrow, half)] = low

    @pl.when(step == pl.num_programs(0) - 1)
    def _():
        spread(d_total[...], back_outs)
        if forward:
            spread(scratch[3][...], outs)


def ffn_backward(core, chunks, back_chunks, pack, steps, forward):
    count, (rows, width) = len(chunks), chunks[0].shape
    tokens = count * rows
    block = TILE + TILE // 2
    ways = 2 if forward else 1
    side_width = (2 * width if forward else 0) + steps * block
    results = pl.pallas_call(
        functools.partial(ffn_backward_kernel, count, len(back_chunks), forward),
        grid=(steps,),
        in_specs=[pl.BlockSpec(memory_space=pltpu.SMEM)]
        + [whole(v.shape) for v in (*chunks, *back_chunks)]
        + weight_specs(width, steps),
        out_specs=[whole((rows, width))] * (ways * count)
        + [whole((tokens, steps * block)), whole((tokens, side_width))],
        out_shape=chunk_shapes(count, rows, width) * ways
        + [
            jax.ShapeDtypeStruct((tokens, steps * block), BF16),
            jax.ShapeDtypeStruct((tokens, side_width), BF16),
        ],
        scratch_shapes=[pltpu.VMEM((tokens, width), BF16)] * 2
        + [pltpu.VMEM((tokens, width), F32)] * ways,
        compiler_params=pltpu.CompilerParams(vmem_limit_bytes=VMEM_LIMIT),
        cost_estimate=pl.CostEstimate(
            flops=2 * tokens * width * (4 + ways) * TILE * steps,
            bytes_accessed=2 * width * 3 * TILE * steps + 4 * tokens * side_width,
            transcendentals=tokens * TILE * steps,
        ),
        name="ffn_both" if forward else "ffn_backward",
    )(core, *chunks, *back_chunks, pack, pack)
    return results[:count], results[count : ways * count], results[-2], results[-1]


def gradient_kernel(edge, cut, *refs):
    one_own, one_other, two_own, two_other, own_ref, other_ref = refs[:6]
    out_ref = refs[-1]
    step = pl.program_id(0)

    def product(own_left, other_left, columns):
        total = times_rows(own_left[...], own_ref[:, columns])
        total += times_rows(other_left[...], other_ref[:, columns])
        out_ref[:, columns] = total.astype(BF16)

    @pl.when(step < edge)
    def _():
        product(one_own, one_other, slice(None))

    @pl.when(step > edge if cut else step >= edge)
    def _():
        product(two_own, two_other, slice(None))

    if cut:

        @pl.when(step == edge)
        def _():
            product(one_own, one_other, slice(0, cut))
            product(two_own, two_other, slice(cut, None))


def gradient(lefts, own, other, other_start, block, steps, columns, width, out_width, out_start, target):
    tokens = own.shape[0]
    edge, cut = divmod(columns, block)

    def left_spec(index):
        return pl.BlockSpec((tokens, width), lambda j: (0, index))

    in_specs = [left_spec(index) for unused, index in lefts] + [
        pl.BlockSpec((tokens, block), lambda j: (0, j)),
        pl.BlockSpec((tokens, block), lambda j: (0, other_start + j)),
    ]
    operands = [array for array, unused in lefts] + [own, other]
    aliases = {}
    if target is not None:
        in_specs.append(pl.BlockSpec(memory_space=pl.ANY))
        operands.append(target)
        aliases = {len(operands) - 1: 0}
    return pl.pallas_call(
        functools.partial(gradient_kernel, edge, cut),
        grid=(steps,),
        in_specs=in_specs,
        out_specs=pl.BlockSpec((width, block), lambda j: (0, out_start + j)),
        out_shape=jax.ShapeDtypeStruct((width, out_width), BF16),
        input_output_aliases=aliases,
        compiler_params=pltpu.CompilerParams(vmem_limit_bytes=VMEM_LIMIT),
        cost_estimate=pl.CostEstimate(
            flops=4 * tokens * width * block * steps,
            bytes_accessed=2 * width * block * steps,
            transcendentals=0,
        ),
        name="weight_gradient",
    )(*operands)


def turn(rows, cosine, sine):
    half = rows.shape[1] // 2
    first, second = rows[:, :half], rows[:, half:]
    return jnp.concatenate(
        [first * cosine - second * sine, second * cosine + first * sine], axis=1
    )


def head_backward(d_rows, raw, cosine, sine, gain):
    d_normed = turn(d_rows, cosine, -sine)
    spread_of = lax.rsqrt(jnp.mean(raw * raw, axis=1, keepdims=True) + EPSILON)
    d_gain = jnp.sum(d_normed * raw * spread_of, axis=0, keepdims=True)
    scaled = d_normed * gain
    inner = jnp.mean(scaled * raw, axis=1, keepdims=True)
    d_raw = spread_of * scaled - raw * (spread_of * spread_of * spread_of * inner)
    return d_raw.astype(BF16), d_gain


def heads_kernel(groups, raw_ref, cos_ref, sin_ref, query_gain_ref, key_gain_ref, q_ref, kv_ref):
    size = query_gain_ref.shape[1]
    kv_heads = raw_ref.shape[1] // ((groups + 2) * size)
    cosine, sine = cos_ref[...], sin_ref[...]
    for group in range(kv_heads):
        start = group * (groups + 2) * size
        for member in range(groups):
            raw = raw_ref[:, start + member * size : start + (member + 1) * size]
            head = group * groups + member
            rows = turn(norm_rows(raw, query_gain_ref[...]), cosine, sine)
            q_ref[:, head * size : (head + 1) * size] = rows.astype(BF16)
        start += groups * size
        rows = turn(norm_rows(raw_ref[:, start : start + size], key_gain_ref[...]), cosine, sine)
        kv_ref[:, group * size : (group + 1) * size] = rows.astype(BF16)
        value_start = (kv_heads + group) * size
        kv_ref[:, value_start : value_start + size] = raw_ref[
            :, start + size : start + 2 * size
        ].astype(BF16)


def head_probs(key, query, scale, barred):
    scores = times_t(key, query) * scale + barred
    probs = jnp.exp(scores - jnp.max(scores, axis=0, keepdims=True))
    return probs / jnp.sum(probs, axis=0, keepdims=True)


def attend_kernel(scale, size, q_ref, kv_ref, barred_ref, out_ref):
    kv_heads = kv_ref.shape[1] // (2 * size)
    groups = q_ref.shape[1] // (kv_heads * size)
    barred = barred_ref[...].astype(F32)
    for head in range(kv_heads * groups):
        group = head // groups
        columns = slice(head * size, (head + 1) * size)
        key = kv_ref[:, group * size : (group + 1) * size]
        value = kv_ref[:, (kv_heads + group) * size : (kv_heads + group + 1) * size]
        probs = head_probs(key, q_ref[:, columns], scale, barred).astype(BF16)
        out_ref[:, columns] = times_rows(value, probs).T.astype(BF16)


def attend_backward_kernel(
    scale, first_ref, second_ref, third_ref, fourth_ref, weight_ref, q_ref, kv_ref, barred_ref, raw_ref, cos_ref, sin_ref, gain_ref,
    dq_ref, near_ref, cross_ref, gain_grad_ref,
):
    size = gain_ref.shape[1]
    kv_heads = kv_ref.shape[1] // (2 * size)
    groups = q_ref.shape[1] // (kv_heads * size)
    rows = kv_ref.shape[0] // 4
    cosine, sine, gain = cos_ref[...], sin_ref[...], gain_ref[...]
    barred = barred_ref[...].astype(F32)
    back = jnp.concatenate(
        [ref[...] for ref in (first_ref, second_ref, third_ref, fourth_ref)], axis=0
    )
    d_attended = times(back, weight_ref[...]).astype(BF16)
    gain_grad = jnp.zeros_like(gain)
    for group in range(kv_heads):
        columns = slice(group * size, (group + 1) * size)
        value_columns = slice((kv_heads + group) * size, (kv_heads + group + 1) * size)
        key, value = kv_ref[:, columns], kv_ref[:, value_columns]
        d_key = d_value = None
        for member in range(groups):
            head = group * groups + member
            head_columns = slice(head * size, (head + 1) * size)
            query, d_out = q_ref[:, head_columns], d_attended[:, head_columns]
            probs = head_probs(key, query, scale, barred)
            d_probs = times_t(value, d_out)
            inner = jnp.sum(probs * d_probs, axis=0, keepdims=True)
            d_scores = (probs * (d_probs - inner)).astype(BF16)
            part_value = times(probs.astype(BF16), d_out)
            part_key = times(d_scores, query) * scale
            d_value = part_value if d_value is None else d_value + part_value
            d_key = part_key if d_key is None else d_key + part_key
            d_query = (times_rows(key, d_scores) * scale).T
            start = (group * (groups + 2) + member) * size
            d_raw, d_gain = head_backward(
                d_query, raw_ref[:, start : start + size], cosine, sine, gain
            )
            dq_ref[:, head_columns] = d_raw
            gain_grad += d_gain
        for part, place in ((d_key, columns), (d_value, value_columns)):
            near_ref[:rows, place] = part[:rows]
            near_ref[rows:, place] = part[2 * rows : 3 * rows]
            cross_ref[:rows, place] = part[rows : 2 * rows].astype(BF16)
            cross_ref[rows:, place] = part[3 * rows :].astype(BF16)
    gain_grad_ref[...] = gain_grad


def assemble_kernel(groups, dq_ref, near_ref, cross_ref, far_ref, raw_ref, cos_ref, sin_ref, gain_ref, out_ref, gain_grad_ref):
    size = gain_ref.shape[1]
    kv_heads = raw_ref.shape[1] // ((groups + 2) * size)
    rows = raw_ref.shape[0]
    both = near_ref[:rows, :] + cross_ref[:rows, :].astype(F32) + far_ref[...].astype(F32)
    gain_grad = jnp.zeros_like(gain_ref[...])
    for group in range(kv_heads):
        start = group * (groups + 2) * size
        out_ref[:, start : start + groups * size] = dq_ref[
            :, group * groups * size : (group + 1) * groups * size
        ]
        start += groups * size
        d_raw, d_gain = head_backward(
            both[:, group * size : (group + 1) * size],
            raw_ref[:, start : start + size],
            cos_ref[...],
            sin_ref[...],
            gain_ref[...],
        )
        gain_grad += d_gain
        out_ref[:, start : start + size] = d_raw
        value_start = (kv_heads + group) * size
        out_ref[:, start + size : start + 2 * size] = both[
            :, value_start : value_start + size
        ].astype(BF16)
    gain_grad_ref[...] = gain_grad


def sum_chips(partial):
    return lax.psum_scatter(partial, CHIP_AXES, scatter_dimension=0, tiled=True)


def gather_pack(pack):
    chips = lax.axis_size(CHIP_AXES)
    core = lax.axis_index("core")
    plane = lax.all_to_all(
        jnp.broadcast_to(pack, (chips,) + pack.shape),
        CHIP_AXES,
        split_axis=0,
        concat_axis=0,
        tiled=True,
    )
    other = swap_core(plane)
    both = jnp.zeros((chips, CORES) + pack.shape, BF16)
    both = lax.dynamic_update_slice(both, plane[:, None], (0, core, 0, 0))
    both = lax.dynamic_update_slice(both, other[:, None], (0, 1 - core, 0, 0))
    return both.reshape(-1, pack.shape[1])


def finish_kernel(steps, core_ref, sum_ref, other_ref, gateup_ref, down_ref, *rest):
    core = core_ref[0]
    rows, hidden = down_ref.shape
    padded = steps * TILE
    half = TILE // 2
    first = core == 0
    mine = sum_ref[pl.ds(pl.multiple_of(core * rows, rows), rows), :].astype(F32)
    other = other_ref[...].astype(F32)
    low = jnp.where(first, mine, other)
    high = jnp.where(first, other, mine)
    gateup_ref[:, 0, :] = low[:, :hidden]
    gateup_ref[:, 1, :] = high[:, :hidden]
    for step in range(steps):
        source = padded + step * half
        for part, columns in enumerate((low, high)):
            place = step * TILE + part * half
            size = min(half, hidden - place)
            if size > 0:
                down_ref[:, place : place + size] = columns[:, source : source + size]
    for ref in rest:
        start = padded + steps * half
        size = low.shape[1] - start
        ref[:, :size] = low[:, start:]
        ref[:, size:] = high[:, start:]


def finish(summed, steps, hidden):
    core = lax.axis_index("core")
    rows, columns = summed.shape[0] // 2, summed.shape[1]
    other = swap_core(lax.dynamic_slice_in_dim(summed, (1 - core) * rows, rows, 0))
    extra = 2 * (columns - steps * (TILE + TILE // 2))
    return pl.pallas_call(
        functools.partial(finish_kernel, steps),
        grid=(1,),
        in_specs=[
            pl.BlockSpec(memory_space=pltpu.SMEM),
            whole(summed.shape),
            whole(other.shape),
        ],
        out_specs=[whole((rows, 2, hidden)), whole((rows, hidden))]
        + [whole((rows, extra))] * (extra > 0),
        out_shape=[
            jax.ShapeDtypeStruct((rows, 2, hidden), F32),
            jax.ShapeDtypeStruct((rows, hidden), F32),
        ]
        + [jax.ShapeDtypeStruct((rows, extra), F32)] * (extra > 0),
        compiler_params=pltpu.CompilerParams(vmem_limit_bytes=VMEM_LIMIT),
        cost_estimate=pl.CostEstimate(
            flops=4 * rows * columns, bytes_accessed=16 * rows * columns, transcendentals=0
        ),
        name="finish_gradients",
    )(core.reshape(1).astype(jnp.int32), summed, other)


def halves(proj, out):
    first = lax.axis_index("core") == 0
    half = (proj.shape[1] + out.shape[1]) // 2
    late = jnp.concatenate([proj[:, half:], out], axis=1)
    early = proj[:, :half]
    return jnp.where(first, early, late), jnp.where(first, late, early)


def body(
    hidden_in,
    cotangent,
    seq_lengths,
    deal_order,
    mixer_gain,
    mixer_project,
    mixer_kernel,
    mixer_output,
    first_gain,
    first_gateup,
    first_down,
    attend_gain,
    attend_project,
    query_gain,
    key_gain,
    attend_output,
    second_gain,
    second_gateup,
    second_down,
):
    shards = lax.axis_size(TOKEN_AXES)
    contexts = lax.axis_size(CTX_AXES)
    members = lax.axis_size("tp")
    row_count, width = hidden_in.shape
    piece_rows = row_count // shards
    part_rows = piece_rows // members
    chunk = row_count // members
    device = lax.axis_index(TOKEN_AXES)
    own = lax.axis_index("tp")
    core = lax.axis_index("core")
    core_ref = core.reshape(1).astype(jnp.int32)
    depth = mixer_gain.shape[0]
    channels = mixer_output.shape[0]
    hidden = first_down.shape[0]
    heads_width = attend_output.shape[0]
    steps = -(-hidden // TILE)
    padded = steps * TILE
    ffn_width = 3 * padded
    block = TILE + TILE // 2

    def pack_ffn(gateup, down):
        wide = jnp.pad(gateup, ((0, 0), (0, 0), (0, padded - hidden)))
        wide = wide.reshape(depth, 2, steps, TILE).transpose(0, 2, 1, 3).reshape(depth, -1)
        return [wide, jnp.pad(down.T, ((0, 0), (0, padded - hidden)))]

    mixer_pack = jnp.concatenate([mixer_project.reshape(depth, -1), mixer_output.T], axis=1)
    first_pack = jnp.concatenate(
        pack_ffn(first_gateup, first_down) + [attend_project, attend_output.T], axis=1
    )
    second_pack = jnp.concatenate(pack_ffn(second_gateup, second_down), axis=1)
    piece_table = deal_order.reshape(shards, shards, piece_rows)[:, :, 0]
    anchor = piece_table // row_count
    anchor_piece = piece_table % row_count // piece_rows
    send_piece = jnp.sum(jnp.where(anchor == device, anchor_piece, 0), axis=1)
    my_anchor = lax.dynamic_index_in_dim(anchor, device, 0, keepdims=False)
    gains_row = jnp.concatenate(
        [mixer_gain, first_gain, attend_gain, second_gain, jnp.zeros((width - 4 * depth,), BF16)]
    )

    def my_part(rows):
        parts = rows.reshape(shards, members, part_rows, width)
        return lax.dynamic_index_in_dim(parts, own, 1, keepdims=False)[send_piece]

    outgoing = jnp.concatenate(
        [
            my_part(hidden_in),
            my_part(cotangent),
            jnp.broadcast_to(gains_row, (shards, 1, width)),
        ],
        axis=1,
    )
    arrived = lax.all_to_all(outgoing, TOKEN_AXES, split_axis=0, concat_axis=0, tiled=True)
    arrived, mixer_pack, first_pack = lax.optimization_barrier((arrived, mixer_pack, first_pack))
    first_all = lax.all_gather(first_pack, TOKEN_AXES, axis=0, tiled=True)
    second_all = lax.all_gather(second_pack, TOKEN_AXES, axis=0, tiled=True)
    project_b = first_all[:, ffn_width : ffn_width + attend_project.shape[1]]
    output_b_t = first_all[:, ffn_width + attend_project.shape[1] :]
    mixer_all = gather_pack(mixer_pack)
    project_a = mixer_all[:, : 3 * channels]
    output_a_t = mixer_all[:, 3 * channels :]
    gains = (
        arrived[:, 2 * part_rows, : 4 * depth]
        .reshape(shards, 4, depth)
        .transpose(1, 0, 2)
        .reshape(4, width)
        .astype(F32)
    )
    gain_a, gain_f, gain_b, gain_s = gains[0], gains[1], gains[2], gains[3]
    parts = arrived[:, : 2 * part_rows][my_anchor]
    own_tokens = parts[:, :part_rows].reshape(chunk, width)
    own_back = parts[:, part_rows:].reshape(chunk, width)
    stream0 = own_tokens.astype(F32)
    upstream = own_back.astype(F32)
    both = tp_gather(jnp.concatenate([own_tokens, own_back]))
    back_s = jnp.concatenate([slot[chunk:] for slot in both])

    gathered = jnp.arange(row_count)
    member_of = (own - gathered // chunk) % members
    offsets = (
        gathered % chunk // part_rows * piece_rows + member_of * part_rows + gathered % part_rows
    )
    to_gathered = (offsets[:, None] == gathered[None, :]).astype(BF16)
    to_dealt = (offsets[None, :] == gathered[:, None]).astype(BF16)
    tokens = times(to_dealt, jnp.concatenate([slot[:chunk] for slot in both]))

    kernel_taps = mixer_kernel.shape[0]
    halo = kernel_taps - 1
    local_rows = device * row_count + jnp.arange(row_count)
    halo_segment, unused = locate(
        seq_lengths, local_rows[0] - halo + jnp.arange(row_count + halo)
    )
    segment, places = locate(seq_lengths, device * row_count + offsets)
    ctx = lax.axis_index(CTX_AXES)
    group_rows = jnp.concatenate(
        [
            (lax.axis_index(GROUP_AXES) * contexts + (ctx ^ mask)) * row_count + offsets
            for mask in range(contexts)
        ]
    )
    key_segment, key_places = locate(seq_lengths, group_rows)
    allowed = (segment[None, :] == key_segment[:, None]) & (key_places[:, None] <= places[None, :])
    barred = jnp.where(allowed, 0.0, NEGATIVE).astype(BF16)
    half_dim = HD // 2
    frequency = ROPE_BASE ** (-(jnp.arange(half_dim).astype(F32) * 2.0 / HD))
    angles = places.astype(F32)[:, None] * frequency[None, :]
    cosine = jnp.cos(angles)
    sine = jnp.sin(angles)

    kernel_local = lax.dynamic_slice_in_dim(mixer_kernel, own * channels, channels, 1).astype(F32)
    mixer_in = norm_rows(tokens, gain_a).astype(BF16)
    mixer_in_other = swap_core(mixer_in)
    halo_pad = 16
    halo_in = from_behind(mixer_in[row_count - halo_pad :], 1)
    proj_a = times(jnp.concatenate([halo_in, mixer_in]), project_a)
    proj_b_part = proj_a[:, :channels]
    proj_c_part = proj_a[halo_pad:, channels : 2 * channels]
    proj_x_part = proj_a[:, 2 * channels :]
    extended = (proj_b_part * proj_x_part)[halo_pad - halo :].astype(BF16).astype(F32)
    conv_out = shortconv(extended, kernel_local, halo_segment)
    gated_rows = (proj_c_part * conv_out).astype(BF16)
    gated_parts = arrange(to_gathered, gated_rows)
    stream1, normed = add_norm(
        tp_scatter(tp_chunks(times_t(gated_parts, output_a_t))), stream0, gain_f
    )

    normed_f = tp_gather(normed)
    stream2, normed = add_norm(
        tp_scatter(ffn_forward(normed_f, first_all, steps)), stream1, gain_b
    )

    groups = H // KVH
    score_scale = HD ** (-0.5)
    qgain_f = query_gain.astype(F32)[None]
    kgain_f = key_gain.astype(F32)[None]
    attend_in = jnp.concatenate(tp_gather(normed))
    proj_b = times(attend_in, project_b)
    kv_width = 2 * HD * (proj_b.shape[1] // (HD * (groups + 2)))
    query_b, key_value = one_step(
        functools.partial(heads_kernel, groups),
        [proj_b, cosine, sine, qgain_f, kgain_f],
        [
            jax.ShapeDtypeStruct((row_count, heads_width), BF16),
            jax.ShapeDtypeStruct((row_count, kv_width), BF16),
        ],
        SMALL_LIMIT,
        "heads",
        20 * proj_b.size,
    )
    key_value_z = swap_ctx(key_value, 2)
    key_value_core = swap_core(jnp.concatenate([key_value, key_value_z]))
    key_value_all = jnp.concatenate(
        [key_value, key_value_core[:row_count], key_value_z, key_value_core[row_count:]]
    )
    attend_flops = 2 * key_value_all.shape[0] * query_b.size
    (attended,) = one_step(
        functools.partial(attend_kernel, score_scale, HD),
        [query_b, key_value_all, barred],
        [jax.ShapeDtypeStruct(query_b.shape, BF16)],
        MIDDLE_LIMIT,
        "attend",
        2 * attend_flops,
    )
    stream3, normed = add_norm(
        tp_scatter(tp_chunks(times_t(attended, output_b_t))), stream2, gain_s
    )

    normed_s = tp_gather(normed)
    d_chunks, out_chunks, keep, side = ffn_backward(
        core_ref, normed_s, [back_s], second_all, steps, True
    )
    d_stream3, back_b, gain_s_grad = norm_backward(
        tp_scatter(d_chunks), stream3, gain_s, upstream
    )
    out_others = [shift_tp(out_chunks[k], -k) for k in range(1, members)]
    side_other = swap_core(side)
    ffn_lefts = [(side, 0), (side_other, 0), (side, 1), (side_other, 1)]
    ffn_cols = steps * block
    side_start = 2 * width // block
    partial = gradient(
        ffn_lefts, keep, side_other, side_start, block, steps, padded, width, ffn_cols, 0, None
    )

    back_b = tp_gather(back_b)
    back_b, partial = lax.optimization_barrier((back_b, partial))
    second_sums = sum_chips(partial)
    attend_in_other = swap_core(attend_in)
    pair_rows = 2 * row_count
    d_query, near, cross, qgain_grad = one_step(
        functools.partial(attend_backward_kernel, score_scale),
        [*back_b, output_b_t, query_b, key_value_all, barred, proj_b, cosine, sine, qgain_f],
        [
            jax.ShapeDtypeStruct(query_b.shape, BF16),
            jax.ShapeDtypeStruct((pair_rows, kv_width), F32),
            jax.ShapeDtypeStruct((pair_rows, kv_width), BF16),
            jax.ShapeDtypeStruct((1, HD), F32),
        ],
        MIDDLE_LIMIT,
        "attend_backward",
        5 * attend_flops,
    )
    back_b = jnp.concatenate(back_b)
    back_b_other = swap_core(back_b)
    cross = swap_core(cross)
    far = (near[row_count:] + cross[row_count:].astype(F32)).astype(BF16)
    d_proj_b, kgain_grad = one_step(
        functools.partial(assemble_kernel, groups),
        [d_query, near, cross, swap_ctx(far, 2), proj_b, cosine, sine, kgain_f],
        [jax.ShapeDtypeStruct(proj_b.shape, BF16), jax.ShapeDtypeStruct((1, HD), F32)],
        SMALL_LIMIT,
        "assemble",
        20 * proj_b.size,
    )
    d_stream2, back_f, gain_b_grad = norm_backward(
        tp_scatter(tp_chunks(times_t(d_proj_b, project_b))), stream2, gain_b, d_stream3
    )
    keep, send = halves(d_proj_b, attended)
    first_core = core == 0
    attend_cols = keep.shape[1]
    small_tile = 2 * (heads_width + attend_project.shape[1]) // 16
    third = gradient(
        [
            (attend_in, 0),
            (attend_in_other, 0),
            (jnp.where(first_core, attend_in, back_b), 0),
            (jnp.where(first_core, attend_in_other, back_b_other), 0),
        ],
        keep,
        swap_core(send),
        0,
        small_tile,
        attend_cols // small_tile,
        attend_project.shape[1] - attend_cols,
        width,
        ffn_cols + attend_cols,
        ffn_cols // small_tile,
        None,
    )

    back_f = tp_gather(back_f)
    back_f, third = lax.optimization_barrier((back_f, third))
    left_x, left_b = jnp.concatenate(normed_f), jnp.concatenate(back_f)
    left_others = [swap_core(left_x), swap_core(left_b)]
    d_chunks, unused, keep, side = ffn_backward(
        core_ref, normed_f, back_f, first_all, steps, False
    )
    d_chunks, left_others = lax.optimization_barrier((d_chunks, left_others))
    d_chunks, side_other = lax.optimization_barrier((d_chunks, swap_core(side)))
    ffn_lefts = [(left_x, 0), (left_others[0], 0), (left_b, 0), (left_others[1], 0)]
    partial = gradient(
        ffn_lefts,
        keep,
        side_other,
        0,
        block,
        steps,
        padded,
        width,
        ffn_cols + attend_cols,
        0,
        third,
    )

    d_parts, partial = lax.optimization_barrier((tp_scatter(d_chunks), partial))
    d_stream1, back_a, gain_f_grad = norm_backward(d_parts, stream1, gain_f, d_stream2)

    back_a = tp_gather(back_a)
    first_sums = sum_chips(partial)
    back_a = arrange(to_dealt, jnp.concatenate(back_a))
    back_a_other = swap_core(back_a)
    d_gated = times(back_a, output_a_t)
    d_cgate = d_gated * conv_out
    d_conv = d_gated * proj_c_part
    unused, pullback = jax.vjp(
        lambda ext_rows, kernel_in: shortconv(ext_rows, kernel_in, halo_segment),
        extended,
        kernel_local,
    )
    d_extended, kernel_grad = pullback(d_conv)
    returned = from_behind(d_extended[:halo], -1)
    d_product = d_extended[halo:] + jnp.concatenate(
        [jnp.zeros((row_count - halo, channels), F32), returned]
    )
    d_proj_a = jnp.concatenate(
        [
            d_product * proj_x_part[halo_pad:],
            d_cgate,
            d_product * proj_b_part[halo_pad:],
        ],
        axis=1,
    ).astype(BF16)
    d_proj_a, out_others = lax.optimization_barrier((d_proj_a, out_others))
    stream4 = stream3 + add_parts([out_chunks[0], *out_others])
    d_chunks = tp_chunks(times_t(arrange(to_gathered, d_proj_a), project_a))
    keep, send = halves(d_proj_a, gated_rows)
    mixer_cols = keep.shape[1]
    partial = gradient(
        [
            (mixer_in, 0),
            (mixer_in_other, 0),
            (jnp.where(first_core, mixer_in, back_a), 0),
            (jnp.where(first_core, mixer_in_other, back_a_other), 0),
        ],
        keep,
        swap_core(send),
        0,
        mixer_cols,
        1,
        3 * channels - mixer_cols,
        width,
        mixer_cols,
        0,
        None,
    )
    kernel_cols = kernel_taps * channels
    gain_start = kernel_cols + 2 * HD
    shared = jnp.concatenate([kernel_grad.reshape(-1), qgain_grad[0], kgain_grad[0]])
    early_gains = [
        grad.reshape(shards, depth) for grad in (gain_f_grad, gain_b_grad, gain_s_grad)
    ]
    early_row = jnp.concatenate(
        [
            jnp.broadcast_to(shared, (shards, gain_start)),
            jnp.pad(
                jnp.concatenate(early_gains, axis=1),
                ((0, 0), (0, width - gain_start - 3 * depth)),
            ),
        ],
        axis=1,
    )
    d_parts, early_row = lax.optimization_barrier((tp_scatter(d_chunks), early_row))
    unused, d_stream0, gain_a_grad = norm_backward(d_parts, stream0, gain_a, d_stream1)

    slot_for_anchor = jnp.sum(
        jnp.where(
            my_anchor[None, :] == jnp.arange(shards)[:, None], jnp.arange(shards)[None, :], 0
        ),
        axis=1,
    )
    late_start = gain_start + 3 * depth
    late_row = jnp.pad(
        gain_a_grad.reshape(shards, depth), ((0, 0), (late_start, width - late_start - depth))
    )
    leaving = jnp.concatenate(
        [d_stream0, stream4.astype(BF16), (early_row + late_row).astype(BF16)]
    )
    line = jnp.arange(shards * piece_rows)
    target, item = line // piece_rows, line % piece_rows
    source = jnp.where(
        item < 2 * part_rows,
        item // part_rows * chunk
        + jnp.repeat(slot_for_anchor, piece_rows) * part_rows
        + item % part_rows,
        jnp.where(item == 2 * part_rows, 2 * chunk + target, -1),
    )
    to_leaving = (source[:, None] == jnp.arange(leaving.shape[0])[None, :]).astype(BF16)
    leaving = arrange(to_leaving, leaving)
    home = lax.all_to_all(
        leaving.reshape(shards, piece_rows, width),
        TOKEN_AXES,
        split_axis=0,
        concat_axis=0,
        tiled=True,
    )
    second_grads = finish(second_sums, steps, hidden)
    home, partial, second_grads = lax.optimization_barrier((home, partial, second_grads))
    place = jnp.arange(2 * chunk + 8)
    small_line = (place == 2 * chunk) | (place == 2 * chunk + 1)
    wanted = (
        place % chunk // part_rows * piece_rows
        + place // chunk * part_rows
        + place % part_rows
    )
    to_payload = jnp.where(
        (place < 2 * chunk)[:, None],
        wanted[:, None] == line[None, :],
        small_line[:, None] & (item == 2 * part_rows)[None, :],
    ).astype(BF16)
    payload = times(to_payload, home.reshape(shards * piece_rows, width))
    rounded = payload.astype(BF16).astype(F32)
    payload = jnp.where((place == 2 * chunk + 1)[:, None], payload - rounded, payload)
    last = tp_gather(payload.astype(BF16))
    mixer_home = lax.all_to_all(
        partial.reshape(shards, depth, mixer_cols),
        TOKEN_AXES,
        split_axis=0,
        concat_axis=0,
        tiled=True,
    )
    home_rows = (
        jnp.repeat(jnp.tile(send_piece, members), part_rows) * piece_rows
        + member_of * part_rows
        + gathered % part_rows
    )
    to_arrival = (home_rows[None, :] == gathered[:, None]).astype(BF16)
    input_gradient = arrange(to_arrival, jnp.concatenate([slot[:chunk] for slot in last]))
    layer_out = arrange(to_arrival, jnp.concatenate([slot[chunk : 2 * chunk] for slot in last]))
    first_sums, layer_out, input_gradient = lax.optimization_barrier(
        (first_sums, layer_out, input_gradient)
    )
    *first_grads, attend_grads = finish(first_sums, steps, hidden)
    first_grads, attend_grads, mixer_home = lax.optimization_barrier(
        (first_grads, attend_grads, mixer_home)
    )
    mixer_home = mixer_home.reshape(shards // CORES, CORES, depth, mixer_cols)
    mixer_grads = jnp.sum(mixer_home.astype(F32), axis=0)
    mixer_grads = jnp.concatenate([mixer_grads[0], mixer_grads[1]], axis=1)
    smalls = [
        slot[2 * chunk].astype(F32) + slot[2 * chunk + 1].astype(F32) for slot in last
    ]
    totals = sum(smalls)
    kernel_rows = jnp.stack([small[:kernel_cols].reshape(kernel_taps, channels) for small in smalls])
    kernel_total = jnp.concatenate(
        [
            lax.dynamic_index_in_dim(kernel_rows, (own - member) % members, 0, keepdims=False)
            for member in range(members)
        ],
        axis=1,
    )
    qgain_total = totals[kernel_cols : kernel_cols + HD]
    kgain_total = totals[kernel_cols + HD : kernel_cols + 2 * HD]
    gain_totals = totals[gain_start : gain_start + 4 * depth].reshape(4, depth)

    gateup_s_grad, down_s_grad = second_grads
    gateup_f_grad, down_f_grad = first_grads
    proj_cols = attend_project.shape[1]
    return (
        layer_out,
        input_gradient,
        gain_totals[3],
        mixer_grads[:, : 3 * channels].reshape(depth, 3, channels),
        kernel_total,
        mixer_grads[:, 3 * channels :].T,
        gain_totals[0],
        gateup_f_grad,
        down_f_grad.T,
        gain_totals[1],
        attend_grads[:, :proj_cols],
        qgain_total,
        kgain_total,
        attend_grads[:, proj_cols:].T,
        gain_totals[2],
        gateup_s_grad,
        down_s_grad.T,
    )


def solution(mesh):
    names = TOKEN_AXES + ("tp",)
    rings = mesh.shape["fsdp"] // 2, 2, mesh.shape["ctx"] // 2, 2, mesh.shape["tp"]
    tokens = P(TOKEN_AXES, None)
    rows = P(TOKEN_AXES)
    three = P(TOKEN_AXES, None, "tp")
    two = P(TOKEN_AXES, "tp")
    turned = P("tp", TOKEN_AXES)
    return jax.shard_map(
        body,
        mesh=Mesh(mesh.devices.reshape(rings), names),
        in_specs=(
            tokens, tokens, P(), P(),
            rows, three, P(), turned,
            rows, three, turned,
            rows, two, P(), P(), turned,
            rows, three, turned,
        ),
        out_specs=(
            tokens, tokens,
            rows, three, P(), turned,
            rows, three, turned,
            rows, two, P(), P(), turned,
            rows, three, turned,
        ),
        check_vma=False,
    )
```

```python
import functools

import jax
import jax.numpy as jnp
from jax import lax
from jax.experimental import pallas as pl
from jax.experimental.pallas import tpu as pltpu
from jax.sharding import Mesh, PartitionSpec as P

H = 24
KVH = 8
HD = 64

EPSILON = 1e-05
ROPE_BASE = 1000000.0
NEGATIVE = -1e30

CHIP_AXES = ("x", "z_hi", "z_lo")
TOKEN_AXES = CHIP_AXES + ("core",)
GROUP_AXES = ("x", "z_hi")
CTX_AXES = ("z_lo", "core")
Z_AXES = ("z_hi", "z_lo")
CORES = 2
TILE = 256
VMEM_LIMIT = 48 * 1024 * 1024
MIDDLE_LIMIT = 24 * 1024 * 1024
SMALL_LIMIT = 12 * 1024 * 1024
F32 = jnp.float32
BF16 = jnp.bfloat16


def norm_rows(values, scales):
    return values * lax.rsqrt(jnp.mean(values * values, axis=-1, keepdims=True) + EPSILON) * scales


def locate(lengths, positions):
    seq_ends = jnp.cumsum(lengths)
    segment = jnp.sum((positions[:, None] >= seq_ends[None, :]).astype(jnp.int32), axis=1)
    starts = seq_ends - lengths
    first_row = jnp.sum(
        jnp.where(segment[:, None] == jnp.arange(lengths.shape[0])[None, :], starts[None, :], 0),
        axis=1,
    )
    return (segment, positions - first_row)


def shortconv(extended, kernel_in, segment):
    kernel_taps = kernel_in.shape[0]
    out_rows = extended.shape[0] - kernel_taps + 1
    result = kernel_in[0] * extended[kernel_taps - 1 :]
    for t in range(1, kernel_taps):
        earlier = extended[kernel_taps - 1 - t : kernel_taps - 1 - t + out_rows]
        same_seq = (
            segment[kernel_taps - 1 - t : kernel_taps - 1 - t + out_rows]
            == segment[kernel_taps - 1 :]
        ).astype(F32)[:, None]
        result = result + kernel_in[t] * earlier * same_seq
    return result


def from_behind(block, distance):
    devices = range(lax.axis_size(CTX_AXES))
    route = [(i - distance, i) for i in devices if i - distance in devices]
    return lax.ppermute(block, CTX_AXES, route)


def swap_ctx(block, mask):
    return lax.ppermute(block, CTX_AXES, [(i, i ^ mask) for i in range(lax.axis_size(CTX_AXES))])


def swap_core(block):
    return lax.ppermute(block, "core", [(0, 1), (1, 0)])


def shift_tp(block, distance):
    members = lax.axis_size("tp")
    return lax.ppermute(block, "tp", [(i, (i + distance) % members) for i in range(members)])


def tp_gather(shard):
    return [shard] + [shift_tp(shard, k) for k in range(1, lax.axis_size("tp"))]


def tp_chunks(partial):
    rows = partial.shape[0] // lax.axis_size("tp")
    return [
        partial[k * rows : (k + 1) * rows].astype(F32 if k == 0 else BF16)
        for k in range(lax.axis_size("tp"))
    ]


def tp_scatter(chunks):
    return [chunks[0]] + [shift_tp(chunks[k], -k) for k in range(1, len(chunks))]


def add_parts(parts):
    total = parts[0]
    for part in parts[1:]:
        total = total + part.astype(F32)
    return total


def arrange(order, rows):
    return times(order, rows).astype(BF16)


def times(left, right):
    return lax.dot_general(left, right, (((1,), (0,)), ((), ())), preferred_element_type=F32)


def times_t(left, right):
    return lax.dot_general(left, right, (((1,), (1,)), ((), ())), preferred_element_type=F32)


def times_rows(left, right):
    return lax.dot_general(left, right, (((0,), (0,)), ((), ())), preferred_element_type=F32)


def assemble(chunk_refs, target):
    rows = chunk_refs[0].shape[0]
    for k, ref in enumerate(chunk_refs):
        target[k * rows : (k + 1) * rows, :] = ref[...]


def spread(total, chunk_refs):
    rows = chunk_refs[0].shape[0]
    for k, ref in enumerate(chunk_refs):
        ref[...] = total[k * rows : (k + 1) * rows, :].astype(ref.dtype)


def whole(shape):
    return pl.BlockSpec(shape, lambda *_: (0,) * len(shape))


def one_step(kernel, operands, out_shape, limit, name, flops):
    size = sum(v.size * v.dtype.itemsize for v in list(operands) + list(out_shape))
    return pl.pallas_call(
        kernel,
        grid=(1,),
        in_specs=[whole(v.shape) for v in operands],
        out_specs=[whole(v.shape) for v in out_shape],
        out_shape=out_shape,
        compiler_params=pltpu.CompilerParams(vmem_limit_bytes=limit),
        cost_estimate=pl.CostEstimate(flops=flops, bytes_accessed=size, transcendentals=0),
        name=name,
    )(*operands)


def sum_refs(refs):
    total = refs[0][...]
    for ref in refs[1:]:
        total = total + ref[...].astype(F32)
    return total


def add_norm_kernel(*refs):
    stream_ref, gain_ref, out_ref, normed_ref = refs[-4:]
    stream = stream_ref[...] + sum_refs(refs[:-4])
    out_ref[...] = stream
    normed_ref[...] = norm_rows(stream, gain_ref[...]).astype(BF16)


def add_norm(parts, stream, gain):
    return one_step(
        add_norm_kernel,
        [*parts, stream, gain[None]],
        [jax.ShapeDtypeStruct(stream.shape, F32), jax.ShapeDtypeStruct(stream.shape, BF16)],
        SMALL_LIMIT,
        "add_norm",
        10 * stream.size,
    )


def norm_backward_kernel(*refs):
    stream_ref, gain_ref, upward_ref, out_ref, rounded_ref, gain_grad_ref = refs[-6:]
    stream = stream_ref[...]
    d_normed = sum_refs(refs[:-6])
    spread_of = lax.rsqrt(jnp.mean(stream * stream, axis=1, keepdims=True) + EPSILON)
    gain_grad_ref[...] = jnp.sum(d_normed * stream * spread_of, axis=0, keepdims=True)
    scaled = d_normed * gain_ref[...]
    inner = jnp.mean(scaled * stream, axis=1, keepdims=True)
    result = upward_ref[...] + spread_of * scaled - stream * (
        spread_of * spread_of * spread_of * inner
    )
    out_ref[...] = result
    rounded_ref[...] = result.astype(BF16)


def norm_backward(parts, stream, gain, upward):
    out, rounded, gain_grad = one_step(
        norm_backward_kernel,
        [*parts, stream, gain[None], upward],
        [
            jax.ShapeDtypeStruct(stream.shape, F32),
            jax.ShapeDtypeStruct(stream.shape, BF16),
            jax.ShapeDtypeStruct((1, stream.shape[1]), F32),
        ],
        SMALL_LIMIT,
        "norm_backward",
        20 * stream.size,
    )
    return out, rounded, gain_grad[0]


def weight_specs(depth, steps):
    return [
        pl.BlockSpec((depth, 2 * TILE), lambda j: (0, j)),
        pl.BlockSpec((depth, TILE), lambda j: (0, 2 * steps + j)),
    ]


def chunk_shapes(count, rows, width):
    return [jax.ShapeDtypeStruct((rows, width), F32 if k == 0 else BF16) for k in range(count)]


def ffn_forward_kernel(count, *refs):
    x_refs, (gu_ref, dn_ref), outs = refs[:count], refs[count : count + 2], refs[count + 2 : -2]
    x_all, total = refs[-2:]
    step = pl.program_id(0)

    @pl.when(step == 0)
    def _():
        assemble(x_refs, x_all)
        total[...] = jnp.zeros_like(total)

    both = times(x_all[...], gu_ref[...])
    gate, up = both[:, :TILE], both[:, TILE:]
    active = (gate * jax.nn.sigmoid(gate) * up).astype(BF16)
    total[...] += times_t(active, dn_ref[...])

    @pl.when(step == pl.num_programs(0) - 1)
    def _():
        spread(total[...], outs)


def ffn_forward(chunks, pack, steps):
    count, (rows, width) = len(chunks), chunks[0].shape
    tokens = count * rows
    return pl.pallas_call(
        functools.partial(ffn_forward_kernel, count),
        grid=(steps,),
        in_specs=[whole((rows, width))] * count + weight_specs(width, steps),
        out_specs=[whole((rows, width))] * count,
        out_shape=chunk_shapes(count, rows, width),
        scratch_shapes=[pltpu.VMEM((tokens, width), BF16), pltpu.VMEM((tokens, width), F32)],
        compiler_params=pltpu.CompilerParams(vmem_limit_bytes=VMEM_LIMIT),
        cost_estimate=pl.CostEstimate(
            flops=2 * tokens * width * 3 * TILE * steps,
            bytes_accessed=2 * width * 3 * TILE * steps,
            transcendentals=tokens * TILE * steps,
        ),
        name="ffn_forward",
    )(*chunks, pack, pack)


def ffn_backward_kernel(count, back_count, forward, core_ref, *refs):
    x_refs, b_refs = refs[:count], refs[count : count + back_count]
    place = count + back_count
    gu_ref, dn_ref = refs[place : place + 2]
    place += 2
    back_outs = refs[place : place + count]
    place += count
    if forward:
        outs = refs[place : place + count]
        place += count
    keep_ref, side_ref = refs[place : place + 2]
    scratch = refs[place + 2 :]
    x_all, b_all, d_total = scratch[:3]
    step = pl.program_id(0)
    width = x_all.shape[1]

    @pl.when(step == 0)
    def _():
        assemble(x_refs, x_all)
        assemble(b_refs, b_all)
        if forward:
            side_ref[:, :width] = x_all[...]
            side_ref[:, width : 2 * width] = b_all[...]
        d_total[...] = jnp.zeros_like(d_total)
        if forward:
            scratch[3][...] = jnp.zeros_like(scratch[3])

    both = times(x_all[...], gu_ref[...])
    gate, up = both[:, :TILE], both[:, TILE:]
    d_active = times(b_all[...], dn_ref[...])
    sigmoid = jax.nn.sigmoid(gate)
    silu = gate * sigmoid
    active = (silu * up).astype(BF16)
    if forward:
        scratch[3][...] += times_t(active, dn_ref[...])
    d_gate = (d_active * up * (sigmoid * (1.0 + gate * (1.0 - sigmoid)))).astype(BF16)
    d_up = (d_active * silu).astype(BF16)
    d_total[...] += times_t(jnp.concatenate([d_gate, d_up], axis=1), gu_ref[...])
    first = core_ref[0] == 0
    half = TILE // 2
    low, high = active[:, :half], active[:, half:]
    offset = 2 * width if forward else 0
    wide = pl.multiple_of(step * TILE, TILE)
    narrow = pl.multiple_of(pl.num_programs(0) * TILE + step * half, half)
    side_wide = pl.multiple_of(offset + wide, TILE)
    side_narrow = pl.multiple_of(offset + narrow, half)

    @pl.when(first)
    def _():
        keep_ref[:, pl.ds(wide, TILE)] = d_gate
        keep_ref[:, pl.ds(narrow, half)] = low
        side_ref[:, pl.ds(side_wide, TILE)] = d_up
        side_ref[:, pl.ds(side_narrow, half)] = high

    @pl.when(jnp.logical_not(first))
    def _():
        keep_ref[:, pl.ds(wide, TILE)] = d_up
        keep_ref[:, pl.ds(narrow, half)] = high
        side_ref[:, pl.ds(side_wide, TILE)] = d_gate
        side_ref[:, pl.ds(side_narrow, half)] = low

    @pl.when(step == pl.num_programs(0) - 1)
    def _():
        spread(d_total[...], back_outs)
        if forward:
            spread(scratch[3][...], outs)


def ffn_backward(core, chunks, back_chunks, pack, steps, forward):
    count, (rows, width) = len(chunks), chunks[0].shape
    tokens = count * rows
    block = TILE + TILE // 2
    ways = 2 if forward else 1
    side_width = (2 * width if forward else 0) + steps * block
    results = pl.pallas_call(
        functools.partial(ffn_backward_kernel, count, len(back_chunks), forward),
        grid=(steps,),
        in_specs=[pl.BlockSpec(memory_space=pltpu.SMEM)]
        + [whole(v.shape) for v in (*chunks, *back_chunks)]
        + weight_specs(width, steps),
        out_specs=[whole((rows, width))] * (ways * count)
        + [whole((tokens, steps * block)), whole((tokens, side_width))],
        out_shape=chunk_shapes(count, rows, width) * ways
        + [
            jax.ShapeDtypeStruct((tokens, steps * block), BF16),
            jax.ShapeDtypeStruct((tokens, side_width), BF16),
        ],
        scratch_shapes=[pltpu.VMEM((tokens, width), BF16)] * 2
        + [pltpu.VMEM((tokens, width), F32)] * ways,
        compiler_params=pltpu.CompilerParams(vmem_limit_bytes=VMEM_LIMIT),
        cost_estimate=pl.CostEstimate(
            flops=2 * tokens * width * (4 + ways) * TILE * steps,
            bytes_accessed=2 * width * 3 * TILE * steps + 4 * tokens * side_width,
            transcendentals=tokens * TILE * steps,
        ),
        name="ffn_both" if forward else "ffn_backward",
    )(core, *chunks, *back_chunks, pack, pack)
    return results[:count], results[count : ways * count], results[-2], results[-1]


def gradient_kernel(edge, cut, *refs):
    one_own, one_other, two_own, two_other, own_ref, other_ref = refs[:6]
    out_ref = refs[-1]
    step = pl.program_id(0)

    def product(own_left, other_left, columns):
        total = times_rows(own_left[...], own_ref[:, columns])
        total += times_rows(other_left[...], other_ref[:, columns])
        out_ref[:, columns] = total.astype(BF16)

    @pl.when(step < edge)
    def _():
        product(one_own, one_other, slice(None))

    @pl.when(step > edge if cut else step >= edge)
    def _():
        product(two_own, two_other, slice(None))

    if cut:

        @pl.when(step == edge)
        def _():
            product(one_own, one_other, slice(0, cut))
            product(two_own, two_other, slice(cut, None))


def gradient(lefts, own, other, other_start, block, steps, columns, width, out_width, out_start, target):
    tokens = own.shape[0]
    edge, cut = divmod(columns, block)

    def left_spec(index):
        return pl.BlockSpec((tokens, width), lambda j: (0, index))

    in_specs = [left_spec(index) for unused, index in lefts] + [
        pl.BlockSpec((tokens, block), lambda j: (0, j)),
        pl.BlockSpec((tokens, block), lambda j: (0, other_start + j)),
    ]
    operands = [array for array, unused in lefts] + [own, other]
    aliases = {}
    if target is not None:
        in_specs.append(pl.BlockSpec(memory_space=pl.ANY))
        operands.append(target)
        aliases = {len(operands) - 1: 0}
    return pl.pallas_call(
        functools.partial(gradient_kernel, edge, cut),
        grid=(steps,),
        in_specs=in_specs,
        out_specs=pl.BlockSpec((width, block), lambda j: (0, out_start + j)),
        out_shape=jax.ShapeDtypeStruct((width, out_width), BF16),
        input_output_aliases=aliases,
        compiler_params=pltpu.CompilerParams(vmem_limit_bytes=VMEM_LIMIT),
        cost_estimate=pl.CostEstimate(
            flops=4 * tokens * width * block * steps,
            bytes_accessed=2 * width * block * steps,
            transcendentals=0,
        ),
        name="weight_gradient",
    )(*operands)


def turn(rows, cosine, sine):
    half = rows.shape[1] // 2
    first, second = rows[:, :half], rows[:, half:]
    return jnp.concatenate(
        [first * cosine - second * sine, second * cosine + first * sine], axis=1
    )


def head_backward(d_rows, raw, cosine, sine, gain):
    d_normed = turn(d_rows, cosine, -sine)
    spread_of = lax.rsqrt(jnp.mean(raw * raw, axis=1, keepdims=True) + EPSILON)
    d_gain = jnp.sum(d_normed * raw * spread_of, axis=0, keepdims=True)
    scaled = d_normed * gain
    inner = jnp.mean(scaled * raw, axis=1, keepdims=True)
    d_raw = spread_of * scaled - raw * (spread_of * spread_of * spread_of * inner)
    return d_raw.astype(BF16), d_gain


def heads_kernel(groups, raw_ref, cos_ref, sin_ref, query_gain_ref, key_gain_ref, q_ref, kv_ref):
    size = query_gain_ref.shape[1]
    kv_heads = raw_ref.shape[1] // ((groups + 2) * size)
    cosine, sine = cos_ref[...], sin_ref[...]
    for group in range(kv_heads):
        start = group * (groups + 2) * size
        for member in range(groups):
            raw = raw_ref[:, start + member * size : start + (member + 1) * size]
            head = group * groups + member
            rows = turn(norm_rows(raw, query_gain_ref[...]), cosine, sine)
            q_ref[:, head * size : (head + 1) * size] = rows.astype(BF16)
        start += groups * size
        rows = turn(norm_rows(raw_ref[:, start : start + size], key_gain_ref[...]), cosine, sine)
        kv_ref[:, group * size : (group + 1) * size] = rows.astype(BF16)
        value_start = (kv_heads + group) * size
        kv_ref[:, value_start : value_start + size] = raw_ref[
            :, start + size : start + 2 * size
        ].astype(BF16)


def head_probs(key, query, scale, barred):
    scores = times_t(key, query) * scale + barred
    probs = jnp.exp(scores - jnp.max(scores, axis=0, keepdims=True))
    return probs / jnp.sum(probs, axis=0, keepdims=True)


def attend_kernel(scale, size, q_ref, kv_ref, barred_ref, out_ref):
    kv_heads = kv_ref.shape[1] // (2 * size)
    groups = q_ref.shape[1] // (kv_heads * size)
    barred = barred_ref[...].astype(F32)
    for head in range(kv_heads * groups):
        group = head // groups
        columns = slice(head * size, (head + 1) * size)
        key = kv_ref[:, group * size : (group + 1) * size]
        value = kv_ref[:, (kv_heads + group) * size : (kv_heads + group + 1) * size]
        probs = head_probs(key, q_ref[:, columns], scale, barred).astype(BF16)
        out_ref[:, columns] = times_rows(value, probs).T.astype(BF16)


def attend_backward_kernel(
    scale, first_ref, second_ref, third_ref, fourth_ref, weight_ref, q_ref, kv_ref, barred_ref, raw_ref, cos_ref, sin_ref, gain_ref,
    dq_ref, near_ref, cross_ref, gain_grad_ref,
):
    size = gain_ref.shape[1]
    kv_heads = kv_ref.shape[1] // (2 * size)
    groups = q_ref.shape[1] // (kv_heads * size)
    rows = kv_ref.shape[0] // 4
    cosine, sine, gain = cos_ref[...], sin_ref[...], gain_ref[...]
    barred = barred_ref[...].astype(F32)
    back = jnp.concatenate(
        [ref[...] for ref in (first_ref, second_ref, third_ref, fourth_ref)], axis=0
    )
    d_attended = times(back, weight_ref[...]).astype(BF16)
    gain_grad = jnp.zeros_like(gain)
    for group in range(kv_heads):
        columns = slice(group * size, (group + 1) * size)
        value_columns = slice((kv_heads + group) * size, (kv_heads + group + 1) * size)
        key, value = kv_ref[:, columns], kv_ref[:, value_columns]
        d_key = d_value = None
        for member in range(groups):
            head = group * groups + member
            head_columns = slice(head * size, (head + 1) * size)
            query, d_out = q_ref[:, head_columns], d_attended[:, head_columns]
            probs = head_probs(key, query, scale, barred)
            d_probs = times_t(value, d_out)
            inner = jnp.sum(probs * d_probs, axis=0, keepdims=True)
            d_scores = (probs * (d_probs - inner)).astype(BF16)
            part_value = times(probs.astype(BF16), d_out)
            part_key = times(d_scores, query) * scale
            d_value = part_value if d_value is None else d_value + part_value
            d_key = part_key if d_key is None else d_key + part_key
            d_query = (times_rows(key, d_scores) * scale).T
            start = (group * (groups + 2) + member) * size
            d_raw, d_gain = head_backward(
                d_query, raw_ref[:, start : start + size], cosine, sine, gain
            )
            dq_ref[:, head_columns] = d_raw
            gain_grad += d_gain
        for part, place in ((d_key, columns), (d_value, value_columns)):
            near_ref[:rows, place] = part[:rows]
            near_ref[rows:, place] = part[2 * rows : 3 * rows]
            cross_ref[:rows, place] = part[rows : 2 * rows].astype(BF16)
            cross_ref[rows:, place] = part[3 * rows :].astype(BF16)
    gain_grad_ref[...] = gain_grad


def assemble_kernel(groups, dq_ref, near_ref, cross_ref, far_ref, raw_ref, cos_ref, sin_ref, gain_ref, out_ref, gain_grad_ref):
    size = gain_ref.shape[1]
    kv_heads = raw_ref.shape[1] // ((groups + 2) * size)
    rows = raw_ref.shape[0]
    both = near_ref[:rows, :] + cross_ref[:rows, :].astype(F32) + far_ref[...].astype(F32)
    gain_grad = jnp.zeros_like(gain_ref[...])
    for group in range(kv_heads):
        start = group * (groups + 2) * size
        out_ref[:, start : start + groups * size] = dq_ref[
            :, group * groups * size : (group + 1) * groups * size
        ]
        start += groups * size
        d_raw, d_gain = head_backward(
            both[:, group * size : (group + 1) * size],
            raw_ref[:, start : start + size],
            cos_ref[...],
            sin_ref[...],
            gain_ref[...],
        )
        gain_grad += d_gain
        out_ref[:, start : start + size] = d_raw
        value_start = (kv_heads + group) * size
        out_ref[:, start + size : start + 2 * size] = both[
            :, value_start : value_start + size
        ].astype(BF16)
    gain_grad_ref[...] = gain_grad


def sum_chips(partial):
    return lax.psum_scatter(partial, CHIP_AXES, scatter_dimension=0, tiled=True)


def gather_pack(pack):
    chips = lax.axis_size(CHIP_AXES)
    core = lax.axis_index("core")
    plane = lax.all_to_all(
        jnp.broadcast_to(pack, (chips,) + pack.shape),
        CHIP_AXES,
        split_axis=0,
        concat_axis=0,
        tiled=True,
    )
    other = swap_core(plane)
    both = jnp.zeros((chips, CORES) + pack.shape, BF16)
    both = lax.dynamic_update_slice(both, plane[:, None], (0, core, 0, 0))
    both = lax.dynamic_update_slice(both, other[:, None], (0, 1 - core, 0, 0))
    return both.reshape(-1, pack.shape[1])


def finish_kernel(steps, core_ref, sum_ref, other_ref, gateup_ref, down_ref, *rest):
    core = core_ref[0]
    rows, hidden = down_ref.shape
    padded = steps * TILE
    half = TILE // 2
    first = core == 0
    mine = sum_ref[pl.ds(pl.multiple_of(core * rows, rows), rows), :].astype(F32)
    other = other_ref[...].astype(F32)
    low = jnp.where(first, mine, other)
    high = jnp.where(first, other, mine)
    gateup_ref[:, 0, :] = low[:, :hidden]
    gateup_ref[:, 1, :] = high[:, :hidden]
    for step in range(steps):
        source = padded + step * half
        for part, columns in enumerate((low, high)):
            place = step * TILE + part * half
            size = min(half, hidden - place)
            if size > 0:
                down_ref[:, place : place + size] = columns[:, source : source + size]
    for ref in rest:
        start = padded + steps * half
        size = low.shape[1] - start
        ref[:, :size] = low[:, start:]
        ref[:, size:] = high[:, start:]


def finish(summed, steps, hidden):
    core = lax.axis_index("core")
    rows, columns = summed.shape[0] // 2, summed.shape[1]
    other = swap_core(lax.dynamic_slice_in_dim(summed, (1 - core) * rows, rows, 0))
    extra = 2 * (columns - steps * (TILE + TILE // 2))
    return pl.pallas_call(
        functools.partial(finish_kernel, steps),
        grid=(1,),
        in_specs=[
            pl.BlockSpec(memory_space=pltpu.SMEM),
            whole(summed.shape),
            whole(other.shape),
        ],
        out_specs=[whole((rows, 2, hidden)), whole((rows, hidden))]
        + [whole((rows, extra))] * (extra > 0),
        out_shape=[
            jax.ShapeDtypeStruct((rows, 2, hidden), F32),
            jax.ShapeDtypeStruct((rows, hidden), F32),
        ]
        + [jax.ShapeDtypeStruct((rows, extra), F32)] * (extra > 0),
        compiler_params=pltpu.CompilerParams(vmem_limit_bytes=VMEM_LIMIT),
        cost_estimate=pl.CostEstimate(
            flops=4 * rows * columns, bytes_accessed=16 * rows * columns, transcendentals=0
        ),
        name="finish_gradients",
    )(core.reshape(1).astype(jnp.int32), summed, other)


def halves(proj, out):
    first = lax.axis_index("core") == 0
    half = (proj.shape[1] + out.shape[1]) // 2
    late = jnp.concatenate([proj[:, half:], out], axis=1)
    early = proj[:, :half]
    return jnp.where(first, early, late), jnp.where(first, late, early)


def body(
    hidden_in,
    cotangent,
    seq_lengths,
    deal_order,
    mixer_gain,
    mixer_project,
    mixer_kernel,
    mixer_output,
    first_gain,
    first_gateup,
    first_down,
    attend_gain,
    attend_project,
    query_gain,
    key_gain,
    attend_output,
    second_gain,
    second_gateup,
    second_down,
):
    shards = lax.axis_size(TOKEN_AXES)
    contexts = lax.axis_size(CTX_AXES)
    members = lax.axis_size("tp")
    row_count, width = hidden_in.shape
    piece_rows = row_count // shards
    part_rows = piece_rows // members
    chunk = row_count // members
    device = lax.axis_index(TOKEN_AXES)
    own = lax.axis_index("tp")
    core = lax.axis_index("core")
    core_ref = core.reshape(1).astype(jnp.int32)
    depth = mixer_gain.shape[0]
    channels = mixer_output.shape[0]
    hidden = first_down.shape[0]
    heads_width = attend_output.shape[0]
    steps = -(-hidden // TILE)
    padded = steps * TILE
    ffn_width = 3 * padded
    block = TILE + TILE // 2

    def pack_ffn(gateup, down):
        wide = jnp.pad(gateup, ((0, 0), (0, 0), (0, padded - hidden)))
        wide = wide.reshape(depth, 2, steps, TILE).transpose(0, 2, 1, 3).reshape(depth, -1)
        return [wide, jnp.pad(down.T, ((0, 0), (0, padded - hidden)))]

    mixer_pack = jnp.concatenate([mixer_project.reshape(depth, -1), mixer_output.T], axis=1)
    first_pack = jnp.concatenate(
        pack_ffn(first_gateup, first_down) + [attend_project, attend_output.T], axis=1
    )
    second_pack = jnp.concatenate(pack_ffn(second_gateup, second_down), axis=1)
    piece_table = deal_order.reshape(shards, shards, piece_rows)[:, :, 0]
    anchor = piece_table // row_count
    anchor_piece = piece_table % row_count // piece_rows
    send_piece = jnp.sum(jnp.where(anchor == device, anchor_piece, 0), axis=1)
    my_anchor = lax.dynamic_index_in_dim(anchor, device, 0, keepdims=False)
    gains_row = jnp.concatenate(
        [mixer_gain, first_gain, attend_gain, second_gain, jnp.zeros((width - 4 * depth,), BF16)]
    )

    def my_part(rows):
        parts = rows.reshape(shards, members, part_rows, width)
        return lax.dynamic_index_in_dim(parts, own, 1, keepdims=False)[send_piece]

    outgoing = jnp.concatenate(
        [
            my_part(hidden_in),
            my_part(cotangent),
            jnp.broadcast_to(gains_row, (shards, 1, width)),
        ],
        axis=1,
    )
    arrived = lax.all_to_all(outgoing, TOKEN_AXES, split_axis=0, concat_axis=0, tiled=True)
    arrived, mixer_pack, first_pack = lax.optimization_barrier((arrived, mixer_pack, first_pack))
    first_all = lax.all_gather(first_pack, TOKEN_AXES, axis=0, tiled=True)
    second_all = lax.all_gather(second_pack, TOKEN_AXES, axis=0, tiled=True)
    project_b = first_all[:, ffn_width : ffn_width + attend_project.shape[1]]
    output_b_t = first_all[:, ffn_width + attend_project.shape[1] :]
    mixer_all = gather_pack(mixer_pack)
    project_a = mixer_all[:, : 3 * channels]
    output_a_t = mixer_all[:, 3 * channels :]
    gains = (
        arrived[:, 2 * part_rows, : 4 * depth]
        .reshape(shards, 4, depth)
        .transpose(1, 0, 2)
        .reshape(4, width)
        .astype(F32)
    )
    gain_a, gain_f, gain_b, gain_s = gains[0], gains[1], gains[2], gains[3]
    parts = arrived[:, : 2 * part_rows][my_anchor]
    own_tokens = parts[:, :part_rows].reshape(chunk, width)
    own_back = parts[:, part_rows:].reshape(chunk, width)
    stream0 = own_tokens.astype(F32)
    upstream = own_back.astype(F32)
    both = tp_gather(jnp.concatenate([own_tokens, own_back]))
    back_s = jnp.concatenate([slot[chunk:] for slot in both])

    gathered = jnp.arange(row_count)
    member_of = (own - gathered // chunk) % members
    offsets = (
        gathered % chunk // part_rows * piece_rows + member_of * part_rows + gathered % part_rows
    )
    to_gathered = (offsets[:, None] == gathered[None, :]).astype(BF16)
    to_dealt = (offsets[None, :] == gathered[:, None]).astype(BF16)
    tokens = times(to_dealt, jnp.concatenate([slot[:chunk] for slot in both]))

    kernel_taps = mixer_kernel.shape[0]
    halo = kernel_taps - 1
    local_rows = device * row_count + jnp.arange(row_count)
    halo_segment, unused = locate(
        seq_lengths, local_rows[0] - halo + jnp.arange(row_count + halo)
    )
    segment, places = locate(seq_lengths, device * row_count + offsets)
    ctx = lax.axis_index(CTX_AXES)
    group_rows = jnp.concatenate(
        [
            (lax.axis_index(GROUP_AXES) * contexts + (ctx ^ mask)) * row_count + offsets
            for mask in range(contexts)
        ]
    )
    key_segment, key_places = locate(seq_lengths, group_rows)
    allowed = (segment[None, :] == key_segment[:, None]) & (key_places[:, None] <= places[None, :])
    barred = jnp.where(allowed, 0.0, NEGATIVE).astype(BF16)
    half_dim = HD // 2
    frequency = ROPE_BASE ** (-(jnp.arange(half_dim).astype(F32) * 2.0 / HD))
    angles = places.astype(F32)[:, None] * frequency[None, :]
    cosine = jnp.cos(angles)
    sine = jnp.sin(angles)

    kernel_local = lax.dynamic_slice_in_dim(mixer_kernel, own * channels, channels, 1).astype(F32)
    mixer_in = norm_rows(tokens, gain_a).astype(BF16)
    mixer_in_other = swap_core(mixer_in)
    halo_pad = 16
    halo_in = from_behind(mixer_in[row_count - halo_pad :], 1)
    proj_a = times(jnp.concatenate([halo_in, mixer_in]), project_a)
    proj_b_part = proj_a[:, :channels]
    proj_c_part = proj_a[halo_pad:, channels : 2 * channels]
    proj_x_part = proj_a[:, 2 * channels :]
    extended = (proj_b_part * proj_x_part)[halo_pad - halo :].astype(BF16).astype(F32)
    conv_out = shortconv(extended, kernel_local, halo_segment)
    gated_rows = (proj_c_part * conv_out).astype(BF16)
    gated_parts = arrange(to_gathered, gated_rows)
    stream1, normed = add_norm(
        tp_scatter(tp_chunks(times_t(gated_parts, output_a_t))), stream0, gain_f
    )

    normed_f = tp_gather(normed)
    stream2, normed = add_norm(
        tp_scatter(ffn_forward(normed_f, first_all, steps)), stream1, gain_b
    )

    groups = H // KVH
    score_scale = HD ** (-0.5)
    qgain_f = query_gain.astype(F32)[None]
    kgain_f = key_gain.astype(F32)[None]
    attend_in = jnp.concatenate(tp_gather(normed))
    proj_b = times(attend_in, project_b)
    kv_width = 2 * HD * (proj_b.shape[1] // (HD * (groups + 2)))
    query_b, key_value = one_step(
        functools.partial(heads_kernel, groups),
        [proj_b, cosine, sine, qgain_f, kgain_f],
        [
            jax.ShapeDtypeStruct((row_count, heads_width), BF16),
            jax.ShapeDtypeStruct((row_count, kv_width), BF16),
        ],
        SMALL_LIMIT,
        "heads",
        20 * proj_b.size,
    )
    key_value_z = swap_ctx(key_value, 2)
    key_value_core = swap_core(jnp.concatenate([key_value, key_value_z]))
    key_value_all = jnp.concatenate(
        [key_value, key_value_core[:row_count], key_value_z, key_value_core[row_count:]]
    )
    attend_flops = 2 * key_value_all.shape[0] * query_b.size
    (attended,) = one_step(
        functools.partial(attend_kernel, score_scale, HD),
        [query_b, key_value_all, barred],
        [jax.ShapeDtypeStruct(query_b.shape, BF16)],
        MIDDLE_LIMIT,
        "attend",
        2 * attend_flops,
    )
    stream3, normed = add_norm(
        tp_scatter(tp_chunks(times_t(attended, output_b_t))), stream2, gain_s
    )

    normed_s = tp_gather(normed)
    d_chunks, out_chunks, keep, side = ffn_backward(
        core_ref, normed_s, [back_s], second_all, steps, True
    )
    d_stream3, back_b, gain_s_grad = norm_backward(
        tp_scatter(d_chunks), stream3, gain_s, upstream
    )
    out_others = [shift_tp(out_chunks[k], -k) for k in range(1, members)]
    side_other = swap_core(side)
    ffn_lefts = [(side, 0), (side_other, 0), (side, 1), (side_other, 1)]
    ffn_cols = steps * block
    side_start = 2 * width // block
    partial = gradient(
        ffn_lefts, keep, side_other, side_start, block, steps, padded, width, ffn_cols, 0, None
    )

    back_b = tp_gather(back_b)
    back_b, partial = lax.optimization_barrier((back_b, partial))
    second_sums = sum_chips(partial)
    attend_in_other = swap_core(attend_in)
    pair_rows = 2 * row_count
    d_query, near, cross, qgain_grad = one_step(
        functools.partial(attend_backward_kernel, score_scale),
        [*back_b, output_b_t, query_b, key_value_all, barred, proj_b, cosine, sine, qgain_f],
        [
            jax.ShapeDtypeStruct(query_b.shape, BF16),
            jax.ShapeDtypeStruct((pair_rows, kv_width), F32),
            jax.ShapeDtypeStruct((pair_rows, kv_width), BF16),
            jax.ShapeDtypeStruct((1, HD), F32),
        ],
        MIDDLE_LIMIT,
        "attend_backward",
        5 * attend_flops,
    )
    back_b = jnp.concatenate(back_b)
    back_b_other = swap_core(back_b)
    cross = swap_core(cross)
    far = (near[row_count:] + cross[row_count:].astype(F32)).astype(BF16)
    d_proj_b, kgain_grad = one_step(
        functools.partial(assemble_kernel, groups),
        [d_query, near, cross, swap_ctx(far, 2), proj_b, cosine, sine, kgain_f],
        [jax.ShapeDtypeStruct(proj_b.shape, BF16), jax.ShapeDtypeStruct((1, HD), F32)],
        SMALL_LIMIT,
        "assemble",
        20 * proj_b.size,
    )
    d_proj_b, out_others = lax.optimization_barrier((d_proj_b, out_others))
    d_stream2, back_f, gain_b_grad = norm_backward(
        tp_scatter(tp_chunks(times_t(d_proj_b, project_b))), stream2, gain_b, d_stream3
    )
    keep, send = halves(d_proj_b, attended)
    first_core = core == 0
    attend_cols = keep.shape[1]
    small_tile = 2 * (heads_width + attend_project.shape[1]) // 16
    third = gradient(
        [
            (attend_in, 0),
            (attend_in_other, 0),
            (jnp.where(first_core, attend_in, back_b), 0),
            (jnp.where(first_core, attend_in_other, back_b_other), 0),
        ],
        keep,
        swap_core(send),
        0,
        small_tile,
        attend_cols // small_tile,
        attend_project.shape[1] - attend_cols,
        width,
        ffn_cols + attend_cols,
        ffn_cols // small_tile,
        None,
    )

    back_f = tp_gather(back_f)
    back_f, third = lax.optimization_barrier((back_f, third))
    left_x, left_b = jnp.concatenate(normed_f), jnp.concatenate(back_f)
    left_others = [swap_core(left_x), swap_core(left_b)]
    d_chunks, unused, keep, side = ffn_backward(
        core_ref, normed_f, back_f, first_all, steps, False
    )
    d_chunks, left_others = lax.optimization_barrier((d_chunks, left_others))
    d_chunks, side_other = lax.optimization_barrier((d_chunks, swap_core(side)))
    ffn_lefts = [(left_x, 0), (left_others[0], 0), (left_b, 0), (left_others[1], 0)]
    partial = gradient(
        ffn_lefts,
        keep,
        side_other,
        0,
        block,
        steps,
        padded,
        width,
        ffn_cols + attend_cols,
        0,
        third,
    )

    d_parts, partial = lax.optimization_barrier((tp_scatter(d_chunks), partial))
    d_stream1, back_a, gain_f_grad = norm_backward(d_parts, stream1, gain_f, d_stream2)

    back_a = tp_gather(back_a)
    first_sums = sum_chips(partial)
    back_a = arrange(to_dealt, jnp.concatenate(back_a))
    back_a_other = swap_core(back_a)
    d_gated = times(back_a, output_a_t)
    d_cgate = d_gated * conv_out
    d_conv = d_gated * proj_c_part
    unused, pullback = jax.vjp(
        lambda ext_rows, kernel_in: shortconv(ext_rows, kernel_in, halo_segment),
        extended,
        kernel_local,
    )
    d_extended, kernel_grad = pullback(d_conv)
    returned = from_behind(d_extended[:halo], -1)
    d_product = d_extended[halo:] + jnp.concatenate(
        [jnp.zeros((row_count - halo, channels), F32), returned]
    )
    d_proj_a = jnp.concatenate(
        [
            d_product * proj_x_part[halo_pad:],
            d_cgate,
            d_product * proj_b_part[halo_pad:],
        ],
        axis=1,
    ).astype(BF16)
    stream4 = stream3 + add_parts([out_chunks[0], *out_others])
    d_chunks = tp_chunks(times_t(arrange(to_gathered, d_proj_a), project_a))
    keep, send = halves(d_proj_a, gated_rows)
    mixer_cols = keep.shape[1]
    partial = gradient(
        [
            (mixer_in, 0),
            (mixer_in_other, 0),
            (jnp.where(first_core, mixer_in, back_a), 0),
            (jnp.where(first_core, mixer_in_other, back_a_other), 0),
        ],
        keep,
        swap_core(send),
        0,
        mixer_cols,
        1,
        3 * channels - mixer_cols,
        width,
        mixer_cols,
        0,
        None,
    )
    kernel_cols = kernel_taps * channels
    gain_start = kernel_cols + 2 * HD
    shared = jnp.concatenate([kernel_grad.reshape(-1), qgain_grad[0], kgain_grad[0]])
    early_gains = [
        grad.reshape(shards, depth) for grad in (gain_f_grad, gain_b_grad, gain_s_grad)
    ]
    early_row = jnp.concatenate(
        [
            jnp.broadcast_to(shared, (shards, gain_start)),
            jnp.pad(
                jnp.concatenate(early_gains, axis=1),
                ((0, 0), (0, width - gain_start - 3 * depth)),
            ),
        ],
        axis=1,
    )
    d_parts, early_row = lax.optimization_barrier((tp_scatter(d_chunks), early_row))
    unused, d_stream0, gain_a_grad = norm_backward(d_parts, stream0, gain_a, d_stream1)

    slot_for_anchor = jnp.sum(
        jnp.where(
            my_anchor[None, :] == jnp.arange(shards)[:, None], jnp.arange(shards)[None, :], 0
        ),
        axis=1,
    )
    late_start = gain_start + 3 * depth
    late_row = jnp.pad(
        gain_a_grad.reshape(shards, depth), ((0, 0), (late_start, width - late_start - depth))
    )
    leaving = jnp.concatenate(
        [d_stream0, stream4.astype(BF16), (early_row + late_row).astype(BF16)]
    )
    line = jnp.arange(shards * piece_rows)
    target, item = line // piece_rows, line % piece_rows
    source = jnp.where(
        item < 2 * part_rows,
        item // part_rows * chunk
        + jnp.repeat(slot_for_anchor, piece_rows) * part_rows
        + item % part_rows,
        jnp.where(item == 2 * part_rows, 2 * chunk + target, -1),
    )
    to_leaving = (source[:, None] == jnp.arange(leaving.shape[0])[None, :]).astype(BF16)
    leaving = arrange(to_leaving, leaving)
    home = lax.all_to_all(
        leaving.reshape(shards, piece_rows, width),
        TOKEN_AXES,
        split_axis=0,
        concat_axis=0,
        tiled=True,
    )
    second_grads = finish(second_sums, steps, hidden)
    home, partial, second_grads = lax.optimization_barrier((home, partial, second_grads))
    place = jnp.arange(2 * chunk + 8)
    small_line = (place == 2 * chunk) | (place == 2 * chunk + 1)
    wanted = (
        place % chunk // part_rows * piece_rows
        + place // chunk * part_rows
        + place % part_rows
    )
    to_payload = jnp.where(
        (place < 2 * chunk)[:, None],
        wanted[:, None] == line[None, :],
        small_line[:, None] & (item == 2 * part_rows)[None, :],
    ).astype(BF16)
    payload = times(to_payload, home.reshape(shards * piece_rows, width))
    rounded = payload.astype(BF16).astype(F32)
    payload = jnp.where((place == 2 * chunk + 1)[:, None], payload - rounded, payload)
    last = tp_gather(payload.astype(BF16))
    mixer_home = lax.all_to_all(
        partial.reshape(shards, depth, mixer_cols),
        TOKEN_AXES,
        split_axis=0,
        concat_axis=0,
        tiled=True,
    )
    home_rows = (
        jnp.repeat(jnp.tile(send_piece, members), part_rows) * piece_rows
        + member_of * part_rows
        + gathered % part_rows
    )
    to_arrival = (home_rows[None, :] == gathered[:, None]).astype(BF16)
    input_gradient = arrange(to_arrival, jnp.concatenate([slot[:chunk] for slot in last]))
    layer_out = arrange(to_arrival, jnp.concatenate([slot[chunk : 2 * chunk] for slot in last]))
    first_sums, layer_out, input_gradient = lax.optimization_barrier(
        (first_sums, layer_out, input_gradient)
    )
    *first_grads, attend_grads = finish(first_sums, steps, hidden)
    first_grads, attend_grads, mixer_home = lax.optimization_barrier(
        (first_grads, attend_grads, mixer_home)
    )
    mixer_home = mixer_home.reshape(shards // CORES, CORES, depth, mixer_cols)
    mixer_grads = jnp.sum(mixer_home.astype(F32), axis=0)
    mixer_grads = jnp.concatenate([mixer_grads[0], mixer_grads[1]], axis=1)
    smalls = [
        slot[2 * chunk].astype(F32) + slot[2 * chunk + 1].astype(F32) for slot in last
    ]
    totals = sum(smalls)
    kernel_rows = jnp.stack([small[:kernel_cols].reshape(kernel_taps, channels) for small in smalls])
    kernel_total = jnp.concatenate(
        [
            lax.dynamic_index_in_dim(kernel_rows, (own - member) % members, 0, keepdims=False)
            for member in range(members)
        ],
        axis=1,
    )
    qgain_total = totals[kernel_cols : kernel_cols + HD]
    kgain_total = totals[kernel_cols + HD : kernel_cols + 2 * HD]
    gain_totals = totals[gain_start : gain_start + 4 * depth].reshape(4, depth)

    gateup_s_grad, down_s_grad = second_grads
    gateup_f_grad, down_f_grad = first_grads
    proj_cols = attend_project.shape[1]
    return (
        layer_out,
        input_gradient,
        gain_totals[3],
        mixer_grads[:, : 3 * channels].reshape(depth, 3, channels),
        kernel_total,
        mixer_grads[:, 3 * channels :].T,
        gain_totals[0],
        gateup_f_grad,
        down_f_grad.T,
        gain_totals[1],
        attend_grads[:, :proj_cols],
        qgain_total,
        kgain_total,
        attend_grads[:, proj_cols:].T,
        gain_totals[2],
        gateup_s_grad,
        down_s_grad.T,
    )


def solution(mesh):
    names = TOKEN_AXES + ("tp",)
    rings = mesh.shape["fsdp"] // 2, 2, mesh.shape["ctx"] // 2, 2, mesh.shape["tp"]
    tokens = P(TOKEN_AXES, None)
    rows = P(TOKEN_AXES)
    three = P(TOKEN_AXES, None, "tp")
    two = P(TOKEN_AXES, "tp")
    turned = P("tp", TOKEN_AXES)
    return jax.shard_map(
        body,
        mesh=Mesh(mesh.devices.reshape(rings), names),
        in_specs=(
            tokens, tokens, P(), P(),
            rows, three, P(), turned,
            rows, three, turned,
            rows, two, P(), P(), turned,
            rows, three, turned,
        ),
        out_specs=(
            tokens, tokens,
            rows, three, P(), turned,
            rows, three, turned,
            rows, two, P(), P(), turned,
            rows, three, turned,
        ),
        check_vma=False,
    )
```
